32 devices in a mesh: fsdp: 2 (over y), context: 8 (over z, x), tensor: 2 (over core).
Axes of the slice: x: 2, y: 2, z: 4, core: 2. Of those that a mesh axis runs over, the one named last changes fastest.
Arguments:
- tokens: bfloat16 [2, 2048, 2048], P(None, ('fsdp', 'context'), 'tensor'), may hold values from -6 to 6
- cotangent: bfloat16 [2, 2048, 2048], P(None, ('fsdp', 'context'), 'tensor'), may hold values from -6 to 6
- lengths: int32 [2, 2, 4], replicated, may hold values from 1 to 512, 1024 in all within a row
- permutation: int32 [2, 2048], replicated, may hold values from 0 to 2047, as said below
- ln_gain: bfloat16 [2048], P('fsdp'), may hold values from 0.099609375 to 1.8984375
- ln_bias: bfloat16 [2048], P('fsdp'), may hold values from -3 to 3
- qkv_weight: bfloat16 [2048, 3, 2048], P('fsdp', None, 'tensor'), may hold values from -0.125 to 0.125
- qkv_bias: bfloat16 [3, 32, 64], P(None, 'tensor', 'fsdp'), may hold values from -3 to 3
- dense_weight: bfloat16 [2048, 2048], P('tensor', 'fsdp'), may hold values from -1 to 1
- dense_bias: bfloat16 [2048], P('fsdp'), may hold values from -4.5 to 4.5
- fc1_weight: bfloat16 [2048, 8192], P('fsdp', 'tensor'), may hold values from -0.125 to 0.125
- fc1_bias: bfloat16 [32, 256], P('tensor', 'fsdp'), may hold values from -3 to 3
- fc2_weight: bfloat16 [8192, 2048], P('tensor', 'fsdp'), may hold values from -0.0625 to 0.0625
- fc2_bias: bfloat16 [2048], P('fsdp'), may hold values from -4.5 to 4.5
Outputs:
- layer_out: bfloat16 [2, 2048, 2048], P(None, ('fsdp', 'context'), 'tensor')
- grad_tokens: bfloat16 [2, 2048, 2048], P(None, ('fsdp', 'context'), 'tensor')
- grad_ln_gain: float32 [2048], P('fsdp')
- grad_ln_bias: float32 [2048], P('fsdp')
- grad_qkv_weight: float32 [2048, 3, 2048], P('fsdp', None, 'tensor')
- grad_qkv_bias: float32 [3, 32, 64], P(None, 'tensor', 'fsdp')
- grad_dense_weight: float32 [2048, 2048], P('tensor', 'fsdp')
- grad_dense_bias: float32 [2048], P('fsdp')
- grad_fc1_weight: float32 [2048, 8192], P('fsdp', 'tensor')
- grad_fc1_bias: float32 [32, 256], P('tensor', 'fsdp')
- grad_fc2_weight: float32 [8192, 2048], P('tensor', 'fsdp')
- grad_fc2_bias: float32 [2048], P('fsdp')
The draws below stay inside these ranges and needn't reach their ends.
Inputs may be any that keep to these rules, and one draw needn't show every extreme that they name: Each micro-batch's lengths of one pack sum to 1024. Each row is a permutation; the 128 arriving tokens at rows s * 128 to (s + 1) * 128 - 1 take exactly 8 positions of every aligned block of 128 layout positions.
All inputs are finite; a program needn't handle non-finite values.
Results may differ from the reference program's by a relative error of at most 0.033.
Values may be sent and summed in bfloat16 or wider, within the bound.
A program may use at most 320 MiB of HBM per device.

```python
import math
import jax
import jax.numpy as jnp
import numpy as np
from jax import lax

D = 2048
H = 32
HD = 64
ROT = 32
FF = 8192
TOK_CTX = 128
MICRO = 2
PACK_LEN = 1024
PACKS = 2
TOKENS = 2048
SEQS = 4
LONGEST = 512


def draw_permutation(key, part):
    total = TOKENS
    count = TOK_CTX
    groups = total // count
    share = count // groups

    def single_batch(batch_key):
        key_slots, key_places = jax.random.split(batch_key)
        slot_perm = jax.vmap(lambda subkey: jax.random.permutation(subkey, count))(jax.random.split(key_slots, groups))
        place_perm = jax.vmap(lambda subkey: jax.random.permutation(subkey, count))(jax.random.split(key_places, groups))
        entry = jnp.arange(count, dtype=jnp.int32)
        destination = entry // share
        within = entry % share
        source = jnp.arange(groups, dtype=jnp.int32)[:, None]
        position = place_perm[destination[None, :], source * share + within[None, :]]
        target = destination[None, :] * count + position
        flat_slot = source * count + slot_perm
        return jnp.zeros(total, jnp.int32).at[flat_slot.reshape(-1)].set(target.reshape(-1).astype(jnp.int32))
    return jax.vmap(single_batch)(jax.random.split(key, MICRO)).astype(jnp.int32)


def steps_of(key, dims, pieces, low, largest):
    def one(axis_at, blocks):
        heights = jax.random.uniform(jax.random.fold_in(jax.random.fold_in(key, 6), axis_at), (blocks,), jnp.float32, low / len(pieces), largest / len(pieces))
        return jnp.repeat(jnp.exp(heights), dims[axis_at] // blocks).reshape((-1,) + (1,) * (len(dims) - axis_at - 1))

    level = one(*pieces[0])
    for cut in pieces[1:]:
        level = level * one(*cut)
    return level


def length_profile(amount, total, reach, skew):
    weights = [(1 << 20) // math.isqrt(standing ** skew) + 1 for standing in range(2, amount + 1)]
    rest, given = total - reach - (amount - 1), [1] * (amount - 1)
    while rest > 0:
        movable = [i for i in range(amount - 1) if given[i] < reach]
        mass, budget = sum([weights[i] for i in movable]), rest
        for i in movable:
            extra = min(reach - given[i], max(1, budget * weights[i] // mass), rest)
            given[i] = given[i] + extra
            rest = rest - extra
    return np.array([reach] + given)


def ragged(rng, amount, total, reach, slope):
    if amount == 2:
        one = jax.random.randint(rng, (), max(1, total - reach), min(reach, total - 1) + 1)
        return jnp.stack([one, total - one])
    tallies = jnp.asarray(length_profile(amount, total, reach, slope), jnp.int32)
    couples = (amount - 1) // 2
    donor, receiver = tallies[1:1 + 2 * couples:2], tallies[2:2 + 2 * couples:2]
    room = jnp.minimum(donor - 1, reach - receiver)
    shifted = jax.random.randint(jax.random.fold_in(rng, 1), (couples,), 0, 1 << 20) % (room + 1)
    tallies = tallies.at[1:1 + 2 * couples:2].set(donor - shifted).at[2:2 + 2 * couples:2].set(receiver + shifted)
    return tallies[jax.random.permutation(jax.random.fold_in(rng, 2), amount)]


def scatter_about(rng, extent, width, limit, cuts=(), kind=jnp.bfloat16):
    level = steps_of(rng, extent, cuts, -0.22, 0.18) if cuts else 1.0
    entries = jax.random.normal(rng, extent, jnp.float32) * width * level
    return jnp.minimum(jnp.maximum(entries, -limit), limit).astype(kind)


def setup_inputs(seed: int = 0) -> dict:
    key_of = jax.random.split(jax.random.key(seed), 15)
    return {
        "tokens": scatter_about(key_of[0], (MICRO, TOKENS, D), 1.0, 6.0, ((1, 16), (2, 2))),
        "cotangent": scatter_about(key_of[1], (MICRO, TOKENS, D), 1.0, 6.0, ((1, 16), (2, 2))),
        "lengths": jax.vmap(lambda own: ragged(own, SEQS, PACK_LEN, LONGEST, 2))(jax.random.split(key_of[2], MICRO * PACKS)).reshape((MICRO, PACKS, SEQS)).astype(jnp.int32),
        "permutation": draw_permutation(jax.random.fold_in(key_of[14], 71), 0),
        "ln_gain": jnp.clip(1.0 + 0.18 * jax.random.normal(key_of[4], (D,), jnp.float32), 0.099609375, 1.8984375).astype(jnp.bfloat16),
        "ln_bias": scatter_about(key_of[5], (D,), 0.5, 3.0, ((0, 2),)),
        "qkv_weight": scatter_about(key_of[6], (D, 3, D), D ** -0.5, 0.125, ((0, 2), (2, 2))),
        "qkv_bias": scatter_about(key_of[7], (3, H, HD), 0.5, 3.0, ((1, 2), (2, 2))),
        "dense_weight": scatter_about(key_of[8], (D, D), (D // 64) ** -0.5, 1.0, ((0, 2), (1, 2))),
        "dense_bias": scatter_about(key_of[9], (D,), 0.75, 4.5, ((0, 2),)),
        "fc1_weight": scatter_about(key_of[10], (D, FF), D ** -0.5, 0.125, ((0, 2), (1, 2))),
        "fc1_bias": scatter_about(key_of[11], (H, FF // H), 0.5, 3.0, ((0, 2), (1, 2))),
        "fc2_weight": scatter_about(key_of[12], (FF, D), FF ** -0.5, 0.0625, ((0, 2), (1, 2))),
        "fc2_bias": scatter_about(key_of[13], (D,), 0.75, 4.5, ((0, 2),)),
    }


EPSILON = 1e-05
ROPE_BASE = 10000.0
NEG_FILL = -1e+30
HIGHEST = lax.Precision.HIGHEST

@jax.custom_vjp
def low(v):
    return lax.optimization_barrier(v.astype(jnp.bfloat16)).astype(jnp.float32)

@jax.custom_vjp
def low_back(v):
    return v

def low_keep(v):
    return (low(v), None)

def low_pass(kept, grad):
    return (grad,)

def back_keep(v):
    return (v, None)

def back_low(kept, grad):
    return (low(grad),)
low.defvjp(low_keep, low_pass)
low_back.defvjp(back_keep, back_low)

def layer_norm(values, gain, shift):
    center = values - lax.optimization_barrier(jnp.mean(values, axis=-1, keepdims=True))
    spread = lax.optimization_barrier(jnp.mean(center * center, axis=-1, keepdims=True))
    return center * lax.rsqrt(spread + EPSILON) * gain + shift

def rotate(values, position):
    half = ROT // 2
    freq = ROPE_BASE ** (-2.0 * jnp.arange(half, dtype=jnp.float32) / ROT)
    angles = position[:, None] * freq[None, :]
    cosine = jnp.cos(angles)[:, None, :]
    sine = jnp.sin(angles)[:, None, :]
    first = values[..., :half]
    second = values[..., half:ROT]
    return jnp.concatenate([first * cosine - second * sine, second * cosine + first * sine, values[..., ROT:]], axis=-1)

def segment_layout(length_row, places):
    ends = jnp.cumsum(length_row).astype(jnp.int32)
    starts = ends - length_row
    segment = lax.optimization_barrier(jnp.sum((places[:, None] >= ends[None, :]).astype(jnp.int32), axis=1))
    match = segment[:, None] == jnp.arange(length_row.shape[0], dtype=jnp.int32)[None, :]
    begin = lax.optimization_barrier(jnp.sum(jnp.where(match, starts[None, :], 0), axis=1))
    return (segment, (places - begin).astype(jnp.int32))

def attention(query, keys, values, segment, places):
    total_rows = query.shape[0]
    block_rows = min(512, total_rows)
    count = total_rows // block_rows
    scale = HD ** (-0.5)

    def one_block(inputs):
        query_block, segment_block, place_block = inputs
        scores = low_back(jnp.einsum('qhe,khe->hqk', query_block, keys, precision=HIGHEST) * scale)
        allowed = (segment_block[:, None] == segment[None, :]) & (places[None, :] <= place_block[:, None])
        scores = jnp.where(allowed[None], scores, NEG_FILL)
        weights_p = low(jax.nn.softmax(scores, axis=-1))
        return jnp.einsum('hqk,khe->qhe', weights_p, values, precision=HIGHEST)
    result = lax.map(jax.checkpoint(one_block), (query.reshape(count, block_rows, H, HD), segment.reshape(count, block_rows), places.reshape(count, block_rows)))
    return result.reshape(total_rows, H, HD)

def reference(tokens, cotangent, lengths, permutation, ln_gain, ln_bias, qkv_weight, qkv_bias, dense_weight, dense_bias, fc1_weight, fc1_bias, fc2_weight, fc2_bias):
    inverse = jnp.argsort(permutation, axis=1).astype(jnp.int32)
    layout = jnp.take_along_axis(tokens.astype(jnp.float32), inverse[:, :, None], axis=1)
    grads_in = jnp.take_along_axis(cotangent.astype(jnp.float32), inverse[:, :, None], axis=1)
    pack_len = TOKENS // PACKS
    pack_count = MICRO * PACKS
    places = jnp.arange(pack_len, dtype=jnp.int32)
    segments, positions = jax.vmap(lambda length_row: segment_layout(length_row, places))(lengths.reshape(pack_count, SEQS))
    params = (ln_gain.astype(jnp.float32), ln_bias.astype(jnp.float32), qkv_weight.astype(jnp.float32), qkv_bias.astype(jnp.float32), dense_weight.astype(jnp.float32), dense_bias.astype(jnp.float32), fc1_weight.astype(jnp.float32), fc1_bias.astype(jnp.float32), fc2_weight.astype(jnp.float32), fc2_bias.astype(jnp.float32))

    def forward(weights, inputs):
        gain, shift, w_qkv, b_qkv, w_dense, b_dense, w_fc1, b_fc1, w_fc2, b_fc2 = weights

        def pack_step(carry, item):
            x_pack, segment_pack, position_pack = item
            normed = low(layer_norm(x_pack, gain, shift))
            qkv = low_back(jnp.einsum('rd,dce->rce', normed, w_qkv, precision=HIGHEST) + b_qkv.reshape(3, D))
            angle_pos = position_pack.astype(jnp.float32)
            query = low(rotate(qkv[:, 0].reshape(-1, H, HD), angle_pos))
            key_rows = low(rotate(qkv[:, 1].reshape(-1, H, HD), angle_pos))
            value_rows = low(qkv[:, 2].reshape(-1, H, HD))
            attended = low_back(low(attention(query, key_rows, value_rows, segment_pack, places).reshape(-1, D)))
            pre_act = low_back(jnp.dot(normed, w_fc1, precision=HIGHEST) + b_fc1.reshape(FF))
            activ = low(jax.nn.gelu(pre_act, approximate=True))
            result = x_pack + jnp.dot(attended, w_dense, precision=HIGHEST) + b_dense + jnp.dot(activ, w_fc2, precision=HIGHEST) + b_fc2
            return (carry, result)
        _, outputs = lax.scan(pack_step, jnp.zeros((), jnp.float32), (inputs, segments, positions))
        return outputs
    result, pullback = jax.vjp(forward, params, layout.reshape(pack_count, pack_len, D))
    grad_params, grad_layout = pullback(grads_in.reshape(pack_count, pack_len, D))
    layer_out = jnp.take_along_axis(result.reshape(MICRO, TOKENS, D), permutation[:, :, None], axis=1).astype(jnp.bfloat16)
    grad_tokens = jnp.take_along_axis(grad_layout.reshape(MICRO, TOKENS, D), permutation[:, :, None], axis=1).astype(jnp.bfloat16)
    return (layer_out, grad_tokens, grad_params[0], grad_params[1], grad_params[2], grad_params[3], grad_params[4], grad_params[5], grad_params[6], grad_params[7], grad_params[8], grad_params[9])
```

```python
from functools import partial

import jax
import jax.numpy as jnp
from jax import lax
from jax.experimental import pallas as pl
from jax.experimental.pallas import tpu as pltpu
from jax.sharding import Mesh
from jax.sharding import PartitionSpec as P

ROT = 32
FS, CT, TE = "fsdp", "context", "tensor"


EPSILON = 1e-05
ROPE_BASE = 10000.0
NEG_FILL = -1e30


def layer_norm(values, gain, shift):
    center = values - jnp.mean(values, axis=-1, keepdims=True)
    spread = jnp.mean(center * center, axis=-1, keepdims=True)
    return center * lax.rsqrt(spread + EPSILON) * gain + shift


def rotate(values, position):
    half = ROT // 2
    freq = ROPE_BASE ** (-2.0 * jnp.arange(half, dtype=jnp.float32) / ROT)
    angles = position[:, None] * freq[None, :]
    cosine = jnp.cos(angles)[:, None, :]
    sine = jnp.sin(angles)[:, None, :]
    first = values[..., :half]
    second = values[..., half:ROT]
    return jnp.concatenate(
        [first * cosine - second * sine, second * cosine + first * sine, values[..., ROT:]], axis=-1
    )


def segment_layout(length_row, places):
    count = length_row.shape[0]
    upto = jnp.arange(count)[:, None] >= jnp.arange(count)[None, :]
    ends = jnp.sum(jnp.where(upto, length_row[None, :], 0), axis=1)
    starts = ends - length_row
    segment = jnp.sum((places[:, None] >= ends[None, :]).astype(jnp.int32), axis=1)
    match = segment[:, None] == jnp.arange(length_row.shape[0], dtype=jnp.int32)[None, :]
    begin = jnp.sum(jnp.where(match, starts[None, :], 0), axis=1)
    return (segment, places - begin)


def rows_block(source, block_index, block_rows, head_count, head_width):
    return lax.dynamic_slice_in_dim(source, block_index * block_rows, block_rows, 0).reshape(
        block_rows, head_count, head_width
    )


def pair_mask(query_segment, query_place, key_segment, key_place):
    return (
        (query_segment[:, None] == key_segment[None, :])
        & (key_place[None, :] <= query_place[:, None])
    )[None]


def key_scores(
    query,
    keys_all,
    key_segment,
    key_place,
    query_segment,
    query_place,
    block_index,
    block_rows,
    scale,
):
    row_count, head_count, head_width = query.shape
    key_block = rows_block(keys_all, block_index, block_rows, head_count, head_width)
    scores = (
        jnp.einsum("qhe,khe->hqk", query, key_block, preferred_element_type=jnp.float32) * scale
    )
    segment_block = lax.dynamic_slice_in_dim(key_segment, block_index * block_rows, block_rows, 0)
    place_block = lax.dynamic_slice_in_dim(key_place, block_index * block_rows, block_rows, 0)
    return (scores, pair_mask(query_segment, query_place, segment_block, place_block), key_block)


def attend_forward(
    query,
    keys_all,
    values_all,
    key_segment,
    key_place,
    query_segment,
    query_place,
    first_block,
    last_block,
    block_rows,
    scale,
):
    row_count, head_count, head_width = query.shape

    def find_peak(block_index, carry):
        peak, total = carry
        scores, allowed, _ = key_scores(
            query,
            keys_all,
            key_segment,
            key_place,
            query_segment,
            query_place,
            block_index,
            block_rows,
            scale,
        )
        fresh = jnp.maximum(peak, jnp.max(jnp.where(allowed, scores, NEG_FILL), axis=-1))
        added = jnp.sum(jnp.where(allowed, jnp.exp(scores - fresh[..., None]), 0.0), axis=-1)
        return (fresh, total * jnp.exp(peak - fresh) + added)

    start_carry = (
        jnp.full((head_count, row_count), NEG_FILL, jnp.float32),
        jnp.zeros((head_count, row_count), jnp.float32),
    )
    peak, total = lax.fori_loop(first_block, last_block + 1, find_peak, start_carry)
    log_total = peak + jnp.log(total)

    def weigh(block_index, accum):
        scores, allowed, _ = key_scores(
            query,
            keys_all,
            key_segment,
            key_place,
            query_segment,
            query_place,
            block_index,
            block_rows,
            scale,
        )
        attend_weights = jnp.where(allowed, jnp.exp(scores - log_total[..., None]), 0.0).astype(
            jnp.bfloat16
        )
        values = rows_block(values_all, block_index, block_rows, head_count, head_width)
        return accum + jnp.einsum(
            "hqk,khe->qhe", attend_weights, values, preferred_element_type=jnp.float32
        )

    attended = lax.fori_loop(
        first_block, last_block + 1, weigh, jnp.zeros(query.shape, jnp.float32)
    )
    return (attended, log_total)


def attend_backward(
    query,
    keys_all,
    values_all,
    key_segment,
    key_place,
    query_segment,
    query_place,
    first_block,
    last_block,
    block_rows,
    scale,
    log_total,
    grad_out,
    delta,
):
    row_count, head_count, head_width = query.shape

    def step_back(block_index, carry):
        scores, allowed, key_block = key_scores(
            query,
            keys_all,
            key_segment,
            key_place,
            query_segment,
            query_place,
            block_index,
            block_rows,
            scale,
        )
        values = rows_block(values_all, block_index, block_rows, head_count, head_width)
        attend_weights = jnp.where(allowed, jnp.exp(scores - log_total[..., None]), 0.0)
        grad_weights = jnp.einsum(
            "qhe,khe->hqk", grad_out, values, preferred_element_type=jnp.float32
        )
        grad_scores = (attend_weights * (grad_weights - delta[..., None])).astype(jnp.bfloat16)
        grad_query = (
            carry[0]
            + jnp.einsum("hqk,khe->qhe", grad_scores, key_block, preferred_element_type=jnp.float32)
            * scale
        )
        grad_keys, grad_values = (carry[1], carry[2])
        key_part = (
            jnp.einsum("hqk,qhe->khe", grad_scores, query, preferred_element_type=jnp.float32)
            * scale
        ).reshape(block_rows, head_count * head_width)
        value_part = jnp.einsum(
            "hqk,qhe->khe",
            attend_weights.astype(jnp.bfloat16),
            grad_out,
            preferred_element_type=jnp.float32,
        ).reshape(block_rows, head_count * head_width)
        block_start = block_index * block_rows
        grad_keys = lax.dynamic_update_slice_in_dim(
            grad_keys,
            lax.dynamic_slice_in_dim(grad_keys, block_start, block_rows, 0) + key_part,
            block_start,
            0,
        )
        grad_values = lax.dynamic_update_slice_in_dim(
            grad_values,
            lax.dynamic_slice_in_dim(grad_values, block_start, block_rows, 0) + value_part,
            block_start,
            0,
        )
        return (grad_query, grad_keys, grad_values)

    start_carry = (
        jnp.zeros(query.shape, jnp.float32),
        jnp.zeros(keys_all.shape, jnp.float32),
        jnp.zeros(values_all.shape, jnp.float32),
    )
    return lax.fori_loop(first_block, last_block + 1, step_back, start_carry)


def body(
    tokens,
    cotangent,
    lengths,
    permutation,
    ln_gain,
    ln_bias,
    qkv_weight,
    qkv_bias,
    dense_weight,
    dense_bias,
    fc1_weight,
    fc1_bias,
    fc2_weight,
    fc2_bias,
):
    gain_all, shift_all, w_qkv, b_qkv, w_dense, b_dense, w_fc1, b_fc1, w_fc2, b_fc2 = (
        lax.all_gather(ln_gain, FS, axis=0, tiled=True),
        lax.all_gather(ln_bias, FS, axis=0, tiled=True),
        lax.all_gather(qkv_weight, FS, axis=0, tiled=True),
        lax.all_gather(qkv_bias, FS, axis=2, tiled=True),
        lax.all_gather(dense_weight, FS, axis=1, tiled=True),
        lax.all_gather(dense_bias, FS, axis=0, tiled=True),
        lax.all_gather(fc1_weight, FS, axis=0, tiled=True),
        lax.all_gather(fc1_bias, FS, axis=1, tiled=True),
        lax.all_gather(fc2_weight, FS, axis=1, tiled=True),
        lax.all_gather(fc2_bias, FS, axis=0, tiled=True),
    )
    gain_f = gain_all.astype(jnp.float32)
    shift_f = shift_all.astype(jnp.float32)
    local_width = w_qkv.shape[2]
    head_count = b_qkv.shape[1]
    head_width = b_qkv.shape[2]
    hidden_local = w_fc1.shape[1]
    qkv_shift = b_qkv.astype(jnp.float32).reshape(3, local_width)
    fc1_shift = b_fc1.astype(jnp.float32).reshape(hidden_local)
    micro_count = tokens.shape[0]
    row_count = tokens.shape[1]
    feature_share = tokens.shape[2]
    all_rows = micro_count * row_count
    pack_length = row_count * lax.axis_size(CT)
    block_rows = min(512, pack_length)
    group_index = lax.axis_index((FS, CT))
    pack_index = lax.axis_index(FS)
    context_index = lax.axis_index(CT)
    tensor_index = lax.axis_index(TE)
    out_shift = lax.dynamic_slice_in_dim(
        b_dense.astype(jnp.float32) + b_fc2.astype(jnp.float32),
        tensor_index * feature_share,
        feature_share,
        0,
    )
    scale = head_width ** (-0.5)
    counting = jnp.arange(row_count, dtype=jnp.int32)
    pack_places = jnp.arange(pack_length, dtype=jnp.int32)
    query_place = lax.dynamic_slice_in_dim(pack_places, context_index * row_count, row_count, 0)
    last_query_block = (context_index * row_count + row_count - 1) // block_rows
    sent_tokens = []
    sent_cot = []
    slot_sources = []
    arrive_slots = []
    return_orders = []
    key_segments = []
    query_segments = []
    query_positions = []
    first_blocks = []
    length_rows = []
    for micro_index in range(micro_count):
        perm_row = permutation[micro_index]
        own_targets = lax.dynamic_slice_in_dim(perm_row, group_index * row_count, row_count, 0)
        send_order = jnp.argsort(own_targets // row_count, stable=True)
        return_orders.append(jnp.zeros(row_count, jnp.int32).at[send_order].set(counting))
        here = perm_row // row_count == group_index
        arriving = jnp.argsort(jnp.where(here, 0, 1), stable=True)[:row_count]
        arrive_slot = perm_row[arriving] % row_count
        arrive_slots.append(arrive_slot)
        slot_sources.append(jnp.zeros(row_count, jnp.int32).at[arrive_slot].set(counting))
        sent_tokens.append(tokens[micro_index][send_order])
        sent_cot.append(cotangent[micro_index][send_order])
        length_row = lax.dynamic_index_in_dim(lengths[micro_index], pack_index, 0, keepdims=False)
        length_rows.append(length_row)
        key_segment, key_position = segment_layout(length_row, pack_places)
        key_segments.append(key_segment)
        query_segments.append(
            lax.dynamic_slice_in_dim(key_segment, context_index * row_count, row_count, 0)
        )
        query_position = lax.dynamic_slice_in_dim(
            key_position, context_index * row_count, row_count, 0
        )
        query_positions.append(query_position)
        first_blocks.append((query_place[0] - query_position[0]) // block_rows)
    received = (
        lax.all_to_all(
            jnp.stack(sent_tokens), (FS, CT), split_axis=1, concat_axis=1, tiled=True
        ),
        lax.all_to_all(
            jnp.stack(sent_cot), (FS, CT), split_axis=1, concat_axis=1, tiled=True
        ),
    )
    own_tokens = jnp.concatenate(
        [received[0][m][slot_sources[m]] for m in range(micro_count)], axis=0
    )
    own_cot = jnp.concatenate([received[1][m][slot_sources[m]] for m in range(micro_count)], axis=0)
    full_tokens, full_cot = (
        lax.all_gather(own_tokens, TE, axis=1, tiled=True),
        lax.all_gather(own_cot, TE, axis=1, tiled=True),
    )
    normed, norm_back = jax.vjp(layer_norm, full_tokens.astype(jnp.float32), gain_f, shift_f)
    normed_b = normed.astype(jnp.bfloat16)
    qkv = jnp.einsum("rd,dce->rce", normed_b, w_qkv, preferred_element_type=jnp.float32) + qkv_shift
    angle_pos = jnp.concatenate(query_positions, axis=0).astype(jnp.float32)
    query_rot, rope_back = jax.vjp(
        lambda inner: rotate(inner, angle_pos), qkv[:, 0].reshape(all_rows, head_count, head_width)
    )
    key_rot = rotate(qkv[:, 1].reshape(all_rows, head_count, head_width), angle_pos)
    query_b = query_rot.astype(jnp.bfloat16)
    key_b = key_rot.reshape(all_rows, local_width).astype(jnp.bfloat16)
    value_b = qkv[:, 2].astype(jnp.bfloat16)
    keys_all, values_all = (
        lax.all_gather(
            key_b.reshape(micro_count, row_count, local_width), CT, axis=1, tiled=True
        ),
        lax.all_gather(
            value_b.reshape(micro_count, row_count, local_width), CT, axis=1, tiled=True
        ),
    )
    attended_list = []
    log_list = []
    for micro_index in range(micro_count):
        rows = slice(micro_index * row_count, (micro_index + 1) * row_count)
        attended_one, log_one = attend_forward(
            query_b[rows],
            keys_all[micro_index],
            values_all[micro_index],
            key_segments[micro_index],
            pack_places,
            query_segments[micro_index],
            query_place,
            first_blocks[micro_index],
            last_query_block,
            block_rows,
            scale,
        )
        attended_list.append(attended_one)
        log_list.append(log_one)
    attended = jnp.concatenate(attended_list, axis=0)
    attended_b = attended.reshape(all_rows, local_width).astype(jnp.bfloat16)
    pre_act = jnp.dot(normed_b, w_fc1, preferred_element_type=jnp.float32) + fc1_shift
    activ, gelu_back = jax.vjp(partial(jax.nn.gelu, approximate=True), pre_act)
    activ_b = activ.astype(jnp.bfloat16)
    partial_out = jnp.dot(attended_b, w_dense, preferred_element_type=jnp.float32) + jnp.dot(
        activ_b, w_fc2, preferred_element_type=jnp.float32
    )
    branch = lax.psum_scatter(
        partial_out.astype(jnp.bfloat16), TE, scatter_dimension=1, tiled=True
    ).astype(jnp.float32)
    layer_rows = (own_tokens.astype(jnp.float32) + branch + out_shift).astype(jnp.bfloat16)
    grad_attended = jnp.einsum(
        "rd,ed->re", full_cot, w_dense, preferred_element_type=jnp.float32
    ).astype(jnp.bfloat16)
    grad_activ = jnp.einsum("rd,hd->rh", full_cot, w_fc2, preferred_element_type=jnp.float32)
    grad_pre = gelu_back(grad_activ)[0].astype(jnp.bfloat16)
    grad_heads = grad_attended.reshape(all_rows, head_count, head_width)
    delta_list = []
    for micro_index in range(micro_count):
        rows = slice(micro_index * row_count, (micro_index + 1) * row_count)
        delta_list.append(
            jnp.einsum(
                "qhe,qhe->hq", grad_heads[rows].astype(jnp.float32), attended_list[micro_index]
            )
        )
    query_grads = []
    key_parts = []
    value_parts = []
    for micro_index in range(micro_count):
        rows = slice(micro_index * row_count, (micro_index + 1) * row_count)
        grad_query_one, grad_keys_one, grad_values_one = attend_backward(
            query_b[rows],
            keys_all[micro_index],
            values_all[micro_index],
            key_segments[micro_index],
            pack_places,
            query_segments[micro_index],
            query_place,
            first_blocks[micro_index],
            last_query_block,
            block_rows,
            scale,
            log_list[micro_index],
            grad_heads[rows],
            delta_list[micro_index],
        )
        query_grads.append(grad_query_one)
        key_parts.append(grad_keys_one)
        value_parts.append(grad_values_one)
    grad_keys, grad_values = (
        lax.psum_scatter(
            jnp.stack(key_parts).astype(jnp.bfloat16), CT, scatter_dimension=1, tiled=True
        ).astype(jnp.float32),
        lax.psum_scatter(
            jnp.stack(value_parts).astype(jnp.bfloat16), CT, scatter_dimension=1, tiled=True
        ).astype(jnp.float32),
    )
    grad_keys = grad_keys.reshape(all_rows, local_width)
    grad_values = grad_values.reshape(all_rows, local_width)
    grad_query = jnp.concatenate(query_grads, axis=0)
    grad_query_pre = rope_back(grad_query)[0].reshape(all_rows, local_width)
    grad_key_pre = rope_back(grad_keys.reshape(all_rows, head_count, head_width))[0].reshape(
        all_rows, local_width
    )
    grad_qkv = jnp.stack([grad_query_pre, grad_key_pre, grad_values], axis=1).astype(jnp.bfloat16)
    grad_normed_part = jnp.einsum(
        "rce,dce->rd", grad_qkv, w_qkv, preferred_element_type=jnp.float32
    ) + jnp.einsum("rh,dh->rd", grad_pre, w_fc1, preferred_element_type=jnp.float32)
    grad_normed = lax.psum(grad_normed_part.astype(jnp.bfloat16), TE).astype(jnp.float32)
    grad_input, grad_gain, grad_shift = norm_back(grad_normed)
    cot_f = full_cot.astype(jnp.float32)
    grad_own = lax.dynamic_slice_in_dim(
        cot_f + grad_input, tensor_index * feature_share, feature_share, 1
    ).astype(jnp.bfloat16)
    cot_total = jnp.sum(cot_f, axis=0)
    part_qkv_w = jnp.einsum("rd,rce->dce", normed_b, grad_qkv, preferred_element_type=jnp.float32)
    part_qkv_b = jnp.sum(grad_qkv.astype(jnp.float32), axis=0).reshape(b_qkv.shape)
    part_dense_w = jnp.einsum("re,rd->ed", attended_b, full_cot, preferred_element_type=jnp.float32)
    part_fc1_w = jnp.einsum("rd,rh->dh", normed_b, grad_pre, preferred_element_type=jnp.float32)
    part_fc1_b = jnp.sum(grad_pre.astype(jnp.float32), axis=0).reshape(b_fc1.shape)
    part_fc2_w = jnp.einsum("rh,rd->hd", activ_b, full_cot, preferred_element_type=jnp.float32)
    back_rows = []
    back_grads = []
    for micro_index in range(micro_count):
        rows = slice(micro_index * row_count, (micro_index + 1) * row_count)
        back_rows.append(layer_rows[rows][arrive_slots[micro_index]])
        back_grads.append(grad_own[rows][arrive_slots[micro_index]])
    returned = (
        lax.all_to_all(
            jnp.stack(back_rows), (FS, CT), split_axis=1, concat_axis=1, tiled=True
        ),
        lax.all_to_all(
            jnp.stack(back_grads), (FS, CT), split_axis=1, concat_axis=1, tiled=True
        ),
    )
    layer_out = jnp.stack([returned[0][m][return_orders[m]] for m in range(micro_count)])
    grad_tokens = jnp.stack([returned[1][m][return_orders[m]] for m in range(micro_count)])
    shares = (
        lax.psum_scatter(
            grad_gain.astype(jnp.bfloat16), (FS, CT), scatter_dimension=0, tiled=True
        ).astype(jnp.float32),
        lax.psum_scatter(
            grad_shift.astype(jnp.bfloat16), (FS, CT), scatter_dimension=0, tiled=True
        ).astype(jnp.float32),
        lax.psum_scatter(
            part_qkv_w.astype(jnp.bfloat16), (FS, CT), scatter_dimension=0, tiled=True
        ).astype(jnp.float32),
        lax.psum_scatter(
            part_qkv_b.astype(jnp.bfloat16), (FS, CT), scatter_dimension=2, tiled=True
        ).astype(jnp.float32),
        lax.psum_scatter(
            part_dense_w.astype(jnp.bfloat16), (FS, CT), scatter_dimension=1, tiled=True
        ).astype(jnp.float32),
        lax.psum_scatter(
            cot_total.astype(jnp.bfloat16), (FS, CT), scatter_dimension=0, tiled=True
        ).astype(jnp.float32),
        lax.psum_scatter(
            part_fc1_w.astype(jnp.bfloat16), (FS, CT), scatter_dimension=0, tiled=True
        ).astype(jnp.float32),
        lax.psum_scatter(
            part_fc1_b.astype(jnp.bfloat16), (FS, CT), scatter_dimension=1, tiled=True
        ).astype(jnp.float32),
        lax.psum_scatter(
            part_fc2_w.astype(jnp.bfloat16), (FS, CT), scatter_dimension=1, tiled=True
        ).astype(jnp.float32),
        lax.psum_scatter(
            cot_total.astype(jnp.bfloat16), (FS, CT), scatter_dimension=0, tiled=True
        ).astype(jnp.float32),
    )
    reduced = (
        lax.all_gather(shares[0].astype(jnp.bfloat16), CT, axis=0, tiled=True).astype(
            jnp.float32
        ),
        lax.all_gather(shares[1].astype(jnp.bfloat16), CT, axis=0, tiled=True).astype(
            jnp.float32
        ),
        lax.all_gather(shares[2].astype(jnp.bfloat16), CT, axis=0, tiled=True).astype(
            jnp.float32
        ),
        lax.all_gather(shares[3].astype(jnp.bfloat16), CT, axis=2, tiled=True).astype(
            jnp.float32
        ),
        lax.all_gather(shares[4].astype(jnp.bfloat16), CT, axis=1, tiled=True).astype(
            jnp.float32
        ),
        lax.all_gather(shares[5].astype(jnp.bfloat16), CT, axis=0, tiled=True).astype(
            jnp.float32
        ),
        lax.all_gather(shares[6].astype(jnp.bfloat16), CT, axis=0, tiled=True).astype(
            jnp.float32
        ),
        lax.all_gather(shares[7].astype(jnp.bfloat16), CT, axis=1, tiled=True).astype(
            jnp.float32
        ),
        lax.all_gather(shares[8].astype(jnp.bfloat16), CT, axis=1, tiled=True).astype(
            jnp.float32
        ),
        lax.all_gather(shares[9].astype(jnp.bfloat16), CT, axis=0, tiled=True).astype(
            jnp.float32
        ),
    )
    return (
        layer_out,
        grad_tokens,
        reduced[0],
        reduced[1],
        reduced[2],
        reduced[3],
        reduced[4],
        reduced[5],
        reduced[6],
        reduced[7],
        reduced[8],
        reduced[9],
    )


MESH = pl.DeviceIdType.MESH
AXES = ("y", "h", "l", "x", "t")
BLOCK = 256
SPAN = 512


def fits(mesh):
    return (mesh.shape[FS], mesh.shape[CT], mesh.shape[TE]) == (2, 8, 2)


def place():
    return tuple(lax.axis_index(a) for a in AXES)


def greet(peers):
    barrier = pltpu.get_barrier_semaphore()
    total = 0
    for device, there in peers:
        if there is True:
            pl.semaphore_signal(barrier, inc=1, device_id=device, device_id_type=MESH)
            total += 1
        else:

            @pl.when(there)
            def _(device=device):
                pl.semaphore_signal(barrier, inc=1, device_id=device, device_id_type=MESH)

            total = total + there.astype(jnp.int32)
    pl.semaphore_wait(barrier, total)


def spread_kernel(
    tok, cot, w_q, w_d, w_1, w_2, small, tok_all, cot_all, q_out, d_out, o_1, o_2, small_out,
    local_sem, send_sem, recv_sem,
):
    y, h, l, x, t = place()
    z = 2 * h + l
    rows, half = tok.shape[1], tok.shape[2]
    other_y, other_x, other_t = {"y": 1 - y}, {"x": 1 - x}, {"t": 1 - t}

    def along(zz):
        return {"h": zz // 2, "l": lax.rem(zz, 2)}

    greet(
        [(other_y, True), (other_x, True), (other_t, True)]
        + [(along(lax.max(z - 1, 0)), z > 0), (along(lax.min(z + 1, 3)), z < 3)]
    )
    units = [(tok, tok_all, 0, 1), (tok, tok_all, 1, 1), (cot, cot_all, 0, 2)]
    numbers = {}

    def number(key):
        return numbers.setdefault(key, len(numbers))

    def region(unit, chunk, core):
        _, out, m, n = units[unit]
        dy, dx, way, k = chunk
        yy = 1 - y if dy else y
        xx = 1 - x if dx else x
        zz = z - k if way == "up" else z + k
        group = yy * 8 + zz * 2 + xx
        return out.at[
            pl.ds(m, n),
            pl.ds(pl.multiple_of(group * rows, rows), rows),
            pl.ds(pl.multiple_of(core * half, half), half),
        ]

    def own(unit):
        array, _, m, n = units[unit]
        return array.at[pl.ds(m, n)]

    started = []

    def send(unit, chunk, key, device):
        source = own(unit) if chunk == (0, 0, "up", 0) else region(unit, chunk, t)
        i = number((unit,) + key)
        copy = pltpu.make_async_remote_copy(
            src_ref=source, dst_ref=region(unit, chunk, t), send_sem=send_sem.at[i],
            recv_sem=recv_sem.at[i], device_id=device, device_id_type=MESH,
        )
        copy.start()
        return copy

    def arrive(unit, chunk, key, core):
        i = number((unit,) + key)
        ref = region(unit, chunk, core)
        pltpu.make_async_remote_copy(
            src_ref=ref, dst_ref=ref, send_sem=send_sem.at[i], recv_sem=recv_sem.at[i],
            device_id=other_t, device_id_type=MESH,
        ).wait_recv()

    def sent(unit, chunk, key):
        i = number((unit,) + key)
        ref = own(unit)
        pltpu.make_async_remote_copy(
            src_ref=ref, dst_ref=ref, send_sem=send_sem.at[i], recv_sem=recv_sem.at[i],
            device_id=other_t, device_id_type=MESH,
        ).wait_send()

    def when(there, what):
        if there is True:
            what()
        else:
            pl.when(there)(what)

    def there_of(way, k):
        return True if k == 0 else (z >= k if way == "up" else z + k <= 3)

    def to_core(unit, chunk):
        key = chunk + ("core",)
        send(unit, chunk, key, other_t)
        started.append((unit, chunk, key, None))

    def onward(unit, chunk, axis):
        dy, dx, way, k = chunk
        key = ((1, dx, way, k) if axis == "y" else (dy, 1, way, k)) + ("link",)
        send(unit, chunk, key, other_y if axis == "y" else other_x)
        started.append((unit, chunk, key, None))

    def up_down(unit, chunk):
        dy, dx, way, k = chunk
        for going in ("up", "down") if k == 0 else (way,):
            can = z < 3 if going == "up" else z > 0
            key = (dy, dx, going, k + 1, "link")
            target = along(lax.min(z + 1, 3) if going == "up" else lax.max(z - 1, 0))
            when(can, lambda: send(unit, chunk, key, target) and None)
            started.append((unit, chunk, key, going))

    def got(unit, chunk):
        arrive(unit, chunk, chunk + ("link",), t)

    steps = [[("up", 0)], [("up", 1), ("down", 1)], [("up", 2), ("down", 2)], [("up", 3), ("down", 3)]]
    block = (y * 4 + l * 2 + x, (1 - y) * 4 + l * 2 + x)
    pieces = []
    depth = w_1.shape[0]
    for b, to in ((block[1], True), (block[0], False)):
        row = pl.ds(pl.multiple_of(y * depth, depth), depth)
        wide, narrow = w_1.shape[1] // 8, w_d.shape[0] // 8
        pieces.append([
            (w_1.at[:, pl.ds(pl.multiple_of(b * wide, wide), wide)], o_1.at[row]),
            (w_2.at[pl.ds(pl.multiple_of(b * wide, wide), wide)], o_2.at[:, row]),
            (w_q.at[:, :, pl.ds(pl.multiple_of(b * narrow, narrow), narrow)], q_out.at[:, row]),
            (w_d.at[pl.ds(pl.multiple_of(b * narrow, narrow), narrow)], d_out.at[:, row]),
            (small, small_out.at[y]),
        ])
    locals_, weights = [], []
    first = (0, 0, "up", 0)
    for u in range(3):
        up_down(u, first) if u else None
    for u in range(3):
        onward(u, first, "y")
    for i, (source, target) in enumerate(pieces[0]):
        copy = pltpu.make_async_remote_copy(
            src_ref=source, dst_ref=target, send_sem=send_sem.at[number(("w", i))],
            recv_sem=recv_sem.at[number(("w", i))], device_id=other_y, device_id_type=MESH,
        )
        copy.start()
        weights.append(copy)
    for u in range(3):
        onward(u, first, "x")
        to_core(u, first)
        copy = pltpu.make_async_copy(own(u), region(u, first, t), local_sem.at[len(locals_)])
        copy.start()
        locals_.append(copy)
    for source, target in pieces[1]:
        copy = pltpu.make_async_copy(source, target, local_sem.at[len(locals_)])
        copy.start()
        locals_.append(copy)

    got(0, (1, 0, "up", 0))
    onward(0, (1, 0, "up", 0), "x")
    up_down(0, first)
    up_down(0, (1, 0, "up", 0))
    to_core(0, (1, 0, "up", 0))

    def rest_of_first():
        for dy in (0, 1):
            got(0, (dy, 1, "up", 0))
            up_down(0, (dy, 1, "up", 0))
            to_core(0, (dy, 1, "up", 0))

    def z_step(s):
        for u in (1, 2):
            for way, k in steps[s]:
                def act(u=u, c=(0, 0, way, k)):
                    got(u, c)
                    up_down(u, c) if c[3] < 3 else None
                    onward(u, c, "y")
                    onward(u, c, "x")
                    to_core(u, c)
                when(there_of(way, k), act)

    def y_step(s):
        for u in (1, 2):
            for way, k in steps[s]:
                def act(u=u, c=(1, 0, way, k)):
                    got(u, c)
                    onward(u, c, "x")
                    to_core(u, c)
                when(there_of(way, k), act)

    def x_step(s):
        for u in (1, 2):
            for way, k in steps[s]:
                def act(u=u, way=way, k=k):
                    for dy in (0, 1):
                        got(u, (dy, 1, way, k))
                        to_core(u, (dy, 1, way, k))
                when(there_of(way, k), act)

    def first_step(s):
        for way, k in steps[s]:
            def act(way=way, k=k):
                for dy in (0, 1):
                    for dx in (0, 1):
                        c = (dy, dx, way, k)
                        got(0, c)
                        up_down(0, c) if k < 3 else None
                        to_core(0, c)
            when(there_of(way, k), act)

    z_step(1)
    rest_of_first()
    y_step(0)
    z_step(2)
    y_step(1)
    x_step(0)
    first_step(1)
    z_step(3)
    y_step(2)
    x_step(1)
    first_step(2)
    y_step(3)
    x_step(2)
    first_step(3)
    x_step(3)
    for u in range(3):
        for dy in (0, 1):
            for dx in (0, 1):
                for s in range(4):
                    for way, k in steps[s]:
                        c = (dy, dx, way, k)
                        when(there_of(way, k), lambda: arrive(u, c, c + ("core",), 1 - t))
    for copy in locals_:
        copy.wait()
    for copy in weights:
        copy.wait()
    for unit, chunk, key, going in started:
        there = there_of(*chunk[2:])
        if going is not None:
            can = z < 3 if going == "up" else z > 0
            there = can if there is True else can & there
        when(there, lambda: sent(unit, chunk, key))


def spread(tokens, cotangent, w_q, w_d, w_1, w_2, small):
    micro, rows, half = tokens.shape
    everything = jax.ShapeDtypeStruct((micro, rows * 16, half * 2), tokens.dtype)
    depth = w_1.shape[0] * 2
    outs = [
        everything,
        everything,
        jax.ShapeDtypeStruct((3, depth, w_q.shape[2] // 8), w_q.dtype),
        jax.ShapeDtypeStruct((w_d.shape[0] // 8, depth), w_d.dtype),
        jax.ShapeDtypeStruct((depth, w_1.shape[1] // 8), w_1.dtype),
        jax.ShapeDtypeStruct((w_2.shape[0] // 8, depth), w_2.dtype),
        jax.ShapeDtypeStruct((2,) + small.shape, small.dtype),
    ]
    return pl.pallas_call(
        spread_kernel,
        out_shape=outs,
        in_specs=[pl.BlockSpec(memory_space=pl.ANY)] * 7,
        out_specs=[pl.BlockSpec(memory_space=pl.ANY)] * 7,
        scratch_shapes=[
            pltpu.SemaphoreType.DMA((8,)),
            pltpu.SemaphoreType.DMA((176,)),
            pltpu.SemaphoreType.DMA((176,)),
        ],
        compiler_params=pltpu.CompilerParams(collective_id=0, has_side_effects=True),
        name="spread",
    )(tokens, cotangent, w_q, w_d, w_1, w_2, small)


def join_kernel(count, parts, outs, local_sem, send_sem, recv_sem):
    y, h, l, x, t = place()
    device = {"y": {"y": 1 - y}, "l": {"l": 1 - l}, "x": {"x": 1 - x}}
    greet([(device[a], True) for a in ("y", "l", "x")])

    def half_of(i, yy):
        ref, d_axis, _, _ = parts[i]
        n = ref.shape[d_axis] // 2
        where = [slice(None)] * len(ref.shape)
        where[d_axis] = pl.ds(pl.multiple_of(yy * n, n), n)
        return ref.at[tuple(where)]

    def spot(i, yy, ll, xx):
        ref, _, b_axis, _ = parts[i]
        n = ref.shape[b_axis]
        where = [slice(None)] * len(ref.shape)
        where[b_axis] = pl.ds(pl.multiple_of((yy * 4 + ll * 2 + xx) * n, n), n)
        return outs[i].at[tuple(where)]

    numbers = {}

    def number(key):
        return numbers.setdefault(key, len(numbers))

    sends = []

    def send(i, source, target, key, axis):
        n = number((i,) + key)
        copy = pltpu.make_async_remote_copy(
            src_ref=source, dst_ref=target, send_sem=send_sem.at[n], recv_sem=recv_sem.at[n],
            device_id=device[axis], device_id_type=MESH,
        )
        copy.start()
        sends.append(copy)

    def got(i, target, key):
        n = number((i,) + key)
        pltpu.make_async_remote_copy(
            src_ref=target, dst_ref=target, send_sem=send_sem.at[n], recv_sem=recv_sem.at[n],
            device_id=device["y"], device_id_type=MESH,
        ).wait_recv()

    every = range(count)
    hop = {"x": "l", "l": "x"}
    first = {i: parts[i][3] for i in every}
    for i in every:
        send(i, half_of(i, 1 - y), spot(i, y, l, x), ("y",), "y")
    for i in every:
        send(i, half_of(i, y), spot(i, y, l, x), (0, first[i]), first[i])
    for i in every:
        send(i, half_of(i, y), spot(i, y, l, x), (0, hop[first[i]]), hop[first[i]])
    locals_ = []
    for i in every:
        copy = pltpu.make_async_copy(half_of(i, y), spot(i, y, l, x), local_sem.at[i])
        copy.start()
        locals_.append(copy)

    def beside(i, axis, yy):
        return spot(i, yy, 1 - l if axis == "l" else l, 1 - x if axis == "x" else x)

    for i in every:
        a = first[i]
        got(i, beside(i, a, y), (0, a))
        send(i, beside(i, a, y), beside(i, a, y), (0, "far"), hop[a])
    for i in every:
        got(i, spot(i, 1 - y, l, x), ("y",))
        send(i, spot(i, 1 - y, l, x), spot(i, 1 - y, l, x), (1, first[i]), first[i])
        send(i, spot(i, 1 - y, l, x), spot(i, 1 - y, l, x), (1, hop[first[i]]), hop[first[i]])
    for i in every:
        a = first[i]
        got(i, beside(i, a, 1 - y), (1, a))
        send(i, beside(i, a, 1 - y), beside(i, a, 1 - y), (1, "far"), hop[a])
    for i in every:
        for yy, side in ((y, 0), (1 - y, 1)):
            got(i, beside(i, hop[first[i]], yy), (side, hop[first[i]]))
            got(i, spot(i, yy, 1 - l, 1 - x), (side, "far"))
    for copy in locals_:
        copy.wait()
    for copy in sends:
        copy.wait_send()


def join(arrays, plan, shapes, collective_id, name):
    count = len(arrays)

    def kernel(*refs):
        parts = [(refs[i],) + plan[i] for i in range(count)]
        join_kernel(count, parts, refs[count : 2 * count], *refs[2 * count :])

    return pl.pallas_call(
        kernel,
        out_shape=[jax.ShapeDtypeStruct(s, a.dtype) for s, a in zip(shapes, arrays)],
        in_specs=[pl.BlockSpec(memory_space=pl.ANY)] * count,
        out_specs=[pl.BlockSpec(memory_space=pl.ANY)] * count,
        scratch_shapes=[
            pltpu.SemaphoreType.DMA((count,)),
            pltpu.SemaphoreType.DMA((7 * count,)),
            pltpu.SemaphoreType.DMA((7 * count,)),
        ],
        compiler_params=pltpu.CompilerParams(collective_id=collective_id, has_side_effects=True),
        name=name,
    )(*arrays)


def swap_rotary(values):
    lane = lax.rem(lax.broadcasted_iota(jnp.int32, values.shape, 1), 64)
    half = ROT // 2
    width = values.shape[1]
    return jnp.where(
        lane < half, pltpu.roll(values, width - half, 1), pltpu.roll(values, half, 1)
    )


def attend_kernel(rows_ref, seg_q, seg_k, cos_ref, sin_ref, out_ref, grad_ref, gq, gk, gv):
    pack_rows, width = rows_ref.shape[1], out_ref.shape[2]
    scale = 64 ** (-0.5)
    lane = lax.broadcasted_iota(jnp.int32, (1, width), 1)
    gk[...] = jnp.zeros_like(gk)
    gv[...] = jnp.zeros_like(gv)
    nt = (((1,), (1,)), ((), ()))
    tn = (((0,), (0,)), ((), ()))

    def dot(a, b, dims=(((1,), (0,)), ((), ()))):
        return lax.dot_general(a, b, dims, preferred_element_type=jnp.float32)

    for block in range(pack_rows // BLOCK):
        low = max(0, block * BLOCK - SPAN)
        high = (block + 1) * BLOCK
        here = slice(block * BLOCK, high)
        keys = rows_ref[0, low:high, width : 2 * width]
        values = rows_ref[0, low:high, 2 * width : 3 * width]
        seg_here = seg_q[0, here, :]
        seg_there = seg_k[0, :, low:high]
        row = lax.broadcasted_iota(jnp.int32, (BLOCK, high - low), 0) + block * BLOCK
        column = lax.broadcasted_iota(jnp.int32, (BLOCK, high - low), 1) + low
        allowed = (seg_here == seg_there) & (column <= row)
        attended = None
        for head in range(2):
            mine = (lane // 64) == head
            query = jnp.where(mine, rows_ref[0, here, 0:width], 0)
            grad = jnp.where(mine, rows_ref[0, here, 3 * width : 4 * width], 0)
            key = jnp.where(mine, keys, 0)
            value = jnp.where(mine, values, 0)
            scores = jnp.where(allowed, dot(query, key, nt) * scale, NEG_FILL)
            peak = jnp.max(scores, axis=1, keepdims=True)
            weights = jnp.exp(scores - peak)
            weights = weights * (1.0 / jnp.sum(weights, axis=1, keepdims=True))
            weights_b = weights.astype(jnp.bfloat16)
            out = dot(weights_b, value)
            attended = out if attended is None else attended + out
            delta = jnp.sum(grad.astype(jnp.float32) * out, axis=1, keepdims=True)
            inner = dot(grad, value, nt)
            grad_scores = (weights * (inner - delta)).astype(jnp.bfloat16)
            part = dot(grad_scores, key) * scale
            if head == 0:
                gq[here, :] = part
            else:
                gq[here, :] += part
            gk[low:high, :] += dot(grad_scores, query, tn)
            gv[low:high, :] += dot(weights_b, grad, tn)
        out_ref[0, here, :] = attended.astype(jnp.bfloat16)
    cos = cos_ref[0]
    sin = sin_ref[0]
    q_all = gq[...]
    grad_ref[0, :, 0:width] = (q_all * cos - swap_rotary(q_all) * sin).astype(jnp.bfloat16)
    k_all = gk[...] * scale
    grad_ref[0, :, width : 2 * width] = (k_all * cos - swap_rotary(k_all) * sin).astype(jnp.bfloat16)
    grad_ref[0, :, 2 * width : 3 * width] = gv[...].astype(jnp.bfloat16)


def attend(rows, segment, cos, sin):
    packs, pack_rows, wide = rows.shape
    width = wide // 4
    return pl.pallas_call(
        attend_kernel,
        grid=(packs,),
        out_shape=[
            jax.ShapeDtypeStruct((packs, pack_rows, width), jnp.bfloat16),
            jax.ShapeDtypeStruct((packs, pack_rows, 3 * width), jnp.bfloat16),
        ],
        in_specs=[
            pl.BlockSpec((1, pack_rows, wide), lambda i: (i, 0, 0)),
            pl.BlockSpec((1, pack_rows, 1), lambda i: (i, 0, 0)),
            pl.BlockSpec((1, 1, pack_rows), lambda i: (i, 0, 0)),
            pl.BlockSpec((1, pack_rows, width), lambda i: (i, 0, 0)),
            pl.BlockSpec((1, pack_rows, width), lambda i: (i, 0, 0)),
        ],
        out_specs=[
            pl.BlockSpec((1, pack_rows, width), lambda i: (i, 0, 0)),
            pl.BlockSpec((1, pack_rows, 3 * width), lambda i: (i, 0, 0)),
        ],
        scratch_shapes=[pltpu.VMEM((pack_rows, width), jnp.float32)] * 3,
        compiler_params=pltpu.CompilerParams(vmem_limit_bytes=48 << 20),
        cost_estimate=pl.CostEstimate(
            flops=packs * 14 * pack_rows * pack_rows * width, bytes_accessed=packs * pack_rows * width * 24, transcendentals=0
        ),
        name="attend",
    )(rows, segment[:, :, None], segment[:, None, :], cos, sin)


def fast_body(
    tokens, cotangent, lengths, permutation, ln_gain, ln_bias, qkv_weight, qkv_bias,
    dense_weight, dense_bias, fc1_weight, fc1_bias, fc2_weight, fc2_bias,
):
    y, h, l, x, t = place()
    f32, bf16 = jnp.float32, jnp.bfloat16
    micro, rows, share = tokens.shape
    width = share * 2
    total = rows * 16
    pack_rows = rows * 8
    packs = total // pack_rows
    block = y * 4 + l * 2 + x
    wide = fc1_weight.shape[1] // 8
    narrow = dense_weight.shape[0] // 8
    small = jnp.concatenate(
        [a.reshape(-1) for a in (ln_gain, ln_bias, dense_bias, fc2_bias, qkv_bias, fc1_bias)]
    )
    small = jnp.pad(small, (0, 64 * 128 - small.shape[0])).reshape(64, 128)
    tok_all, cot_all, w_q, w_d, w_1, w_2, small = spread(
        tokens, cotangent, qkv_weight.transpose(1, 0, 2), dense_weight, fc1_weight, fc2_weight, small
    )
    small = small.reshape(2, 64 * 128).astype(f32)
    gain = small[:, 0:share].reshape(width)
    shift = small[:, share : 2 * share].reshape(width)
    out_shift = (small[:, 2 * share : 3 * share] + small[:, 3 * share : 4 * share]).reshape(width)
    at = 4 * share
    q_shift = small[:, at : at + qkv_bias.size].reshape((2,) + qkv_bias.shape)
    q_shift = q_shift.transpose(1, 2, 0, 3).reshape(3, -1)
    at += qkv_bias.size
    f_shift = small[:, at : at + fc1_bias.size].reshape((2,) + fc1_bias.shape).transpose(1, 0, 2).reshape(-1)
    q_shift = lax.dynamic_slice_in_dim(q_shift, block * narrow, narrow, 1)
    f_shift = lax.dynamic_slice_in_dim(f_shift, block * wide, wide, 0)

    places = jnp.arange(pack_rows, dtype=jnp.int32)
    segment, position = jax.vmap(lambda row: segment_layout(row, places))(
        lengths.reshape(micro * packs, -1)
    )
    position = position.reshape(micro, total).astype(f32)
    chosen = (permutation[:, None, :] == jnp.arange(total, dtype=jnp.int32)[None, :, None]).astype(bf16)
    half = ROT // 2
    freq = ROPE_BASE ** (-2.0 * jnp.arange(half, dtype=f32) / ROT)

    def tables(pos):
        angles = pos[..., None] * freq
        cos, sin = jnp.cos(angles), jnp.sin(angles)
        rest = jnp.ones(pos.shape + (64 - ROT,), f32)
        cos = jnp.concatenate([cos, cos, rest], -1)
        sin = jnp.concatenate([-sin, sin, 0 * rest], -1)
        return jnp.concatenate([cos, cos], -1), jnp.concatenate([sin, sin], -1)

    cos_l, sin_l = tables(position)
    pos_a = jnp.einsum("mla,ml->ma", chosen, position, precision=lax.Precision.HIGHEST)
    cos_a, sin_a = tables(pos_a)

    xs = tok_all.astype(f32)
    center = xs - jnp.mean(xs, axis=-1, keepdims=True)
    r = lax.rsqrt(jnp.mean(center * center, axis=-1, keepdims=True) + EPSILON)
    normed = (center * r * gain + shift).astype(bf16)
    pre = jnp.einsum("mrd,dh->mrh", normed, w_1, preferred_element_type=f32) + f_shift
    activ, gelu_back = jax.vjp(partial(jax.nn.gelu, approximate=True), pre)
    activ = activ.astype(bf16)
    grad_activ = jnp.einsum("mrd,hd->mrh", cot_all, w_2, preferred_element_type=f32)
    grad_pre = gelu_back(grad_activ)[0].astype(bf16)
    g_w1 = jnp.einsum("mrd,mrh->dh", normed, grad_pre, preferred_element_type=f32).astype(bf16)
    g_w2 = jnp.einsum("mrh,mrd->hd", activ, cot_all, preferred_element_type=f32).astype(bf16)
    qkv = [
        jnp.einsum("mrd,de->mre", normed, w_q[c], preferred_element_type=f32) + q_shift[c]
        for c in range(3)
    ]

    def rotated(v):
        lane = lax.broadcasted_iota(jnp.int32, v.shape, 2) % 64
        other = jnp.where(lane < half, jnp.roll(v, -half, 2), jnp.roll(v, half, 2))
        return v * cos_a + other * sin_a

    grad_att = jnp.einsum("mrd,ed->mre", cot_all, w_d, preferred_element_type=f32)
    four = jnp.concatenate([rotated(qkv[0]), rotated(qkv[1]), qkv[2], grad_att], -1).astype(bf16)
    laid = jnp.einsum("mla,mae->mle", chosen, four, preferred_element_type=f32).astype(bf16)
    attended, grad_qkv = attend(
        laid.reshape(micro * packs, pack_rows, -1),
        segment,
        cos_l.reshape(micro * packs, pack_rows, -1),
        sin_l.reshape(micro * packs, pack_rows, -1),
    )
    back = jnp.concatenate([attended, grad_qkv], -1).reshape(micro, total, 4 * narrow)
    back = jnp.einsum("mla,mle->mae", chosen, back, preferred_element_type=f32).astype(bf16)
    attended, grad_qkv = back[..., :narrow], back[..., narrow:]
    g_wd = jnp.einsum("mre,mrd->ed", attended, cot_all, preferred_element_type=f32).astype(bf16)
    g_wq = jnp.stack(
        [
            jnp.einsum(
                "mrd,mre->de", normed, grad_qkv[..., c * narrow : (c + 1) * narrow], preferred_element_type=f32
            )
            for c in range(3)
        ]
    ).astype(bf16)

    def side(v):
        v = v.reshape(micro, 2, 2, 4 * rows, v.shape[-1])
        return lax.dynamic_index_in_dim(v, h, 2, keepdims=False).reshape(micro, 2, 4, rows, v.shape[-1])

    out_part = jnp.einsum("mycre,ed->ycmrd", side(attended), w_d, preferred_element_type=f32) + jnp.einsum(
        "mycre,ed->ycmrd", side(activ), w_2, preferred_element_type=f32
    )
    g_side = side(grad_qkv)
    norm_part = jnp.einsum("mycre,de->ycmrd", side(grad_pre), w_1, preferred_element_type=f32) + sum(
        jnp.einsum(
            "mycre,de->ycmrd", g_side[..., c * narrow : (c + 1) * narrow], w_q[c], preferred_element_type=f32
        )
        for c in range(3)
    )

    def summed(v):
        v = v.astype(bf16)
        v = lax.psum_scatter(v, "t", scatter_dimension=4, tiled=True)
        v = lax.psum_scatter(v, "y", scatter_dimension=0, tiled=True)
        v = v.reshape((2, 2) + v.shape[2:])
        v = lax.psum_scatter(v, "l", scatter_dimension=0, tiled=True)
        v = lax.psum_scatter(v, "x", scatter_dimension=1, tiled=True)
        return v.reshape(micro, rows, share).astype(f32)

    out_sum, norm_sum = summed(out_part), summed(norm_part)
    at = t * share

    def mine(v):
        return lax.dynamic_slice_in_dim(v, at, share, 0)

    layer_out = (tokens.astype(f32) + out_sum + mine(out_shift)).astype(bf16)
    group = y * 8 + h * 4 + l * 2 + x
    x_rows = lax.dynamic_slice_in_dim(tok_all, group * rows, rows, 1).astype(f32)
    x_mid = x_rows - jnp.mean(x_rows, axis=-1, keepdims=True)
    r_own = lax.rsqrt(jnp.mean(x_mid * x_mid, axis=-1, keepdims=True) + EPSILON)
    hat = lax.dynamic_slice_in_dim(x_mid * r_own, at, share, 2)
    scaled = mine(gain) * norm_sum
    sums = lax.psum(jnp.stack([scaled.sum(-1), (scaled * hat).sum(-1)]), "t") / width
    grad_tokens = (
        cotangent.astype(f32) + r_own * (scaled - sums[0][..., None] - hat * sums[1][..., None])
    ).astype(bf16)

    g_small = jnp.stack([(norm_sum * hat).sum((0, 1)), norm_sum.sum((0, 1))])
    g_small = lax.psum(g_small, ("y", "h", "l", "x"))
    g_small = lax.all_gather(g_small, "t", axis=1, tiled=True)
    g_small = lax.dynamic_slice_in_dim(g_small, y * share, share, 1)
    g_bias = jnp.concatenate([grad_qkv.astype(f32).sum((0, 1)), grad_pre.astype(f32).sum((0, 1))])
    g_bias = lax.all_gather(g_bias, ("y", "l", "x"), axis=0)
    g_qb = g_bias[:, : 3 * narrow].reshape(8, 3, narrow).transpose(1, 0, 2).reshape(3, -1, 64)
    g_qb = lax.dynamic_slice_in_dim(g_qb, y * 32, 32, 2)
    g_fb = g_bias[:, 3 * narrow :].reshape(16, -1)
    g_fb = lax.dynamic_slice_in_dim(g_fb, y * fc1_bias.shape[1], fc1_bias.shape[1], 1)
    cot_sum = lax.dynamic_slice_in_dim(
        cot_all.reshape(micro * total, width), y * share, share, 1
    ).astype(f32).sum(0)

    j_1, j_2 = join(
        [g_w1, g_w2], [(0, 1, "x"), (1, 0, "l")], [fc1_weight.shape, fc2_weight.shape], 1, "join_mlp"
    )
    j_q, j_d = join(
        [g_wq, g_wd],
        [(1, 2, "x"), (1, 0, "l")],
        [(3,) + dense_weight.shape, dense_weight.shape],
        2,
        "join_att",
    )
    return (
        layer_out,
        grad_tokens,
        g_small[0],
        g_small[1],
        j_q.astype(f32).transpose(1, 0, 2),
        g_qb,
        j_d.astype(f32),
        cot_sum,
        j_1.astype(f32),
        g_fb,
        j_2.astype(f32),
        cot_sum,
    )


def fast_solution(mesh):
    small_mesh = Mesh(mesh.devices.reshape(2, 2, 2, 2, 2), AXES)
    rows = P(None, ("y", "h", "l", "x"), "t")
    weights = (
        P("y"), P("y"), P("y", None, "t"), P(None, "t", "y"), P("t", "y"), P("y"), P("y", "t"),
        P("t", "y"), P("t", "y"), P("y"),
    )
    return jax.shard_map(
        fast_body,
        mesh=small_mesh,
        in_specs=(rows, rows, P(), P()) + weights,
        out_specs=(rows, rows) + weights,
        check_vma=False,
    )


def solution(mesh):
    if fits(mesh):
        return fast_solution(mesh)
    in_specs = (
        P(None, (FS, CT), TE),
        P(None, (FS, CT), TE),
        P(),
        P(),
        P(FS),
        P(FS),
        P(FS, None, TE),
        P(None, TE, FS),
        P(TE, FS),
        P(FS),
        P(FS, TE),
        P(TE, FS),
        P(TE, FS),
        P(FS),
    )
    out_specs = (
        P(None, (FS, CT), TE),
        P(None, (FS, CT), TE),
        P(FS),
        P(FS),
        P(FS, None, TE),
        P(None, TE, FS),
        P(TE, FS),
        P(FS),
        P(FS, TE),
        P(TE, FS),
        P(TE, FS),
        P(FS),
    )
    return jax.shard_map(body, mesh=mesh, in_specs=in_specs, out_specs=out_specs, check_vma=False)
```

```python
from functools import partial

import jax
import jax.numpy as jnp
from jax import lax
from jax.experimental import pallas as pl
from jax.experimental.pallas import tpu as pltpu
from jax.sharding import Mesh
from jax.sharding import PartitionSpec as P

ROT = 32
FS, CT, TE = "fsdp", "context", "tensor"


EPSILON = 1e-05
ROPE_BASE = 10000.0
NEG_FILL = -1e30


def layer_norm(values, gain, shift):
    center = values - jnp.mean(values, axis=-1, keepdims=True)
    spread = jnp.mean(center * center, axis=-1, keepdims=True)
    return center * lax.rsqrt(spread + EPSILON) * gain + shift


def rotate(values, position):
    half = ROT // 2
    freq = ROPE_BASE ** (-2.0 * jnp.arange(half, dtype=jnp.float32) / ROT)
    angles = position[:, None] * freq[None, :]
    cosine = jnp.cos(angles)[:, None, :]
    sine = jnp.sin(angles)[:, None, :]
    first = values[..., :half]
    second = values[..., half:ROT]
    return jnp.concatenate(
        [first * cosine - second * sine, second * cosine + first * sine, values[..., ROT:]], axis=-1
    )


def segment_layout(length_row, places):
    count = length_row.shape[0]
    upto = jnp.arange(count)[:, None] >= jnp.arange(count)[None, :]
    ends = jnp.sum(jnp.where(upto, length_row[None, :], 0), axis=1)
    starts = ends - length_row
    segment = jnp.sum((places[:, None] >= ends[None, :]).astype(jnp.int32), axis=1)
    match = segment[:, None] == jnp.arange(length_row.shape[0], dtype=jnp.int32)[None, :]
    begin = jnp.sum(jnp.where(match, starts[None, :], 0), axis=1)
    return (segment, places - begin)


def rows_block(source, block_index, block_rows, head_count, head_width):
    return lax.dynamic_slice_in_dim(source, block_index * block_rows, block_rows, 0).reshape(
        block_rows, head_count, head_width
    )


def pair_mask(query_segment, query_place, key_segment, key_place):
    return (
        (query_segment[:, None] == key_segment[None, :])
        & (key_place[None, :] <= query_place[:, None])
    )[None]


def key_scores(
    query,
    keys_all,
    key_segment,
    key_place,
    query_segment,
    query_place,
    block_index,
    block_rows,
    scale,
):
    row_count, head_count, head_width = query.shape
    key_block = rows_block(keys_all, block_index, block_rows, head_count, head_width)
    scores = (
        jnp.einsum("qhe,khe->hqk", query, key_block, preferred_element_type=jnp.float32) * scale
    )
    segment_block = lax.dynamic_slice_in_dim(key_segment, block_index * block_rows, block_rows, 0)
    place_block = lax.dynamic_slice_in_dim(key_place, block_index * block_rows, block_rows, 0)
    return (scores, pair_mask(query_segment, query_place, segment_block, place_block), key_block)


def attend_forward(
    query,
    keys_all,
    values_all,
    key_segment,
    key_place,
    query_segment,
    query_place,
    first_block,
    last_block,
    block_rows,
    scale,
):
    row_count, head_count, head_width = query.shape

    def find_peak(block_index, carry):
        peak, total = carry
        scores, allowed, _ = key_scores(
            query,
            keys_all,
            key_segment,
            key_place,
            query_segment,
            query_place,
            block_index,
            block_rows,
            scale,
        )
        fresh = jnp.maximum(peak, jnp.max(jnp.where(allowed, scores, NEG_FILL), axis=-1))
        added = jnp.sum(jnp.where(allowed, jnp.exp(scores - fresh[..., None]), 0.0), axis=-1)
        return (fresh, total * jnp.exp(peak - fresh) + added)

    start_carry = (
        jnp.full((head_count, row_count), NEG_FILL, jnp.float32),
        jnp.zeros((head_count, row_count), jnp.float32),
    )
    peak, total = lax.fori_loop(first_block, last_block + 1, find_peak, start_carry)
    log_total = peak + jnp.log(total)

    def weigh(block_index, accum):
        scores, allowed, _ = key_scores(
            query,
            keys_all,
            key_segment,
            key_place,
            query_segment,
            query_place,
            block_index,
            block_rows,
            scale,
        )
        attend_weights = jnp.where(allowed, jnp.exp(scores - log_total[..., None]), 0.0).astype(
            jnp.bfloat16
        )
        values = rows_block(values_all, block_index, block_rows, head_count, head_width)
        return accum + jnp.einsum(
            "hqk,khe->qhe", attend_weights, values, preferred_element_type=jnp.float32
        )

    attended = lax.fori_loop(
        first_block, last_block + 1, weigh, jnp.zeros(query.shape, jnp.float32)
    )
    return (attended, log_total)


def attend_backward(
    query,
    keys_all,
    values_all,
    key_segment,
    key_place,
    query_segment,
    query_place,
    first_block,
    last_block,
    block_rows,
    scale,
    log_total,
    grad_out,
    delta,
):
    row_count, head_count, head_width = query.shape

    def step_back(block_index, carry):
        scores, allowed, key_block = key_scores(
            query,
            keys_all,
            key_segment,
            key_place,
            query_segment,
            query_place,
            block_index,
            block_rows,
            scale,
        )
        values = rows_block(values_all, block_index, block_rows, head_count, head_width)
        attend_weights = jnp.where(allowed, jnp.exp(scores - log_total[..., None]), 0.0)
        grad_weights = jnp.einsum(
            "qhe,khe->hqk", grad_out, values, preferred_element_type=jnp.float32
        )
        grad_scores = (attend_weights * (grad_weights - delta[..., None])).astype(jnp.bfloat16)
        grad_query = (
            carry[0]
            + jnp.einsum("hqk,khe->qhe", grad_scores, key_block, preferred_element_type=jnp.float32)
            * scale
        )
        grad_keys, grad_values = (carry[1], carry[2])
        key_part = (
            jnp.einsum("hqk,qhe->khe", grad_scores, query, preferred_element_type=jnp.float32)
            * scale
        ).reshape(block_rows, head_count * head_width)
        value_part = jnp.einsum(
            "hqk,qhe->khe",
            attend_weights.astype(jnp.bfloat16),
            grad_out,
            preferred_element_type=jnp.float32,
        ).reshape(block_rows, head_count * head_width)
        block_start = block_index * block_rows
        grad_keys = lax.dynamic_update_slice_in_dim(
            grad_keys,
            lax.dynamic_slice_in_dim(grad_keys, block_start, block_rows, 0) + key_part,
            block_start,
            0,
        )
        grad_values = lax.dynamic_update_slice_in_dim(
            grad_values,
            lax.dynamic_slice_in_dim(grad_values, block_start, block_rows, 0) + value_part,
            block_start,
            0,
        )
        return (grad_query, grad_keys, grad_values)

    start_carry = (
        jnp.zeros(query.shape, jnp.float32),
        jnp.zeros(keys_all.shape, jnp.float32),
        jnp.zeros(values_all.shape, jnp.float32),
    )
    return lax.fori_loop(first_block, last_block + 1, step_back, start_carry)


def body(
    tokens,
    cotangent,
    lengths,
    permutation,
    ln_gain,
    ln_bias,
    qkv_weight,
    qkv_bias,
    dense_weight,
    dense_bias,
    fc1_weight,
    fc1_bias,
    fc2_weight,
    fc2_bias,
):
    gain_all, shift_all, w_qkv, b_qkv, w_dense, b_dense, w_fc1, b_fc1, w_fc2, b_fc2 = (
        lax.all_gather(ln_gain, FS, axis=0, tiled=True),
        lax.all_gather(ln_bias, FS, axis=0, tiled=True),
        lax.all_gather(qkv_weight, FS, axis=0, tiled=True),
        lax.all_gather(qkv_bias, FS, axis=2, tiled=True),
        lax.all_gather(dense_weight, FS, axis=1, tiled=True),
        lax.all_gather(dense_bias, FS, axis=0, tiled=True),
        lax.all_gather(fc1_weight, FS, axis=0, tiled=True),
        lax.all_gather(fc1_bias, FS, axis=1, tiled=True),
        lax.all_gather(fc2_weight, FS, axis=1, tiled=True),
        lax.all_gather(fc2_bias, FS, axis=0, tiled=True),
    )
    gain_f = gain_all.astype(jnp.float32)
    shift_f = shift_all.astype(jnp.float32)
    local_width = w_qkv.shape[2]
    head_count = b_qkv.shape[1]
    head_width = b_qkv.shape[2]
    hidden_local = w_fc1.shape[1]
    qkv_shift = b_qkv.astype(jnp.float32).reshape(3, local_width)
    fc1_shift = b_fc1.astype(jnp.float32).reshape(hidden_local)
    micro_count = tokens.shape[0]
    row_count = tokens.shape[1]
    feature_share = tokens.shape[2]
    all_rows = micro_count * row_count
    pack_length = row_count * lax.axis_size(CT)
    block_rows = min(512, pack_length)
    group_index = lax.axis_index((FS, CT))
    pack_index = lax.axis_index(FS)
    context_index = lax.axis_index(CT)
    tensor_index = lax.axis_index(TE)
    out_shift = lax.dynamic_slice_in_dim(
        b_dense.astype(jnp.float32) + b_fc2.astype(jnp.float32),
        tensor_index * feature_share,
        feature_share,
        0,
    )
    scale = head_width ** (-0.5)
    counting = jnp.arange(row_count, dtype=jnp.int32)
    pack_places = jnp.arange(pack_length, dtype=jnp.int32)
    query_place = lax.dynamic_slice_in_dim(pack_places, context_index * row_count, row_count, 0)
    last_query_block = (context_index * row_count + row_count - 1) // block_rows
    sent_tokens = []
    sent_cot = []
    slot_sources = []
    arrive_slots = []
    return_orders = []
    key_segments = []
    query_segments = []
    query_positions = []
    first_blocks = []
    length_rows = []
    for micro_index in range(micro_count):
        perm_row = permutation[micro_index]
        own_targets = lax.dynamic_slice_in_dim(perm_row, group_index * row_count, row_count, 0)
        send_order = jnp.argsort(own_targets // row_count, stable=True)
        return_orders.append(jnp.zeros(row_count, jnp.int32).at[send_order].set(counting))
        here = perm_row // row_count == group_index
        arriving = jnp.argsort(jnp.where(here, 0, 1), stable=True)[:row_count]
        arrive_slot = perm_row[arriving] % row_count
        arrive_slots.append(arrive_slot)
        slot_sources.append(jnp.zeros(row_count, jnp.int32).at[arrive_slot].set(counting))
        sent_tokens.append(tokens[micro_index][send_order])
        sent_cot.append(cotangent[micro_index][send_order])
        length_row = lax.dynamic_index_in_dim(lengths[micro_index], pack_index, 0, keepdims=False)
        length_rows.append(length_row)
        key_segment, key_position = segment_layout(length_row, pack_places)
        key_segments.append(key_segment)
        query_segments.append(
            lax.dynamic_slice_in_dim(key_segment, context_index * row_count, row_count, 0)
        )
        query_position = lax.dynamic_slice_in_dim(
            key_position, context_index * row_count, row_count, 0
        )
        query_positions.append(query_position)
        first_blocks.append((query_place[0] - query_position[0]) // block_rows)
    received = (
        lax.all_to_all(
            jnp.stack(sent_tokens), (FS, CT), split_axis=1, concat_axis=1, tiled=True
        ),
        lax.all_to_all(
            jnp.stack(sent_cot), (FS, CT), split_axis=1, concat_axis=1, tiled=True
        ),
    )
    own_tokens = jnp.concatenate(
        [received[0][m][slot_sources[m]] for m in range(micro_count)], axis=0
    )
    own_cot = jnp.concatenate([received[1][m][slot_sources[m]] for m in range(micro_count)], axis=0)
    full_tokens, full_cot = (
        lax.all_gather(own_tokens, TE, axis=1, tiled=True),
        lax.all_gather(own_cot, TE, axis=1, tiled=True),
    )
    normed, norm_back = jax.vjp(layer_norm, full_tokens.astype(jnp.float32), gain_f, shift_f)
    normed_b = normed.astype(jnp.bfloat16)
    qkv = jnp.einsum("rd,dce->rce", normed_b, w_qkv, preferred_element_type=jnp.float32) + qkv_shift
    angle_pos = jnp.concatenate(query_positions, axis=0).astype(jnp.float32)
    query_rot, rope_back = jax.vjp(
        lambda inner: rotate(inner, angle_pos), qkv[:, 0].reshape(all_rows, head_count, head_width)
    )
    key_rot = rotate(qkv[:, 1].reshape(all_rows, head_count, head_width), angle_pos)
    query_b = query_rot.astype(jnp.bfloat16)
    key_b = key_rot.reshape(all_rows, local_width).astype(jnp.bfloat16)
    value_b = qkv[:, 2].astype(jnp.bfloat16)
    keys_all, values_all = (
        lax.all_gather(
            key_b.reshape(micro_count, row_count, local_width), CT, axis=1, tiled=True
        ),
        lax.all_gather(
            value_b.reshape(micro_count, row_count, local_width), CT, axis=1, tiled=True
        ),
    )
    attended_list = []
    log_list = []
    for micro_index in range(micro_count):
        rows = slice(micro_index * row_count, (micro_index + 1) * row_count)
        attended_one, log_one = attend_forward(
            query_b[rows],
            keys_all[micro_index],
            values_all[micro_index],
            key_segments[micro_index],
            pack_places,
            query_segments[micro_index],
            query_place,
            first_blocks[micro_index],
            last_query_block,
            block_rows,
            scale,
        )
        attended_list.append(attended_one)
        log_list.append(log_one)
    attended = jnp.concatenate(attended_list, axis=0)
    attended_b = attended.reshape(all_rows, local_width).astype(jnp.bfloat16)
    pre_act = jnp.dot(normed_b, w_fc1, preferred_element_type=jnp.float32) + fc1_shift
    activ, gelu_back = jax.vjp(partial(jax.nn.gelu, approximate=True), pre_act)
    activ_b = activ.astype(jnp.bfloat16)
    partial_out = jnp.dot(attended_b, w_dense, preferred_element_type=jnp.float32) + jnp.dot(
        activ_b, w_fc2, preferred_element_type=jnp.float32
    )
    branch = lax.psum_scatter(
        partial_out.astype(jnp.bfloat16), TE, scatter_dimension=1, tiled=True
    ).astype(jnp.float32)
    layer_rows = (own_tokens.astype(jnp.float32) + branch + out_shift).astype(jnp.bfloat16)
    grad_attended = jnp.einsum(
        "rd,ed->re", full_cot, w_dense, preferred_element_type=jnp.float32
    ).astype(jnp.bfloat16)
    grad_activ = jnp.einsum("rd,hd->rh", full_cot, w_fc2, preferred_element_type=jnp.float32)
    grad_pre = gelu_back(grad_activ)[0].astype(jnp.bfloat16)
    grad_heads = grad_attended.reshape(all_rows, head_count, head_width)
    delta_list = []
    for micro_index in range(micro_count):
        rows = slice(micro_index * row_count, (micro_index + 1) * row_count)
        delta_list.append(
            jnp.einsum(
                "qhe,qhe->hq", grad_heads[rows].astype(jnp.float32), attended_list[micro_index]
            )
        )
    query_grads = []
    key_parts = []
    value_parts = []
    for micro_index in range(micro_count):
        rows = slice(micro_index * row_count, (micro_index + 1) * row_count)
        grad_query_one, grad_keys_one, grad_values_one = attend_backward(
            query_b[rows],
            keys_all[micro_index],
            values_all[micro_index],
            key_segments[micro_index],
            pack_places,
            query_segments[micro_index],
            query_place,
            first_blocks[micro_index],
            last_query_block,
            block_rows,
            scale,
            log_list[micro_index],
            grad_heads[rows],
            delta_list[micro_index],
        )
        query_grads.append(grad_query_one)
        key_parts.append(grad_keys_one)
        value_parts.append(grad_values_one)
    grad_keys, grad_values = (
        lax.psum_scatter(
            jnp.stack(key_parts).astype(jnp.bfloat16), CT, scatter_dimension=1, tiled=True
        ).astype(jnp.float32),
        lax.psum_scatter(
            jnp.stack(value_parts).astype(jnp.bfloat16), CT, scatter_dimension=1, tiled=True
        ).astype(jnp.float32),
    )
    grad_keys = grad_keys.reshape(all_rows, local_width)
    grad_values = grad_values.reshape(all_rows, local_width)
    grad_query = jnp.concatenate(query_grads, axis=0)
    grad_query_pre = rope_back(grad_query)[0].reshape(all_rows, local_width)
    grad_key_pre = rope_back(grad_keys.reshape(all_rows, head_count, head_width))[0].reshape(
        all_rows, local_width
    )
    grad_qkv = jnp.stack([grad_query_pre, grad_key_pre, grad_values], axis=1).astype(jnp.bfloat16)
    grad_normed_part = jnp.einsum(
        "rce,dce->rd", grad_qkv, w_qkv, preferred_element_type=jnp.float32
    ) + jnp.einsum("rh,dh->rd", grad_pre, w_fc1, preferred_element_type=jnp.float32)
    grad_normed = lax.psum(grad_normed_part.astype(jnp.bfloat16), TE).astype(jnp.float32)
    grad_input, grad_gain, grad_shift = norm_back(grad_normed)
    cot_f = full_cot.astype(jnp.float32)
    grad_own = lax.dynamic_slice_in_dim(
        cot_f + grad_input, tensor_index * feature_share, feature_share, 1
    ).astype(jnp.bfloat16)
    cot_total = jnp.sum(cot_f, axis=0)
    part_qkv_w = jnp.einsum("rd,rce->dce", normed_b, grad_qkv, preferred_element_type=jnp.float32)
    part_qkv_b = jnp.sum(grad_qkv.astype(jnp.float32), axis=0).reshape(b_qkv.shape)
    part_dense_w = jnp.einsum("re,rd->ed", attended_b, full_cot, preferred_element_type=jnp.float32)
    part_fc1_w = jnp.einsum("rd,rh->dh", normed_b, grad_pre, preferred_element_type=jnp.float32)
    part_fc1_b = jnp.sum(grad_pre.astype(jnp.float32), axis=0).reshape(b_fc1.shape)
    part_fc2_w = jnp.einsum("rh,rd->hd", activ_b, full_cot, preferred_element_type=jnp.float32)
    back_rows = []
    back_grads = []
    for micro_index in range(micro_count):
        rows = slice(micro_index * row_count, (micro_index + 1) * row_count)
        back_rows.append(layer_rows[rows][arrive_slots[micro_index]])
        back_grads.append(grad_own[rows][arrive_slots[micro_index]])
    returned = (
        lax.all_to_all(
            jnp.stack(back_rows), (FS, CT), split_axis=1, concat_axis=1, tiled=True
        ),
        lax.all_to_all(
            jnp.stack(back_grads), (FS, CT), split_axis=1, concat_axis=1, tiled=True
        ),
    )
    layer_out = jnp.stack([returned[0][m][return_orders[m]] for m in range(micro_count)])
    grad_tokens = jnp.stack([returned[1][m][return_orders[m]] for m in range(micro_count)])
    shares = (
        lax.psum_scatter(
            grad_gain.astype(jnp.bfloat16), (FS, CT), scatter_dimension=0, tiled=True
        ).astype(jnp.float32),
        lax.psum_scatter(
            grad_shift.astype(jnp.bfloat16), (FS, CT), scatter_dimension=0, tiled=True
        ).astype(jnp.float32),
        lax.psum_scatter(
            part_qkv_w.astype(jnp.bfloat16), (FS, CT), scatter_dimension=0, tiled=True
        ).astype(jnp.float32),
        lax.psum_scatter(
            part_qkv_b.astype(jnp.bfloat16), (FS, CT), scatter_dimension=2, tiled=True
        ).astype(jnp.float32),
        lax.psum_scatter(
            part_dense_w.astype(jnp.bfloat16), (FS, CT), scatter_dimension=1, tiled=True
        ).astype(jnp.float32),
        lax.psum_scatter(
            cot_total.astype(jnp.bfloat16), (FS, CT), scatter_dimension=0, tiled=True
        ).astype(jnp.float32),
        lax.psum_scatter(
            part_fc1_w.astype(jnp.bfloat16), (FS, CT), scatter_dimension=0, tiled=True
        ).astype(jnp.float32),
        lax.psum_scatter(
            part_fc1_b.astype(jnp.bfloat16), (FS, CT), scatter_dimension=1, tiled=True
        ).astype(jnp.float32),
        lax.psum_scatter(
            part_fc2_w.astype(jnp.bfloat16), (FS, CT), scatter_dimension=1, tiled=True
        ).astype(jnp.float32),
        lax.psum_scatter(
            cot_total.astype(jnp.bfloat16), (FS, CT), scatter_dimension=0, tiled=True
        ).astype(jnp.float32),
    )
    reduced = (
        lax.all_gather(shares[0].astype(jnp.bfloat16), CT, axis=0, tiled=True).astype(
            jnp.float32
        ),
        lax.all_gather(shares[1].astype(jnp.bfloat16), CT, axis=0, tiled=True).astype(
            jnp.float32
        ),
        lax.all_gather(shares[2].astype(jnp.bfloat16), CT, axis=0, tiled=True).astype(
            jnp.float32
        ),
        lax.all_gather(shares[3].astype(jnp.bfloat16), CT, axis=2, tiled=True).astype(
            jnp.float32
        ),
        lax.all_gather(shares[4].astype(jnp.bfloat16), CT, axis=1, tiled=True).astype(
            jnp.float32
        ),
        lax.all_gather(shares[5].astype(jnp.bfloat16), CT, axis=0, tiled=True).astype(
            jnp.float32
        ),
        lax.all_gather(shares[6].astype(jnp.bfloat16), CT, axis=0, tiled=True).astype(
            jnp.float32
        ),
        lax.all_gather(shares[7].astype(jnp.bfloat16), CT, axis=1, tiled=True).astype(
            jnp.float32
        ),
        lax.all_gather(shares[8].astype(jnp.bfloat16), CT, axis=1, tiled=True).astype(
            jnp.float32
        ),
        lax.all_gather(shares[9].astype(jnp.bfloat16), CT, axis=0, tiled=True).astype(
            jnp.float32
        ),
    )
    return (
        layer_out,
        grad_tokens,
        reduced[0],
        reduced[1],
        reduced[2],
        reduced[3],
        reduced[4],
        reduced[5],
        reduced[6],
        reduced[7],
        reduced[8],
        reduced[9],
    )


MESH = pl.DeviceIdType.MESH
AXES = ("y", "h", "l", "x", "t")
BLOCK = 256
SPAN = 512


def fits(mesh):
    return (mesh.shape[FS], mesh.shape[CT], mesh.shape[TE]) == (2, 8, 2)


def place():
    return tuple(lax.axis_index(a) for a in AXES)


def greet(peers):
    barrier = pltpu.get_barrier_semaphore()
    total = 0
    for device, there in peers:
        if there is True:
            pl.semaphore_signal(barrier, inc=1, device_id=device, device_id_type=MESH)
            total += 1
        else:

            @pl.when(there)
            def _(device=device):
                pl.semaphore_signal(barrier, inc=1, device_id=device, device_id_type=MESH)

            total = total + there.astype(jnp.int32)
    pl.semaphore_wait(barrier, total)


def spread_kernel(
    tok, cot, w_q, w_d, w_1, w_2, small, tok_all, cot_all, q_out, d_out, o_1, o_2, small_out,
    local_sem, send_sem, recv_sem,
):
    y, h, l, x, t = place()
    z = 2 * h + l
    rows, half = tok.shape[1], tok.shape[2]
    other_y, other_x, other_t = {"y": 1 - y}, {"x": 1 - x}, {"t": 1 - t}

    def along(zz):
        return {"h": zz // 2, "l": lax.rem(zz, 2)}

    greet(
        [(other_y, True), (other_x, True), (other_t, True)]
        + [(along(lax.max(z - 1, 0)), z > 0), (along(lax.min(z + 1, 3)), z < 3)]
    )
    units = [(tok, tok_all, 0, 1), (tok, tok_all, 1, 1), (cot, cot_all, 0, 2)]
    numbers = {}

    def number(key):
        return numbers.setdefault(key, len(numbers))

    def region(unit, chunk, core):
        _, out, m, n = units[unit]
        dy, dx, way, k = chunk
        yy = 1 - y if dy else y
        xx = 1 - x if dx else x
        zz = z - k if way == "up" else z + k
        group = yy * 8 + zz * 2 + xx
        return out.at[
            pl.ds(m, n),
            pl.ds(pl.multiple_of(group * rows, rows), rows),
            pl.ds(pl.multiple_of(core * half, half), half),
        ]

    def own(unit):
        array, _, m, n = units[unit]
        return array.at[pl.ds(m, n)]

    started = []

    def send(unit, chunk, key, device):
        source = own(unit) if chunk == (0, 0, "up", 0) else region(unit, chunk, t)
        i = number((unit,) + key)
        copy = pltpu.make_async_remote_copy(
            src_ref=source, dst_ref=region(unit, chunk, t), send_sem=send_sem.at[i],
            recv_sem=recv_sem.at[i], device_id=device, device_id_type=MESH,
        )
        copy.start()
        return copy

    def arrive(unit, chunk, key, core):
        i = number((unit,) + key)
        ref = region(unit, chunk, core)
        pltpu.make_async_remote_copy(
            src_ref=ref, dst_ref=ref, send_sem=send_sem.at[i], recv_sem=recv_sem.at[i],
            device_id=other_t, device_id_type=MESH,
        ).wait_recv()

    def sent(unit, chunk, key):
        i = number((unit,) + key)
        ref = own(unit)
        pltpu.make_async_remote_copy(
            src_ref=ref, dst_ref=ref, send_sem=send_sem.at[i], recv_sem=recv_sem.at[i],
            device_id=other_t, device_id_type=MESH,
        ).wait_send()

    def when(there, what):
        if there is True:
            what()
        else:
            pl.when(there)(what)

    def there_of(way, k):
        return True if k == 0 else (z >= k if way == "up" else z + k <= 3)

    def to_core(unit, chunk):
        key = chunk + ("core",)
        send(unit, chunk, key, other_t)
        started.append((unit, chunk, key, None))

    def onward(unit, chunk, axis):
        dy, dx, way, k = chunk
        key = ((1, dx, way, k) if axis == "y" else (dy, 1, way, k)) + ("link",)
        send(unit, chunk, key, other_y if axis == "y" else other_x)
        started.append((unit, chunk, key, None))

    def up_down(unit, chunk):
        dy, dx, way, k = chunk
        for going in ("up", "down") if k == 0 else (way,):
            can = z < 3 if going == "up" else z > 0
            key = (dy, dx, going, k + 1, "link")
            target = along(lax.min(z + 1, 3) if going == "up" else lax.max(z - 1, 0))
            when(can, lambda: send(unit, chunk, key, target) and None)
            started.append((unit, chunk, key, going))

    def got(unit, chunk):
        arrive(unit, chunk, chunk + ("link",), t)

    steps = [[("up", 0)], [("up", 1), ("down", 1)], [("up", 2), ("down", 2)], [("up", 3), ("down", 3)]]
    block = (y * 4 + l * 2 + x, (1 - y) * 4 + l * 2 + x)
    pieces = []
    depth = w_1.shape[0]
    for b, to in ((block[1], True), (block[0], False)):
        row = pl.ds(pl.multiple_of(y * depth, depth), depth)
        wide, narrow = w_1.shape[1] // 8, w_d.shape[0] // 8
        pieces.append([
            (w_1.at[:, pl.ds(pl.multiple_of(b * wide, wide), wide)], o_1.at[row]),
            (w_2.at[pl.ds(pl.multiple_of(b * wide, wide), wide)], o_2.at[:, row]),
            (w_q.at[:, :, pl.ds(pl.multiple_of(b * narrow, narrow), narrow)], q_out.at[:, row]),
            (w_d.at[pl.ds(pl.multiple_of(b * narrow, narrow), narrow)], d_out.at[:, row]),
            (small, small_out.at[y]),
        ])
    locals_, weights = [], []
    first = (0, 0, "up", 0)
    for u in range(3):
        up_down(u, first) if u else None
    for u in range(3):
        onward(u, first, "y")
    for i, (source, target) in enumerate(pieces[0]):
        copy = pltpu.make_async_remote_copy(
            src_ref=source, dst_ref=target, send_sem=send_sem.at[number(("w", i))],
            recv_sem=recv_sem.at[number(("w", i))], device_id=other_y, device_id_type=MESH,
        )
        copy.start()
        weights.append(copy)
    for u in range(3):
        onward(u, first, "x")
        to_core(u, first)
        copy = pltpu.make_async_copy(own(u), region(u, first, t), local_sem.at[len(locals_)])
        copy.start()
        locals_.append(copy)
    for source, target in pieces[1]:
        copy = pltpu.make_async_copy(source, target, local_sem.at[len(locals_)])
        copy.start()
        locals_.append(copy)

    got(0, (1, 0, "up", 0))
    onward(0, (1, 0, "up", 0), "x")
    up_down(0, first)
    up_down(0, (1, 0, "up", 0))
    to_core(0, (1, 0, "up", 0))

    def rest_of_first():
        for dy in (0, 1):
            got(0, (dy, 1, "up", 0))
            up_down(0, (dy, 1, "up", 0))
            to_core(0, (dy, 1, "up", 0))

    def z_step(s):
        for u in (1, 2):
            for way, k in steps[s]:
                def act(u=u, c=(0, 0, way, k)):
                    got(u, c)
                    up_down(u, c) if c[3] < 3 else None
                    onward(u, c, "y")
                    onward(u, c, "x")
                    to_core(u, c)
                when(there_of(way, k), act)

    def y_step(s):
        for u in (1, 2):
            for way, k in steps[s]:
                def act(u=u, c=(1, 0, way, k)):
                    got(u, c)
                    onward(u, c, "x")
                    to_core(u, c)
                when(there_of(way, k), act)

    def x_step(s):
        for u in (1, 2):
            for way, k in steps[s]:
                def act(u=u, way=way, k=k):
                    for dy in (0, 1):
                        got(u, (dy, 1, way, k))
                        to_core(u, (dy, 1, way, k))
                when(there_of(way, k), act)

    def first_step(s):
        for way, k in steps[s]:
            def act(way=way, k=k):
                for dy in (0, 1):
                    for dx in (0, 1):
                        c = (dy, dx, way, k)
                        got(0, c)
                        up_down(0, c) if k < 3 else None
                        to_core(0, c)
            when(there_of(way, k), act)

    z_step(1)
    rest_of_first()
    y_step(0)
    z_step(2)
    y_step(1)
    x_step(0)
    first_step(1)
    z_step(3)
    y_step(2)
    x_step(1)
    first_step(2)
    y_step(3)
    x_step(2)
    first_step(3)
    x_step(3)
    for u in range(3):
        for dy in (0, 1):
            for dx in (0, 1):
                for s in range(4):
                    for way, k in steps[s]:
                        c = (dy, dx, way, k)
                        when(there_of(way, k), lambda: arrive(u, c, c + ("core",), 1 - t))
    for copy in locals_:
        copy.wait()
    for copy in weights:
        copy.wait()
    for unit, chunk, key, going in started:
        there = there_of(*chunk[2:])
        if going is not None:
            can = z < 3 if going == "up" else z > 0
            there = can if there is True else can & there
        when(there, lambda: sent(unit, chunk, key))


def spread(tokens, cotangent, w_q, w_d, w_1, w_2, small):
    micro, rows, half = tokens.shape
    everything = jax.ShapeDtypeStruct((micro, rows * 16, half * 2), tokens.dtype)
    depth = w_1.shape[0] * 2
    outs = [
        everything,
        everything,
        jax.ShapeDtypeStruct((3, depth, w_q.shape[2] // 8), w_q.dtype),
        jax.ShapeDtypeStruct((w_d.shape[0] // 8, depth), w_d.dtype),
        jax.ShapeDtypeStruct((depth, w_1.shape[1] // 8), w_1.dtype),
        jax.ShapeDtypeStruct((w_2.shape[0] // 8, depth), w_2.dtype),
        jax.ShapeDtypeStruct((2,) + small.shape, small.dtype),
    ]
    return pl.pallas_call(
        spread_kernel,
        out_shape=outs,
        in_specs=[pl.BlockSpec(memory_space=pl.ANY)] * 7,
        out_specs=[pl.BlockSpec(memory_space=pl.ANY)] * 7,
        scratch_shapes=[
            pltpu.SemaphoreType.DMA((8,)),
            pltpu.SemaphoreType.DMA((176,)),
            pltpu.SemaphoreType.DMA((176,)),
        ],
        compiler_params=pltpu.CompilerParams(collective_id=0, has_side_effects=True),
        name="spread",
    )(tokens, cotangent, w_q, w_d, w_1, w_2, small)


def join_kernel(count, parts, outs, local_sem, send_sem, recv_sem):
    y, h, l, x, t = place()
    device = {"y": {"y": 1 - y}, "l": {"l": 1 - l}, "x": {"x": 1 - x}}
    greet([(device[a], True) for a in ("y", "l", "x")])

    def half_of(i, yy):
        ref, d_axis, _, _ = parts[i]
        if d_axis is None:
            return ref
        n = ref.shape[d_axis] // 2
        where = [slice(None)] * len(ref.shape)
        where[d_axis] = pl.ds(pl.multiple_of(yy * n, n), n)
        return ref.at[tuple(where)]

    def spot(i, yy, ll, xx):
        ref, _, b_axis, _ = parts[i]
        n = ref.shape[b_axis]
        where = [slice(None)] * len(ref.shape)
        where[b_axis] = pl.ds(pl.multiple_of((yy * 4 + ll * 2 + xx) * n, n), n)
        return outs[i].at[tuple(where)]

    numbers = {}

    def number(key):
        return numbers.setdefault(key, len(numbers))

    sends = []

    def send(i, source, target, key, axis):
        n = number((i,) + key)
        copy = pltpu.make_async_remote_copy(
            src_ref=source, dst_ref=target, send_sem=send_sem.at[n], recv_sem=recv_sem.at[n],
            device_id=device[axis], device_id_type=MESH,
        )
        copy.start()
        sends.append(copy)

    def got(i, target, key):
        n = number((i,) + key)
        pltpu.make_async_remote_copy(
            src_ref=target, dst_ref=target, send_sem=send_sem.at[n], recv_sem=recv_sem.at[n],
            device_id=device["y"], device_id_type=MESH,
        ).wait_recv()

    every = range(count)
    hop = {"x": "l", "l": "x"}
    first = {i: parts[i][3] for i in every}
    for i in every:
        send(i, half_of(i, 1 - y), spot(i, y, l, x), ("y",), "y")
    for i in every:
        send(i, half_of(i, y), spot(i, y, l, x), (0, first[i]), first[i])
    for i in every:
        send(i, half_of(i, y), spot(i, y, l, x), (0, hop[first[i]]), hop[first[i]])
    locals_ = []
    for i in every:
        copy = pltpu.make_async_copy(half_of(i, y), spot(i, y, l, x), local_sem.at[i])
        copy.start()
        locals_.append(copy)

    def beside(i, axis, yy):
        return spot(i, yy, 1 - l if axis == "l" else l, 1 - x if axis == "x" else x)

    for i in every:
        a = first[i]
        got(i, beside(i, a, y), (0, a))
        send(i, beside(i, a, y), beside(i, a, y), (0, "far"), hop[a])
    for i in every:
        got(i, spot(i, 1 - y, l, x), ("y",))
        send(i, spot(i, 1 - y, l, x), spot(i, 1 - y, l, x), (1, first[i]), first[i])
        send(i, spot(i, 1 - y, l, x), spot(i, 1 - y, l, x), (1, hop[first[i]]), hop[first[i]])
    for i in every:
        a = first[i]
        got(i, beside(i, a, 1 - y), (1, a))
        send(i, beside(i, a, 1 - y), beside(i, a, 1 - y), (1, "far"), hop[a])
    for i in every:
        for yy, side in ((y, 0), (1 - y, 1)):
            got(i, beside(i, hop[first[i]], yy), (side, hop[first[i]]))
            got(i, spot(i, yy, 1 - l, 1 - x), (side, "far"))
    for copy in locals_:
        copy.wait()
    for copy in sends:
        copy.wait_send()


def join(arrays, plan, shapes, collective_id, name):
    count = len(arrays)

    def kernel(*refs):
        parts = [(refs[i],) + plan[i] for i in range(count)]
        join_kernel(count, parts, refs[count : 2 * count], *refs[2 * count :])

    return pl.pallas_call(
        kernel,
        out_shape=[jax.ShapeDtypeStruct(s, a.dtype) for s, a in zip(shapes, arrays)],
        in_specs=[pl.BlockSpec(memory_space=pl.ANY)] * count,
        out_specs=[pl.BlockSpec(memory_space=pl.ANY)] * count,
        scratch_shapes=[
            pltpu.SemaphoreType.DMA((count,)),
            pltpu.SemaphoreType.DMA((7 * count,)),
            pltpu.SemaphoreType.DMA((7 * count,)),
        ],
        compiler_params=pltpu.CompilerParams(collective_id=collective_id, has_side_effects=True),
        name=name,
    )(*arrays)


NN = (((1,), (0,)), ((), ()))
NT = (((1,), (1,)), ((), ()))
TN = (((0,), (0,)), ((), ()))


def dot(a, b, dims=NN):
    return lax.dot_general(a, b, dims, preferred_element_type=jnp.float32)


def fold_kernel(
    activ, grad_pre, back, tok_all, cot, w_1, w_2, w_q, w_d, gain, out_shift, layer_out, grad_out, ln_out,
    act_v, pre_v, back_v, tok_v, give, core_in, give_n, sum_in, stat_v, stat_in, ln_v, ln_in,
    load_sem, core_send, core_recv, hop_send, hop_recv, small_send, small_recv,
):
    y, h, l, x, t = place()
    rows, share = cot.shape[1], cot.shape[2]
    both = 2 * rows
    device = {"y": {"y": 1 - y}, "l": {"l": 1 - l}, "x": {"x": 1 - x}, "t": {"t": 1 - t}, "h": {"h": 1 - h}}
    narrow = w_d.shape[0]
    loads = []

    def load(source, target):
        copy = pltpu.make_async_copy(source, target, load_sem.at[len(loads)])
        copy.start()
        loads.append(copy)

    def group_rows(dy, dl, dx):
        yy = 1 - y if dy else y
        ll = 1 - l if dl else l
        xx = 1 - x if dx else x
        return pl.ds(pl.multiple_of((yy * 8 + h * 4 + ll * 2 + xx) * rows, rows), rows)

    owners = [(1, 0, 1), (1, 1, 1), (0, 0, 1), (0, 1, 1), (1, 0, 0), (1, 1, 0), (0, 1, 0), (0, 0, 0)]
    arrived = {}
    for o, owner in enumerate(owners):
        start = len(loads)
        for m in range(2):
            there = pl.ds(m * rows, rows)
            load(activ.at[m, group_rows(*owner)], act_v.at[o, there])
            load(back.at[m, group_rows(*owner)], back_v.at[o, there])
            load(grad_pre.at[m, group_rows(*owner)], pre_v.at[o, there])
        arrived[o] = loads[start:]
    start = len(loads)
    for m in range(2):
        load(tok_all.at[m, group_rows(0, 0, 0)], tok_v.at[pl.ds(m * rows, rows)])
    tok_loads = loads[start:]
    greet([(device[a], True) for a in ("t", "x", "y", "l", "h")])

    def part(a, o, tt):
        columns = pl.ds(pl.multiple_of(tt * share, share), share)
        if a == 0:
            return dot(act_v[o], w_2[:, columns]) + dot(back_v[o, :, 0:narrow], w_d[:, columns])
        total = dot(pre_v[o], w_1[columns, :], NT)
        for c in range(3):
            total += dot(back_v[o, :, (c + 1) * narrow : (c + 2) * narrow], w_q[c, columns, :], NT)
        return total

    core = {}

    def offer(a, o):
        if o in arrived:
            for copy in arrived.pop(o):
                copy.wait()
        i = a * 8 + o
        give[i] = part(a, o, 1 - t).astype(jnp.bfloat16)
        core[i] = pltpu.make_async_remote_copy(
            src_ref=give.at[i], dst_ref=core_in.at[i], send_sem=core_send.at[i], recv_sem=core_recv.at[i],
            device_id=device["t"], device_id_type=MESH,
        )
        core[i].start()

    hops = {0: ("x", "y", "l"), 1: ("y", "x", "l")}
    place_of = {"y": 0, "l": 1, "x": 2}
    slots, passed = {}, {}

    def slot(a, stage, owner):
        return slots.setdefault((a, stage, owner), len(slots))

    def total_of(a, o, stage):
        i = a * 8 + o
        total = part(a, o, t)
        core[i].wait_recv()
        total += core_in[i].astype(jnp.float32)
        for s in range(stage):
            n = slot(a, s, owners[o])
            passed[n].wait_recv()
            total += sum_in[n].astype(jnp.float32)
        return total

    def stage_owners(a, stage):
        done = [place_of[d] for d in hops[a][:stage]]
        now = place_of[hops[a][stage]]
        return [o for o, w in enumerate(owners) if all(w[d] == 0 for d in done) and w[now] == 1]

    def pass_on(a, o, stage):
        axis = hops[a][stage]
        seen = list(owners[o])
        seen[place_of[axis]] = 0
        n = slot(a, stage, tuple(seen))
        give_n[n] = total_of(a, o, stage).astype(jnp.bfloat16)
        passed[n] = pltpu.make_async_remote_copy(
            src_ref=give_n.at[n], dst_ref=sum_in.at[n], send_sem=hop_send.at[n], recv_sem=hop_recv.at[n],
            device_id=device[axis], device_id_type=MESH,
        )
        passed[n].start()

    order = []
    for stage in range(3):
        for pair in zip(stage_owners(0, stage), stage_owners(1, stage)):
            order += [(a, o, stage) for a, o in enumerate(pair)]
    ahead = 2
    queue = [(a, o) for a, o, _ in order] + [(0, 7), (1, 7)]
    for a, o in queue[:ahead]:
        offer(a, o)
    for i, (a, o, stage) in enumerate(order):
        if stage == 0:
            offer(*queue[i + ahead])
            pass_on(a, o, stage)
            if i == 7:
                for item in queue[i + ahead + 1 :]:
                    offer(*item)
        else:
            pass_on(a, o, stage)
    for copy in tok_loads:
        copy.wait()
    mine = pl.ds(pl.multiple_of(t * share, share), share)
    values = tok_v[...].astype(jnp.float32)
    mean = jnp.mean(values, axis=1, keepdims=True)
    spread_of = jnp.mean((values - mean) ** 2, axis=1, keepdims=True)
    r = lax.rsqrt(spread_of + EPSILON)
    token = tok_v[:, mine].astype(jnp.float32)
    hat = (token - mean) * r
    norm_sum = total_of(1, 7, 3)
    scaled = norm_sum * gain[:, mine]
    stat_v[:, 0:128] = jnp.broadcast_to(jnp.sum(scaled, axis=1, keepdims=True), (both, 128))
    stat_v[:, 128:256] = jnp.broadcast_to(jnp.sum(scaled * hat, axis=1, keepdims=True), (both, 128))
    stat = pltpu.make_async_remote_copy(
        src_ref=stat_v, dst_ref=stat_in, send_sem=small_send.at[0], recv_sem=small_recv.at[0],
        device_id=device["t"], device_id_type=MESH,
    )
    stat.start()
    top = lax.broadcasted_iota(jnp.int32, (8, share), 0) == 0
    ln_v[0] = jnp.where(
        top, jnp.sum(norm_sum * hat, axis=0, keepdims=True), jnp.sum(norm_sum, axis=0, keepdims=True)
    )
    smalls = [stat]

    def swap(step, axis):
        copy = pltpu.make_async_remote_copy(
            src_ref=ln_v.at[step], dst_ref=ln_in.at[step], send_sem=small_send.at[step + 1],
            recv_sem=small_recv.at[step + 1], device_id=device[axis], device_id_type=MESH,
        )
        copy.start()
        smalls.append(copy)
        return copy

    first = swap(0, "h")
    out = token + total_of(0, 7, 3) + out_shift[:, mine]
    for m in range(2):
        layer_out[m] = out[m * rows : (m + 1) * rows].astype(jnp.bfloat16)
    first.wait_recv()
    ln_v[1] = ln_v[0] + ln_in[0]
    second = swap(1, "l")
    stat.wait_recv()
    width = 2 * share
    mean_t = (stat_v[:, 0:1] + stat_in[:, 0:1]) / width
    mean_h = (stat_v[:, 128:129] + stat_in[:, 128:129]) / width
    grad = r * (scaled - mean_t - hat * mean_h)
    for m in range(2):
        grad_out[m] = (cot[m].astype(jnp.float32) + grad[m * rows : (m + 1) * rows]).astype(jnp.bfloat16)
    second.wait_recv()
    ln_v[2] = ln_v[1] + ln_in[1]
    swap(2, "x").wait_recv()
    ln_v[3] = ln_v[2] + ln_in[2]
    swap(3, "y").wait_recv()
    ln_v[4] = ln_v[3] + ln_in[3]
    swap(4, "t").wait_recv()
    ln_out[...] = jnp.where(t == y, ln_v[4], ln_in[4])
    for copy in core.values():
        copy.wait_send()
    for copy in passed.values():
        copy.wait_send()
    for copy in smalls:
        copy.wait_send()


def fold(activ, grad_pre, back, tok_all, cot, w_1, w_2, w_q, w_d, gain, out_shift):
    micro, rows, share = cot.shape
    both = micro * rows
    narrow = w_d.shape[0]
    held = lambda n, w: pltpu.VMEM((n, both, w), jnp.bfloat16)
    sem = pltpu.SemaphoreType.DMA
    any_, vmem = pl.BlockSpec(memory_space=pl.ANY), pl.BlockSpec(memory_space=pltpu.VMEM)
    return pl.pallas_call(
        fold_kernel,
        out_shape=[
            jax.ShapeDtypeStruct(cot.shape, cot.dtype),
            jax.ShapeDtypeStruct(cot.shape, cot.dtype),
            jax.ShapeDtypeStruct((8, share), jnp.float32),
        ],
        in_specs=[any_] * 4 + [vmem] * 7,
        out_specs=[vmem] * 3,
        scratch_shapes=[
            held(8, w_1.shape[1]),
            held(8, w_1.shape[1]),
            held(8, 4 * narrow),
            pltpu.VMEM((both, 2 * share), jnp.bfloat16),
            held(16, share),
            held(16, share),
            held(14, share),
            held(14, share),
            pltpu.VMEM((both, 256), jnp.float32),
            pltpu.VMEM((both, 256), jnp.float32),
            pltpu.VMEM((5, 8, share), jnp.float32),
            pltpu.VMEM((5, 8, share), jnp.float32),
            sem((50,)),
            sem((16,)),
            sem((16,)),
            sem((14,)),
            sem((14,)),
            sem((6,)),
            sem((6,)),
        ],
        compiler_params=pltpu.CompilerParams(
            collective_id=3, has_side_effects=True, vmem_limit_bytes=60 << 20
        ),
        name="fold",
    )(activ, grad_pre, back, tok_all, cot, w_1, w_2, w_q, w_d, gain, out_shift)


ROOT = 0.7978845608028654
CUBE = 0.044715


def rows_kernel(
    tok, cot, w_1, w_2, w_q, w_d, gain, shift, f_shift, q_shift,
    normed_out, activ_out, pre_out, four_out, g_1, g_2, cot_sum, pre_sum, acc_1, acc_2,
):
    step = pl.program_id(0)

    @pl.when(step == 0)
    def _():
        acc_1[...] = jnp.zeros_like(acc_1)
        acc_2[...] = jnp.zeros_like(acc_2)
        cot_sum[...] = jnp.zeros_like(cot_sum)
        pre_sum[...] = jnp.zeros_like(pre_sum)

    f32, bf16 = jnp.float32, jnp.bfloat16
    values = tok[0].astype(f32)
    center = values - jnp.mean(values, axis=1, keepdims=True)
    r = lax.rsqrt(jnp.mean(center * center, axis=1, keepdims=True) + EPSILON)
    normed = (center * r * gain[...] + shift[...]).astype(bf16)
    normed_out[0] = normed
    cots = cot[0]
    pre = dot(normed, w_1[...]) + f_shift[...]
    square = pre * pre
    curve = jnp.tanh(ROOT * (pre + CUBE * pre * square))
    activ = (0.5 * pre * (1.0 + curve)).astype(bf16)
    slope = 0.5 * (1.0 + curve) + 0.5 * pre * (1.0 - curve * curve) * (ROOT * (1.0 + 3.0 * CUBE * square))
    grad_pre = (dot(cots, w_2[...], NT) * slope).astype(bf16)
    activ_out[0] = activ
    pre_out[0] = grad_pre
    narrow = w_d.shape[0]
    for c in range(3):
        at = slice(c * narrow, (c + 1) * narrow)
        four_out[0, :, at] = (dot(normed, w_q[c]) + q_shift[:, at]).astype(bf16)
    four_out[0, :, 3 * narrow :] = dot(cots, w_d[...], NT).astype(bf16)
    acc_1[...] += dot(normed, grad_pre, TN)
    acc_2[...] += dot(activ, cots, TN)
    cot_sum[...] += jnp.sum(cots.astype(f32), axis=0, keepdims=True)
    pre_sum[...] += jnp.sum(grad_pre.astype(f32), axis=0, keepdims=True)

    @pl.when(step == pl.num_programs(0) - 1)
    def _():
        g_1[...] = acc_1[...].astype(bf16)
        g_2[...] = acc_2[...].astype(bf16)


def row_work(tok_all, cot_all, w_1, w_2, w_q, w_d, gain, shift, f_shift, q_shift, size):
    micro, total, width = tok_all.shape
    per = total // size
    wide = w_1.shape[1]
    narrow = w_d.shape[0]
    bf16, f32 = jnp.bfloat16, jnp.float32

    def block(w):
        return pl.BlockSpec((1, size, w), lambda i: (i // per, i % per, 0))

    def whole(a):
        return pl.BlockSpec(a.shape, lambda i: (0,) * len(a.shape), pipeline_mode=pl.Buffered(1))

    def fixed(*s):
        return pl.BlockSpec(s, lambda i: (0,) * len(s))

    consts = (w_1, w_2, w_q, w_d, gain, shift, f_shift, q_shift)
    return pl.pallas_call(
        rows_kernel,
        grid=(micro * per,),
        out_shape=[
            jax.ShapeDtypeStruct(tok_all.shape, bf16),
            jax.ShapeDtypeStruct((micro, total, wide), bf16),
            jax.ShapeDtypeStruct((micro, total, wide), bf16),
            jax.ShapeDtypeStruct((micro, total, 4 * narrow), bf16),
            jax.ShapeDtypeStruct(w_1.shape, bf16),
            jax.ShapeDtypeStruct(w_2.shape, bf16),
            jax.ShapeDtypeStruct((1, width), f32),
            jax.ShapeDtypeStruct((1, wide), f32),
        ],
        in_specs=[block(width), block(width)] + [whole(a) for a in consts],
        out_specs=[
            block(width), block(wide), block(wide), block(4 * narrow),
            fixed(*w_1.shape), fixed(*w_2.shape), fixed(1, width), fixed(1, wide),
        ],
        scratch_shapes=[pltpu.VMEM(w_1.shape, f32), pltpu.VMEM(w_2.shape, f32)],
        compiler_params=pltpu.CompilerParams(vmem_limit_bytes=60 << 20),
        name="row_work",
    )(tok_all, cot_all, *consts)


def swap_rotary(values):
    lane = lax.rem(lax.broadcasted_iota(jnp.int32, values.shape, 1), 64)
    half = ROT // 2
    width = values.shape[1]
    return jnp.where(
        lane < half, pltpu.roll(values, width - half, 1), pltpu.roll(values, half, 1)
    )


def attend_kernel(four, perm, seg_q, seg_k, pos, freq, sign, back_ref, laid, gq, gk, gv, cos_v, sin_v):
    pack = pl.program_id(1)
    pack_rows, width = back_ref.shape[1], back_ref.shape[2] // 4
    bf16, f32 = jnp.bfloat16, jnp.float32
    scale = 64 ** (-0.5)
    lane = lax.broadcasted_iota(jnp.int32, (1, width), 1)
    total = four.shape[1]
    for block in range(pack_rows // BLOCK):
        here = slice(block * BLOCK, (block + 1) * BLOCK)
        target = pack * pack_rows + block * BLOCK + lax.broadcasted_iota(jnp.int32, (BLOCK, total), 0)
        chosen = jnp.where(perm[0] == target, 1.0, 0.0).astype(bf16)
        got = dot(chosen, four[0])
        angle = pos[0, here, :] * freq[...]
        cos, sin = jnp.cos(angle), jnp.sin(angle) * sign[...]
        cos_v[here, :] = cos
        sin_v[here, :] = sin
        for c in range(2):
            at = slice(c * width, (c + 1) * width)
            part = got[:, at]
            laid[here, at] = (part * cos + swap_rotary(part) * sin).astype(bf16)
        laid[here, 2 * width :] = got[:, 2 * width :].astype(bf16)
    gk[...] = jnp.zeros_like(gk)
    gv[...] = jnp.zeros_like(gv)
    for block in range(pack_rows // BLOCK):
        low = max(0, block * BLOCK - SPAN)
        high = (block + 1) * BLOCK
        here = slice(block * BLOCK, high)
        keys = laid[low:high, width : 2 * width]
        values = laid[low:high, 2 * width : 3 * width]
        row = lax.broadcasted_iota(jnp.int32, (BLOCK, high - low), 0) + block * BLOCK
        column = lax.broadcasted_iota(jnp.int32, (BLOCK, high - low), 1) + low
        allowed = (seg_q[0, here, :] == seg_k[0, :, low:high]) & (column <= row)
        attended = None
        for head in range(2):
            mine = (lane // 64) == head
            query = jnp.where(mine, laid[here, 0:width], 0)
            grad = jnp.where(mine, laid[here, 3 * width : 4 * width], 0)
            key = jnp.where(mine, keys, 0)
            value = jnp.where(mine, values, 0)
            scores = jnp.where(allowed, dot(query, key, NT) * scale, NEG_FILL)
            peak = jnp.max(scores, axis=1, keepdims=True)
            weights = jnp.exp(scores - peak)
            weights = weights * (1.0 / jnp.sum(weights, axis=1, keepdims=True))
            weights_b = weights.astype(bf16)
            out = dot(weights_b, value)
            attended = out if attended is None else attended + out
            delta = jnp.sum(grad.astype(f32) * out, axis=1, keepdims=True)
            inner = dot(grad, value, NT)
            grad_scores = (weights * (inner - delta)).astype(bf16)
            part = dot(grad_scores, key)
            if head == 0:
                gq[here, :] = part
            else:
                gq[here, :] += part
            gk[low:high, :] += dot(grad_scores, query, TN)
            gv[low:high, :] += dot(weights_b, grad, TN)
        back_ref[0, here, 0:width] = attended.astype(bf16)
    for c, ref in ((1, gq), (2, gk)):
        grads = ref[...] * scale
        turned = grads * cos_v[...] - swap_rotary(grads) * sin_v[...]
        back_ref[0, :, c * width : (c + 1) * width] = turned.astype(bf16)
    back_ref[0, :, 3 * width :] = gv[...].astype(bf16)


def attend(four, permutation, segment, position, packs):
    micro, total, wide = four.shape
    pack_rows = total // packs
    width = wide // 4
    lane = jnp.arange(width, dtype=jnp.int32) % 64
    power = ROPE_BASE ** (-2.0 * (lane % (ROT // 2)).astype(jnp.float32) / ROT)
    freq = jnp.where(lane < ROT, power, 0.0)[None, :]
    sign = jnp.where(lane < ROT // 2, -1.0, 1.0)[None, :]

    def by_pack(*s):
        return pl.BlockSpec((1,) + s, lambda m, k: (m * packs + k, 0, 0))

    line = pl.BlockSpec((1, width), lambda m, k: (0, 0))
    plane = pltpu.VMEM((pack_rows, width), jnp.float32)
    return pl.pallas_call(
        attend_kernel,
        grid=(micro, packs),
        out_shape=jax.ShapeDtypeStruct((micro * packs, pack_rows, wide), jnp.bfloat16),
        in_specs=[
            pl.BlockSpec((1, total, wide), lambda m, k: (m, 0, 0)),
            pl.BlockSpec((1, 1, total), lambda m, k: (m, 0, 0)),
            by_pack(pack_rows, 1),
            by_pack(1, pack_rows),
            by_pack(pack_rows, 1),
            line,
            line,
        ],
        out_specs=by_pack(pack_rows, wide),
        scratch_shapes=[pltpu.VMEM((pack_rows, wide), jnp.bfloat16)] + [plane] * 5,
        compiler_params=pltpu.CompilerParams(vmem_limit_bytes=48 << 20),
        name="attend",
    )(
        four, permutation[:, None, :], segment[:, :, None], segment[:, None, :],
        position.astype(jnp.float32)[:, :, None], freq, sign,
    )


def after_kernel(laid, perm, normed, cot, back_out, g_d, g_q, qkv_sum, acc_d, acc_q):
    step = pl.program_id(0)

    @pl.when(step == 0)
    def _():
        acc_d[...] = jnp.zeros_like(acc_d)
        acc_q[...] = jnp.zeros_like(acc_q)
        qkv_sum[...] = jnp.zeros_like(qkv_sum)

    f32, bf16 = jnp.float32, jnp.bfloat16
    size, total = normed.shape[1], laid.shape[1]
    narrow = laid.shape[2] // 4
    column = lax.broadcasted_iota(jnp.int32, (size, total), 1)
    chosen = jnp.where(perm[0] == column, 1.0, 0.0).astype(bf16)
    back = dot(chosen, laid[0]).astype(bf16)
    back_out[0] = back
    grads = back[:, narrow:]
    acc_d[...] += dot(back[:, :narrow], cot[0], TN)
    acc_q[...] += dot(normed[0], grads, TN)
    qkv_sum[...] += jnp.sum(grads.astype(f32), axis=0, keepdims=True)

    @pl.when(step == pl.num_programs(0) - 1)
    def _():
        g_d[...] = acc_d[...].astype(bf16)
        for c in range(3):
            g_q[c] = acc_q[:, c * narrow : (c + 1) * narrow].astype(bf16)


def after(laid, permutation, normed, cot_all, size):
    micro, total, wide = laid.shape
    width = normed.shape[2]
    narrow = wide // 4
    per = total // size

    def block(w):
        return pl.BlockSpec((1, size, w), lambda i: (i // per, i % per, 0))

    def fixed(*s):
        return pl.BlockSpec(s, lambda i: (0,) * len(s))

    return pl.pallas_call(
        after_kernel,
        grid=(micro * per,),
        out_shape=[
            jax.ShapeDtypeStruct(laid.shape, jnp.bfloat16),
            jax.ShapeDtypeStruct((narrow, width), jnp.bfloat16),
            jax.ShapeDtypeStruct((3, width, narrow), jnp.bfloat16),
            jax.ShapeDtypeStruct((1, 3 * narrow), jnp.float32),
        ],
        in_specs=[
            pl.BlockSpec((1, total, wide), lambda i: (i // per, 0, 0)),
            block(1),
            block(width),
            block(width),
        ],
        out_specs=[block(wide), fixed(narrow, width), fixed(3, width, narrow), fixed(1, 3 * narrow)],
        scratch_shapes=[
            pltpu.VMEM((narrow, width), jnp.float32),
            pltpu.VMEM((width, 3 * narrow), jnp.float32),
        ],
        compiler_params=pltpu.CompilerParams(vmem_limit_bytes=48 << 20),
        name="after",
    )(laid, permutation[:, :, None], normed, cot_all)


def fast_body(
    tokens, cotangent, lengths, permutation, ln_gain, ln_bias, qkv_weight, qkv_bias,
    dense_weight, dense_bias, fc1_weight, fc1_bias, fc2_weight, fc2_bias,
):
    y, h, l, x, t = place()
    f32 = jnp.float32
    micro, rows, share = tokens.shape
    width = share * 2
    total = rows * 16
    pack_rows = rows * 8
    packs = total // pack_rows
    block = y * 4 + l * 2 + x
    wide = fc1_weight.shape[1] // 8
    narrow = dense_weight.shape[0] // 8
    small = jnp.concatenate(
        [a.reshape(-1) for a in (ln_gain, ln_bias, dense_bias, fc2_bias, qkv_bias, fc1_bias)]
    )
    small = jnp.pad(small, (0, 64 * 128 - small.shape[0])).reshape(64, 128)
    tok_all, cot_all, w_q, w_d, w_1, w_2, small = spread(
        tokens, cotangent, qkv_weight.transpose(1, 0, 2), dense_weight, fc1_weight, fc2_weight, small
    )
    small = small.reshape(2, 64 * 128).astype(f32)
    gain = small[:, 0:share].reshape(1, width)
    shift = small[:, share : 2 * share].reshape(1, width)
    out_shift = (small[:, 2 * share : 3 * share] + small[:, 3 * share : 4 * share]).reshape(1, width)
    at = 4 * share
    q_shift = small[:, at : at + qkv_bias.size].reshape((2,) + qkv_bias.shape)
    q_shift = q_shift.transpose(1, 2, 0, 3).reshape(3, -1)
    at += qkv_bias.size
    f_shift = small[:, at : at + fc1_bias.size].reshape((2,) + fc1_bias.shape).transpose(1, 0, 2).reshape(-1)
    q_shift = lax.dynamic_slice_in_dim(q_shift, block * narrow, narrow, 1).reshape(1, -1)
    f_shift = lax.dynamic_slice_in_dim(f_shift, block * wide, wide, 0).reshape(1, -1)

    places = jnp.arange(pack_rows, dtype=jnp.int32)
    segment, position = jax.vmap(lambda row: segment_layout(row, places))(
        lengths.reshape(micro * packs, -1)
    )
    normed, activ, grad_pre, four, g_w1, g_w2, cot_sum, pre_sum = row_work(
        tok_all, cot_all, w_1, w_2, w_q, w_d, gain, shift, f_shift, q_shift, 4 * rows
    )
    laid = attend(four, permutation, segment, position, packs)
    back, g_wd, g_wq, qkv_sum = after(
        laid.reshape(micro, total, -1), permutation, normed, cot_all, 4 * rows
    )
    layer_out, grad_tokens, g_ln = fold(
        activ, grad_pre, back, tok_all, cotangent, w_1, w_2, w_q, w_d, gain, out_shift
    )
    g_bias = jnp.pad(jnp.concatenate([qkv_sum, pre_sum], 1), ((0, 7), (0, 0)))
    j_1, j_2 = join(
        [g_w1, g_w2], [(0, 1, "x"), (1, 0, "l")], [fc1_weight.shape, fc2_weight.shape], 1, "join_mlp"
    )
    j_q, j_d, j_b = join(
        [g_wq, g_wd, g_bias],
        [(1, 2, "x"), (1, 0, "l"), (None, 0, "l")],
        [(3,) + dense_weight.shape, dense_weight.shape, (64, g_bias.shape[1])],
        2,
        "join_att",
    )
    g_bias = j_b.reshape(8, 8, -1)[:, 0]
    g_qb = g_bias[:, : 3 * narrow].reshape(8, 3, narrow).transpose(1, 0, 2).reshape(3, -1, 64)
    g_qb = lax.dynamic_slice_in_dim(g_qb, y * qkv_bias.shape[2], qkv_bias.shape[2], 2)
    g_fb = g_bias[:, 3 * narrow :].reshape(fc1_bias.shape[0], -1)
    g_fb = lax.dynamic_slice_in_dim(g_fb, y * fc1_bias.shape[1], fc1_bias.shape[1], 1)
    cot_sum = lax.dynamic_slice_in_dim(cot_sum[0], y * share, share, 0)
    return (
        layer_out,
        grad_tokens,
        g_ln[0],
        g_ln[1],
        j_q.astype(f32).transpose(1, 0, 2),
        g_qb,
        j_d.astype(f32),
        cot_sum,
        j_1.astype(f32),
        g_fb,
        j_2.astype(f32),
        cot_sum,
    )


def fast_solution(mesh):
    small_mesh = Mesh(mesh.devices.reshape(2, 2, 2, 2, 2), AXES)
    rows = P(None, ("y", "h", "l", "x"), "t")
    weights = (
        P("y"), P("y"), P("y", None, "t"), P(None, "t", "y"), P("t", "y"), P("y"), P("y", "t"),
        P("t", "y"), P("t", "y"), P("y"),
    )
    return jax.shard_map(
        fast_body,
        mesh=small_mesh,
        in_specs=(rows, rows, P(), P()) + weights,
        out_specs=(rows, rows) + weights,
        check_vma=False,
    )


def solution(mesh):
    if fits(mesh):
        return fast_solution(mesh)
    in_specs = (
        P(None, (FS, CT), TE),
        P(None, (FS, CT), TE),
        P(),
        P(),
        P(FS),
        P(FS),
        P(FS, None, TE),
        P(None, TE, FS),
        P(TE, FS),
        P(FS),
        P(FS, TE),
        P(TE, FS),
        P(TE, FS),
        P(FS),
    )
    out_specs = (
        P(None, (FS, CT), TE),
        P(None, (FS, CT), TE),
        P(FS),
        P(FS),
        P(FS, None, TE),
        P(None, TE, FS),
        P(TE, FS),
        P(FS),
        P(FS, TE),
        P(TE, FS),
        P(TE, FS),
        P(FS),
    )
    return jax.shard_map(body, mesh=mesh, in_specs=in_specs, out_specs=out_specs, check_vma=False)
```

```python
from functools import partial

import jax
import jax.numpy as jnp
from jax import lax
from jax.experimental import pallas as pl
from jax.experimental.pallas import tpu as pltpu
from jax.sharding import Mesh
from jax.sharding import PartitionSpec as P

ROT = 32
FS, CT, TE = "fsdp", "context", "tensor"


EPSILON = 1e-05
ROPE_BASE = 10000.0
NEG_FILL = -1e30


def layer_norm(values, gain, shift):
    center = values - jnp.mean(values, axis=-1, keepdims=True)
    spread = jnp.mean(center * center, axis=-1, keepdims=True)
    return center * lax.rsqrt(spread + EPSILON) * gain + shift


def rotate(values, position):
    half = ROT // 2
    freq = ROPE_BASE ** (-2.0 * jnp.arange(half, dtype=jnp.float32) / ROT)
    angles = position[:, None] * freq[None, :]
    cosine = jnp.cos(angles)[:, None, :]
    sine = jnp.sin(angles)[:, None, :]
    first = values[..., :half]
    second = values[..., half:ROT]
    return jnp.concatenate(
        [first * cosine - second * sine, second * cosine + first * sine, values[..., ROT:]], axis=-1
    )


def segment_layout(length_row, places):
    count = length_row.shape[0]
    upto = jnp.arange(count)[:, None] >= jnp.arange(count)[None, :]
    ends = jnp.sum(jnp.where(upto, length_row[None, :], 0), axis=1)
    starts = ends - length_row
    segment = jnp.sum((places[:, None] >= ends[None, :]).astype(jnp.int32), axis=1)
    match = segment[:, None] == jnp.arange(length_row.shape[0], dtype=jnp.int32)[None, :]
    begin = jnp.sum(jnp.where(match, starts[None, :], 0), axis=1)
    return (segment, places - begin)


def rows_block(source, block_index, block_rows, head_count, head_width):
    return lax.dynamic_slice_in_dim(source, block_index * block_rows, block_rows, 0).reshape(
        block_rows, head_count, head_width
    )


def pair_mask(query_segment, query_place, key_segment, key_place):
    return (
        (query_segment[:, None] == key_segment[None, :])
        & (key_place[None, :] <= query_place[:, None])
    )[None]


def key_scores(
    query,
    keys_all,
    key_segment,
    key_place,
    query_segment,
    query_place,
    block_index,
    block_rows,
    scale,
):
    row_count, head_count, head_width = query.shape
    key_block = rows_block(keys_all, block_index, block_rows, head_count, head_width)
    scores = (
        jnp.einsum("qhe,khe->hqk", query, key_block, preferred_element_type=jnp.float32) * scale
    )
    segment_block = lax.dynamic_slice_in_dim(key_segment, block_index * block_rows, block_rows, 0)
    place_block = lax.dynamic_slice_in_dim(key_place, block_index * block_rows, block_rows, 0)
    return (scores, pair_mask(query_segment, query_place, segment_block, place_block), key_block)


def attend_forward(
    query,
    keys_all,
    values_all,
    key_segment,
    key_place,
    query_segment,
    query_place,
    first_block,
    last_block,
    block_rows,
    scale,
):
    row_count, head_count, head_width = query.shape

    def find_peak(block_index, carry):
        peak, total = carry
        scores, allowed, _ = key_scores(
            query,
            keys_all,
            key_segment,
            key_place,
            query_segment,
            query_place,
            block_index,
            block_rows,
            scale,
        )
        fresh = jnp.maximum(peak, jnp.max(jnp.where(allowed, scores, NEG_FILL), axis=-1))
        added = jnp.sum(jnp.where(allowed, jnp.exp(scores - fresh[..., None]), 0.0), axis=-1)
        return (fresh, total * jnp.exp(peak - fresh) + added)

    start_carry = (
        jnp.full((head_count, row_count), NEG_FILL, jnp.float32),
        jnp.zeros((head_count, row_count), jnp.float32),
    )
    peak, total = lax.fori_loop(first_block, last_block + 1, find_peak, start_carry)
    log_total = peak + jnp.log(total)

    def weigh(block_index, accum):
        scores, allowed, _ = key_scores(
            query,
            keys_all,
            key_segment,
            key_place,
            query_segment,
            query_place,
            block_index,
            block_rows,
            scale,
        )
        attend_weights = jnp.where(allowed, jnp.exp(scores - log_total[..., None]), 0.0).astype(
            jnp.bfloat16
        )
        values = rows_block(values_all, block_index, block_rows, head_count, head_width)
        return accum + jnp.einsum(
            "hqk,khe->qhe", attend_weights, values, preferred_element_type=jnp.float32
        )

    attended = lax.fori_loop(
        first_block, last_block + 1, weigh, jnp.zeros(query.shape, jnp.float32)
    )
    return (attended, log_total)


def attend_backward(
    query,
    keys_all,
    values_all,
    key_segment,
    key_place,
    query_segment,
    query_place,
    first_block,
    last_block,
    block_rows,
    scale,
    log_total,
    grad_out,
    delta,
):
    row_count, head_count, head_width = query.shape

    def step_back(block_index, carry):
        scores, allowed, key_block = key_scores(
            query,
            keys_all,
            key_segment,
            key_place,
            query_segment,
            query_place,
            block_index,
            block_rows,
            scale,
        )
        values = rows_block(values_all, block_index, block_rows, head_count, head_width)
        attend_weights = jnp.where(allowed, jnp.exp(scores - log_total[..., None]), 0.0)
        grad_weights = jnp.einsum(
            "qhe,khe->hqk", grad_out, values, preferred_element_type=jnp.float32
        )
        grad_scores = (attend_weights * (grad_weights - delta[..., None])).astype(jnp.bfloat16)
        grad_query = (
            carry[0]
            + jnp.einsum("hqk,khe->qhe", grad_scores, key_block, preferred_element_type=jnp.float32)
            * scale
        )
        grad_keys, grad_values = (carry[1], carry[2])
        key_part = (
            jnp.einsum("hqk,qhe->khe", grad_scores, query, preferred_element_type=jnp.float32)
            * scale
        ).reshape(block_rows, head_count * head_width)
        value_part = jnp.einsum(
            "hqk,qhe->khe",
            attend_weights.astype(jnp.bfloat16),
            grad_out,
            preferred_element_type=jnp.float32,
        ).reshape(block_rows, head_count * head_width)
        block_start = block_index * block_rows
        grad_keys = lax.dynamic_update_slice_in_dim(
            grad_keys,
            lax.dynamic_slice_in_dim(grad_keys, block_start, block_rows, 0) + key_part,
            block_start,
            0,
        )
        grad_values = lax.dynamic_update_slice_in_dim(
            grad_values,
            lax.dynamic_slice_in_dim(grad_values, block_start, block_rows, 0) + value_part,
            block_start,
            0,
        )
        return (grad_query, grad_keys, grad_values)

    start_carry = (
        jnp.zeros(query.shape, jnp.float32),
        jnp.zeros(keys_all.shape, jnp.float32),
        jnp.zeros(values_all.shape, jnp.float32),
    )
    return lax.fori_loop(first_block, last_block + 1, step_back, start_carry)


def body(
    tokens,
    cotangent,
    lengths,
    permutation,
    ln_gain,
    ln_bias,
    qkv_weight,
    qkv_bias,
    dense_weight,
    dense_bias,
    fc1_weight,
    fc1_bias,
    fc2_weight,
    fc2_bias,
):
    gain_all, shift_all, w_qkv, b_qkv, w_dense, b_dense, w_fc1, b_fc1, w_fc2, b_fc2 = (
        lax.all_gather(ln_gain, FS, axis=0, tiled=True),
        lax.all_gather(ln_bias, FS, axis=0, tiled=True),
        lax.all_gather(qkv_weight, FS, axis=0, tiled=True),
        lax.all_gather(qkv_bias, FS, axis=2, tiled=True),
        lax.all_gather(dense_weight, FS, axis=1, tiled=True),
        lax.all_gather(dense_bias, FS, axis=0, tiled=True),
        lax.all_gather(fc1_weight, FS, axis=0, tiled=True),
        lax.all_gather(fc1_bias, FS, axis=1, tiled=True),
        lax.all_gather(fc2_weight, FS, axis=1, tiled=True),
        lax.all_gather(fc2_bias, FS, axis=0, tiled=True),
    )
    gain_f = gain_all.astype(jnp.float32)
    shift_f = shift_all.astype(jnp.float32)
    local_width = w_qkv.shape[2]
    head_count = b_qkv.shape[1]
    head_width = b_qkv.shape[2]
    hidden_local = w_fc1.shape[1]
    qkv_shift = b_qkv.astype(jnp.float32).reshape(3, local_width)
    fc1_shift = b_fc1.astype(jnp.float32).reshape(hidden_local)
    micro_count = tokens.shape[0]
    row_count = tokens.shape[1]
    feature_share = tokens.shape[2]
    all_rows = micro_count * row_count
    pack_length = row_count * lax.axis_size(CT)
    block_rows = min(512, pack_length)
    group_index = lax.axis_index((FS, CT))
    pack_index = lax.axis_index(FS)
    context_index = lax.axis_index(CT)
    tensor_index = lax.axis_index(TE)
    out_shift = lax.dynamic_slice_in_dim(
        b_dense.astype(jnp.float32) + b_fc2.astype(jnp.float32),
        tensor_index * feature_share,
        feature_share,
        0,
    )
    scale = head_width ** (-0.5)
    counting = jnp.arange(row_count, dtype=jnp.int32)
    pack_places = jnp.arange(pack_length, dtype=jnp.int32)
    query_place = lax.dynamic_slice_in_dim(pack_places, context_index * row_count, row_count, 0)
    last_query_block = (context_index * row_count + row_count - 1) // block_rows
    sent_tokens = []
    sent_cot = []
    slot_sources = []
    arrive_slots = []
    return_orders = []
    key_segments = []
    query_segments = []
    query_positions = []
    first_blocks = []
    length_rows = []
    for micro_index in range(micro_count):
        perm_row = permutation[micro_index]
        own_targets = lax.dynamic_slice_in_dim(perm_row, group_index * row_count, row_count, 0)
        send_order = jnp.argsort(own_targets // row_count, stable=True)
        return_orders.append(jnp.zeros(row_count, jnp.int32).at[send_order].set(counting))
        here = perm_row // row_count == group_index
        arriving = jnp.argsort(jnp.where(here, 0, 1), stable=True)[:row_count]
        arrive_slot = perm_row[arriving] % row_count
        arrive_slots.append(arrive_slot)
        slot_sources.append(jnp.zeros(row_count, jnp.int32).at[arrive_slot].set(counting))
        sent_tokens.append(tokens[micro_index][send_order])
        sent_cot.append(cotangent[micro_index][send_order])
        length_row = lax.dynamic_index_in_dim(lengths[micro_index], pack_index, 0, keepdims=False)
        length_rows.append(length_row)
        key_segment, key_position = segment_layout(length_row, pack_places)
        key_segments.append(key_segment)
        query_segments.append(
            lax.dynamic_slice_in_dim(key_segment, context_index * row_count, row_count, 0)
        )
        query_position = lax.dynamic_slice_in_dim(
            key_position, context_index * row_count, row_count, 0
        )
        query_positions.append(query_position)
        first_blocks.append((query_place[0] - query_position[0]) // block_rows)
    received = (
        lax.all_to_all(
            jnp.stack(sent_tokens), (FS, CT), split_axis=1, concat_axis=1, tiled=True
        ),
        lax.all_to_all(
            jnp.stack(sent_cot), (FS, CT), split_axis=1, concat_axis=1, tiled=True
        ),
    )
    own_tokens = jnp.concatenate(
        [received[0][m][slot_sources[m]] for m in range(micro_count)], axis=0
    )
    own_cot = jnp.concatenate([received[1][m][slot_sources[m]] for m in range(micro_count)], axis=0)
    full_tokens, full_cot = (
        lax.all_gather(own_tokens, TE, axis=1, tiled=True),
        lax.all_gather(own_cot, TE, axis=1, tiled=True),
    )
    normed, norm_back = jax.vjp(layer_norm, full_tokens.astype(jnp.float32), gain_f, shift_f)
    normed_b = normed.astype(jnp.bfloat16)
    qkv = jnp.einsum("rd,dce->rce", normed_b, w_qkv, preferred_element_type=jnp.float32) + qkv_shift
    angle_pos = jnp.concatenate(query_positions, axis=0).astype(jnp.float32)
    query_rot, rope_back = jax.vjp(
        lambda inner: rotate(inner, angle_pos), qkv[:, 0].reshape(all_rows, head_count, head_width)
    )
    key_rot = rotate(qkv[:, 1].reshape(all_rows, head_count, head_width), angle_pos)
    query_b = query_rot.astype(jnp.bfloat16)
    key_b = key_rot.reshape(all_rows, local_width).astype(jnp.bfloat16)
    value_b = qkv[:, 2].astype(jnp.bfloat16)
    keys_all, values_all = (
        lax.all_gather(
            key_b.reshape(micro_count, row_count, local_width), CT, axis=1, tiled=True
        ),
        lax.all_gather(
            value_b.reshape(micro_count, row_count, local_width), CT, axis=1, tiled=True
        ),
    )
    attended_list = []
    log_list = []
    for micro_index in range(micro_count):
        rows = slice(micro_index * row_count, (micro_index + 1) * row_count)
        attended_one, log_one = attend_forward(
            query_b[rows],
            keys_all[micro_index],
            values_all[micro_index],
            key_segments[micro_index],
            pack_places,
            query_segments[micro_index],
            query_place,
            first_blocks[micro_index],
            last_query_block,
            block_rows,
            scale,
        )
        attended_list.append(attended_one)
        log_list.append(log_one)
    attended = jnp.concatenate(attended_list, axis=0)
    attended_b = attended.reshape(all_rows, local_width).astype(jnp.bfloat16)
    pre_act = jnp.dot(normed_b, w_fc1, preferred_element_type=jnp.float32) + fc1_shift
    activ, gelu_back = jax.vjp(partial(jax.nn.gelu, approximate=True), pre_act)
    activ_b = activ.astype(jnp.bfloat16)
    partial_out = jnp.dot(attended_b, w_dense, preferred_element_type=jnp.float32) + jnp.dot(
        activ_b, w_fc2, preferred_element_type=jnp.float32
    )
    branch = lax.psum_scatter(
        partial_out.astype(jnp.bfloat16), TE, scatter_dimension=1, tiled=True
    ).astype(jnp.float32)
    layer_rows = (own_tokens.astype(jnp.float32) + branch + out_shift).astype(jnp.bfloat16)
    grad_attended = jnp.einsum(
        "rd,ed->re", full_cot, w_dense, preferred_element_type=jnp.float32
    ).astype(jnp.bfloat16)
    grad_activ = jnp.einsum("rd,hd->rh", full_cot, w_fc2, preferred_element_type=jnp.float32)
    grad_pre = gelu_back(grad_activ)[0].astype(jnp.bfloat16)
    grad_heads = grad_attended.reshape(all_rows, head_count, head_width)
    delta_list = []
    for micro_index in range(micro_count):
        rows = slice(micro_index * row_count, (micro_index + 1) * row_count)
        delta_list.append(
            jnp.einsum(
                "qhe,qhe->hq", grad_heads[rows].astype(jnp.float32), attended_list[micro_index]
            )
        )
    query_grads = []
    key_parts = []
    value_parts = []
    for micro_index in range(micro_count):
        rows = slice(micro_index * row_count, (micro_index + 1) * row_count)
        grad_query_one, grad_keys_one, grad_values_one = attend_backward(
            query_b[rows],
            keys_all[micro_index],
            values_all[micro_index],
            key_segments[micro_index],
            pack_places,
            query_segments[micro_index],
            query_place,
            first_blocks[micro_index],
            last_query_block,
            block_rows,
            scale,
            log_list[micro_index],
            grad_heads[rows],
            delta_list[micro_index],
        )
        query_grads.append(grad_query_one)
        key_parts.append(grad_keys_one)
        value_parts.append(grad_values_one)
    grad_keys, grad_values = (
        lax.psum_scatter(
            jnp.stack(key_parts).astype(jnp.bfloat16), CT, scatter_dimension=1, tiled=True
        ).astype(jnp.float32),
        lax.psum_scatter(
            jnp.stack(value_parts).astype(jnp.bfloat16), CT, scatter_dimension=1, tiled=True
        ).astype(jnp.float32),
    )
    grad_keys = grad_keys.reshape(all_rows, local_width)
    grad_values = grad_values.reshape(all_rows, local_width)
    grad_query = jnp.concatenate(query_grads, axis=0)
    grad_query_pre = rope_back(grad_query)[0].reshape(all_rows, local_width)
    grad_key_pre = rope_back(grad_keys.reshape(all_rows, head_count, head_width))[0].reshape(
        all_rows, local_width
    )
    grad_qkv = jnp.stack([grad_query_pre, grad_key_pre, grad_values], axis=1).astype(jnp.bfloat16)
    grad_normed_part = jnp.einsum(
        "rce,dce->rd", grad_qkv, w_qkv, preferred_element_type=jnp.float32
    ) + jnp.einsum("rh,dh->rd", grad_pre, w_fc1, preferred_element_type=jnp.float32)
    grad_normed = lax.psum(grad_normed_part.astype(jnp.bfloat16), TE).astype(jnp.float32)
    grad_input, grad_gain, grad_shift = norm_back(grad_normed)
    cot_f = full_cot.astype(jnp.float32)
    grad_own = lax.dynamic_slice_in_dim(
        cot_f + grad_input, tensor_index * feature_share, feature_share, 1
    ).astype(jnp.bfloat16)
    cot_total = jnp.sum(cot_f, axis=0)
    part_qkv_w = jnp.einsum("rd,rce->dce", normed_b, grad_qkv, preferred_element_type=jnp.float32)
    part_qkv_b = jnp.sum(grad_qkv.astype(jnp.float32), axis=0).reshape(b_qkv.shape)
    part_dense_w = jnp.einsum("re,rd->ed", attended_b, full_cot, preferred_element_type=jnp.float32)
    part_fc1_w = jnp.einsum("rd,rh->dh", normed_b, grad_pre, preferred_element_type=jnp.float32)
    part_fc1_b = jnp.sum(grad_pre.astype(jnp.float32), axis=0).reshape(b_fc1.shape)
    part_fc2_w = jnp.einsum("rh,rd->hd", activ_b, full_cot, preferred_element_type=jnp.float32)
    back_rows = []
    back_grads = []
    for micro_index in range(micro_count):
        rows = slice(micro_index * row_count, (micro_index + 1) * row_count)
        back_rows.append(layer_rows[rows][arrive_slots[micro_index]])
        back_grads.append(grad_own[rows][arrive_slots[micro_index]])
    returned = (
        lax.all_to_all(
            jnp.stack(back_rows), (FS, CT), split_axis=1, concat_axis=1, tiled=True
        ),
        lax.all_to_all(
            jnp.stack(back_grads), (FS, CT), split_axis=1, concat_axis=1, tiled=True
        ),
    )
    layer_out = jnp.stack([returned[0][m][return_orders[m]] for m in range(micro_count)])
    grad_tokens = jnp.stack([returned[1][m][return_orders[m]] for m in range(micro_count)])
    shares = (
        lax.psum_scatter(
            grad_gain.astype(jnp.bfloat16), (FS, CT), scatter_dimension=0, tiled=True
        ).astype(jnp.float32),
        lax.psum_scatter(
            grad_shift.astype(jnp.bfloat16), (FS, CT), scatter_dimension=0, tiled=True
        ).astype(jnp.float32),
        lax.psum_scatter(
            part_qkv_w.astype(jnp.bfloat16), (FS, CT), scatter_dimension=0, tiled=True
        ).astype(jnp.float32),
        lax.psum_scatter(
            part_qkv_b.astype(jnp.bfloat16), (FS, CT), scatter_dimension=2, tiled=True
        ).astype(jnp.float32),
        lax.psum_scatter(
            part_dense_w.astype(jnp.bfloat16), (FS, CT), scatter_dimension=1, tiled=True
        ).astype(jnp.float32),
        lax.psum_scatter(
            cot_total.astype(jnp.bfloat16), (FS, CT), scatter_dimension=0, tiled=True
        ).astype(jnp.float32),
        lax.psum_scatter(
            part_fc1_w.astype(jnp.bfloat16), (FS, CT), scatter_dimension=0, tiled=True
        ).astype(jnp.float32),
        lax.psum_scatter(
            part_fc1_b.astype(jnp.bfloat16), (FS, CT), scatter_dimension=1, tiled=True
        ).astype(jnp.float32),
        lax.psum_scatter(
            part_fc2_w.astype(jnp.bfloat16), (FS, CT), scatter_dimension=1, tiled=True
        ).astype(jnp.float32),
        lax.psum_scatter(
            cot_total.astype(jnp.bfloat16), (FS, CT), scatter_dimension=0, tiled=True
        ).astype(jnp.float32),
    )
    reduced = (
        lax.all_gather(shares[0].astype(jnp.bfloat16), CT, axis=0, tiled=True).astype(
            jnp.float32
        ),
        lax.all_gather(shares[1].astype(jnp.bfloat16), CT, axis=0, tiled=True).astype(
            jnp.float32
        ),
        lax.all_gather(shares[2].astype(jnp.bfloat16), CT, axis=0, tiled=True).astype(
            jnp.float32
        ),
        lax.all_gather(shares[3].astype(jnp.bfloat16), CT, axis=2, tiled=True).astype(
            jnp.float32
        ),
        lax.all_gather(shares[4].astype(jnp.bfloat16), CT, axis=1, tiled=True).astype(
            jnp.float32
        ),
        lax.all_gather(shares[5].astype(jnp.bfloat16), CT, axis=0, tiled=True).astype(
            jnp.float32
        ),
        lax.all_gather(shares[6].astype(jnp.bfloat16), CT, axis=0, tiled=True).astype(
            jnp.float32
        ),
        lax.all_gather(shares[7].astype(jnp.bfloat16), CT, axis=1, tiled=True).astype(
            jnp.float32
        ),
        lax.all_gather(shares[8].astype(jnp.bfloat16), CT, axis=1, tiled=True).astype(
            jnp.float32
        ),
        lax.all_gather(shares[9].astype(jnp.bfloat16), CT, axis=0, tiled=True).astype(
            jnp.float32
        ),
    )
    return (
        layer_out,
        grad_tokens,
        reduced[0],
        reduced[1],
        reduced[2],
        reduced[3],
        reduced[4],
        reduced[5],
        reduced[6],
        reduced[7],
        reduced[8],
        reduced[9],
    )


MESH = pl.DeviceIdType.MESH
AXES = ("y", "h", "l", "x", "t")
BLOCK = 256
SPAN = 512


def fits(mesh):
    return (mesh.shape[FS], mesh.shape[CT], mesh.shape[TE]) == (2, 8, 2)


def place():
    return tuple(lax.axis_index(a) for a in AXES)


def greet(peers):
    barrier = pltpu.get_barrier_semaphore()
    total = 0
    for device, there in peers:
        if there is True:
            pl.semaphore_signal(barrier, inc=1, device_id=device, device_id_type=MESH)
            total += 1
        else:

            @pl.when(there)
            def _(device=device):
                pl.semaphore_signal(barrier, inc=1, device_id=device, device_id_type=MESH)

            total = total + there.astype(jnp.int32)
    pl.semaphore_wait(barrier, total)


def spread_kernel(
    tok, cot, w_q, w_d, w_1, w_2, small, tok_all, cot_all, q_out, d_out, o_1, o_2, small_out,
    local_sem, send_sem, recv_sem,
):
    y, h, l, x, t = place()
    z = 2 * h + l
    rows, half = tok.shape[1], tok.shape[2]
    other_y, other_x, other_t = {"y": 1 - y}, {"x": 1 - x}, {"t": 1 - t}

    def along(zz):
        return {"h": zz // 2, "l": lax.rem(zz, 2)}

    greet(
        [(other_y, True), (other_x, True), (other_t, True)]
        + [(along(lax.max(z - 1, 0)), z > 0), (along(lax.min(z + 1, 3)), z < 3)]
    )
    units = [(tok, tok_all, 0, 1), (tok, tok_all, 1, 1), (cot, cot_all, 0, 2)]
    numbers = {}

    def number(key):
        return numbers.setdefault(key, len(numbers))

    def region(unit, chunk, core):
        _, out, m, n = units[unit]
        dy, dx, way, k = chunk
        yy = 1 - y if dy else y
        xx = 1 - x if dx else x
        zz = z - k if way == "up" else z + k
        group = yy * 8 + zz * 2 + xx
        return out.at[
            pl.ds(m, n),
            pl.ds(pl.multiple_of(group * rows, rows), rows),
            pl.ds(pl.multiple_of(core * half, half), half),
        ]

    def own(unit):
        array, _, m, n = units[unit]
        return array.at[pl.ds(m, n)]

    started = []

    def send(unit, chunk, key, device):
        source = own(unit) if chunk == (0, 0, "up", 0) else region(unit, chunk, t)
        i = number((unit,) + key)
        copy = pltpu.make_async_remote_copy(
            src_ref=source, dst_ref=region(unit, chunk, t), send_sem=send_sem.at[i],
            recv_sem=recv_sem.at[i], device_id=device, device_id_type=MESH,
        )
        copy.start()
        return copy

    def arrive(unit, chunk, key, core):
        i = number((unit,) + key)
        ref = region(unit, chunk, core)
        pltpu.make_async_remote_copy(
            src_ref=ref, dst_ref=ref, send_sem=send_sem.at[i], recv_sem=recv_sem.at[i],
            device_id=other_t, device_id_type=MESH,
        ).wait_recv()

    def sent(unit, chunk, key):
        i = number((unit,) + key)
        ref = own(unit)
        pltpu.make_async_remote_copy(
            src_ref=ref, dst_ref=ref, send_sem=send_sem.at[i], recv_sem=recv_sem.at[i],
            device_id=other_t, device_id_type=MESH,
        ).wait_send()

    def when(there, what):
        if there is True:
            what()
        else:
            pl.when(there)(what)

    def there_of(way, k):
        return True if k == 0 else (z >= k if way == "up" else z + k <= 3)

    def to_core(unit, chunk):
        key = chunk + ("core",)
        send(unit, chunk, key, other_t)
        started.append((unit, chunk, key, None))

    def onward(unit, chunk, axis):
        dy, dx, way, k = chunk
        key = ((1, dx, way, k) if axis == "y" else (dy, 1, way, k)) + ("link",)
        send(unit, chunk, key, other_y if axis == "y" else other_x)
        started.append((unit, chunk, key, None))

    def up_down(unit, chunk):
        dy, dx, way, k = chunk
        for going in ("up", "down") if k == 0 else (way,):
            can = z < 3 if going == "up" else z > 0
            key = (dy, dx, going, k + 1, "link")
            target = along(lax.min(z + 1, 3) if going == "up" else lax.max(z - 1, 0))
            when(can, lambda: send(unit, chunk, key, target) and None)
            started.append((unit, chunk, key, going))

    def got(unit, chunk):
        arrive(unit, chunk, chunk + ("link",), t)

    steps = [[("up", 0)], [("up", 1), ("down", 1)], [("up", 2), ("down", 2)], [("up", 3), ("down", 3)]]
    block = (y * 4 + l * 2 + x, (1 - y) * 4 + l * 2 + x)
    pieces = []
    depth = w_1.shape[0]
    for b, to in ((block[1], True), (block[0], False)):
        row = pl.ds(pl.multiple_of(y * depth, depth), depth)
        wide, narrow = w_1.shape[1] // 8, w_d.shape[0] // 8
        pieces.append([
            (w_1.at[:, pl.ds(pl.multiple_of(b * wide, wide), wide)], o_1.at[row]),
            (w_2.at[pl.ds(pl.multiple_of(b * wide, wide), wide)], o_2.at[:, row]),
            (w_q.at[:, :, pl.ds(pl.multiple_of(b * narrow, narrow), narrow)], q_out.at[:, row]),
            (w_d.at[pl.ds(pl.multiple_of(b * narrow, narrow), narrow)], d_out.at[:, row]),
            (small, small_out.at[y]),
        ])
    locals_, weights = [], []
    first = (0, 0, "up", 0)
    for u in range(3):
        up_down(u, first) if u else None
    for u in range(3):
        onward(u, first, "y")
    for i, (source, target) in enumerate(pieces[0]):
        copy = pltpu.make_async_remote_copy(
            src_ref=source, dst_ref=target, send_sem=send_sem.at[number(("w", i))],
            recv_sem=recv_sem.at[number(("w", i))], device_id=other_y, device_id_type=MESH,
        )
        copy.start()
        weights.append(copy)
    for u in range(3):
        onward(u, first, "x")
        to_core(u, first)
        copy = pltpu.make_async_copy(own(u), region(u, first, t), local_sem.at[len(locals_)])
        copy.start()
        locals_.append(copy)
    for source, target in pieces[1]:
        copy = pltpu.make_async_copy(source, target, local_sem.at[len(locals_)])
        copy.start()
        locals_.append(copy)

    got(0, (1, 0, "up", 0))
    onward(0, (1, 0, "up", 0), "x")
    up_down(0, first)
    up_down(0, (1, 0, "up", 0))
    to_core(0, (1, 0, "up", 0))

    def rest_of_first():
        for dy in (0, 1):
            got(0, (dy, 1, "up", 0))
            up_down(0, (dy, 1, "up", 0))
            to_core(0, (dy, 1, "up", 0))

    def z_step(s):
        for u in (1, 2):
            for way, k in steps[s]:
                def act(u=u, c=(0, 0, way, k)):
                    got(u, c)
                    up_down(u, c) if c[3] < 3 else None
                    onward(u, c, "y")
                    onward(u, c, "x")
                    to_core(u, c)
                when(there_of(way, k), act)

    def y_step(s):
        for u in (1, 2):
            for way, k in steps[s]:
                def act(u=u, c=(1, 0, way, k)):
                    got(u, c)
                    onward(u, c, "x")
                    to_core(u, c)
                when(there_of(way, k), act)

    def x_step(s):
        for u in (1, 2):
            for way, k in steps[s]:
                def act(u=u, way=way, k=k):
                    for dy in (0, 1):
                        got(u, (dy, 1, way, k))
                        to_core(u, (dy, 1, way, k))
                when(there_of(way, k), act)

    def first_step(s):
        for way, k in steps[s]:
            def act(way=way, k=k):
                for dy in (0, 1):
                    for dx in (0, 1):
                        c = (dy, dx, way, k)
                        got(0, c)
                        up_down(0, c) if k < 3 else None
                        to_core(0, c)
            when(there_of(way, k), act)

    z_step(1)
    rest_of_first()
    y_step(0)
    z_step(2)
    y_step(1)
    x_step(0)
    first_step(1)
    z_step(3)
    y_step(2)
    x_step(1)
    first_step(2)
    y_step(3)
    x_step(2)
    first_step(3)
    x_step(3)
    for u in range(3):
        for dy in (0, 1):
            for dx in (0, 1):
                for s in range(4):
                    for way, k in steps[s]:
                        c = (dy, dx, way, k)
                        when(there_of(way, k), lambda: arrive(u, c, c + ("core",), 1 - t))
    for copy in locals_:
        copy.wait()
    for copy in weights:
        copy.wait()
    for unit, chunk, key, going in started:
        there = there_of(*chunk[2:])
        if going is not None:
            can = z < 3 if going == "up" else z > 0
            there = can if there is True else can & there
        when(there, lambda: sent(unit, chunk, key))


def spread(tokens, cotangent, w_q, w_d, w_1, w_2, small):
    micro, rows, half = tokens.shape
    everything = jax.ShapeDtypeStruct((micro, rows * 16, half * 2), tokens.dtype)
    depth = w_1.shape[0] * 2
    outs = [
        everything,
        everything,
        jax.ShapeDtypeStruct((3, depth, w_q.shape[2] // 8), w_q.dtype),
        jax.ShapeDtypeStruct((w_d.shape[0] // 8, depth), w_d.dtype),
        jax.ShapeDtypeStruct((depth, w_1.shape[1] // 8), w_1.dtype),
        jax.ShapeDtypeStruct((w_2.shape[0] // 8, depth), w_2.dtype),
        jax.ShapeDtypeStruct((2,) + small.shape, small.dtype),
    ]
    return pl.pallas_call(
        spread_kernel,
        out_shape=outs,
        in_specs=[pl.BlockSpec(memory_space=pl.ANY)] * 7,
        out_specs=[pl.BlockSpec(memory_space=pl.ANY)] * 7,
        scratch_shapes=[
            pltpu.SemaphoreType.DMA((8,)),
            pltpu.SemaphoreType.DMA((176,)),
            pltpu.SemaphoreType.DMA((176,)),
        ],
        compiler_params=pltpu.CompilerParams(collective_id=0, has_side_effects=True),
        name="spread",
    )(tokens, cotangent, w_q, w_d, w_1, w_2, small)


class Join:
    def __init__(self, parts, outs, local_sem, send_sem, recv_sem):
        self.parts, self.outs = parts, outs
        self.local_sem, self.send_sem, self.recv_sem = local_sem, send_sem, recv_sem
        self.y, self.h, self.l, self.x, self.t = place()
        self.device = {"y": {"y": 1 - self.y}, "l": {"l": 1 - self.l}, "x": {"x": 1 - self.x}}
        self.numbers, self.sends = {}, []
        self.every = range(len(parts))
        self.first = [p[3] for p in parts]
        self.then = ["l" if p[3] == "x" else "x" for p in parts]

    def half_of(self, i, yy):
        ref, d_axis, _, _ = self.parts[i]
        if d_axis is None:
            return ref
        n = ref.shape[d_axis] // 2
        where = [slice(None)] * len(ref.shape)
        where[d_axis] = pl.ds(pl.multiple_of(yy * n, n), n)
        return ref.at[tuple(where)]

    def spot(self, i, yy, ll, xx):
        ref, _, b_axis, _ = self.parts[i]
        n = ref.shape[b_axis]
        where = [slice(None)] * len(ref.shape)
        where[b_axis] = pl.ds(pl.multiple_of((yy * 4 + ll * 2 + xx) * n, n), n)
        return self.outs[i].at[tuple(where)]

    def own(self, i, yy):
        return self.spot(i, yy, self.l, self.x)

    def beside(self, i, axis, yy):
        l, x = self.l, self.x
        return self.spot(i, yy, 1 - l if axis == "l" else l, 1 - x if axis == "x" else x)

    def copy(self, n, source, target, axis):
        return pltpu.make_async_remote_copy(
            src_ref=source, dst_ref=target, send_sem=self.send_sem.at[n], recv_sem=self.recv_sem.at[n],
            device_id=self.device[axis], device_id_type=MESH,
        )

    def send(self, i, source, target, key, axis):
        n = self.numbers.setdefault((i,) + key, len(self.numbers))
        self.copy(n, source, target, axis).start()
        self.sends.append((n, i, axis))

    def got(self, i, target, key):
        self.copy(self.numbers[(i,) + key], target, target, "y").wait_recv()

    def bring(self):
        for i in self.every:
            self.send(i, self.half_of(i, 1 - self.y), self.own(i, self.y), ("y",), "y")

    def offer(self, axis):
        for want in (True, False):
            for i in self.every:
                if (self.first[i] == axis) is want:
                    self.send(i, self.half_of(i, self.y), self.own(i, self.y), (0, axis), axis)

    def kept(self, i):
        return pltpu.make_async_copy(self.half_of(i, self.y), self.own(i, self.y), self.local_sem.at[i])

    def keep(self):
        for i in self.every:
            self.kept(i).start()

    def far(self, side):
        yy = 1 - self.y if side else self.y
        for i in self.every:
            a = self.first[i]
            self.got(i, self.beside(i, a, yy), (side, a))
            self.send(i, self.beside(i, a, yy), self.beside(i, a, yy), (side, "far"), self.then[i])

    def brought(self):
        for i in self.every:
            ref = self.own(i, 1 - self.y)
            self.got(i, ref, ("y",))
            self.send(i, ref, ref, (1, self.first[i]), self.first[i])
            self.send(i, ref, ref, (1, self.then[i]), self.then[i])

    def end(self):
        for i in self.every:
            for side, yy in ((0, self.y), (1, 1 - self.y)):
                self.got(i, self.beside(i, self.then[i], yy), (side, self.then[i]))
                self.got(i, self.spot(i, yy, 1 - self.l, 1 - self.x), (side, "far"))
        for i in self.every:
            self.kept(i).wait()
        for n, i, axis in self.sends:
            self.copy(n, self.own(i, self.y), self.own(i, self.y), axis).wait_send()


def join_sems(count):
    sem = pltpu.SemaphoreType.DMA
    return [sem((count,)), sem((7 * count,)), sem((7 * count,))]


NN = (((1,), (0,)), ((), ()))
NT = (((1,), (1,)), ((), ()))
TN = (((0,), (0,)), ((), ()))


def dot(a, b, dims=NN):
    return lax.dot_general(a, b, dims, preferred_element_type=jnp.float32)


def fold_kernel(
    activ, grad_pre, back, tok_all, g_q, g_d, g_b, cot, w_1, w_2, w_q, w_d, gain, out_shift,
    layer_out, grad_out, ln_out, j_q, j_d, j_b, act_v, pre_v, back_v, tok_v, give, core_in, give_n, sum_in, stat_v, stat_in, ln_v, ln_in,
    load_sem, core_send, core_recv, hop_send, hop_recv, small_send, small_recv, *join_sem,
):
    y, h, l, x, t = place()
    rows, share = cot.shape[1], cot.shape[2]
    both = 2 * rows
    device = {"y": {"y": 1 - y}, "l": {"l": 1 - l}, "x": {"x": 1 - x}, "t": {"t": 1 - t}, "h": {"h": 1 - h}}
    narrow = w_d.shape[0]
    loads = []

    def load(source, target):
        copy = pltpu.make_async_copy(source, target, load_sem.at[len(loads)])
        copy.start()
        loads.append(copy)

    def group_rows(dy, dl, dx):
        yy = 1 - y if dy else y
        ll = 1 - l if dl else l
        xx = 1 - x if dx else x
        return pl.ds(pl.multiple_of((yy * 8 + h * 4 + ll * 2 + xx) * rows, rows), rows)

    owners = [(1, 1, 0), (1, 1, 1), (0, 1, 0), (0, 1, 1), (1, 0, 0), (1, 0, 1), (0, 0, 1), (0, 0, 0)]
    arrived = {}
    for o, owner in enumerate(owners):
        start = len(loads)
        for m in range(2):
            there = pl.ds(m * rows, rows)
            load(activ.at[m, group_rows(*owner)], act_v.at[o, there])
            load(back.at[m, group_rows(*owner)], back_v.at[o, there])
            load(grad_pre.at[m, group_rows(*owner)], pre_v.at[o, there])
        arrived[o] = loads[start:]
    start = len(loads)
    for m in range(2):
        load(tok_all.at[m, group_rows(0, 0, 0)], tok_v.at[pl.ds(m * rows, rows)])
    tok_loads = loads[start:]
    greet([(device[a], True) for a in ("t", "x", "y", "l", "h")])
    parts = [(g_q, 1, 2, "x"), (g_d, 1, 0, "l"), (g_b, None, 0, "l")]
    gather = Join(parts, (j_q, j_d, j_b), *join_sem)
    gather.bring()
    gather.offer("x")
    gather.keep()

    def part(a, o, tt):
        columns = pl.ds(pl.multiple_of(tt * share, share), share)
        if a == 0:
            return dot(act_v[o], w_2[:, columns]) + dot(back_v[o, :, 0:narrow], w_d[:, columns])
        total = dot(pre_v[o], w_1[columns, :], NT)
        for c in range(3):
            total += dot(back_v[o, :, (c + 1) * narrow : (c + 2) * narrow], w_q[c, columns, :], NT)
        return total

    core = {}

    def offer(a, o):
        if o in arrived:
            for copy in arrived.pop(o):
                copy.wait()
        i = a * 8 + o
        give[i] = part(a, o, 1 - t).astype(jnp.bfloat16)
        core[i] = pltpu.make_async_remote_copy(
            src_ref=give.at[i], dst_ref=core_in.at[i], send_sem=core_send.at[i], recv_sem=core_recv.at[i],
            device_id=device["t"], device_id_type=MESH,
        )
        core[i].start()

    hops = {0: ("l", "y", "x"), 1: ("y", "x", "l")}
    place_of = {"y": 0, "l": 1, "x": 2}
    slots, passed = {}, {}

    def slot(a, stage, owner):
        return slots.setdefault((a, stage, owner), len(slots))

    def total_of(a, o, stage):
        i = a * 8 + o
        total = part(a, o, t)
        core[i].wait_recv()
        total += core_in[i].astype(jnp.float32)
        for s in range(stage):
            n = slot(a, s, owners[o])
            passed[n].wait_recv()
            total += sum_in[n].astype(jnp.float32)
        return total

    def stage_owners(a, stage):
        done = [place_of[d] for d in hops[a][:stage]]
        now = place_of[hops[a][stage]]
        return [o for o, w in enumerate(owners) if all(w[d] == 0 for d in done) and w[now] == 1]

    def pass_on(a, o, stage):
        axis = hops[a][stage]
        seen = list(owners[o])
        seen[place_of[axis]] = 0
        n = slot(a, stage, tuple(seen))
        give_n[n] = total_of(a, o, stage).astype(jnp.bfloat16)
        passed[n] = pltpu.make_async_remote_copy(
            src_ref=give_n.at[n], dst_ref=sum_in.at[n], send_sem=hop_send.at[n], recv_sem=hop_recv.at[n],
            device_id=device[axis], device_id_type=MESH,
        )
        passed[n].start()

    order = []
    for stage in range(3):
        for pair in zip(stage_owners(0, stage), stage_owners(1, stage)):
            order += [(a, o, stage) for a, o in enumerate(pair)]
    ahead = 2
    queue = [(a, o) for a, o, _ in order] + [(0, 7), (1, 7)]
    for a, o in queue[:ahead]:
        offer(a, o)
    for i, (a, o, stage) in enumerate(order):
        if stage == 0:
            offer(*queue[i + ahead])
            pass_on(a, o, stage)
            if i == 7:
                gather.offer("l")
                for item in queue[i + ahead + 1 :]:
                    offer(*item)
                gather.far(0)
                gather.brought()
        else:
            pass_on(a, o, stage)
            if i == 11:
                gather.far(1)
    for copy in tok_loads:
        copy.wait()
    mine = pl.ds(pl.multiple_of(t * share, share), share)
    values = tok_v[...].astype(jnp.float32)
    mean = jnp.mean(values, axis=1, keepdims=True)
    spread_of = jnp.mean((values - mean) ** 2, axis=1, keepdims=True)
    r = lax.rsqrt(spread_of + EPSILON)
    token = tok_v[:, mine].astype(jnp.float32)
    hat = (token - mean) * r
    norm_sum = total_of(1, 7, 3)
    scaled = norm_sum * gain[:, mine]
    stat_v[:, 0:128] = jnp.broadcast_to(jnp.sum(scaled, axis=1, keepdims=True), (both, 128))
    stat_v[:, 128:256] = jnp.broadcast_to(jnp.sum(scaled * hat, axis=1, keepdims=True), (both, 128))
    stat = pltpu.make_async_remote_copy(
        src_ref=stat_v, dst_ref=stat_in, send_sem=small_send.at[0], recv_sem=small_recv.at[0],
        device_id=device["t"], device_id_type=MESH,
    )
    stat.start()
    top = lax.broadcasted_iota(jnp.int32, (8, share), 0) == 0
    ln_v[0] = jnp.where(
        top, jnp.sum(norm_sum * hat, axis=0, keepdims=True), jnp.sum(norm_sum, axis=0, keepdims=True)
    )
    smalls = [stat]

    def swap(step, axis):
        copy = pltpu.make_async_remote_copy(
            src_ref=ln_v.at[step], dst_ref=ln_in.at[step], send_sem=small_send.at[step + 1],
            recv_sem=small_recv.at[step + 1], device_id=device[axis], device_id_type=MESH,
        )
        copy.start()
        smalls.append(copy)
        return copy

    first = swap(0, "h")
    out = token + total_of(0, 7, 3) + out_shift[:, mine]
    for m in range(2):
        layer_out[m] = out[m * rows : (m + 1) * rows].astype(jnp.bfloat16)
    first.wait_recv()
    ln_v[1] = ln_v[0] + ln_in[0]
    second = swap(1, "l")
    stat.wait_recv()
    width = 2 * share
    mean_t = (stat_v[:, 0:1] + stat_in[:, 0:1]) / width
    mean_h = (stat_v[:, 128:129] + stat_in[:, 128:129]) / width
    grad = r * (scaled - mean_t - hat * mean_h)
    for m in range(2):
        grad_out[m] = (cot[m].astype(jnp.float32) + grad[m * rows : (m + 1) * rows]).astype(jnp.bfloat16)
    second.wait_recv()
    ln_v[2] = ln_v[1] + ln_in[1]
    swap(2, "x").wait_recv()
    ln_v[3] = ln_v[2] + ln_in[2]
    swap(3, "y").wait_recv()
    ln_v[4] = ln_v[3] + ln_in[3]
    swap(4, "t").wait_recv()
    ln_out[...] = jnp.where(t == y, ln_v[4], ln_in[4])
    for copy in core.values():
        copy.wait_send()
    for copy in passed.values():
        copy.wait_send()
    for copy in smalls:
        copy.wait_send()
    gather.end()


def fold(activ, grad_pre, back, tok_all, g_q, g_d, g_b, cot, w_1, w_2, w_q, w_d, gain, out_shift):
    micro, rows, share = cot.shape
    both = micro * rows
    narrow = w_d.shape[0]
    held = lambda n, w: pltpu.VMEM((n, both, w), jnp.bfloat16)
    sem = pltpu.SemaphoreType.DMA
    any_, vmem = pl.BlockSpec(memory_space=pl.ANY), pl.BlockSpec(memory_space=pltpu.VMEM)
    return pl.pallas_call(
        fold_kernel,
        out_shape=[
            jax.ShapeDtypeStruct(cot.shape, cot.dtype),
            jax.ShapeDtypeStruct(cot.shape, cot.dtype),
            jax.ShapeDtypeStruct((8, share), jnp.float32),
            jax.ShapeDtypeStruct((3, share, share), g_q.dtype),
            jax.ShapeDtypeStruct((share, share), g_d.dtype),
            jax.ShapeDtypeStruct((64, g_b.shape[1]), g_b.dtype),
        ],
        in_specs=[any_] * 7 + [vmem] * 7,
        out_specs=[vmem] * 3 + [any_] * 3,
        scratch_shapes=[
            held(8, w_1.shape[1]),
            held(8, w_1.shape[1]),
            held(8, 4 * narrow),
            pltpu.VMEM((both, 2 * share), jnp.bfloat16),
            held(16, share),
            held(16, share),
            held(14, share),
            held(14, share),
            pltpu.VMEM((both, 256), jnp.float32),
            pltpu.VMEM((both, 256), jnp.float32),
            pltpu.VMEM((5, 8, share), jnp.float32),
            pltpu.VMEM((5, 8, share), jnp.float32),
            sem((50,)),
            sem((16,)),
            sem((16,)),
            sem((14,)),
            sem((14,)),
            sem((6,)),
            sem((6,)),
        ]
        + join_sems(3),
        compiler_params=pltpu.CompilerParams(
            collective_id=3, has_side_effects=True, vmem_limit_bytes=60 << 20
        ),
        name="fold",
    )(activ, grad_pre, back, tok_all, g_q, g_d, g_b, cot, w_1, w_2, w_q, w_d, gain, out_shift)


ROOT = 0.7978845608028654
CUBE = 0.044715


def rows_kernel(
    tok, cot, w_1, w_2, w_q, w_d, gain, shift, f_shift, q_shift,
    normed_out, activ_out, pre_out, four_out, g_1, g_2, cot_sum, pre_sum, acc_1, acc_2,
):
    step = pl.program_id(0)

    @pl.when(step == 0)
    def _():
        acc_1[...] = jnp.zeros_like(acc_1)
        acc_2[...] = jnp.zeros_like(acc_2)
        cot_sum[...] = jnp.zeros_like(cot_sum)
        pre_sum[...] = jnp.zeros_like(pre_sum)

    f32, bf16 = jnp.float32, jnp.bfloat16
    values = tok[0].astype(f32)
    center = values - jnp.mean(values, axis=1, keepdims=True)
    r = lax.rsqrt(jnp.mean(center * center, axis=1, keepdims=True) + EPSILON)
    normed = (center * r * gain[...] + shift[...]).astype(bf16)
    normed_out[0] = normed
    cots = cot[0]
    pre = dot(normed, w_1[...]) + f_shift[...]
    square = pre * pre
    curve = jnp.tanh(ROOT * (pre + CUBE * pre * square))
    activ = (0.5 * pre * (1.0 + curve)).astype(bf16)
    slope = 0.5 * (1.0 + curve) + 0.5 * pre * (1.0 - curve * curve) * (ROOT * (1.0 + 3.0 * CUBE * square))
    grad_pre = (dot(cots, w_2[...], NT) * slope).astype(bf16)
    activ_out[0] = activ
    pre_out[0] = grad_pre
    narrow = w_d.shape[0]
    for c in range(3):
        at = slice(c * narrow, (c + 1) * narrow)
        four_out[0, :, at] = (dot(normed, w_q[c]) + q_shift[:, at]).astype(bf16)
    four_out[0, :, 3 * narrow :] = dot(cots, w_d[...], NT).astype(bf16)
    acc_1[...] += dot(normed, grad_pre, TN)
    acc_2[...] += dot(activ, cots, TN)
    cot_sum[...] += jnp.sum(cots.astype(f32), axis=0, keepdims=True)
    pre_sum[...] += jnp.sum(grad_pre.astype(f32), axis=0, keepdims=True)

    @pl.when(step == pl.num_programs(0) - 1)
    def _():
        g_1[...] = acc_1[...].astype(bf16)
        g_2[...] = acc_2[...].astype(bf16)


def row_work(tok_all, cot_all, w_1, w_2, w_q, w_d, gain, shift, f_shift, q_shift, size):
    micro, total, width = tok_all.shape
    per = total // size
    wide = w_1.shape[1]
    narrow = w_d.shape[0]
    bf16, f32 = jnp.bfloat16, jnp.float32

    def block(w):
        return pl.BlockSpec((1, size, w), lambda i: (i // per, i % per, 0))

    def whole(a):
        return pl.BlockSpec(a.shape, lambda i: (0,) * len(a.shape), pipeline_mode=pl.Buffered(1))

    def fixed(*s):
        return pl.BlockSpec(s, lambda i: (0,) * len(s))

    consts = (w_1, w_2, w_q, w_d, gain, shift, f_shift, q_shift)
    return pl.pallas_call(
        rows_kernel,
        grid=(micro * per,),
        out_shape=[
            jax.ShapeDtypeStruct(tok_all.shape, bf16),
            jax.ShapeDtypeStruct((micro, total, wide), bf16),
            jax.ShapeDtypeStruct((micro, total, wide), bf16),
            jax.ShapeDtypeStruct((micro, total, 4 * narrow), bf16),
            jax.ShapeDtypeStruct(w_1.shape, bf16),
            jax.ShapeDtypeStruct(w_2.shape, bf16),
            jax.ShapeDtypeStruct((1, width), f32),
            jax.ShapeDtypeStruct((1, wide), f32),
        ],
        in_specs=[block(width), block(width)] + [whole(a) for a in consts],
        out_specs=[
            block(width), block(wide), block(wide), block(4 * narrow),
            fixed(*w_1.shape), fixed(*w_2.shape), fixed(1, width), fixed(1, wide),
        ],
        scratch_shapes=[pltpu.VMEM(w_1.shape, f32), pltpu.VMEM(w_2.shape, f32)],
        compiler_params=pltpu.CompilerParams(vmem_limit_bytes=60 << 20),
        name="row_work",
    )(tok_all, cot_all, *consts)


def swap_rotary(values):
    lane = lax.rem(lax.broadcasted_iota(jnp.int32, values.shape, 1), 64)
    half = ROT // 2
    width = values.shape[1]
    return jnp.where(
        lane < half, pltpu.roll(values, width - half, 1), pltpu.roll(values, half, 1)
    )


def attend_pack(pack, four, perm, seg_q, seg_k, pos, freq, sign, back_ref, laid, gq, gk, gv, cos_v, sin_v):
    pack_rows, width = laid.shape[0], laid.shape[1] // 4
    bf16, f32 = jnp.bfloat16, jnp.float32
    scale = 64 ** (-0.5)
    lane = lax.broadcasted_iota(jnp.int32, (1, width), 1)
    total = four.shape[1]
    for block in range(pack_rows // BLOCK):
        here = slice(block * BLOCK, (block + 1) * BLOCK)
        target = pack * pack_rows + block * BLOCK + lax.broadcasted_iota(jnp.int32, (BLOCK, total), 0)
        chosen = jnp.where(perm[0] == target, 1.0, 0.0).astype(bf16)
        got = dot(chosen, four[0])
        angle = pos[0, here, :] * freq[...]
        cos, sin = jnp.cos(angle), jnp.sin(angle) * sign[...]
        cos_v[here, :] = cos
        sin_v[here, :] = sin
        for c in range(2):
            at = slice(c * width, (c + 1) * width)
            part = got[:, at]
            laid[here, at] = (part * cos + swap_rotary(part) * sin).astype(bf16)
        laid[here, 2 * width :] = got[:, 2 * width :].astype(bf16)
    gk[...] = jnp.zeros_like(gk)
    gv[...] = jnp.zeros_like(gv)
    for block in range(pack_rows // BLOCK):
        low = max(0, block * BLOCK - SPAN)
        high = (block + 1) * BLOCK
        here = slice(block * BLOCK, high)
        keys = laid[low:high, width : 2 * width]
        values = laid[low:high, 2 * width : 3 * width]
        row = lax.broadcasted_iota(jnp.int32, (BLOCK, high - low), 0) + block * BLOCK
        column = lax.broadcasted_iota(jnp.int32, (BLOCK, high - low), 1) + low
        allowed = (seg_q[0, here, :] == seg_k[0, :, low:high]) & (column <= row)
        attended = None
        for head in range(2):
            mine = (lane // 64) == head
            query = jnp.where(mine, laid[here, 0:width], 0)
            grad = jnp.where(mine, laid[here, 3 * width : 4 * width], 0)
            key = jnp.where(mine, keys, 0)
            value = jnp.where(mine, values, 0)
            scores = jnp.where(allowed, dot(query, key, NT) * scale, NEG_FILL)
            peak = jnp.max(scores, axis=1, keepdims=True)
            weights = jnp.exp(scores - peak)
            weights = weights * (1.0 / jnp.sum(weights, axis=1, keepdims=True))
            weights_b = weights.astype(bf16)
            out = dot(weights_b, value)
            attended = out if attended is None else attended + out
            delta = jnp.sum(grad.astype(f32) * out, axis=1, keepdims=True)
            inner = dot(grad, value, NT)
            grad_scores = (weights * (inner - delta)).astype(bf16)
            part = dot(grad_scores, key)
            if head == 0:
                gq[here, :] = part
            else:
                gq[here, :] += part
            gk[low:high, :] += dot(grad_scores, query, TN)
            gv[low:high, :] += dot(weights_b, grad, TN)
        back_ref[here, 0:width] = attended.astype(bf16)
    for c, ref in ((1, gq), (2, gk)):
        grads = ref[...] * scale
        turned = grads * cos_v[...] - swap_rotary(grads) * sin_v[...]
        back_ref[:, c * width : (c + 1) * width] = turned.astype(bf16)
    back_ref[:, 3 * width :] = gv[...].astype(bf16)


def heads_kernel(
    packs, all_packs, four, perm, seg_q, seg_k, pos, freq, sign, perm_c, normed, cot, g_1, g_2,
    back_out, g_d, g_q, qkv_sum, j_1, j_2,
    held, laid, gq, gk, gv, cos_v, sin_v, acc_d, acc_q, *join_sem,
):
    step = pl.program_id(0)
    last = pl.num_programs(0) - 1
    gather = Join([(g_1, 0, 1, "x"), (g_2, 1, 0, "l")], (j_1, j_2), *join_sem)
    f32, bf16 = jnp.float32, jnp.bfloat16

    @pl.when(step == 0)
    def _():
        greet([(d, True) for d in gather.device.values()])
        gather.bring()
        gather.offer("x")
        gather.offer("l")
        gather.keep()
        acc_d[...] = jnp.zeros_like(acc_d)
        acc_q[...] = jnp.zeros_like(acc_q)
        qkv_sum[...] = jnp.zeros_like(qkv_sum)

    @pl.when(step == all_packs - 1)
    def _():
        gather.far(0)

    @pl.when(step == all_packs)
    def _():
        gather.brought()

    @pl.when(step < all_packs)
    def _():
        attend_pack(
            lax.rem(step, packs), four, perm, seg_q, seg_k, pos, freq, sign,
            held.at[step], laid, gq, gk, gv, cos_v, sin_v,
        )

    @pl.when(step >= all_packs)
    def _():
        size, total = normed.shape[1], four.shape[1]
        narrow = acc_d.shape[0]
        per = total // size
        pack_rows = held.shape[1]
        first = (step - all_packs) // per * packs
        column = lax.broadcasted_iota(jnp.int32, (size, pack_rows), 1)
        back = None
        for k in range(packs):
            chosen = jnp.where(perm_c[0] == column + k * pack_rows, 1.0, 0.0).astype(bf16)
            part = dot(chosen, held[first + k])
            back = part if back is None else back + part
        back = back.astype(bf16)
        back_out[0] = back
        grads = back[:, narrow:]
        acc_d[...] += dot(back[:, :narrow], cot[0], TN)
        acc_q[...] += dot(normed[0], grads, TN)
        qkv_sum[...] += jnp.sum(grads.astype(f32), axis=0, keepdims=True)

    @pl.when(step == last)
    def _():
        narrow = acc_d.shape[0]
        g_d[...] = acc_d[...].astype(bf16)
        for c in range(3):
            g_q[c] = acc_q[:, c * narrow : (c + 1) * narrow].astype(bf16)
        gather.far(1)
        gather.end()


def heads(four, permutation, segment, position, normed, cot_all, g_1, g_2, packs, size):
    micro, total, wide = four.shape
    pack_rows = total // packs
    width = wide // 4
    deep = normed.shape[2]
    all_packs = micro * packs
    per = total // size
    lane = jnp.arange(width, dtype=jnp.int32) % 64
    power = ROPE_BASE ** (-2.0 * (lane % (ROT // 2)).astype(jnp.float32) / ROT)
    freq = jnp.where(lane < ROT, power, 0.0)[None, :]
    sign = jnp.where(lane < ROT // 2, -1.0, 1.0)[None, :]

    def by_pack(*s):
        return pl.BlockSpec((1,) + s, lambda i: (jnp.minimum(i, all_packs - 1), 0, 0))

    def by_micro(*s):
        return pl.BlockSpec((1,) + s, lambda i: (jnp.minimum(i, all_packs - 1) // packs, 0, 0))

    def block(w):
        def index(i):
            n = jnp.maximum(i - all_packs, 0)
            return (n // per, lax.rem(n, per), 0)

        return pl.BlockSpec((1, size, w), index)

    def fixed(*s):
        return pl.BlockSpec(s, lambda i: (0,) * len(s))

    any_ = pl.BlockSpec(memory_space=pl.ANY)
    plane = pltpu.VMEM((pack_rows, width), jnp.float32)
    return pl.pallas_call(
        partial(heads_kernel, packs, all_packs),
        grid=(all_packs + micro * per,),
        out_shape=[
            jax.ShapeDtypeStruct(four.shape, jnp.bfloat16),
            jax.ShapeDtypeStruct((width, deep), jnp.bfloat16),
            jax.ShapeDtypeStruct((3, deep, width), jnp.bfloat16),
            jax.ShapeDtypeStruct((1, 3 * width), jnp.float32),
            jax.ShapeDtypeStruct((deep // 2, g_1.shape[1] * 8), g_1.dtype),
            jax.ShapeDtypeStruct((g_2.shape[0] * 8, deep // 2), g_2.dtype),
        ],
        in_specs=[
            by_micro(total, wide),
            by_micro(1, total),
            by_pack(pack_rows, 1),
            by_pack(1, pack_rows),
            by_pack(pack_rows, 1),
            fixed(1, width),
            fixed(1, width),
            block(1),
            block(deep),
            block(deep),
            any_,
            any_,
        ],
        out_specs=[
            block(wide), fixed(width, deep), fixed(3, deep, width), fixed(1, 3 * width), any_, any_,
        ],
        scratch_shapes=[
            pltpu.VMEM((all_packs, pack_rows, wide), jnp.bfloat16),
            pltpu.VMEM((pack_rows, wide), jnp.bfloat16),
        ]
        + [plane] * 5
        + [pltpu.VMEM((width, deep), jnp.float32), pltpu.VMEM((deep, 3 * width), jnp.float32)]
        + join_sems(2),
        compiler_params=pltpu.CompilerParams(
            collective_id=1, has_side_effects=True, vmem_limit_bytes=56 << 20
        ),
        name="heads",
    )(
        four, permutation[:, None, :], segment[:, :, None], segment[:, None, :],
        position.astype(jnp.float32)[:, :, None], freq, sign, permutation[:, :, None], normed, cot_all, g_1, g_2,
    )


def fast_body(
    tokens, cotangent, lengths, permutation, ln_gain, ln_bias, qkv_weight, qkv_bias,
    dense_weight, dense_bias, fc1_weight, fc1_bias, fc2_weight, fc2_bias,
):
    y, h, l, x, t = place()
    f32 = jnp.float32
    micro, rows, share = tokens.shape
    width = share * 2
    total = rows * 16
    pack_rows = rows * 8
    packs = total // pack_rows
    block = y * 4 + l * 2 + x
    wide = fc1_weight.shape[1] // 8
    narrow = dense_weight.shape[0] // 8
    small = jnp.concatenate(
        [a.reshape(-1) for a in (ln_gain, ln_bias, dense_bias, fc2_bias, qkv_bias, fc1_bias)]
    )
    small = jnp.pad(small, (0, 64 * 128 - small.shape[0])).reshape(64, 128)
    tok_all, cot_all, w_q, w_d, w_1, w_2, small = spread(
        tokens, cotangent, qkv_weight.transpose(1, 0, 2), dense_weight, fc1_weight, fc2_weight, small
    )
    small = small.reshape(2, 64 * 128).astype(f32)
    gain = small[:, 0:share].reshape(1, width)
    shift = small[:, share : 2 * share].reshape(1, width)
    out_shift = (small[:, 2 * share : 3 * share] + small[:, 3 * share : 4 * share]).reshape(1, width)
    at = 4 * share
    q_shift = small[:, at : at + qkv_bias.size].reshape((2,) + qkv_bias.shape)
    q_shift = q_shift.transpose(1, 2, 0, 3).reshape(3, -1)
    at += qkv_bias.size
    f_shift = small[:, at : at + fc1_bias.size].reshape((2,) + fc1_bias.shape).transpose(1, 0, 2).reshape(-1)
    q_shift = lax.dynamic_slice_in_dim(q_shift, block * narrow, narrow, 1).reshape(1, -1)
    f_shift = lax.dynamic_slice_in_dim(f_shift, block * wide, wide, 0).reshape(1, -1)

    places = jnp.arange(pack_rows, dtype=jnp.int32)
    segment, position = jax.vmap(lambda row: segment_layout(row, places))(
        lengths.reshape(micro * packs, -1)
    )
    normed, activ, grad_pre, four, g_w1, g_w2, cot_sum, pre_sum = row_work(
        tok_all, cot_all, w_1, w_2, w_q, w_d, gain, shift, f_shift, q_shift, 4 * rows
    )
    back, g_wd, g_wq, qkv_sum, j_1, j_2 = heads(
        four, permutation, segment, position, normed, cot_all, g_w1, g_w2, packs, 4 * rows
    )
    g_bias = jnp.pad(jnp.concatenate([qkv_sum, pre_sum], 1), ((0, 7), (0, 0)))
    layer_out, grad_tokens, g_ln, j_q, j_d, j_b = fold(
        activ, grad_pre, back, tok_all, g_wq, g_wd, g_bias, cotangent, w_1, w_2, w_q, w_d, gain, out_shift
    )
    g_bias = j_b.reshape(8, 8, -1)[:, 0]
    g_qb = g_bias[:, : 3 * narrow].reshape(8, 3, narrow).transpose(1, 0, 2).reshape(3, -1, 64)
    g_qb = lax.dynamic_slice_in_dim(g_qb, y * qkv_bias.shape[2], qkv_bias.shape[2], 2)
    g_fb = g_bias[:, 3 * narrow :].reshape(fc1_bias.shape[0], -1)
    g_fb = lax.dynamic_slice_in_dim(g_fb, y * fc1_bias.shape[1], fc1_bias.shape[1], 1)
    cot_sum = lax.dynamic_slice_in_dim(cot_sum[0], y * share, share, 0)
    return (
        layer_out,
        grad_tokens,
        g_ln[0],
        g_ln[1],
        j_q.astype(f32).transpose(1, 0, 2),
        g_qb,
        j_d.astype(f32),
        cot_sum,
        j_1.astype(f32),
        g_fb,
        j_2.astype(f32),
        cot_sum,
    )


def fast_solution(mesh):
    small_mesh = Mesh(mesh.devices.reshape(2, 2, 2, 2, 2), AXES)
    rows = P(None, ("y", "h", "l", "x"), "t")
    weights = (
        P("y"), P("y"), P("y", None, "t"), P(None, "t", "y"), P("t", "y"), P("y"), P("y", "t"),
        P("t", "y"), P("t", "y"), P("y"),
    )
    return jax.shard_map(
        fast_body,
        mesh=small_mesh,
        in_specs=(rows, rows, P(), P()) + weights,
        out_specs=(rows, rows) + weights,
        check_vma=False,
    )


def solution(mesh):
    if fits(mesh):
        return fast_solution(mesh)
    in_specs = (
        P(None, (FS, CT), TE),
        P(None, (FS, CT), TE),
        P(),
        P(),
        P(FS),
        P(FS),
        P(FS, None, TE),
        P(None, TE, FS),
        P(TE, FS),
        P(FS),
        P(FS, TE),
        P(TE, FS),
        P(TE, FS),
        P(FS),
    )
    out_specs = (
        P(None, (FS, CT), TE),
        P(None, (FS, CT), TE),
        P(FS),
        P(FS),
        P(FS, None, TE),
        P(None, TE, FS),
        P(TE, FS),
        P(FS),
        P(FS, TE),
        P(TE, FS),
        P(TE, FS),
        P(FS),
    )
    return jax.shard_map(body, mesh=mesh, in_specs=in_specs, out_specs=out_specs, check_vma=False)
```

```python
from functools import partial

import jax
import jax.numpy as jnp
from jax import lax
from jax.experimental import pallas as pl
from jax.experimental.pallas import tpu as pltpu
from jax.sharding import Mesh
from jax.sharding import PartitionSpec as P

ROT = 32
FS, CT, TE = "fsdp", "context", "tensor"


EPSILON = 1e-05
ROPE_BASE = 10000.0
NEG_FILL = -1e30


def layer_norm(values, gain, shift):
    center = values - jnp.mean(values, axis=-1, keepdims=True)
    spread = jnp.mean(center * center, axis=-1, keepdims=True)
    return center * lax.rsqrt(spread + EPSILON) * gain + shift


def rotate(values, position):
    half = ROT // 2
    freq = ROPE_BASE ** (-2.0 * jnp.arange(half, dtype=jnp.float32) / ROT)
    angles = position[:, None] * freq[None, :]
    cosine = jnp.cos(angles)[:, None, :]
    sine = jnp.sin(angles)[:, None, :]
    first = values[..., :half]
    second = values[..., half:ROT]
    return jnp.concatenate(
        [first * cosine - second * sine, second * cosine + first * sine, values[..., ROT:]], axis=-1
    )


def segment_layout(length_row, places):
    count = length_row.shape[0]
    upto = jnp.arange(count)[:, None] >= jnp.arange(count)[None, :]
    ends = jnp.sum(jnp.where(upto, length_row[None, :], 0), axis=1)
    starts = ends - length_row
    segment = jnp.sum((places[:, None] >= ends[None, :]).astype(jnp.int32), axis=1)
    match = segment[:, None] == jnp.arange(length_row.shape[0], dtype=jnp.int32)[None, :]
    begin = jnp.sum(jnp.where(match, starts[None, :], 0), axis=1)
    return (segment, places - begin)


def rows_block(source, block_index, block_rows, head_count, head_width):
    return lax.dynamic_slice_in_dim(source, block_index * block_rows, block_rows, 0).reshape(
        block_rows, head_count, head_width
    )


def pair_mask(query_segment, query_place, key_segment, key_place):
    return (
        (query_segment[:, None] == key_segment[None, :])
        & (key_place[None, :] <= query_place[:, None])
    )[None]


def key_scores(
    query,
    keys_all,
    key_segment,
    key_place,
    query_segment,
    query_place,
    block_index,
    block_rows,
    scale,
):
    row_count, head_count, head_width = query.shape
    key_block = rows_block(keys_all, block_index, block_rows, head_count, head_width)
    scores = (
        jnp.einsum("qhe,khe->hqk", query, key_block, preferred_element_type=jnp.float32) * scale
    )
    segment_block = lax.dynamic_slice_in_dim(key_segment, block_index * block_rows, block_rows, 0)
    place_block = lax.dynamic_slice_in_dim(key_place, block_index * block_rows, block_rows, 0)
    return (scores, pair_mask(query_segment, query_place, segment_block, place_block), key_block)


def attend_forward(
    query,
    keys_all,
    values_all,
    key_segment,
    key_place,
    query_segment,
    query_place,
    first_block,
    last_block,
    block_rows,
    scale,
):
    row_count, head_count, head_width = query.shape

    def find_peak(block_index, carry):
        peak, total = carry
        scores, allowed, _ = key_scores(
            query,
            keys_all,
            key_segment,
            key_place,
            query_segment,
            query_place,
            block_index,
            block_rows,
            scale,
        )
        fresh = jnp.maximum(peak, jnp.max(jnp.where(allowed, scores, NEG_FILL), axis=-1))
        added = jnp.sum(jnp.where(allowed, jnp.exp(scores - fresh[..., None]), 0.0), axis=-1)
        return (fresh, total * jnp.exp(peak - fresh) + added)

    start_carry = (
        jnp.full((head_count, row_count), NEG_FILL, jnp.float32),
        jnp.zeros((head_count, row_count), jnp.float32),
    )
    peak, total = lax.fori_loop(first_block, last_block + 1, find_peak, start_carry)
    log_total = peak + jnp.log(total)

    def weigh(block_index, accum):
        scores, allowed, _ = key_scores(
            query,
            keys_all,
            key_segment,
            key_place,
            query_segment,
            query_place,
            block_index,
            block_rows,
            scale,
        )
        attend_weights = jnp.where(allowed, jnp.exp(scores - log_total[..., None]), 0.0).astype(
            jnp.bfloat16
        )
        values = rows_block(values_all, block_index, block_rows, head_count, head_width)
        return accum + jnp.einsum(
            "hqk,khe->qhe", attend_weights, values, preferred_element_type=jnp.float32
        )

    attended = lax.fori_loop(
        first_block, last_block + 1, weigh, jnp.zeros(query.shape, jnp.float32)
    )
    return (attended, log_total)


def attend_backward(
    query,
    keys_all,
    values_all,
    key_segment,
    key_place,
    query_segment,
    query_place,
    first_block,
    last_block,
    block_rows,
    scale,
    log_total,
    grad_out,
    delta,
):
    row_count, head_count, head_width = query.shape

    def step_back(block_index, carry):
        scores, allowed, key_block = key_scores(
            query,
            keys_all,
            key_segment,
            key_place,
            query_segment,
            query_place,
            block_index,
            block_rows,
            scale,
        )
        values = rows_block(values_all, block_index, block_rows, head_count, head_width)
        attend_weights = jnp.where(allowed, jnp.exp(scores - log_total[..., None]), 0.0)
        grad_weights = jnp.einsum(
            "qhe,khe->hqk", grad_out, values, preferred_element_type=jnp.float32
        )
        grad_scores = (attend_weights * (grad_weights - delta[..., None])).astype(jnp.bfloat16)
        grad_query = (
            carry[0]
            + jnp.einsum("hqk,khe->qhe", grad_scores, key_block, preferred_element_type=jnp.float32)
            * scale
        )
        grad_keys, grad_values = (carry[1], carry[2])
        key_part = (
            jnp.einsum("hqk,qhe->khe", grad_scores, query, preferred_element_type=jnp.float32)
            * scale
        ).reshape(block_rows, head_count * head_width)
        value_part = jnp.einsum(
            "hqk,qhe->khe",
            attend_weights.astype(jnp.bfloat16),
            grad_out,
            preferred_element_type=jnp.float32,
        ).reshape(block_rows, head_count * head_width)
        block_start = block_index * block_rows
        grad_keys = lax.dynamic_update_slice_in_dim(
            grad_keys,
            lax.dynamic_slice_in_dim(grad_keys, block_start, block_rows, 0) + key_part,
            block_start,
            0,
        )
        grad_values = lax.dynamic_update_slice_in_dim(
            grad_values,
            lax.dynamic_slice_in_dim(grad_values, block_start, block_rows, 0) + value_part,
            block_start,
            0,
        )
        return (grad_query, grad_keys, grad_values)

    start_carry = (
        jnp.zeros(query.shape, jnp.float32),
        jnp.zeros(keys_all.shape, jnp.float32),
        jnp.zeros(values_all.shape, jnp.float32),
    )
    return lax.fori_loop(first_block, last_block + 1, step_back, start_carry)


def body(
    tokens,
    cotangent,
    lengths,
    permutation,
    ln_gain,
    ln_bias,
    qkv_weight,
    qkv_bias,
    dense_weight,
    dense_bias,
    fc1_weight,
    fc1_bias,
    fc2_weight,
    fc2_bias,
):
    gain_all, shift_all, w_qkv, b_qkv, w_dense, b_dense, w_fc1, b_fc1, w_fc2, b_fc2 = (
        lax.all_gather(ln_gain, FS, axis=0, tiled=True),
        lax.all_gather(ln_bias, FS, axis=0, tiled=True),
        lax.all_gather(qkv_weight, FS, axis=0, tiled=True),
        lax.all_gather(qkv_bias, FS, axis=2, tiled=True),
        lax.all_gather(dense_weight, FS, axis=1, tiled=True),
        lax.all_gather(dense_bias, FS, axis=0, tiled=True),
        lax.all_gather(fc1_weight, FS, axis=0, tiled=True),
        lax.all_gather(fc1_bias, FS, axis=1, tiled=True),
        lax.all_gather(fc2_weight, FS, axis=1, tiled=True),
        lax.all_gather(fc2_bias, FS, axis=0, tiled=True),
    )
    gain_f = gain_all.astype(jnp.float32)
    shift_f = shift_all.astype(jnp.float32)
    local_width = w_qkv.shape[2]
    head_count = b_qkv.shape[1]
    head_width = b_qkv.shape[2]
    hidden_local = w_fc1.shape[1]
    qkv_shift = b_qkv.astype(jnp.float32).reshape(3, local_width)
    fc1_shift = b_fc1.astype(jnp.float32).reshape(hidden_local)
    micro_count = tokens.shape[0]
    row_count = tokens.shape[1]
    feature_share = tokens.shape[2]
    all_rows = micro_count * row_count
    pack_length = row_count * lax.axis_size(CT)
    block_rows = min(512, pack_length)
    group_index = lax.axis_index((FS, CT))
    pack_index = lax.axis_index(FS)
    context_index = lax.axis_index(CT)
    tensor_index = lax.axis_index(TE)
    out_shift = lax.dynamic_slice_in_dim(
        b_dense.astype(jnp.float32) + b_fc2.astype(jnp.float32),
        tensor_index * feature_share,
        feature_share,
        0,
    )
    scale = head_width ** (-0.5)
    counting = jnp.arange(row_count, dtype=jnp.int32)
    pack_places = jnp.arange(pack_length, dtype=jnp.int32)
    query_place = lax.dynamic_slice_in_dim(pack_places, context_index * row_count, row_count, 0)
    last_query_block = (context_index * row_count + row_count - 1) // block_rows
    sent_tokens = []
    sent_cot = []
    slot_sources = []
    arrive_slots = []
    return_orders = []
    key_segments = []
    query_segments = []
    query_positions = []
    first_blocks = []
    length_rows = []
    for micro_index in range(micro_count):
        perm_row = permutation[micro_index]
        own_targets = lax.dynamic_slice_in_dim(perm_row, group_index * row_count, row_count, 0)
        send_order = jnp.argsort(own_targets // row_count, stable=True)
        return_orders.append(jnp.zeros(row_count, jnp.int32).at[send_order].set(counting))
        here = perm_row // row_count == group_index
        arriving = jnp.argsort(jnp.where(here, 0, 1), stable=True)[:row_count]
        arrive_slot = perm_row[arriving] % row_count
        arrive_slots.append(arrive_slot)
        slot_sources.append(jnp.zeros(row_count, jnp.int32).at[arrive_slot].set(counting))
        sent_tokens.append(tokens[micro_index][send_order])
        sent_cot.append(cotangent[micro_index][send_order])
        length_row = lax.dynamic_index_in_dim(lengths[micro_index], pack_index, 0, keepdims=False)
        length_rows.append(length_row)
        key_segment, key_position = segment_layout(length_row, pack_places)
        key_segments.append(key_segment)
        query_segments.append(
            lax.dynamic_slice_in_dim(key_segment, context_index * row_count, row_count, 0)
        )
        query_position = lax.dynamic_slice_in_dim(
            key_position, context_index * row_count, row_count, 0
        )
        query_positions.append(query_position)
        first_blocks.append((query_place[0] - query_position[0]) // block_rows)
    received = (
        lax.all_to_all(
            jnp.stack(sent_tokens), (FS, CT), split_axis=1, concat_axis=1, tiled=True
        ),
        lax.all_to_all(
            jnp.stack(sent_cot), (FS, CT), split_axis=1, concat_axis=1, tiled=True
        ),
    )
    own_tokens = jnp.concatenate(
        [received[0][m][slot_sources[m]] for m in range(micro_count)], axis=0
    )
    own_cot = jnp.concatenate([received[1][m][slot_sources[m]] for m in range(micro_count)], axis=0)
    full_tokens, full_cot = (
        lax.all_gather(own_tokens, TE, axis=1, tiled=True),
        lax.all_gather(own_cot, TE, axis=1, tiled=True),
    )
    normed, norm_back = jax.vjp(layer_norm, full_tokens.astype(jnp.float32), gain_f, shift_f)
    normed_b = normed.astype(jnp.bfloat16)
    qkv = jnp.einsum("rd,dce->rce", normed_b, w_qkv, preferred_element_type=jnp.float32) + qkv_shift
    angle_pos = jnp.concatenate(query_positions, axis=0).astype(jnp.float32)
    query_rot, rope_back = jax.vjp(
        lambda inner: rotate(inner, angle_pos), qkv[:, 0].reshape(all_rows, head_count, head_width)
    )
    key_rot = rotate(qkv[:, 1].reshape(all_rows, head_count, head_width), angle_pos)
    query_b = query_rot.astype(jnp.bfloat16)
    key_b = key_rot.reshape(all_rows, local_width).astype(jnp.bfloat16)
    value_b = qkv[:, 2].astype(jnp.bfloat16)
    keys_all, values_all = (
        lax.all_gather(
            key_b.reshape(micro_count, row_count, local_width), CT, axis=1, tiled=True
        ),
        lax.all_gather(
            value_b.reshape(micro_count, row_count, local_width), CT, axis=1, tiled=True
        ),
    )
    attended_list = []
    log_list = []
    for micro_index in range(micro_count):
        rows = slice(micro_index * row_count, (micro_index + 1) * row_count)
        attended_one, log_one = attend_forward(
            query_b[rows],
            keys_all[micro_index],
            values_all[micro_index],
            key_segments[micro_index],
            pack_places,
            query_segments[micro_index],
            query_place,
            first_blocks[micro_index],
            last_query_block,
            block_rows,
            scale,
        )
        attended_list.append(attended_one)
        log_list.append(log_one)
    attended = jnp.concatenate(attended_list, axis=0)
    attended_b = attended.reshape(all_rows, local_width).astype(jnp.bfloat16)
    pre_act = jnp.dot(normed_b, w_fc1, preferred_element_type=jnp.float32) + fc1_shift
    activ, gelu_back = jax.vjp(partial(jax.nn.gelu, approximate=True), pre_act)
    activ_b = activ.astype(jnp.bfloat16)
    partial_out = jnp.dot(attended_b, w_dense, preferred_element_type=jnp.float32) + jnp.dot(
        activ_b, w_fc2, preferred_element_type=jnp.float32
    )
    branch = lax.psum_scatter(
        partial_out.astype(jnp.bfloat16), TE, scatter_dimension=1, tiled=True
    ).astype(jnp.float32)
    layer_rows = (own_tokens.astype(jnp.float32) + branch + out_shift).astype(jnp.bfloat16)
    grad_attended = jnp.einsum(
        "rd,ed->re", full_cot, w_dense, preferred_element_type=jnp.float32
    ).astype(jnp.bfloat16)
    grad_activ = jnp.einsum("rd,hd->rh", full_cot, w_fc2, preferred_element_type=jnp.float32)
    grad_pre = gelu_back(grad_activ)[0].astype(jnp.bfloat16)
    grad_heads = grad_attended.reshape(all_rows, head_count, head_width)
    delta_list = []
    for micro_index in range(micro_count):
        rows = slice(micro_index * row_count, (micro_index + 1) * row_count)
        delta_list.append(
            jnp.einsum(
                "qhe,qhe->hq", grad_heads[rows].astype(jnp.float32), attended_list[micro_index]
            )
        )
    query_grads = []
    key_parts = []
    value_parts = []
    for micro_index in range(micro_count):
        rows = slice(micro_index * row_count, (micro_index + 1) * row_count)
        grad_query_one, grad_keys_one, grad_values_one = attend_backward(
            query_b[rows],
            keys_all[micro_index],
            values_all[micro_index],
            key_segments[micro_index],
            pack_places,
            query_segments[micro_index],
            query_place,
            first_blocks[micro_index],
            last_query_block,
            block_rows,
            scale,
            log_list[micro_index],
            grad_heads[rows],
            delta_list[micro_index],
        )
        query_grads.append(grad_query_one)
        key_parts.append(grad_keys_one)
        value_parts.append(grad_values_one)
    grad_keys, grad_values = (
        lax.psum_scatter(
            jnp.stack(key_parts).astype(jnp.bfloat16), CT, scatter_dimension=1, tiled=True
        ).astype(jnp.float32),
        lax.psum_scatter(
            jnp.stack(value_parts).astype(jnp.bfloat16), CT, scatter_dimension=1, tiled=True
        ).astype(jnp.float32),
    )
    grad_keys = grad_keys.reshape(all_rows, local_width)
    grad_values = grad_values.reshape(all_rows, local_width)
    grad_query = jnp.concatenate(query_grads, axis=0)
    grad_query_pre = rope_back(grad_query)[0].reshape(all_rows, local_width)
    grad_key_pre = rope_back(grad_keys.reshape(all_rows, head_count, head_width))[0].reshape(
        all_rows, local_width
    )
    grad_qkv = jnp.stack([grad_query_pre, grad_key_pre, grad_values], axis=1).astype(jnp.bfloat16)
    grad_normed_part = jnp.einsum(
        "rce,dce->rd", grad_qkv, w_qkv, preferred_element_type=jnp.float32
    ) + jnp.einsum("rh,dh->rd", grad_pre, w_fc1, preferred_element_type=jnp.float32)
    grad_normed = lax.psum(grad_normed_part.astype(jnp.bfloat16), TE).astype(jnp.float32)
    grad_input, grad_gain, grad_shift = norm_back(grad_normed)
    cot_f = full_cot.astype(jnp.float32)
    grad_own = lax.dynamic_slice_in_dim(
        cot_f + grad_input, tensor_index * feature_share, feature_share, 1
    ).astype(jnp.bfloat16)
    cot_total = jnp.sum(cot_f, axis=0)
    part_qkv_w = jnp.einsum("rd,rce->dce", normed_b, grad_qkv, preferred_element_type=jnp.float32)
    part_qkv_b = jnp.sum(grad_qkv.astype(jnp.float32), axis=0).reshape(b_qkv.shape)
    part_dense_w = jnp.einsum("re,rd->ed", attended_b, full_cot, preferred_element_type=jnp.float32)
    part_fc1_w = jnp.einsum("rd,rh->dh", normed_b, grad_pre, preferred_element_type=jnp.float32)
    part_fc1_b = jnp.sum(grad_pre.astype(jnp.float32), axis=0).reshape(b_fc1.shape)
    part_fc2_w = jnp.einsum("rh,rd->hd", activ_b, full_cot, preferred_element_type=jnp.float32)
    back_rows = []
    back_grads = []
    for micro_index in range(micro_count):
        rows = slice(micro_index * row_count, (micro_index + 1) * row_count)
        back_rows.append(layer_rows[rows][arrive_slots[micro_index]])
        back_grads.append(grad_own[rows][arrive_slots[micro_index]])
    returned = (
        lax.all_to_all(
            jnp.stack(back_rows), (FS, CT), split_axis=1, concat_axis=1, tiled=True
        ),
        lax.all_to_all(
            jnp.stack(back_grads), (FS, CT), split_axis=1, concat_axis=1, tiled=True
        ),
    )
    layer_out = jnp.stack([returned[0][m][return_orders[m]] for m in range(micro_count)])
    grad_tokens = jnp.stack([returned[1][m][return_orders[m]] for m in range(micro_count)])
    shares = (
        lax.psum_scatter(
            grad_gain.astype(jnp.bfloat16), (FS, CT), scatter_dimension=0, tiled=True
        ).astype(jnp.float32),
        lax.psum_scatter(
            grad_shift.astype(jnp.bfloat16), (FS, CT), scatter_dimension=0, tiled=True
        ).astype(jnp.float32),
        lax.psum_scatter(
            part_qkv_w.astype(jnp.bfloat16), (FS, CT), scatter_dimension=0, tiled=True
        ).astype(jnp.float32),
        lax.psum_scatter(
            part_qkv_b.astype(jnp.bfloat16), (FS, CT), scatter_dimension=2, tiled=True
        ).astype(jnp.float32),
        lax.psum_scatter(
            part_dense_w.astype(jnp.bfloat16), (FS, CT), scatter_dimension=1, tiled=True
        ).astype(jnp.float32),
        lax.psum_scatter(
            cot_total.astype(jnp.bfloat16), (FS, CT), scatter_dimension=0, tiled=True
        ).astype(jnp.float32),
        lax.psum_scatter(
            part_fc1_w.astype(jnp.bfloat16), (FS, CT), scatter_dimension=0, tiled=True
        ).astype(jnp.float32),
        lax.psum_scatter(
            part_fc1_b.astype(jnp.bfloat16), (FS, CT), scatter_dimension=1, tiled=True
        ).astype(jnp.float32),
        lax.psum_scatter(
            part_fc2_w.astype(jnp.bfloat16), (FS, CT), scatter_dimension=1, tiled=True
        ).astype(jnp.float32),
        lax.psum_scatter(
            cot_total.astype(jnp.bfloat16), (FS, CT), scatter_dimension=0, tiled=True
        ).astype(jnp.float32),
    )
    reduced = (
        lax.all_gather(shares[0].astype(jnp.bfloat16), CT, axis=0, tiled=True).astype(
            jnp.float32
        ),
        lax.all_gather(shares[1].astype(jnp.bfloat16), CT, axis=0, tiled=True).astype(
            jnp.float32
        ),
        lax.all_gather(shares[2].astype(jnp.bfloat16), CT, axis=0, tiled=True).astype(
            jnp.float32
        ),
        lax.all_gather(shares[3].astype(jnp.bfloat16), CT, axis=2, tiled=True).astype(
            jnp.float32
        ),
        lax.all_gather(shares[4].astype(jnp.bfloat16), CT, axis=1, tiled=True).astype(
            jnp.float32
        ),
        lax.all_gather(shares[5].astype(jnp.bfloat16), CT, axis=0, tiled=True).astype(
            jnp.float32
        ),
        lax.all_gather(shares[6].astype(jnp.bfloat16), CT, axis=0, tiled=True).astype(
            jnp.float32
        ),
        lax.all_gather(shares[7].astype(jnp.bfloat16), CT, axis=1, tiled=True).astype(
            jnp.float32
        ),
        lax.all_gather(shares[8].astype(jnp.bfloat16), CT, axis=1, tiled=True).astype(
            jnp.float32
        ),
        lax.all_gather(shares[9].astype(jnp.bfloat16), CT, axis=0, tiled=True).astype(
            jnp.float32
        ),
    )
    return (
        layer_out,
        grad_tokens,
        reduced[0],
        reduced[1],
        reduced[2],
        reduced[3],
        reduced[4],
        reduced[5],
        reduced[6],
        reduced[7],
        reduced[8],
        reduced[9],
    )


MESH = pl.DeviceIdType.MESH
AXES = ("y", "h", "l", "x", "t")
BLOCK = 256
SPAN = 512


def fits(mesh):
    return (mesh.shape[FS], mesh.shape[CT], mesh.shape[TE]) == (2, 8, 2)


def place():
    return tuple(lax.axis_index(a) for a in AXES)


def greet(peers):
    barrier = pltpu.get_barrier_semaphore()
    total = 0
    for device, there in peers:
        if there is True:
            pl.semaphore_signal(barrier, inc=1, device_id=device, device_id_type=MESH)
            total += 1
        else:

            @pl.when(there)
            def _(device=device):
                pl.semaphore_signal(barrier, inc=1, device_id=device, device_id_type=MESH)

            total = total + there.astype(jnp.int32)
    pl.semaphore_wait(barrier, total)


NN = (((1,), (0,)), ((), ()))
NT = (((1,), (1,)), ((), ()))
TN = (((0,), (0,)), ((), ()))


def dot(a, b, dims=NN):
    return lax.dot_general(a, b, dims, preferred_element_type=jnp.float32)


ROOT = 0.7978845608028654
CUBE = 0.044715
GROUPS = tuple((dy, dx, j) for j in range(4) for dx in (0, 1) for dy in (0, 1))
SMALL_ROWS = 80


def spread_kernel(
    tok, cot, w_q, w_d, w_1, w_2, small,
    tok_all, cot_all, q_out, d_out, o_1, o_2, small_out, normed_out, activ_out, pre_out, four_out,
    g_1, g_2, cot_sum, pre_sum,
    v_q, v_d, v_1, v_2, v_s, acc_1, acc_2, tok_v, cot_v, normed_v, activ_v, pre_v, four_v,
    local_sem, send_sem, recv_sem, in_sem, out_sem,
):
    y, h, l, x, t = place()
    z = 2 * h + l
    rows, half = tok.shape[1], tok.shape[2]
    other_y, other_x, other_t = {"y": 1 - y}, {"x": 1 - x}, {"t": 1 - t}

    def along(zz):
        return {"h": zz // 2, "l": lax.rem(zz, 2)}

    greet(
        [(other_y, True), (other_x, True), (other_t, True)]
        + [(along(lax.max(z - 1, 0)), z > 0), (along(lax.min(z + 1, 3)), z < 3)]
    )
    units = [(tok, tok_all, 0, 1), (tok, tok_all, 1, 1), (cot, cot_all, 0, 2)]
    numbers = {}

    def number(key):
        return numbers.setdefault(key, len(numbers))

    def group_at(dy, dx, zz):
        yy = 1 - y if dy else y
        xx = 1 - x if dx else x
        return yy * 8 + zz * 2 + xx

    def region(unit, chunk, core):
        _, out, m, n = units[unit]
        dy, dx, way, k = chunk
        group = group_at(dy, dx, z - k if way == "up" else z + k)
        return out.at[
            pl.ds(m, n),
            pl.ds(pl.multiple_of(group * rows, rows), rows),
            pl.ds(pl.multiple_of(core * half, half), half),
        ]

    def own(unit):
        array, _, m, n = units[unit]
        return array.at[pl.ds(m, n)]

    started = []

    def link(unit, source, target, key, device):
        i = number((unit,) + key)
        return pltpu.make_async_remote_copy(
            src_ref=source, dst_ref=target, send_sem=send_sem.at[i], recv_sem=recv_sem.at[i],
            device_id=device, device_id_type=MESH,
        )

    def send(unit, chunk, key, device):
        source = own(unit) if chunk == (0, 0, "up", 0) else region(unit, chunk, t)
        link(unit, source, region(unit, chunk, t), key, device).start()

    def arrive(unit, chunk, key, core):
        ref = region(unit, chunk, core)
        link(unit, ref, ref, key, other_t).wait_recv()

    def sent(unit, key):
        link(unit, own(unit), own(unit), key, other_t).wait_send()

    def when(there, what):
        if there is True:
            what()
        else:
            pl.when(there)(what)

    def there_of(way, k):
        return True if k == 0 else (z >= k if way == "up" else z + k <= 3)

    def to_core(unit, chunk):
        key = chunk + ("core",)
        send(unit, chunk, key, other_t)
        started.append((unit, chunk, key, None))

    def onward(unit, chunk, axis):
        dy, dx, way, k = chunk
        key = ((1, dx, way, k) if axis == "y" else (dy, 1, way, k)) + ("link",)
        send(unit, chunk, key, other_y if axis == "y" else other_x)
        started.append((unit, chunk, key, None))

    def up_down(unit, chunk):
        dy, dx, way, k = chunk
        for going in ("up", "down") if k == 0 else (way,):
            can = z < 3 if going == "up" else z > 0
            key = (dy, dx, going, k + 1, "link")
            target = along(lax.min(z + 1, 3) if going == "up" else lax.max(z - 1, 0))
            when(can, lambda: send(unit, chunk, key, target))
            started.append((unit, chunk, key, going))

    def got(unit, chunk):
        arrive(unit, chunk, chunk + ("link",), t)

    steps = [[("up", 0)], [("up", 1), ("down", 1)], [("up", 2), ("down", 2)], [("up", 3), ("down", 3)]]

    def z_step(s):
        for u in (1, 2):
            for way, k in steps[s]:
                def act(u=u, c=(0, 0, way, k)):
                    got(u, c)
                    if c[3] < 3:
                        up_down(u, c)
                    onward(u, c, "x")
                    onward(u, c, "y")
                    to_core(u, c)
                when(there_of(way, k), act)

    def y_step(s):
        for u in (1, 2):
            for way, k in steps[s]:
                def act(u=u, c=(1, 0, way, k)):
                    got(u, c)
                    onward(u, c, "x")
                    to_core(u, c)
                when(there_of(way, k), act)

    def x_step(s, dy):
        for u in (1, 2):
            for way, k in steps[s]:
                def act(u=u, c=(dy, 1, way, k)):
                    got(u, c)
                    to_core(u, c)
                when(there_of(way, k), act)

    def first_step(s):
        for way, k in steps[s]:
            def act(way=way, k=k):
                for dy in (0, 1):
                    for dx in (0, 1):
                        c = (dy, dx, way, k)
                        got(0, c)
                        if k < 3:
                            up_down(0, c)
                        to_core(0, c)
            when(there_of(way, k), act)

    nearest = [
        [(("up", 0), True)],
        [(("up", 1), z > 0), (("down", 1), z == 0)],
        [(("down", 2), z == 0), (("down", 1), (z == 1) | (z == 2)), (("up", 2), z == 3)],
        [(("down", 3), z == 0), (("down", 2), z == 1), (("up", 2), z == 2), (("up", 3), z == 3)],
    ]

    def z_at(j):
        if j == 0:
            return z
        options = [(0, 1, 2, 3), (1, 0, 2, 3), (2, 1, 3, 0), (3, 2, 1, 0)]
        value = options[3][j]
        for zz in (2, 1, 0):
            value = jnp.where(z == zz, options[zz][j], value)
        return value

    def loads(group, slot):
        there = pl.ds(pl.multiple_of(group * rows, rows), rows)
        copies = []
        for m in range(2):
            for n, (source, target) in enumerate(((tok_all, tok_v), (cot_all, cot_v))):
                copies.append(
                    pltpu.make_async_copy(
                        source.at[m, there], target.at[slot, pl.ds(m * rows, rows)], in_sem.at[slot, 2 * m + n]
                    )
                )
        return copies

    def stores(group, slot):
        there = pl.ds(pl.multiple_of(group * rows, rows), rows)
        pairs = ((normed_v, normed_out), (activ_v, activ_out), (pre_v, pre_out), (four_v, four_out))
        return [
            pltpu.make_async_copy(
                source.at[slot, pl.ds(m * rows, rows)], target.at[m, there], out_sem.at[slot, 4 * m + n]
            )
            for m in range(2)
            for n, (source, target) in enumerate(pairs)
        ]

    def fetch(i):
        dy, dx, j = GROUPS[i]
        for (way, k), there in nearest[j]:
            def wait(way=way, k=k):
                for u in range(3):
                    c = (dy, dx, way, k)
                    arrive(u, c, c + ("core",), 1 - t)
            when(there, wait)
        for copy in loads(group_at(dy, dx, z_at(j)), i % 2):
            copy.start()

    block = (y * 4 + l * 2 + x, (1 - y) * 4 + l * 2 + x)
    depth = w_1.shape[0]
    wide, narrow = w_1.shape[1] // 8, w_d.shape[0] // 8
    row = pl.ds(pl.multiple_of(y * depth, depth), depth)

    def pieces(b):
        w = pl.ds(pl.multiple_of(b * wide, wide), wide)
        n = pl.ds(pl.multiple_of(b * narrow, narrow), narrow)
        return [
            (small, small_out.at[y]),
            (w_1.at[:, w], o_1.at[row]),
            (w_2.at[w], o_2.at[:, row]),
            (w_q.at[:, :, n], q_out.at[:, row]),
            (w_d.at[n], d_out.at[:, row]),
        ]

    first = (0, 0, "up", 0)
    for u in (1, 2):
        up_down(u, first)
    for u in range(3):
        onward(u, first, "y")
    weights, locals_ = [], []
    for i, (source, target) in enumerate(pieces(block[1])):
        copy = link("w", source, target, (i,), other_y)
        copy.start()
        weights.append(copy)
    for u in range(3):
        onward(u, first, "x")
        to_core(u, first)
        copy = pltpu.make_async_copy(own(u), region(u, first, t), local_sem.at[len(locals_)])
        copy.start()
        locals_.append(copy)
    for source, target in pieces(block[0]):
        copy = pltpu.make_async_copy(source, target, local_sem.at[len(locals_)])
        copy.start()
        locals_.append(copy)
    acc_1[...] = jnp.zeros_like(acc_1)
    acc_2[...] = jnp.zeros_like(acc_2)
    cot_sum[...] = jnp.zeros_like(cot_sum)
    pre_sum[...] = jnp.zeros_like(pre_sum)
    got(0, (1, 0, "up", 0))
    onward(0, (1, 0, "up", 0), "x")
    up_down(0, first)
    up_down(0, (1, 0, "up", 0))
    to_core(0, (1, 0, "up", 0))
    z_step(1)
    for dy in (0, 1):
        got(0, (dy, 1, "up", 0))
        up_down(0, (dy, 1, "up", 0))
        to_core(0, (dy, 1, "up", 0))
    for event in ((y_step, 0), (z_step, 2), (y_step, 1), (x_step, 0, 0), (x_step, 0, 1)):
        event[0](*event[1:])
    for copy in locals_:
        copy.wait()
    fetch(0)
    for copy in weights:
        copy.wait_recv()
    into = []
    for n, (source, target) in enumerate(
        ((q_out, v_q), (d_out, v_d), (o_1, v_1), (o_2, v_2), (small_out, v_s))
    ):
        copy = pltpu.make_async_copy(source, target, local_sem.at[n])
        copy.start()
        into.append(copy)
    for copy in into:
        copy.wait()
    both = v_s[...].astype(jnp.float32)

    def line(at):
        n = half // 128
        return jnp.concatenate([both[yy, at + r : at + r + 1, :] for yy in range(2) for r in range(n)], axis=1)

    gain, shift = line(0), line(half // 128)
    summed = both[0] + both[1]
    base = 4 * half // 128
    index = lax.broadcasted_iota(jnp.int32, summed.shape, 0)

    def pick(values, at):
        return jnp.sum(jnp.where(index == at, values, 0.0), axis=0, keepdims=True)

    q_shift = [pick(summed, base + c * 8 + block[0]) for c in range(3)]
    f_shift = jnp.concatenate(
        [pick(both[yy], base + 24 + 2 * block[0] + r) for r in range(2) for yy in range(2)], axis=1
    )
    events = {
        0: [(first_step, 1)],
        1: [(z_step, 3)],
        2: [(y_step, 2)],
        3: [(x_step, 1, 0)],
        4: [(x_step, 1, 1)],
        5: [(first_step, 2)],
        7: [(y_step, 3)],
        8: [(x_step, 2, 0), (x_step, 2, 1)],
        10: [(first_step, 3)],
        12: [(x_step, 3, 0)],
        14: [(x_step, 3, 1)],
    }
    count = len(GROUPS)

    def chosen(step):
        value = group_at(*GROUPS[-1][:2], z_at(GROUPS[-1][2]))
        for i in range(count - 1):
            dy, dx, j = GROUPS[i]
            value = jnp.where(step == i, group_at(dy, dx, z_at(j)), value)
        return value

    f32, bf16 = jnp.float32, jnp.bfloat16

    def work(step, carry):
        slot = lax.rem(step, 2)
        for i in range(count - 1):

            @pl.when(step == i)
            def _(i=i):
                for event in events.get(i, []):
                    event[0](*event[1:])
                fetch(i + 1)

        group = chosen(step)
        for copy in loads(group, slot):
            copy.wait()

        @pl.when(step >= 2)
        def _():
            for copy in stores(chosen(step - 2), slot):
                copy.wait()

        values = tok_v[slot].astype(f32)
        center = values - jnp.mean(values, axis=1, keepdims=True)
        r = lax.rsqrt(jnp.mean(center * center, axis=1, keepdims=True) + EPSILON)
        normed = (center * r * gain + shift).astype(bf16)
        normed_v[slot] = normed
        cots = cot_v[slot]
        pre = dot(normed, v_1[...]) + f_shift
        square = pre * pre
        curve = jnp.tanh(ROOT * (pre + CUBE * pre * square))
        activ = (0.5 * pre * (1.0 + curve)).astype(bf16)
        slope = 0.5 * (1.0 + curve) + 0.5 * pre * (1.0 - curve * curve) * (ROOT * (1.0 + 3.0 * CUBE * square))
        grad_pre = (dot(cots, v_2[...], NT) * slope).astype(bf16)
        activ_v[slot] = activ
        pre_v[slot] = grad_pre
        for c in range(3):
            at = slice(c * narrow, (c + 1) * narrow)
            four_v[slot, :, at] = (dot(normed, v_q[c]) + q_shift[c]).astype(bf16)
        four_v[slot, :, 3 * narrow :] = dot(cots, v_d[...], NT).astype(bf16)
        acc_1[...] += dot(normed, grad_pre, TN)
        acc_2[...] += dot(activ, cots, TN)
        cot_sum[...] += jnp.sum(cots.astype(f32), axis=0, keepdims=True)
        pre_sum[...] += jnp.sum(grad_pre.astype(f32), axis=0, keepdims=True)
        for copy in stores(group, slot):
            copy.start()
        return carry

    lax.fori_loop(0, count, work, 0)
    g_1[...] = acc_1[...].astype(bf16)
    g_2[...] = acc_2[...].astype(bf16)
    for i in (count - 2, count - 1):
        dy, dx, j = GROUPS[i]
        for copy in stores(group_at(dy, dx, z_at(j)), i % 2):
            copy.wait()
    for copy in weights:
        copy.wait_send()
    for unit, chunk, key, going in started:
        there = there_of(*chunk[2:])
        if going is not None:
            can = z < 3 if going == "up" else z > 0
            there = can if there is True else can & there
        when(there, lambda: sent(unit, key))


def spread(tokens, cotangent, w_q, w_d, w_1, w_2, small):
    micro, rows, half = tokens.shape
    total, deep = rows * 16, half * 2
    wide, narrow = w_1.shape[1] // 8, w_d.shape[0] // 8
    bf16, f32 = jnp.bfloat16, jnp.float32
    shape = jax.ShapeDtypeStruct
    weights = [(3, deep, narrow), (narrow, deep), (deep, wide), (wide, deep), (2,) + small.shape]
    outs = [(micro, total, deep)] * 2 + weights
    outs += [(micro, total, deep), (micro, total, wide), (micro, total, wide), (micro, total, 4 * narrow)]
    both = micro * rows
    any_, vmem = pl.BlockSpec(memory_space=pl.ANY), pl.BlockSpec(memory_space=pltpu.VMEM)
    sem = pltpu.SemaphoreType.DMA
    return pl.pallas_call(
        spread_kernel,
        out_shape=[shape(s, bf16) for s in outs + [(deep, wide), (wide, deep)]]
        + [shape((1, deep), f32), shape((1, wide), f32)],
        in_specs=[any_] * 7,
        out_specs=[any_] * len(outs) + [vmem] * 4,
        scratch_shapes=[pltpu.VMEM(s, bf16) for s in weights]
        + [pltpu.VMEM((deep, wide), f32), pltpu.VMEM((wide, deep), f32)]
        + [pltpu.VMEM((2, both, w), bf16) for w in (deep, deep, deep, wide, wide, 4 * narrow)]
        + [sem((8,)), sem((176,)), sem((176,)), sem((2, 4)), sem((2, 8))],
        compiler_params=pltpu.CompilerParams(
            collective_id=0, has_side_effects=True, vmem_limit_bytes=56 << 20
        ),
        name="spread",
    )(tokens, cotangent, w_q, w_d, w_1, w_2, small)


class Join:
    def __init__(self, parts, outs, local_sem, send_sem, recv_sem):
        self.parts, self.outs = parts, outs
        self.local_sem, self.send_sem, self.recv_sem = local_sem, send_sem, recv_sem
        self.y, self.h, self.l, self.x, self.t = place()
        self.device = {"y": {"y": 1 - self.y}, "l": {"l": 1 - self.l}, "x": {"x": 1 - self.x}}
        self.numbers, self.sends = {}, []
        self.every = range(len(parts))
        self.first = [p[3] for p in parts]
        self.then = ["l" if p[3] == "x" else "x" for p in parts]

    def half_of(self, i, yy):
        ref, d_axis, _, _ = self.parts[i]
        if d_axis is None:
            return ref
        n = ref.shape[d_axis] // 2
        where = [slice(None)] * len(ref.shape)
        where[d_axis] = pl.ds(pl.multiple_of(yy * n, n), n)
        return ref.at[tuple(where)]

    def spot(self, i, yy, ll, xx):
        ref, _, b_axis, _ = self.parts[i]
        n = ref.shape[b_axis]
        where = [slice(None)] * len(ref.shape)
        where[b_axis] = pl.ds(pl.multiple_of((yy * 4 + ll * 2 + xx) * n, n), n)
        return self.outs[i].at[tuple(where)]

    def own(self, i, yy):
        return self.spot(i, yy, self.l, self.x)

    def beside(self, i, axis, yy):
        l, x = self.l, self.x
        return self.spot(i, yy, 1 - l if axis == "l" else l, 1 - x if axis == "x" else x)

    def copy(self, n, source, target, axis):
        return pltpu.make_async_remote_copy(
            src_ref=source, dst_ref=target, send_sem=self.send_sem.at[n], recv_sem=self.recv_sem.at[n],
            device_id=self.device[axis], device_id_type=MESH,
        )

    def send(self, i, source, target, key, axis):
        n = self.numbers.setdefault((i,) + key, len(self.numbers))
        self.copy(n, source, target, axis).start()
        self.sends.append((n, i, axis))

    def got(self, i, target, key):
        self.copy(self.numbers[(i,) + key], target, target, "y").wait_recv()

    def bring(self):
        for i in self.every:
            self.send(i, self.half_of(i, 1 - self.y), self.own(i, self.y), ("y",), "y")

    def offer(self, axis):
        for want in (True, False):
            for i in self.every:
                if (self.first[i] == axis) is want:
                    self.send(i, self.half_of(i, self.y), self.own(i, self.y), (0, axis), axis)

    def kept(self, i):
        return pltpu.make_async_copy(self.half_of(i, self.y), self.own(i, self.y), self.local_sem.at[i])

    def keep(self):
        for i in self.every:
            self.kept(i).start()

    def far(self, side):
        yy = 1 - self.y if side else self.y
        for i in self.every:
            a = self.first[i]
            self.got(i, self.beside(i, a, yy), (side, a))
            self.send(i, self.beside(i, a, yy), self.beside(i, a, yy), (side, "far"), self.then[i])

    def brought(self):
        for i in self.every:
            ref = self.own(i, 1 - self.y)
            self.got(i, ref, ("y",))
            self.send(i, ref, ref, (1, self.first[i]), self.first[i])
            self.send(i, ref, ref, (1, self.then[i]), self.then[i])

    def end(self):
        for i in self.every:
            for side, yy in ((0, self.y), (1, 1 - self.y)):
                self.got(i, self.beside(i, self.then[i], yy), (side, self.then[i]))
                self.got(i, self.spot(i, yy, 1 - self.l, 1 - self.x), (side, "far"))
        for i in self.every:
            self.kept(i).wait()
        for n, i, axis in self.sends:
            self.copy(n, self.own(i, self.y), self.own(i, self.y), axis).wait_send()


def join_sems(count):
    sem = pltpu.SemaphoreType.DMA
    return [sem((count,)), sem((7 * count,)), sem((7 * count,))]


def fold_kernel(
    activ, grad_pre, back, tok_all, g_q, g_d, g_b, cot, w_1, w_2, w_q, w_d, gain, out_shift,
    layer_out, grad_out, ln_out, j_q, j_d, j_b, act_v, pre_v, back_v, tok_v, give, core_in, give_n, sum_in, stat_v, stat_in, ln_v, ln_in,
    load_sem, core_send, core_recv, hop_send, hop_recv, small_send, small_recv, *join_sem,
):
    y, h, l, x, t = place()
    rows, share = cot.shape[1], cot.shape[2]
    both = 2 * rows
    device = {"y": {"y": 1 - y}, "l": {"l": 1 - l}, "x": {"x": 1 - x}, "t": {"t": 1 - t}, "h": {"h": 1 - h}}
    narrow = w_d.shape[0]
    loads = []

    def load(source, target):
        copy = pltpu.make_async_copy(source, target, load_sem.at[len(loads)])
        copy.start()
        loads.append(copy)

    def group_rows(dy, dl, dx):
        yy = 1 - y if dy else y
        ll = 1 - l if dl else l
        xx = 1 - x if dx else x
        return pl.ds(pl.multiple_of((yy * 8 + h * 4 + ll * 2 + xx) * rows, rows), rows)

    owners = [(1, 1, 0), (1, 1, 1), (0, 1, 0), (0, 1, 1), (1, 0, 0), (1, 0, 1), (0, 0, 1), (0, 0, 0)]
    arrived = {}
    for o, owner in enumerate(owners):
        start = len(loads)
        for m in range(2):
            there = pl.ds(m * rows, rows)
            load(activ.at[m, group_rows(*owner)], act_v.at[o, there])
            load(back.at[m, group_rows(*owner)], back_v.at[o, there])
            load(grad_pre.at[m, group_rows(*owner)], pre_v.at[o, there])
        arrived[o] = loads[start:]
    start = len(loads)
    for m in range(2):
        load(tok_all.at[m, group_rows(0, 0, 0)], tok_v.at[pl.ds(m * rows, rows)])
    tok_loads = loads[start:]
    greet([(device[a], True) for a in ("t", "x", "y", "l", "h")])
    parts = [(g_q, 1, 2, "x"), (g_d, 1, 0, "l"), (g_b, None, 0, "l")]
    gather = Join(parts, (j_q, j_d, j_b), *join_sem)
    gather.bring()
    gather.offer("x")
    gather.keep()

    def part(a, o, tt):
        columns = pl.ds(pl.multiple_of(tt * share, share), share)
        if a == 0:
            return dot(act_v[o], w_2[:, columns]) + dot(back_v[o, :, 0:narrow], w_d[:, columns])
        total = dot(pre_v[o], w_1[columns, :], NT)
        for c in range(3):
            total += dot(back_v[o, :, (c + 1) * narrow : (c + 2) * narrow], w_q[c, columns, :], NT)
        return total

    core = {}

    def offer(a, o):
        if o in arrived:
            for copy in arrived.pop(o):
                copy.wait()
        i = a * 8 + o
        give[i] = part(a, o, 1 - t).astype(jnp.bfloat16)
        core[i] = pltpu.make_async_remote_copy(
            src_ref=give.at[i], dst_ref=core_in.at[i], send_sem=core_send.at[i], recv_sem=core_recv.at[i],
            device_id=device["t"], device_id_type=MESH,
        )
        core[i].start()

    hops = {0: ("l", "y", "x"), 1: ("y", "x", "l")}
    place_of = {"y": 0, "l": 1, "x": 2}
    slots, passed = {}, {}

    def slot(a, stage, owner):
        return slots.setdefault((a, stage, owner), len(slots))

    def total_of(a, o, stage):
        i = a * 8 + o
        total = part(a, o, t)
        core[i].wait_recv()
        total += core_in[i].astype(jnp.float32)
        for s in range(stage):
            n = slot(a, s, owners[o])
            passed[n].wait_recv()
            total += sum_in[n].astype(jnp.float32)
        return total

    def stage_owners(a, stage):
        done = [place_of[d] for d in hops[a][:stage]]
        now = place_of[hops[a][stage]]
        return [o for o, w in enumerate(owners) if all(w[d] == 0 for d in done) and w[now] == 1]

    def pass_on(a, o, stage):
        axis = hops[a][stage]
        seen = list(owners[o])
        seen[place_of[axis]] = 0
        n = slot(a, stage, tuple(seen))
        give_n[n] = total_of(a, o, stage).astype(jnp.bfloat16)
        passed[n] = pltpu.make_async_remote_copy(
            src_ref=give_n.at[n], dst_ref=sum_in.at[n], send_sem=hop_send.at[n], recv_sem=hop_recv.at[n],
            device_id=device[axis], device_id_type=MESH,
        )
        passed[n].start()

    order = []
    for stage in range(3):
        for pair in zip(stage_owners(0, stage), stage_owners(1, stage)):
            order += [(a, o, stage) for a, o in enumerate(pair)]
    ahead = 2
    queue = [(a, o) for a, o, _ in order] + [(0, 7), (1, 7)]
    for a, o in queue[:ahead]:
        offer(a, o)
    for i, (a, o, stage) in enumerate(order):
        if stage == 0:
            offer(*queue[i + ahead])
            pass_on(a, o, stage)
            if i == 7:
                gather.offer("l")
                for item in queue[i + ahead + 1 :]:
                    offer(*item)
                gather.far(0)
                gather.brought()
        else:
            pass_on(a, o, stage)
            if i == 11:
                gather.far(1)
    for copy in tok_loads:
        copy.wait()
    mine = pl.ds(pl.multiple_of(t * share, share), share)
    values = tok_v[...].astype(jnp.float32)
    mean = jnp.mean(values, axis=1, keepdims=True)
    spread_of = jnp.mean((values - mean) ** 2, axis=1, keepdims=True)
    r = lax.rsqrt(spread_of + EPSILON)
    token = tok_v[:, mine].astype(jnp.float32)
    hat = (token - mean) * r
    norm_sum = total_of(1, 7, 3)
    scaled = norm_sum * gain[:, mine]
    stat_v[:, 0:128] = jnp.broadcast_to(jnp.sum(scaled, axis=1, keepdims=True), (both, 128))
    stat_v[:, 128:256] = jnp.broadcast_to(jnp.sum(scaled * hat, axis=1, keepdims=True), (both, 128))
    stat = pltpu.make_async_remote_copy(
        src_ref=stat_v, dst_ref=stat_in, send_sem=small_send.at[0], recv_sem=small_recv.at[0],
        device_id=device["t"], device_id_type=MESH,
    )
    stat.start()
    top = lax.broadcasted_iota(jnp.int32, (8, share), 0) == 0
    ln_v[0] = jnp.where(
        top, jnp.sum(norm_sum * hat, axis=0, keepdims=True), jnp.sum(norm_sum, axis=0, keepdims=True)
    )
    smalls = [stat]

    def swap(step, axis):
        copy = pltpu.make_async_remote_copy(
            src_ref=ln_v.at[step], dst_ref=ln_in.at[step], send_sem=small_send.at[step + 1],
            recv_sem=small_recv.at[step + 1], device_id=device[axis], device_id_type=MESH,
        )
        copy.start()
        smalls.append(copy)
        return copy

    first = swap(0, "h")
    out = token + total_of(0, 7, 3) + out_shift[:, mine]
    for m in range(2):
        layer_out[m] = out[m * rows : (m + 1) * rows].astype(jnp.bfloat16)
    first.wait_recv()
    ln_v[1] = ln_v[0] + ln_in[0]
    second = swap(1, "l")
    stat.wait_recv()
    width = 2 * share
    mean_t = (stat_v[:, 0:1] + stat_in[:, 0:1]) / width
    mean_h = (stat_v[:, 128:129] + stat_in[:, 128:129]) / width
    grad = r * (scaled - mean_t - hat * mean_h)
    for m in range(2):
        grad_out[m] = (cot[m].astype(jnp.float32) + grad[m * rows : (m + 1) * rows]).astype(jnp.bfloat16)
    second.wait_recv()
    ln_v[2] = ln_v[1] + ln_in[1]
    swap(2, "x").wait_recv()
    ln_v[3] = ln_v[2] + ln_in[2]
    swap(3, "y").wait_recv()
    ln_v[4] = ln_v[3] + ln_in[3]
    swap(4, "t").wait_recv()
    ln_out[...] = jnp.where(t == y, ln_v[4], ln_in[4])
    for copy in core.values():
        copy.wait_send()
    for copy in passed.values():
        copy.wait_send()
    for copy in smalls:
        copy.wait_send()
    gather.end()


def fold(activ, grad_pre, back, tok_all, g_q, g_d, g_b, cot, w_1, w_2, w_q, w_d, gain, out_shift):
    micro, rows, share = cot.shape
    both = micro * rows
    narrow = w_d.shape[0]
    held = lambda n, w: pltpu.VMEM((n, both, w), jnp.bfloat16)
    sem = pltpu.SemaphoreType.DMA
    any_, vmem = pl.BlockSpec(memory_space=pl.ANY), pl.BlockSpec(memory_space=pltpu.VMEM)
    return pl.pallas_call(
        fold_kernel,
        out_shape=[
            jax.ShapeDtypeStruct(cot.shape, cot.dtype),
            jax.ShapeDtypeStruct(cot.shape, cot.dtype),
            jax.ShapeDtypeStruct((8, share), jnp.float32),
            jax.ShapeDtypeStruct((3, share, share), g_q.dtype),
            jax.ShapeDtypeStruct((share, share), g_d.dtype),
            jax.ShapeDtypeStruct((64, g_b.shape[1]), g_b.dtype),
        ],
        in_specs=[any_] * 7 + [vmem] * 7,
        out_specs=[vmem] * 3 + [any_] * 3,
        scratch_shapes=[
            held(8, w_1.shape[1]),
            held(8, w_1.shape[1]),
            held(8, 4 * narrow),
            pltpu.VMEM((both, 2 * share), jnp.bfloat16),
            held(16, share),
            held(16, share),
            held(14, share),
            held(14, share),
            pltpu.VMEM((both, 256), jnp.float32),
            pltpu.VMEM((both, 256), jnp.float32),
            pltpu.VMEM((5, 8, share), jnp.float32),
            pltpu.VMEM((5, 8, share), jnp.float32),
            sem((50,)),
            sem((16,)),
            sem((16,)),
            sem((14,)),
            sem((14,)),
            sem((6,)),
            sem((6,)),
        ]
        + join_sems(3),
        compiler_params=pltpu.CompilerParams(
            collective_id=3, has_side_effects=True, vmem_limit_bytes=60 << 20
        ),
        name="fold",
    )(activ, grad_pre, back, tok_all, g_q, g_d, g_b, cot, w_1, w_2, w_q, w_d, gain, out_shift)


def swap_rotary(values):
    lane = lax.rem(lax.broadcasted_iota(jnp.int32, values.shape, 1), 64)
    half = ROT // 2
    width = values.shape[1]
    return jnp.where(
        lane < half, pltpu.roll(values, width - half, 1), pltpu.roll(values, half, 1)
    )


def attend_pack(pack, four, perm, seg_q, seg_k, pos, freq, sign, back_ref, laid, gq, gk, gv, cos_v, sin_v):
    pack_rows, width = laid.shape[0], laid.shape[1] // 4
    bf16, f32 = jnp.bfloat16, jnp.float32
    scale = 64 ** (-0.5)
    lane = lax.broadcasted_iota(jnp.int32, (1, width), 1)
    total = four.shape[1]
    for block in range(pack_rows // BLOCK):
        here = slice(block * BLOCK, (block + 1) * BLOCK)
        target = pack * pack_rows + block * BLOCK + lax.broadcasted_iota(jnp.int32, (BLOCK, total), 0)
        chosen = jnp.where(perm[0] == target, 1.0, 0.0).astype(bf16)
        got = dot(chosen, four[0])
        angle = pos[0, here, :] * freq[...]
        cos, sin = jnp.cos(angle), jnp.sin(angle) * sign[...]
        cos_v[here, :] = cos
        sin_v[here, :] = sin
        for c in range(2):
            at = slice(c * width, (c + 1) * width)
            part = got[:, at]
            laid[here, at] = (part * cos + swap_rotary(part) * sin).astype(bf16)
        laid[here, 2 * width :] = got[:, 2 * width :].astype(bf16)
    gk[...] = jnp.zeros_like(gk)
    gv[...] = jnp.zeros_like(gv)
    for block in range(pack_rows // BLOCK):
        low = max(0, block * BLOCK - SPAN)
        high = (block + 1) * BLOCK
        here = slice(block * BLOCK, high)
        keys = laid[low:high, width : 2 * width]
        values = laid[low:high, 2 * width : 3 * width]
        row = lax.broadcasted_iota(jnp.int32, (BLOCK, high - low), 0) + block * BLOCK
        column = lax.broadcasted_iota(jnp.int32, (BLOCK, high - low), 1) + low
        allowed = (seg_q[0, here, :] == seg_k[0, :, low:high]) & (column <= row)
        attended = None
        for head in range(2):
            mine = (lane // 64) == head
            query = jnp.where(mine, laid[here, 0:width], 0)
            grad = jnp.where(mine, laid[here, 3 * width : 4 * width], 0)
            key = jnp.where(mine, keys, 0)
            value = jnp.where(mine, values, 0)
            scores = jnp.where(allowed, dot(query, key, NT) * scale, NEG_FILL)
            peak = jnp.max(scores, axis=1, keepdims=True)
            weights = jnp.exp(scores - peak)
            weights = weights * (1.0 / jnp.sum(weights, axis=1, keepdims=True))
            weights_b = weights.astype(bf16)
            out = dot(weights_b, value)
            attended = out if attended is None else attended + out
            delta = jnp.sum(grad.astype(f32) * out, axis=1, keepdims=True)
            inner = dot(grad, value, NT)
            grad_scores = (weights * (inner - delta)).astype(bf16)
            part = dot(grad_scores, key)
            if head == 0:
                gq[here, :] = part
            else:
                gq[here, :] += part
            gk[low:high, :] += dot(grad_scores, query, TN)
            gv[low:high, :] += dot(weights_b, grad, TN)
        back_ref[here, 0:width] = attended.astype(bf16)
    for c, ref in ((1, gq), (2, gk)):
        grads = ref[...] * scale
        turned = grads * cos_v[...] - swap_rotary(grads) * sin_v[...]
        back_ref[:, c * width : (c + 1) * width] = turned.astype(bf16)
    back_ref[:, 3 * width :] = gv[...].astype(bf16)


def heads_kernel(
    packs, all_packs, four, perm, seg_q, seg_k, pos, freq, sign, perm_c, normed, cot, g_1, g_2,
    back_out, g_d, g_q, qkv_sum, j_1, j_2,
    held, laid, gq, gk, gv, cos_v, sin_v, acc_d, acc_q, *join_sem,
):
    step = pl.program_id(0)
    last = pl.num_programs(0) - 1
    gather = Join([(g_1, 0, 1, "x"), (g_2, 1, 0, "l")], (j_1, j_2), *join_sem)
    f32, bf16 = jnp.float32, jnp.bfloat16

    @pl.when(step == 0)
    def _():
        greet([(d, True) for d in gather.device.values()])
        gather.bring()
        gather.offer("x")
        gather.offer("l")
        gather.keep()
        acc_d[...] = jnp.zeros_like(acc_d)
        acc_q[...] = jnp.zeros_like(acc_q)
        qkv_sum[...] = jnp.zeros_like(qkv_sum)

    @pl.when(step == all_packs - 1)
    def _():
        gather.far(0)

    @pl.when(step == all_packs)
    def _():
        gather.brought()

    @pl.when(step < all_packs)
    def _():
        attend_pack(
            lax.rem(step, packs), four, perm, seg_q, seg_k, pos, freq, sign,
            held.at[step], laid, gq, gk, gv, cos_v, sin_v,
        )

    @pl.when(step >= all_packs)
    def _():
        size, total = normed.shape[1], four.shape[1]
        narrow = acc_d.shape[0]
        per = total // size
        pack_rows = held.shape[1]
        first = (step - all_packs) // per * packs
        column = lax.broadcasted_iota(jnp.int32, (size, pack_rows), 1)
        back = None
        for k in range(packs):
            chosen = jnp.where(perm_c[0] == column + k * pack_rows, 1.0, 0.0).astype(bf16)
            part = dot(chosen, held[first + k])
            back = part if back is None else back + part
        back = back.astype(bf16)
        back_out[0] = back
        grads = back[:, narrow:]
        acc_d[...] += dot(back[:, :narrow], cot[0], TN)
        acc_q[...] += dot(normed[0], grads, TN)
        qkv_sum[...] += jnp.sum(grads.astype(f32), axis=0, keepdims=True)

    @pl.when(step == last)
    def _():
        narrow = acc_d.shape[0]
        g_d[...] = acc_d[...].astype(bf16)
        for c in range(3):
            g_q[c] = acc_q[:, c * narrow : (c + 1) * narrow].astype(bf16)
        gather.far(1)
        gather.end()


def heads(four, permutation, segment, position, normed, cot_all, g_1, g_2, packs, size):
    micro, total, wide = four.shape
    pack_rows = total // packs
    width = wide // 4
    deep = normed.shape[2]
    all_packs = micro * packs
    per = total // size
    lane = jnp.arange(width, dtype=jnp.int32) % 64
    power = ROPE_BASE ** (-2.0 * (lane % (ROT // 2)).astype(jnp.float32) / ROT)
    freq = jnp.where(lane < ROT, power, 0.0)[None, :]
    sign = jnp.where(lane < ROT // 2, -1.0, 1.0)[None, :]

    def by_pack(*s):
        return pl.BlockSpec((1,) + s, lambda i: (jnp.minimum(i, all_packs - 1), 0, 0))

    def by_micro(*s):
        return pl.BlockSpec((1,) + s, lambda i: (jnp.minimum(i, all_packs - 1) // packs, 0, 0))

    def block(w):
        def index(i):
            n = jnp.maximum(i - all_packs, 0)
            return (n // per, lax.rem(n, per), 0)

        return pl.BlockSpec((1, size, w), index)

    def fixed(*s):
        return pl.BlockSpec(s, lambda i: (0,) * len(s))

    any_ = pl.BlockSpec(memory_space=pl.ANY)
    plane = pltpu.VMEM((pack_rows, width), jnp.float32)
    return pl.pallas_call(
        partial(heads_kernel, packs, all_packs),
        grid=(all_packs + micro * per,),
        out_shape=[
            jax.ShapeDtypeStruct(four.shape, jnp.bfloat16),
            jax.ShapeDtypeStruct((width, deep), jnp.bfloat16),
            jax.ShapeDtypeStruct((3, deep, width), jnp.bfloat16),
            jax.ShapeDtypeStruct((1, 3 * width), jnp.float32),
            jax.ShapeDtypeStruct((deep // 2, g_1.shape[1] * 8), g_1.dtype),
            jax.ShapeDtypeStruct((g_2.shape[0] * 8, deep // 2), g_2.dtype),
        ],
        in_specs=[
            by_micro(total, wide),
            by_micro(1, total),
            by_pack(pack_rows, 1),
            by_pack(1, pack_rows),
            by_pack(pack_rows, 1),
            fixed(1, width),
            fixed(1, width),
            block(1),
            block(deep),
            block(deep),
            any_,
            any_,
        ],
        out_specs=[
            block(wide), fixed(width, deep), fixed(3, deep, width), fixed(1, 3 * width), any_, any_,
        ],
        scratch_shapes=[
            pltpu.VMEM((all_packs, pack_rows, wide), jnp.bfloat16),
            pltpu.VMEM((pack_rows, wide), jnp.bfloat16),
        ]
        + [plane] * 5
        + [pltpu.VMEM((width, deep), jnp.float32), pltpu.VMEM((deep, 3 * width), jnp.float32)]
        + join_sems(2),
        compiler_params=pltpu.CompilerParams(
            collective_id=1, has_side_effects=True, vmem_limit_bytes=56 << 20
        ),
        name="heads",
    )(
        four, permutation[:, None, :], segment[:, :, None], segment[:, None, :],
        position.astype(jnp.float32)[:, :, None], freq, sign, permutation[:, :, None], normed, cot_all, g_1, g_2,
    )


def fast_body(
    tokens, cotangent, lengths, permutation, ln_gain, ln_bias, qkv_weight, qkv_bias,
    dense_weight, dense_bias, fc1_weight, fc1_bias, fc2_weight, fc2_bias,
):
    y, h, l, x, t = place()
    f32 = jnp.float32
    micro, rows, share = tokens.shape
    width = share * 2
    total = rows * 16
    pack_rows = rows * 8
    packs = total // pack_rows
    narrow = dense_weight.shape[0] // 8
    flat = jnp.concatenate([a.reshape(-1, 128) for a in (ln_gain, ln_bias, dense_bias, fc2_bias)])
    turned = qkv_bias.reshape(24, 2, 1, qkv_bias.shape[2])
    at_y = jnp.arange(2)[None, None, :, None] == y
    turned = jnp.where(at_y, turned, jnp.zeros_like(turned)).reshape(24, 128)
    small = jnp.concatenate([flat, turned, fc1_bias])
    small = jnp.pad(small, ((0, SMALL_ROWS - small.shape[0]), (0, 0)))
    (
        tok_all, cot_all, w_q, w_d, w_1, w_2, small, normed, activ, grad_pre, four, g_w1, g_w2, cot_sum, pre_sum,
    ) = spread(
        tokens, cotangent, qkv_weight.transpose(1, 0, 2), dense_weight, fc1_weight, fc2_weight, small
    )
    small = small.reshape(2, -1).astype(f32)
    gain = small[:, 0:share].reshape(1, width)
    out_shift = (small[:, 2 * share : 3 * share] + small[:, 3 * share : 4 * share]).reshape(1, width)

    places = jnp.arange(pack_rows, dtype=jnp.int32)
    segment, position = jax.vmap(lambda row: segment_layout(row, places))(
        lengths.reshape(micro * packs, -1)
    )
    back, g_wd, g_wq, qkv_sum, j_1, j_2 = heads(
        four, permutation, segment, position, normed, cot_all, g_w1, g_w2, packs, 4 * rows
    )
    g_bias = jnp.pad(jnp.concatenate([qkv_sum, pre_sum], 1), ((0, 7), (0, 0)))
    layer_out, grad_tokens, g_ln, j_q, j_d, j_b = fold(
        activ, grad_pre, back, tok_all, g_wq, g_wd, g_bias, cotangent, w_1, w_2, w_q, w_d, gain, out_shift
    )
    g_bias = j_b.reshape(8, 8, -1)[:, 0]
    g_qb = g_bias[:, : 3 * narrow].reshape(8, 3, narrow).transpose(1, 0, 2).reshape(3, -1, 64)
    g_qb = lax.dynamic_slice_in_dim(g_qb, y * qkv_bias.shape[2], qkv_bias.shape[2], 2)
    g_fb = g_bias[:, 3 * narrow :].reshape(fc1_bias.shape[0], -1)
    g_fb = lax.dynamic_slice_in_dim(g_fb, y * fc1_bias.shape[1], fc1_bias.shape[1], 1)
    cot_sum = lax.dynamic_slice_in_dim(cot_sum[0], y * share, share, 0)
    return (
        layer_out,
        grad_tokens,
        g_ln[0],
        g_ln[1],
        j_q.astype(f32).transpose(1, 0, 2),
        g_qb,
        j_d.astype(f32),
        cot_sum,
        j_1.astype(f32),
        g_fb,
        j_2.astype(f32),
        cot_sum,
    )


def fast_solution(mesh):
    small_mesh = Mesh(mesh.devices.reshape(2, 2, 2, 2, 2), AXES)
    rows = P(None, ("y", "h", "l", "x"), "t")
    weights = (
        P("y"), P("y"), P("y", None, "t"), P(None, "t", "y"), P("t", "y"), P("y"), P("y", "t"),
        P("t", "y"), P("t", "y"), P("y"),
    )
    return jax.shard_map(
        fast_body,
        mesh=small_mesh,
        in_specs=(rows, rows, P(), P()) + weights,
        out_specs=(rows, rows) + weights,
        check_vma=False,
    )


def solution(mesh):
    if fits(mesh):
        return fast_solution(mesh)
    in_specs = (
        P(None, (FS, CT), TE),
        P(None, (FS, CT), TE),
        P(),
        P(),
        P(FS),
        P(FS),
        P(FS, None, TE),
        P(None, TE, FS),
        P(TE, FS),
        P(FS),
        P(FS, TE),
        P(TE, FS),
        P(TE, FS),
        P(FS),
    )
    out_specs = (
        P(None, (FS, CT), TE),
        P(None, (FS, CT), TE),
        P(FS),
        P(FS),
        P(FS, None, TE),
        P(None, TE, FS),
        P(TE, FS),
        P(FS),
        P(FS, TE),
        P(TE, FS),
        P(TE, FS),
        P(FS),
    )
    return jax.shard_map(body, mesh=mesh, in_specs=in_specs, out_specs=out_specs, check_vma=False)
```

```python
from functools import partial

import jax
import jax.numpy as jnp
from jax import lax
from jax.experimental import pallas as pl
from jax.experimental.pallas import tpu as pltpu
from jax.sharding import Mesh
from jax.sharding import PartitionSpec as P

ROT = 32
FS, CT, TE = "fsdp", "context", "tensor"


EPSILON = 1e-05
ROPE_BASE = 10000.0
NEG_FILL = -1e30


def layer_norm(values, gain, shift):
    center = values - jnp.mean(values, axis=-1, keepdims=True)
    spread = jnp.mean(center * center, axis=-1, keepdims=True)
    return center * lax.rsqrt(spread + EPSILON) * gain + shift


def rotate(values, position):
    half = ROT // 2
    freq = ROPE_BASE ** (-2.0 * jnp.arange(half, dtype=jnp.float32) / ROT)
    angles = position[:, None] * freq[None, :]
    cosine = jnp.cos(angles)[:, None, :]
    sine = jnp.sin(angles)[:, None, :]
    first = values[..., :half]
    second = values[..., half:ROT]
    return jnp.concatenate(
        [first * cosine - second * sine, second * cosine + first * sine, values[..., ROT:]], axis=-1
    )


def segment_layout(length_row, places):
    count = length_row.shape[0]
    upto = jnp.arange(count)[:, None] >= jnp.arange(count)[None, :]
    ends = jnp.sum(jnp.where(upto, length_row[None, :], 0), axis=1)
    starts = ends - length_row
    segment = jnp.sum((places[:, None] >= ends[None, :]).astype(jnp.int32), axis=1)
    match = segment[:, None] == jnp.arange(length_row.shape[0], dtype=jnp.int32)[None, :]
    begin = jnp.sum(jnp.where(match, starts[None, :], 0), axis=1)
    return (segment, places - begin)


def rows_block(source, block_index, block_rows, head_count, head_width):
    return lax.dynamic_slice_in_dim(source, block_index * block_rows, block_rows, 0).reshape(
        block_rows, head_count, head_width
    )


def pair_mask(query_segment, query_place, key_segment, key_place):
    return (
        (query_segment[:, None] == key_segment[None, :])
        & (key_place[None, :] <= query_place[:, None])
    )[None]


def key_scores(
    query,
    keys_all,
    key_segment,
    key_place,
    query_segment,
    query_place,
    block_index,
    block_rows,
    scale,
):
    row_count, head_count, head_width = query.shape
    key_block = rows_block(keys_all, block_index, block_rows, head_count, head_width)
    scores = (
        jnp.einsum("qhe,khe->hqk", query, key_block, preferred_element_type=jnp.float32) * scale
    )
    segment_block = lax.dynamic_slice_in_dim(key_segment, block_index * block_rows, block_rows, 0)
    place_block = lax.dynamic_slice_in_dim(key_place, block_index * block_rows, block_rows, 0)
    return (scores, pair_mask(query_segment, query_place, segment_block, place_block), key_block)


def attend_forward(
    query,
    keys_all,
    values_all,
    key_segment,
    key_place,
    query_segment,
    query_place,
    first_block,
    last_block,
    block_rows,
    scale,
):
    row_count, head_count, head_width = query.shape

    def find_peak(block_index, carry):
        peak, total = carry
        scores, allowed, _ = key_scores(
            query,
            keys_all,
            key_segment,
            key_place,
            query_segment,
            query_place,
            block_index,
            block_rows,
            scale,
        )
        fresh = jnp.maximum(peak, jnp.max(jnp.where(allowed, scores, NEG_FILL), axis=-1))
        added = jnp.sum(jnp.where(allowed, jnp.exp(scores - fresh[..., None]), 0.0), axis=-1)
        return (fresh, total * jnp.exp(peak - fresh) + added)

    start_carry = (
        jnp.full((head_count, row_count), NEG_FILL, jnp.float32),
        jnp.zeros((head_count, row_count), jnp.float32),
    )
    peak, total = lax.fori_loop(first_block, last_block + 1, find_peak, start_carry)
    log_total = peak + jnp.log(total)

    def weigh(block_index, accum):
        scores, allowed, _ = key_scores(
            query,
            keys_all,
            key_segment,
            key_place,
            query_segment,
            query_place,
            block_index,
            block_rows,
            scale,
        )
        attend_weights = jnp.where(allowed, jnp.exp(scores - log_total[..., None]), 0.0).astype(
            jnp.bfloat16
        )
        values = rows_block(values_all, block_index, block_rows, head_count, head_width)
        return accum + jnp.einsum(
            "hqk,khe->qhe", attend_weights, values, preferred_element_type=jnp.float32
        )

    attended = lax.fori_loop(
        first_block, last_block + 1, weigh, jnp.zeros(query.shape, jnp.float32)
    )
    return (attended, log_total)


def attend_backward(
    query,
    keys_all,
    values_all,
    key_segment,
    key_place,
    query_segment,
    query_place,
    first_block,
    last_block,
    block_rows,
    scale,
    log_total,
    grad_out,
    delta,
):
    row_count, head_count, head_width = query.shape

    def step_back(block_index, carry):
        scores, allowed, key_block = key_scores(
            query,
            keys_all,
            key_segment,
            key_place,
            query_segment,
            query_place,
            block_index,
            block_rows,
            scale,
        )
        values = rows_block(values_all, block_index, block_rows, head_count, head_width)
        attend_weights = jnp.where(allowed, jnp.exp(scores - log_total[..., None]), 0.0)
        grad_weights = jnp.einsum(
            "qhe,khe->hqk", grad_out, values, preferred_element_type=jnp.float32
        )
        grad_scores = (attend_weights * (grad_weights - delta[..., None])).astype(jnp.bfloat16)
        grad_query = (
            carry[0]
            + jnp.einsum("hqk,khe->qhe", grad_scores, key_block, preferred_element_type=jnp.float32)
            * scale
        )
        grad_keys, grad_values = (carry[1], carry[2])
        key_part = (
            jnp.einsum("hqk,qhe->khe", grad_scores, query, preferred_element_type=jnp.float32)
            * scale
        ).reshape(block_rows, head_count * head_width)
        value_part = jnp.einsum(
            "hqk,qhe->khe",
            attend_weights.astype(jnp.bfloat16),
            grad_out,
            preferred_element_type=jnp.float32,
        ).reshape(block_rows, head_count * head_width)
        block_start = block_index * block_rows
        grad_keys = lax.dynamic_update_slice_in_dim(
            grad_keys,
            lax.dynamic_slice_in_dim(grad_keys, block_start, block_rows, 0) + key_part,
            block_start,
            0,
        )
        grad_values = lax.dynamic_update_slice_in_dim(
            grad_values,
            lax.dynamic_slice_in_dim(grad_values, block_start, block_rows, 0) + value_part,
            block_start,
            0,
        )
        return (grad_query, grad_keys, grad_values)

    start_carry = (
        jnp.zeros(query.shape, jnp.float32),
        jnp.zeros(keys_all.shape, jnp.float32),
        jnp.zeros(values_all.shape, jnp.float32),
    )
    return lax.fori_loop(first_block, last_block + 1, step_back, start_carry)


def body(
    tokens,
    cotangent,
    lengths,
    permutation,
    ln_gain,
    ln_bias,
    qkv_weight,
    qkv_bias,
    dense_weight,
    dense_bias,
    fc1_weight,
    fc1_bias,
    fc2_weight,
    fc2_bias,
):
    gain_all, shift_all, w_qkv, b_qkv, w_dense, b_dense, w_fc1, b_fc1, w_fc2, b_fc2 = (
        lax.all_gather(ln_gain, FS, axis=0, tiled=True),
        lax.all_gather(ln_bias, FS, axis=0, tiled=True),
        lax.all_gather(qkv_weight, FS, axis=0, tiled=True),
        lax.all_gather(qkv_bias, FS, axis=2, tiled=True),
        lax.all_gather(dense_weight, FS, axis=1, tiled=True),
        lax.all_gather(dense_bias, FS, axis=0, tiled=True),
        lax.all_gather(fc1_weight, FS, axis=0, tiled=True),
        lax.all_gather(fc1_bias, FS, axis=1, tiled=True),
        lax.all_gather(fc2_weight, FS, axis=1, tiled=True),
        lax.all_gather(fc2_bias, FS, axis=0, tiled=True),
    )
    gain_f = gain_all.astype(jnp.float32)
    shift_f = shift_all.astype(jnp.float32)
    local_width = w_qkv.shape[2]
    head_count = b_qkv.shape[1]
    head_width = b_qkv.shape[2]
    hidden_local = w_fc1.shape[1]
    qkv_shift = b_qkv.astype(jnp.float32).reshape(3, local_width)
    fc1_shift = b_fc1.astype(jnp.float32).reshape(hidden_local)
    micro_count = tokens.shape[0]
    row_count = tokens.shape[1]
    feature_share = tokens.shape[2]
    all_rows = micro_count * row_count
    pack_length = row_count * lax.axis_size(CT)
    block_rows = min(512, pack_length)
    group_index = lax.axis_index((FS, CT))
    pack_index = lax.axis_index(FS)
    context_index = lax.axis_index(CT)
    tensor_index = lax.axis_index(TE)
    out_shift = lax.dynamic_slice_in_dim(
        b_dense.astype(jnp.float32) + b_fc2.astype(jnp.float32),
        tensor_index * feature_share,
        feature_share,
        0,
    )
    scale = head_width ** (-0.5)
    counting = jnp.arange(row_count, dtype=jnp.int32)
    pack_places = jnp.arange(pack_length, dtype=jnp.int32)
    query_place = lax.dynamic_slice_in_dim(pack_places, context_index * row_count, row_count, 0)
    last_query_block = (context_index * row_count + row_count - 1) // block_rows
    sent_tokens = []
    sent_cot = []
    slot_sources = []
    arrive_slots = []
    return_orders = []
    key_segments = []
    query_segments = []
    query_positions = []
    first_blocks = []
    length_rows = []
    for micro_index in range(micro_count):
        perm_row = permutation[micro_index]
        own_targets = lax.dynamic_slice_in_dim(perm_row, group_index * row_count, row_count, 0)
        send_order = jnp.argsort(own_targets // row_count, stable=True)
        return_orders.append(jnp.zeros(row_count, jnp.int32).at[send_order].set(counting))
        here = perm_row // row_count == group_index
        arriving = jnp.argsort(jnp.where(here, 0, 1), stable=True)[:row_count]
        arrive_slot = perm_row[arriving] % row_count
        arrive_slots.append(arrive_slot)
        slot_sources.append(jnp.zeros(row_count, jnp.int32).at[arrive_slot].set(counting))
        sent_tokens.append(tokens[micro_index][send_order])
        sent_cot.append(cotangent[micro_index][send_order])
        length_row = lax.dynamic_index_in_dim(lengths[micro_index], pack_index, 0, keepdims=False)
        length_rows.append(length_row)
        key_segment, key_position = segment_layout(length_row, pack_places)
        key_segments.append(key_segment)
        query_segments.append(
            lax.dynamic_slice_in_dim(key_segment, context_index * row_count, row_count, 0)
        )
        query_position = lax.dynamic_slice_in_dim(
            key_position, context_index * row_count, row_count, 0
        )
        query_positions.append(query_position)
        first_blocks.append((query_place[0] - query_position[0]) // block_rows)
    received = (
        lax.all_to_all(
            jnp.stack(sent_tokens), (FS, CT), split_axis=1, concat_axis=1, tiled=True
        ),
        lax.all_to_all(
            jnp.stack(sent_cot), (FS, CT), split_axis=1, concat_axis=1, tiled=True
        ),
    )
    own_tokens = jnp.concatenate(
        [received[0][m][slot_sources[m]] for m in range(micro_count)], axis=0
    )
    own_cot = jnp.concatenate([received[1][m][slot_sources[m]] for m in range(micro_count)], axis=0)
    full_tokens, full_cot = (
        lax.all_gather(own_tokens, TE, axis=1, tiled=True),
        lax.all_gather(own_cot, TE, axis=1, tiled=True),
    )
    normed, norm_back = jax.vjp(layer_norm, full_tokens.astype(jnp.float32), gain_f, shift_f)
    normed_b = normed.astype(jnp.bfloat16)
    qkv = jnp.einsum("rd,dce->rce", normed_b, w_qkv, preferred_element_type=jnp.float32) + qkv_shift
    angle_pos = jnp.concatenate(query_positions, axis=0).astype(jnp.float32)
    query_rot, rope_back = jax.vjp(
        lambda inner: rotate(inner, angle_pos), qkv[:, 0].reshape(all_rows, head_count, head_width)
    )
    key_rot = rotate(qkv[:, 1].reshape(all_rows, head_count, head_width), angle_pos)
    query_b = query_rot.astype(jnp.bfloat16)
    key_b = key_rot.reshape(all_rows, local_width).astype(jnp.bfloat16)
    value_b = qkv[:, 2].astype(jnp.bfloat16)
    keys_all, values_all = (
        lax.all_gather(
            key_b.reshape(micro_count, row_count, local_width), CT, axis=1, tiled=True
        ),
        lax.all_gather(
            value_b.reshape(micro_count, row_count, local_width), CT, axis=1, tiled=True
        ),
    )
    attended_list = []
    log_list = []
    for micro_index in range(micro_count):
        rows = slice(micro_index * row_count, (micro_index + 1) * row_count)
        attended_one, log_one = attend_forward(
            query_b[rows],
            keys_all[micro_index],
            values_all[micro_index],
            key_segments[micro_index],
            pack_places,
            query_segments[micro_index],
            query_place,
            first_blocks[micro_index],
            last_query_block,
            block_rows,
            scale,
        )
        attended_list.append(attended_one)
        log_list.append(log_one)
    attended = jnp.concatenate(attended_list, axis=0)
    attended_b = attended.reshape(all_rows, local_width).astype(jnp.bfloat16)
    pre_act = jnp.dot(normed_b, w_fc1, preferred_element_type=jnp.float32) + fc1_shift
    activ, gelu_back = jax.vjp(partial(jax.nn.gelu, approximate=True), pre_act)
    activ_b = activ.astype(jnp.bfloat16)
    partial_out = jnp.dot(attended_b, w_dense, preferred_element_type=jnp.float32) + jnp.dot(
        activ_b, w_fc2, preferred_element_type=jnp.float32
    )
    branch = lax.psum_scatter(
        partial_out.astype(jnp.bfloat16), TE, scatter_dimension=1, tiled=True
    ).astype(jnp.float32)
    layer_rows = (own_tokens.astype(jnp.float32) + branch + out_shift).astype(jnp.bfloat16)
    grad_attended = jnp.einsum(
        "rd,ed->re", full_cot, w_dense, preferred_element_type=jnp.float32
    ).astype(jnp.bfloat16)
    grad_activ = jnp.einsum("rd,hd->rh", full_cot, w_fc2, preferred_element_type=jnp.float32)
    grad_pre = gelu_back(grad_activ)[0].astype(jnp.bfloat16)
    grad_heads = grad_attended.reshape(all_rows, head_count, head_width)
    delta_list = []
    for micro_index in range(micro_count):
        rows = slice(micro_index * row_count, (micro_index + 1) * row_count)
        delta_list.append(
            jnp.einsum(
                "qhe,qhe->hq", grad_heads[rows].astype(jnp.float32), attended_list[micro_index]
            )
        )
    query_grads = []
    key_parts = []
    value_parts = []
    for micro_index in range(micro_count):
        rows = slice(micro_index * row_count, (micro_index + 1) * row_count)
        grad_query_one, grad_keys_one, grad_values_one = attend_backward(
            query_b[rows],
            keys_all[micro_index],
            values_all[micro_index],
            key_segments[micro_index],
            pack_places,
            query_segments[micro_index],
            query_place,
            first_blocks[micro_index],
            last_query_block,
            block_rows,
            scale,
            log_list[micro_index],
            grad_heads[rows],
            delta_list[micro_index],
        )
        query_grads.append(grad_query_one)
        key_parts.append(grad_keys_one)
        value_parts.append(grad_values_one)
    grad_keys, grad_values = (
        lax.psum_scatter(
            jnp.stack(key_parts).astype(jnp.bfloat16), CT, scatter_dimension=1, tiled=True
        ).astype(jnp.float32),
        lax.psum_scatter(
            jnp.stack(value_parts).astype(jnp.bfloat16), CT, scatter_dimension=1, tiled=True
        ).astype(jnp.float32),
    )
    grad_keys = grad_keys.reshape(all_rows, local_width)
    grad_values = grad_values.reshape(all_rows, local_width)
    grad_query = jnp.concatenate(query_grads, axis=0)
    grad_query_pre = rope_back(grad_query)[0].reshape(all_rows, local_width)
    grad_key_pre = rope_back(grad_keys.reshape(all_rows, head_count, head_width))[0].reshape(
        all_rows, local_width
    )
    grad_qkv = jnp.stack([grad_query_pre, grad_key_pre, grad_values], axis=1).astype(jnp.bfloat16)
    grad_normed_part = jnp.einsum(
        "rce,dce->rd", grad_qkv, w_qkv, preferred_element_type=jnp.float32
    ) + jnp.einsum("rh,dh->rd", grad_pre, w_fc1, preferred_element_type=jnp.float32)
    grad_normed = lax.psum(grad_normed_part.astype(jnp.bfloat16), TE).astype(jnp.float32)
    grad_input, grad_gain, grad_shift = norm_back(grad_normed)
    cot_f = full_cot.astype(jnp.float32)
    grad_own = lax.dynamic_slice_in_dim(
        cot_f + grad_input, tensor_index * feature_share, feature_share, 1
    ).astype(jnp.bfloat16)
    cot_total = jnp.sum(cot_f, axis=0)
    part_qkv_w = jnp.einsum("rd,rce->dce", normed_b, grad_qkv, preferred_element_type=jnp.float32)
    part_qkv_b = jnp.sum(grad_qkv.astype(jnp.float32), axis=0).reshape(b_qkv.shape)
    part_dense_w = jnp.einsum("re,rd->ed", attended_b, full_cot, preferred_element_type=jnp.float32)
    part_fc1_w = jnp.einsum("rd,rh->dh", normed_b, grad_pre, preferred_element_type=jnp.float32)
    part_fc1_b = jnp.sum(grad_pre.astype(jnp.float32), axis=0).reshape(b_fc1.shape)
    part_fc2_w = jnp.einsum("rh,rd->hd", activ_b, full_cot, preferred_element_type=jnp.float32)
    back_rows = []
    back_grads = []
    for micro_index in range(micro_count):
        rows = slice(micro_index * row_count, (micro_index + 1) * row_count)
        back_rows.append(layer_rows[rows][arrive_slots[micro_index]])
        back_grads.append(grad_own[rows][arrive_slots[micro_index]])
    returned = (
        lax.all_to_all(
            jnp.stack(back_rows), (FS, CT), split_axis=1, concat_axis=1, tiled=True
        ),
        lax.all_to_all(
            jnp.stack(back_grads), (FS, CT), split_axis=1, concat_axis=1, tiled=True
        ),
    )
    layer_out = jnp.stack([returned[0][m][return_orders[m]] for m in range(micro_count)])
    grad_tokens = jnp.stack([returned[1][m][return_orders[m]] for m in range(micro_count)])
    shares = (
        lax.psum_scatter(
            grad_gain.astype(jnp.bfloat16), (FS, CT), scatter_dimension=0, tiled=True
        ).astype(jnp.float32),
        lax.psum_scatter(
            grad_shift.astype(jnp.bfloat16), (FS, CT), scatter_dimension=0, tiled=True
        ).astype(jnp.float32),
        lax.psum_scatter(
            part_qkv_w.astype(jnp.bfloat16), (FS, CT), scatter_dimension=0, tiled=True
        ).astype(jnp.float32),
        lax.psum_scatter(
            part_qkv_b.astype(jnp.bfloat16), (FS, CT), scatter_dimension=2, tiled=True
        ).astype(jnp.float32),
        lax.psum_scatter(
            part_dense_w.astype(jnp.bfloat16), (FS, CT), scatter_dimension=1, tiled=True
        ).astype(jnp.float32),
        lax.psum_scatter(
            cot_total.astype(jnp.bfloat16), (FS, CT), scatter_dimension=0, tiled=True
        ).astype(jnp.float32),
        lax.psum_scatter(
            part_fc1_w.astype(jnp.bfloat16), (FS, CT), scatter_dimension=0, tiled=True
        ).astype(jnp.float32),
        lax.psum_scatter(
            part_fc1_b.astype(jnp.bfloat16), (FS, CT), scatter_dimension=1, tiled=True
        ).astype(jnp.float32),
        lax.psum_scatter(
            part_fc2_w.astype(jnp.bfloat16), (FS, CT), scatter_dimension=1, tiled=True
        ).astype(jnp.float32),
        lax.psum_scatter(
            cot_total.astype(jnp.bfloat16), (FS, CT), scatter_dimension=0, tiled=True
        ).astype(jnp.float32),
    )
    reduced = (
        lax.all_gather(shares[0].astype(jnp.bfloat16), CT, axis=0, tiled=True).astype(
            jnp.float32
        ),
        lax.all_gather(shares[1].astype(jnp.bfloat16), CT, axis=0, tiled=True).astype(
            jnp.float32
        ),
        lax.all_gather(shares[2].astype(jnp.bfloat16), CT, axis=0, tiled=True).astype(
            jnp.float32
        ),
        lax.all_gather(shares[3].astype(jnp.bfloat16), CT, axis=2, tiled=True).astype(
            jnp.float32
        ),
        lax.all_gather(shares[4].astype(jnp.bfloat16), CT, axis=1, tiled=True).astype(
            jnp.float32
        ),
        lax.all_gather(shares[5].astype(jnp.bfloat16), CT, axis=0, tiled=True).astype(
            jnp.float32
        ),
        lax.all_gather(shares[6].astype(jnp.bfloat16), CT, axis=0, tiled=True).astype(
            jnp.float32
        ),
        lax.all_gather(shares[7].astype(jnp.bfloat16), CT, axis=1, tiled=True).astype(
            jnp.float32
        ),
        lax.all_gather(shares[8].astype(jnp.bfloat16), CT, axis=1, tiled=True).astype(
            jnp.float32
        ),
        lax.all_gather(shares[9].astype(jnp.bfloat16), CT, axis=0, tiled=True).astype(
            jnp.float32
        ),
    )
    return (
        layer_out,
        grad_tokens,
        reduced[0],
        reduced[1],
        reduced[2],
        reduced[3],
        reduced[4],
        reduced[5],
        reduced[6],
        reduced[7],
        reduced[8],
        reduced[9],
    )


MESH = pl.DeviceIdType.MESH
AXES = ("y", "h", "l", "x", "t")
BLOCK = 256
SPAN = 512


def fits(mesh):
    return (mesh.shape[FS], mesh.shape[CT], mesh.shape[TE]) == (2, 8, 2)


def place():
    return tuple(lax.axis_index(a) for a in AXES)


def greet(peers):
    barrier = pltpu.get_barrier_semaphore()
    total = 0
    for device, there in peers:
        if there is True:
            pl.semaphore_signal(barrier, inc=1, device_id=device, device_id_type=MESH)
            total += 1
        else:

            @pl.when(there)
            def _(device=device):
                pl.semaphore_signal(barrier, inc=1, device_id=device, device_id_type=MESH)

            total = total + there.astype(jnp.int32)
    pl.semaphore_wait(barrier, total)


NN = (((1,), (0,)), ((), ()))
NT = (((1,), (1,)), ((), ()))
TN = (((0,), (0,)), ((), ()))


def dot(a, b, dims=NN):
    return lax.dot_general(a, b, dims, preferred_element_type=jnp.float32)


ROOT = 0.7978845608028654
CUBE = 0.044715
GROUPS = tuple((dy, dx, j) for j in range(4) for dx in (0, 1) for dy in (0, 1))
SMALL_ROWS = 80
SEQUENCES = 4


def spread_kernel(
    tok, cot, w_q, w_d, w_1, w_2, small,
    tok_all, cot_all, q_out, d_out, o_1, o_2, small_out, normed_out, activ_out, pre_out, four_out,
    g_1, g_2, cot_sum, pre_sum,
    v_q, v_d, v_1, v_2, v_s, acc_1, acc_2, tok_v, cot_v, normed_v, activ_v, pre_v, four_v,
    local_sem, send_sem, recv_sem, in_sem, out_sem,
):
    y, h, l, x, t = place()
    z = 2 * h + l
    rows, half = tok.shape[1], tok.shape[2]
    other_y, other_x, other_t = {"y": 1 - y}, {"x": 1 - x}, {"t": 1 - t}

    def along(zz):
        return {"h": zz // 2, "l": lax.rem(zz, 2)}

    greet(
        [(other_y, True), (other_x, True), (other_t, True)]
        + [(along(lax.max(z - 1, 0)), z > 0), (along(lax.min(z + 1, 3)), z < 3)]
    )
    units = [(tok, tok_all, 0, 1), (tok, tok_all, 1, 1), (cot, cot_all, 0, 2)]
    numbers = {}

    def number(key):
        return numbers.setdefault(key, len(numbers))

    def group_at(dy, dx, zz):
        yy = 1 - y if dy else y
        xx = 1 - x if dx else x
        return yy * 8 + zz * 2 + xx

    def region(unit, chunk, core):
        _, out, m, n = units[unit]
        dy, dx, way, k = chunk
        group = group_at(dy, dx, z - k if way == "up" else z + k)
        return out.at[
            pl.ds(m, n),
            pl.ds(pl.multiple_of(group * rows, rows), rows),
            pl.ds(pl.multiple_of(core * half, half), half),
        ]

    def own(unit):
        array, _, m, n = units[unit]
        return array.at[pl.ds(m, n)]

    started = []

    def link(unit, source, target, key, device):
        i = number((unit,) + key)
        return pltpu.make_async_remote_copy(
            src_ref=source, dst_ref=target, send_sem=send_sem.at[i], recv_sem=recv_sem.at[i],
            device_id=device, device_id_type=MESH,
        )

    def send(unit, chunk, key, device):
        source = own(unit) if chunk == (0, 0, "up", 0) else region(unit, chunk, t)
        link(unit, source, region(unit, chunk, t), key, device).start()

    def arrive(unit, chunk, key, core):
        ref = region(unit, chunk, core)
        link(unit, ref, ref, key, other_t).wait_recv()

    def sent(unit, key):
        link(unit, own(unit), own(unit), key, other_t).wait_send()

    def when(there, what):
        if there is True:
            what()
        else:
            pl.when(there)(what)

    def there_of(way, k):
        return True if k == 0 else (z >= k if way == "up" else z + k <= 3)

    def to_core(unit, chunk):
        key = chunk + ("core",)
        send(unit, chunk, key, other_t)
        started.append((unit, chunk, key, None))

    def onward(unit, chunk, axis):
        dy, dx, way, k = chunk
        key = ((1, dx, way, k) if axis == "y" else (dy, 1, way, k)) + ("link",)
        send(unit, chunk, key, other_y if axis == "y" else other_x)
        started.append((unit, chunk, key, None))

    def up_down(unit, chunk):
        dy, dx, way, k = chunk
        for going in ("up", "down") if k == 0 else (way,):
            can = z < 3 if going == "up" else z > 0
            key = (dy, dx, going, k + 1, "link")
            target = along(lax.min(z + 1, 3) if going == "up" else lax.max(z - 1, 0))
            when(can, lambda: send(unit, chunk, key, target))
            started.append((unit, chunk, key, going))

    def got(unit, chunk):
        arrive(unit, chunk, chunk + ("link",), t)

    steps = [[("up", 0)], [("up", 1), ("down", 1)], [("up", 2), ("down", 2)], [("up", 3), ("down", 3)]]

    def z_step(s):
        for u in (1, 2):
            for way, k in steps[s]:
                def act(u=u, c=(0, 0, way, k)):
                    got(u, c)
                    if c[3] < 3:
                        up_down(u, c)
                    onward(u, c, "x")
                    onward(u, c, "y")
                    to_core(u, c)
                when(there_of(way, k), act)

    def y_step(s):
        for u in (1, 2):
            for way, k in steps[s]:
                def act(u=u, c=(1, 0, way, k)):
                    got(u, c)
                    onward(u, c, "x")
                    to_core(u, c)
                when(there_of(way, k), act)

    def x_step(s, dy):
        for u in (1, 2):
            for way, k in steps[s]:
                def act(u=u, c=(dy, 1, way, k)):
                    got(u, c)
                    to_core(u, c)
                when(there_of(way, k), act)

    def first_step(s):
        for way, k in steps[s]:
            def act(way=way, k=k):
                for dy in (0, 1):
                    for dx in (0, 1):
                        c = (dy, dx, way, k)
                        got(0, c)
                        if k < 3:
                            up_down(0, c)
                        to_core(0, c)
            when(there_of(way, k), act)

    nearest = [
        [(("up", 0), True)],
        [(("up", 1), z > 0), (("down", 1), z == 0)],
        [(("down", 2), z == 0), (("down", 1), (z == 1) | (z == 2)), (("up", 2), z == 3)],
        [(("down", 3), z == 0), (("down", 2), z == 1), (("up", 2), z == 2), (("up", 3), z == 3)],
    ]

    def z_at(j):
        if j == 0:
            return z
        options = [(0, 1, 2, 3), (1, 0, 2, 3), (2, 1, 3, 0), (3, 2, 1, 0)]
        value = options[3][j]
        for zz in (2, 1, 0):
            value = jnp.where(z == zz, options[zz][j], value)
        return value

    def loads(group, slot):
        there = pl.ds(pl.multiple_of(group * rows, rows), rows)
        copies = []
        for m in range(2):
            for n, (source, target) in enumerate(((tok_all, tok_v), (cot_all, cot_v))):
                copies.append(
                    pltpu.make_async_copy(
                        source.at[m, there], target.at[slot, pl.ds(m * rows, rows)], in_sem.at[slot, 2 * m + n]
                    )
                )
        return copies

    def stores(group, slot):
        there = pl.ds(pl.multiple_of(group * rows, rows), rows)
        pairs = ((normed_v, normed_out), (activ_v, activ_out), (pre_v, pre_out), (four_v, four_out))
        return [
            pltpu.make_async_copy(
                source.at[slot, pl.ds(m * rows, rows)], target.at[m, there], out_sem.at[slot, 4 * m + n]
            )
            for m in range(2)
            for n, (source, target) in enumerate(pairs)
        ]

    def fetch(i):
        dy, dx, j = GROUPS[i]
        for (way, k), there in nearest[j]:
            def wait(way=way, k=k):
                for u in range(3):
                    c = (dy, dx, way, k)
                    arrive(u, c, c + ("core",), 1 - t)
            when(there, wait)
        for copy in loads(group_at(dy, dx, z_at(j)), i % 2):
            copy.start()

    block = (y * 4 + l * 2 + x, (1 - y) * 4 + l * 2 + x)
    depth = w_1.shape[0]
    wide, narrow = w_1.shape[1] // 8, w_d.shape[0] // 8
    row = pl.ds(pl.multiple_of(y * depth, depth), depth)

    def pieces(b):
        w = pl.ds(pl.multiple_of(b * wide, wide), wide)
        n = pl.ds(pl.multiple_of(b * narrow, narrow), narrow)
        return [
            (small, small_out.at[y]),
            (w_1.at[:, w], o_1.at[row]),
            (w_2.at[w], o_2.at[:, row]),
            (w_q.at[:, :, n], q_out.at[:, row]),
            (w_d.at[n], d_out.at[:, row]),
        ]

    first = (0, 0, "up", 0)
    for u in (1, 2):
        up_down(u, first)
    for u in range(3):
        onward(u, first, "y")
    weights, locals_ = [], []
    for i, (source, target) in enumerate(pieces(block[1])):
        copy = link("w", source, target, (i,), other_y)
        copy.start()
        weights.append(copy)
    for u in range(3):
        onward(u, first, "x")
        to_core(u, first)
        copy = pltpu.make_async_copy(own(u), region(u, first, t), local_sem.at[len(locals_)])
        copy.start()
        locals_.append(copy)
    for source, target in pieces(block[0]):
        copy = pltpu.make_async_copy(source, target, local_sem.at[len(locals_)])
        copy.start()
        locals_.append(copy)
    acc_1[...] = jnp.zeros_like(acc_1)
    acc_2[...] = jnp.zeros_like(acc_2)
    cot_sum[...] = jnp.zeros_like(cot_sum)
    pre_sum[...] = jnp.zeros_like(pre_sum)
    got(0, (1, 0, "up", 0))
    onward(0, (1, 0, "up", 0), "x")
    up_down(0, first)
    up_down(0, (1, 0, "up", 0))
    to_core(0, (1, 0, "up", 0))
    z_step(1)
    for dy in (0, 1):
        got(0, (dy, 1, "up", 0))
        up_down(0, (dy, 1, "up", 0))
        to_core(0, (dy, 1, "up", 0))
    for event in ((y_step, 0), (z_step, 2), (y_step, 1), (x_step, 0, 0), (x_step, 0, 1)):
        event[0](*event[1:])
    for copy in locals_:
        copy.wait()
    fetch(0)
    for copy in weights:
        copy.wait_recv()
    into = []
    for n, (source, target) in enumerate(
        ((q_out, v_q), (d_out, v_d), (o_1, v_1), (o_2, v_2), (small_out, v_s))
    ):
        copy = pltpu.make_async_copy(source, target, local_sem.at[n])
        copy.start()
        into.append(copy)
    for copy in into:
        copy.wait()
    both = v_s[...].astype(jnp.float32)

    def line(at):
        n = half // 128
        return jnp.concatenate([both[yy, at + r : at + r + 1, :] for yy in range(2) for r in range(n)], axis=1)

    gain, shift = line(0), line(half // 128)
    summed = both[0] + both[1]
    base = 4 * half // 128
    index = lax.broadcasted_iota(jnp.int32, summed.shape, 0)

    def pick(values, at):
        return jnp.sum(jnp.where(index == at, values, 0.0), axis=0, keepdims=True)

    q_shift = [pick(summed, base + c * 8 + block[0]) for c in range(3)]
    f_shift = jnp.concatenate(
        [pick(both[yy], base + 24 + 2 * block[0] + r) for r in range(2) for yy in range(2)], axis=1
    )
    events = {
        0: [(first_step, 1)],
        1: [(z_step, 3)],
        2: [(y_step, 2)],
        3: [(x_step, 1, 0)],
        4: [(x_step, 1, 1)],
        5: [(first_step, 2)],
        7: [(y_step, 3)],
        8: [(x_step, 2, 0), (x_step, 2, 1)],
        10: [(first_step, 3)],
        12: [(x_step, 3, 0)],
        14: [(x_step, 3, 1)],
    }
    count = len(GROUPS)

    def chosen(step):
        value = group_at(*GROUPS[-1][:2], z_at(GROUPS[-1][2]))
        for i in range(count - 1):
            dy, dx, j = GROUPS[i]
            value = jnp.where(step == i, group_at(dy, dx, z_at(j)), value)
        return value

    f32, bf16 = jnp.float32, jnp.bfloat16

    def work(step, carry):
        slot = lax.rem(step, 2)
        for i in range(count - 1):

            @pl.when(step == i)
            def _(i=i):
                for event in events.get(i, []):
                    event[0](*event[1:])
                fetch(i + 1)

        group = chosen(step)
        for copy in loads(group, slot):
            copy.wait()

        @pl.when(step >= 2)
        def _():
            for copy in stores(chosen(step - 2), slot):
                copy.wait()

        values = tok_v[slot].astype(f32)
        center = values - jnp.mean(values, axis=1, keepdims=True)
        r = lax.rsqrt(jnp.mean(center * center, axis=1, keepdims=True) + EPSILON)
        normed = (center * r * gain + shift).astype(bf16)
        normed_v[slot] = normed
        cots = cot_v[slot]
        pre = dot(normed, v_1[...]) + f_shift
        square = pre * pre
        curve = jnp.tanh(ROOT * (pre + CUBE * pre * square))
        activ = (0.5 * pre * (1.0 + curve)).astype(bf16)
        slope = 0.5 * (1.0 + curve) + 0.5 * pre * (1.0 - curve * curve) * (ROOT * (1.0 + 3.0 * CUBE * square))
        grad_pre = (dot(cots, v_2[...], NT) * slope).astype(bf16)
        activ_v[slot] = activ
        pre_v[slot] = grad_pre
        for c in range(3):
            at = slice(c * narrow, (c + 1) * narrow)
            four_v[slot, :, at] = (dot(normed, v_q[c]) + q_shift[c]).astype(bf16)
        four_v[slot, :, 3 * narrow :] = dot(cots, v_d[...], NT).astype(bf16)
        acc_1[...] += dot(normed, grad_pre, TN)
        acc_2[...] += dot(activ, cots, TN)
        cot_sum[...] += jnp.sum(cots.astype(f32), axis=0, keepdims=True)
        pre_sum[...] += jnp.sum(grad_pre.astype(f32), axis=0, keepdims=True)
        for copy in stores(group, slot):
            copy.start()
        return carry

    lax.fori_loop(0, count, work, 0)
    g_1[...] = acc_1[...].astype(bf16)
    g_2[...] = acc_2[...].astype(bf16)
    for i in (count - 2, count - 1):
        dy, dx, j = GROUPS[i]
        for copy in stores(group_at(dy, dx, z_at(j)), i % 2):
            copy.wait()
    for copy in weights:
        copy.wait_send()
    for unit, chunk, key, going in started:
        there = there_of(*chunk[2:])
        if going is not None:
            can = z < 3 if going == "up" else z > 0
            there = can if there is True else can & there
        when(there, lambda: sent(unit, key))


def spread(tokens, cotangent, w_q, w_d, w_1, w_2, small):
    micro, rows, half = tokens.shape
    total, deep = rows * 16, half * 2
    wide, narrow = w_1.shape[1] // 8, w_d.shape[0] // 8
    bf16, f32 = jnp.bfloat16, jnp.float32
    shape = jax.ShapeDtypeStruct
    weights = [(3, deep, narrow), (narrow, deep), (deep, wide), (wide, deep), (2,) + small.shape]
    outs = [(micro, total, deep)] * 2 + weights
    outs += [(micro, total, deep), (micro, total, wide), (micro, total, wide), (micro, total, 4 * narrow)]
    both = micro * rows
    any_, vmem = pl.BlockSpec(memory_space=pl.ANY), pl.BlockSpec(memory_space=pltpu.VMEM)
    sem = pltpu.SemaphoreType.DMA
    return pl.pallas_call(
        spread_kernel,
        out_shape=[shape(s, bf16) for s in outs + [(deep, wide), (wide, deep)]]
        + [shape((1, deep), f32), shape((1, wide), f32)],
        in_specs=[any_] * 7,
        out_specs=[any_] * len(outs) + [vmem] * 4,
        scratch_shapes=[pltpu.VMEM(s, bf16) for s in weights]
        + [pltpu.VMEM((deep, wide), f32), pltpu.VMEM((wide, deep), f32)]
        + [pltpu.VMEM((2, both, w), bf16) for w in (deep, deep, deep, wide, wide, 4 * narrow)]
        + [sem((8,)), sem((176,)), sem((176,)), sem((2, 4)), sem((2, 8))],
        compiler_params=pltpu.CompilerParams(
            collective_id=0, has_side_effects=True, vmem_limit_bytes=56 << 20
        ),
        name="spread",
    )(tokens, cotangent, w_q, w_d, w_1, w_2, small)


class Join:
    def __init__(self, parts, outs, local_sem, send_sem, recv_sem):
        self.parts, self.outs = parts, outs
        self.local_sem, self.send_sem, self.recv_sem = local_sem, send_sem, recv_sem
        self.y, self.h, self.l, self.x, self.t = place()
        self.device = {"y": {"y": 1 - self.y}, "l": {"l": 1 - self.l}, "x": {"x": 1 - self.x}}
        self.numbers, self.sends, self.met = {}, [], set()
        self.every = range(len(parts))
        self.first = [p[3] for p in parts]
        self.then = ["l" if p[3] == "x" else "x" for p in parts]

    def half_of(self, i, yy):
        ref, d_axis, _, _ = self.parts[i]
        if d_axis is None:
            return ref
        n = ref.shape[d_axis] // 2
        where = [slice(None)] * len(ref.shape)
        where[d_axis] = pl.ds(pl.multiple_of(yy * n, n), n)
        return ref.at[tuple(where)]

    def spot(self, i, yy, ll, xx):
        ref, _, b_axis, _ = self.parts[i]
        n = ref.shape[b_axis]
        where = [slice(None)] * len(ref.shape)
        where[b_axis] = pl.ds(pl.multiple_of((yy * 4 + ll * 2 + xx) * n, n), n)
        return self.outs[i].at[tuple(where)]

    def own(self, i, yy):
        return self.spot(i, yy, self.l, self.x)

    def beside(self, i, axis, yy):
        l, x = self.l, self.x
        return self.spot(i, yy, 1 - l if axis == "l" else l, 1 - x if axis == "x" else x)

    def copy(self, n, source, target, axis):
        return pltpu.make_async_remote_copy(
            src_ref=source, dst_ref=target, send_sem=self.send_sem.at[n], recv_sem=self.recv_sem.at[n],
            device_id=self.device[axis], device_id_type=MESH,
        )

    def send(self, i, source, target, key, axis):
        n = self.numbers.setdefault((i,) + key, len(self.numbers))
        self.copy(n, source, target, axis).start()
        self.sends.append((n, i, axis))

    def got(self, i, target, key):
        self.copy(self.numbers[(i,) + key], target, target, "y").wait_recv()

    def bring(self):
        for i in self.every:
            self.send(i, self.half_of(i, 1 - self.y), self.own(i, self.y), ("y",), "y")

    def offer(self, axis):
        for want in (True, False):
            for i in self.every:
                if (self.first[i] == axis) is want:
                    self.send(i, self.half_of(i, self.y), self.own(i, self.y), (0, axis), axis)

    def kept(self, i):
        return pltpu.make_async_copy(self.half_of(i, self.y), self.own(i, self.y), self.local_sem.at[i])

    def keep(self):
        for i in self.every:
            self.kept(i).start()

    def far(self, side, axis=None):
        yy = 1 - self.y if side else self.y
        for i in self.every:
            if axis not in (None, self.then[i]):
                continue
            a = self.first[i]
            self.got(i, self.beside(i, a, yy), (side, a))
            self.send(i, self.beside(i, a, yy), self.beside(i, a, yy), (side, "far"), self.then[i])

    def brought(self, *axes):
        for n, axis in enumerate(axes):
            for i in self.every:
                ref = self.own(i, 1 - self.y)
                if (i, "y") not in self.met:
                    self.met.add((i, "y"))
                    self.got(i, ref, ("y",))
                self.send(i, ref, ref, (1, axis), axis)

    def end(self):
        for i in self.every:
            for side, yy in ((0, self.y), (1, 1 - self.y)):
                self.got(i, self.beside(i, self.then[i], yy), (side, self.then[i]))
                self.got(i, self.spot(i, yy, 1 - self.l, 1 - self.x), (side, "far"))
        for i in self.every:
            self.kept(i).wait()
        for n, i, axis in self.sends:
            self.copy(n, self.own(i, self.y), self.own(i, self.y), axis).wait_send()


def join_sems(count):
    sem = pltpu.SemaphoreType.DMA
    return [sem((count,)), sem((7 * count,)), sem((7 * count,))]


def fold_kernel(
    activ, grad_pre, back, tok_all, g_q, g_d, g_b, cot, w_1, w_2, w_q, w_d, gain, out_shift,
    layer_out, grad_out, ln_out, j_q, j_d, j_b, act_v, pre_v, back_v, tok_v, give, core_in, give_n, sum_in, stat_v, stat_in, ln_v, ln_in,
    load_sem, core_send, core_recv, hop_send, hop_recv, small_send, small_recv, *join_sem,
):
    y, h, l, x, t = place()
    rows, share = cot.shape[1], cot.shape[2]
    both = 2 * rows
    device = {"y": {"y": 1 - y}, "l": {"l": 1 - l}, "x": {"x": 1 - x}, "t": {"t": 1 - t}, "h": {"h": 1 - h}}
    narrow = w_d.shape[0]
    loads = []

    def load(source, target):
        copy = pltpu.make_async_copy(source, target, load_sem.at[len(loads)])
        copy.start()
        loads.append(copy)

    def group_rows(dy, dl, dx):
        yy = 1 - y if dy else y
        ll = 1 - l if dl else l
        xx = 1 - x if dx else x
        return pl.ds(pl.multiple_of((yy * 8 + h * 4 + ll * 2 + xx) * rows, rows), rows)

    owners = [(1, 1, 1), (1, 1, 0), (1, 0, 1), (1, 0, 0), (0, 1, 1), (0, 1, 0), (0, 0, 1), (0, 0, 0)]
    arrived = {}
    for o, owner in enumerate(owners):
        start = len(loads)
        for m in range(2):
            there = pl.ds(m * rows, rows)
            load(activ.at[m, group_rows(*owner)], act_v.at[o, there])
            load(back.at[m, group_rows(*owner)], back_v.at[o, there])
            load(grad_pre.at[m, group_rows(*owner)], pre_v.at[o, there])
        arrived[o] = loads[start:]
    start = len(loads)
    for m in range(2):
        load(tok_all.at[m, group_rows(0, 0, 0)], tok_v.at[pl.ds(m * rows, rows)])
    tok_loads = loads[start:]
    greet([(device[a], True) for a in ("t", "x", "y", "l", "h")])
    two, three = pl.ds(0, 2), pl.ds(2, 1)
    parts = [(g_q.at[two], 1, 2, "x"), (g_q.at[three], 1, 2, "l"), (g_d, 1, 0, "l"), (g_b, None, 0, "l")]
    gather = Join(parts, (j_q.at[two], j_q.at[three], j_d, j_b), *join_sem)
    gather.bring()
    gather.offer("x")
    gather.offer("l")
    gather.keep()

    def part(a, o, tt):
        columns = pl.ds(pl.multiple_of(tt * share, share), share)
        if a == 0:
            return dot(act_v[o], w_2[:, columns]) + dot(back_v[o, :, 0:narrow], w_d[:, columns])
        total = dot(pre_v[o], w_1[columns, :], NT)
        for c in range(3):
            total += dot(back_v[o, :, (c + 1) * narrow : (c + 2) * narrow], w_q[c, columns, :], NT)
        return total

    core = {}

    def offer(a, o):
        if o in arrived:
            for copy in arrived.pop(o):
                copy.wait()
        i = a * 8 + o
        give[i] = part(a, o, 1 - t).astype(jnp.bfloat16)
        core[i] = pltpu.make_async_remote_copy(
            src_ref=give.at[i], dst_ref=core_in.at[i], send_sem=core_send.at[i], recv_sem=core_recv.at[i],
            device_id=device["t"], device_id_type=MESH,
        )
        core[i].start()

    hops = {0: ("y", "l", "x"), 1: ("y", "x", "l")}
    place_of = {"y": 0, "l": 1, "x": 2}
    slots, passed = {}, {}

    def slot(a, stage, owner):
        return slots.setdefault((a, stage, owner), len(slots))

    def total_of(a, o, stage):
        i = a * 8 + o
        total = part(a, o, t)
        core[i].wait_recv()
        total += core_in[i].astype(jnp.float32)
        for s in range(stage):
            n = slot(a, s, owners[o])
            passed[n].wait_recv()
            total += sum_in[n].astype(jnp.float32)
        return total

    def pass_on(a, o, stage):
        axis = hops[a][stage]
        seen = list(owners[o])
        seen[place_of[axis]] = 0
        n = slot(a, stage, tuple(seen))
        give_n[n] = total_of(a, o, stage).astype(jnp.bfloat16)
        passed[n] = pltpu.make_async_remote_copy(
            src_ref=give_n.at[n], dst_ref=sum_in.at[n], send_sem=hop_send.at[n], recv_sem=hop_recv.at[n],
            device_id=device[axis], device_id_type=MESH,
        )
        passed[n].start()

    queue = [(1, 0), (1, 2), (1, 1), (1, 3), (0, 0), (0, 1), (0, 2), (0, 3)]
    for a, o in queue[:2]:
        offer(a, o)
    for i, (a, o) in enumerate(queue):
        if i + 2 < len(queue):
            offer(*queue[i + 2])
        pass_on(a, o, 0)
    gather.brought("x", "l")
    for a, o in [(1, 4), (1, 6), (1, 5), (1, 7), (0, 4), (0, 5), (0, 6), (0, 7)]:
        offer(a, o)
    pass_on(1, 4, 1)
    pass_on(1, 6, 1)
    gather.far(0, "x")
    gather.far(0, "l")
    pass_on(1, 5, 2)
    gather.far(1)
    for copy in tok_loads:
        copy.wait()
    mine = pl.ds(pl.multiple_of(t * share, share), share)
    values = tok_v[...].astype(jnp.float32)
    mean = jnp.mean(values, axis=1, keepdims=True)
    spread_of = jnp.mean((values - mean) ** 2, axis=1, keepdims=True)
    r = lax.rsqrt(spread_of + EPSILON)
    token = tok_v[:, mine].astype(jnp.float32)
    hat = (token - mean) * r
    norm_sum = total_of(1, 7, 3)
    scaled = norm_sum * gain[:, mine]
    stat_v[:, 0:128] = jnp.broadcast_to(jnp.sum(scaled, axis=1, keepdims=True), (both, 128))
    stat_v[:, 128:256] = jnp.broadcast_to(jnp.sum(scaled * hat, axis=1, keepdims=True), (both, 128))
    stat = pltpu.make_async_remote_copy(
        src_ref=stat_v, dst_ref=stat_in, send_sem=small_send.at[0], recv_sem=small_recv.at[0],
        device_id=device["t"], device_id_type=MESH,
    )
    stat.start()
    top = lax.broadcasted_iota(jnp.int32, (8, share), 0) == 0
    ln_v[0] = jnp.where(
        top, jnp.sum(norm_sum * hat, axis=0, keepdims=True), jnp.sum(norm_sum, axis=0, keepdims=True)
    )
    smalls = [stat]

    def swap(step, axis):
        copy = pltpu.make_async_remote_copy(
            src_ref=ln_v.at[step], dst_ref=ln_in.at[step], send_sem=small_send.at[step + 1],
            recv_sem=small_recv.at[step + 1], device_id=device[axis], device_id_type=MESH,
        )
        copy.start()
        smalls.append(copy)
        return copy

    first = swap(0, "h")
    pass_on(0, 4, 1)
    pass_on(0, 5, 1)
    first.wait_recv()
    ln_v[1] = ln_v[0] + ln_in[0]
    second = swap(1, "l")
    stat.wait_recv()
    width = 2 * share
    mean_t = (stat_v[:, 0:1] + stat_in[:, 0:1]) / width
    mean_h = (stat_v[:, 128:129] + stat_in[:, 128:129]) / width
    grad = r * (scaled - mean_t - hat * mean_h)
    for m in range(2):
        grad_out[m] = (cot[m].astype(jnp.float32) + grad[m * rows : (m + 1) * rows]).astype(jnp.bfloat16)
    second.wait_recv()
    ln_v[2] = ln_v[1] + ln_in[1]
    third = swap(2, "x")
    pass_on(0, 6, 2)
    third.wait_recv()
    ln_v[3] = ln_v[2] + ln_in[2]
    fourth = swap(3, "y")
    out = token + total_of(0, 7, 3) + out_shift[:, mine]
    for m in range(2):
        layer_out[m] = out[m * rows : (m + 1) * rows].astype(jnp.bfloat16)
    fourth.wait_recv()
    ln_v[4] = ln_v[3] + ln_in[3]
    swap(4, "t").wait_recv()
    ln_out[...] = jnp.where(t == y, ln_v[4], ln_in[4])
    for copy in core.values():
        copy.wait_send()
    for copy in passed.values():
        copy.wait_send()
    for copy in smalls:
        copy.wait_send()
    gather.end()


def fold(activ, grad_pre, back, tok_all, g_q, g_d, g_b, cot, w_1, w_2, w_q, w_d, gain, out_shift):
    micro, rows, share = cot.shape
    both = micro * rows
    narrow = w_d.shape[0]
    held = lambda n, w: pltpu.VMEM((n, both, w), jnp.bfloat16)
    sem = pltpu.SemaphoreType.DMA
    any_, vmem = pl.BlockSpec(memory_space=pl.ANY), pl.BlockSpec(memory_space=pltpu.VMEM)
    return pl.pallas_call(
        fold_kernel,
        out_shape=[
            jax.ShapeDtypeStruct(cot.shape, cot.dtype),
            jax.ShapeDtypeStruct(cot.shape, cot.dtype),
            jax.ShapeDtypeStruct((8, share), jnp.float32),
            jax.ShapeDtypeStruct((3, share, share), g_q.dtype),
            jax.ShapeDtypeStruct((share, share), g_d.dtype),
            jax.ShapeDtypeStruct((64, g_b.shape[1]), g_b.dtype),
        ],
        in_specs=[any_] * 7 + [vmem] * 7,
        out_specs=[vmem] * 3 + [any_] * 3,
        scratch_shapes=[
            held(8, w_1.shape[1]),
            held(8, w_1.shape[1]),
            held(8, 4 * narrow),
            pltpu.VMEM((both, 2 * share), jnp.bfloat16),
            held(16, share),
            held(16, share),
            held(14, share),
            held(14, share),
            pltpu.VMEM((both, 256), jnp.float32),
            pltpu.VMEM((both, 256), jnp.float32),
            pltpu.VMEM((5, 8, share), jnp.float32),
            pltpu.VMEM((5, 8, share), jnp.float32),
            sem((50,)),
            sem((16,)),
            sem((16,)),
            sem((14,)),
            sem((14,)),
            sem((6,)),
            sem((6,)),
        ]
        + join_sems(4),
        compiler_params=pltpu.CompilerParams(
            collective_id=3, has_side_effects=True, vmem_limit_bytes=60 << 20
        ),
        name="fold",
    )(activ, grad_pre, back, tok_all, g_q, g_d, g_b, cot, w_1, w_2, w_q, w_d, gain, out_shift)


def swap_rotary(values):
    lane = lax.rem(lax.broadcasted_iota(jnp.int32, values.shape, 1), 64)
    half = ROT // 2
    width = values.shape[1]
    return jnp.where(
        lane < half, pltpu.roll(values, width - half, 1), pltpu.roll(values, half, 1)
    )


def attend_pack(pack, four, perm, lengths, freq, sign, back_ref, laid, gq, gk, gv, cos_v, sin_v):
    pack_rows, width = laid.shape[0], laid.shape[1] // 4
    bf16, f32 = jnp.bfloat16, jnp.float32
    scale = 64 ** (-0.5)
    lane = lax.broadcasted_iota(jnp.int32, (1, width), 1)
    total = four.shape[1]

    def starts(shape, block):
        row = lax.broadcasted_iota(jnp.int32, shape, 0) + block * BLOCK
        begin, end = jnp.zeros(shape, jnp.int32), 0
        for i in range(SEQUENCES):
            length = lengths(i)
            end = end + length
            begin += jnp.where(row >= end, length, 0)
        return row, begin

    for block in range(pack_rows // BLOCK):
        here = slice(block * BLOCK, (block + 1) * BLOCK)
        target = pack * pack_rows + block * BLOCK + lax.broadcasted_iota(jnp.int32, (BLOCK, total), 0)
        chosen = jnp.where(perm[0] == target, 1.0, 0.0).astype(bf16)
        got = dot(chosen, four[0])
        row, begin = starts((BLOCK, width), block)
        angle = (row - begin).astype(f32) * freq[...]
        cos, sin = jnp.cos(angle), jnp.sin(angle) * sign[...]
        cos_v[here, :] = cos
        sin_v[here, :] = sin
        for c in range(2):
            at = slice(c * width, (c + 1) * width)
            part = got[:, at]
            laid[here, at] = (part * cos + swap_rotary(part) * sin).astype(bf16)
        laid[here, 2 * width :] = got[:, 2 * width :].astype(bf16)
    gk[...] = jnp.zeros_like(gk)
    gv[...] = jnp.zeros_like(gv)
    for block in range(pack_rows // BLOCK):
        low = max(0, block * BLOCK - SPAN)
        high = (block + 1) * BLOCK
        here = slice(block * BLOCK, high)
        keys = laid[low:high, width : 2 * width]
        values = laid[low:high, 2 * width : 3 * width]
        row, begin = starts((BLOCK, high - low), block)
        column = lax.broadcasted_iota(jnp.int32, (BLOCK, high - low), 1) + low
        allowed = (column >= begin) & (column <= row)
        attended = None
        for head in range(2):
            mine = (lane // 64) == head
            query = jnp.where(mine, laid[here, 0:width], 0)
            grad = jnp.where(mine, laid[here, 3 * width : 4 * width], 0)
            key = jnp.where(mine, keys, 0)
            value = jnp.where(mine, values, 0)
            scores = jnp.where(allowed, dot(query, key, NT) * scale, NEG_FILL)
            peak = jnp.max(scores, axis=1, keepdims=True)
            weights = jnp.exp(scores - peak)
            weights = weights * (1.0 / jnp.sum(weights, axis=1, keepdims=True))
            weights_b = weights.astype(bf16)
            out = dot(weights_b, value)
            attended = out if attended is None else attended + out
            delta = jnp.sum(grad.astype(f32) * out, axis=1, keepdims=True)
            inner = dot(grad, value, NT)
            grad_scores = (weights * (inner - delta)).astype(bf16)
            part = dot(grad_scores, key)
            if head == 0:
                gq[here, :] = part
            else:
                gq[here, :] += part
            gk[low:high, :] += dot(grad_scores, query, TN)
            gv[low:high, :] += dot(weights_b, grad, TN)
        back_ref[here, 0:width] = attended.astype(bf16)
    for c, ref in ((1, gq), (2, gk)):
        grads = ref[...] * scale
        turned = grads * cos_v[...] - swap_rotary(grads) * sin_v[...]
        back_ref[:, c * width : (c + 1) * width] = turned.astype(bf16)
    back_ref[:, 3 * width :] = gv[...].astype(bf16)


def heads_kernel(
    packs, all_packs, lengths, four, perm, freq, sign, normed, cot, g_1, g_2,
    back_out, g_d, g_q, qkv_sum, j_1, j_2,
    held, laid, gq, gk, gv, cos_v, sin_v, acc_d, acc_q, *join_sem,
):
    step = pl.program_id(0)
    last = pl.num_programs(0) - 1
    gather = Join([(g_1, 0, 1, "x"), (g_2, 1, 0, "l")], (j_1, j_2), *join_sem)
    f32, bf16 = jnp.float32, jnp.bfloat16

    @pl.when(step == 0)
    def _():
        greet([(d, True) for d in gather.device.values()])
        gather.bring()
        gather.offer("x")
        gather.offer("l")
        gather.keep()
        acc_d[...] = jnp.zeros_like(acc_d)
        acc_q[...] = jnp.zeros_like(acc_q)
        qkv_sum[...] = jnp.zeros_like(qkv_sum)

    @pl.when(step == all_packs - 1)
    def _():
        gather.far(0)

    @pl.when(step == all_packs)
    def _():
        gather.brought("x", "l")

    @pl.when(step < all_packs)
    def _():
        attend_pack(
            lax.rem(step, packs), four, perm, lambda i: lengths[step, i], freq, sign,
            held.at[step], laid, gq, gk, gv, cos_v, sin_v,
        )

    @pl.when(step >= all_packs)
    def _():
        size, total = normed.shape[1], four.shape[1]
        narrow = acc_d.shape[0]
        per = total // size
        pack_rows = held.shape[1]
        first = (step - all_packs) // per * packs
        at = pl.ds(pl.multiple_of(lax.rem(step - all_packs, per) * size, size), size)
        line = perm[0, :, at]
        row = lax.broadcasted_iota(jnp.int32, (pack_rows, size), 0)
        back = None
        for k in range(packs):
            chosen = jnp.where(line == row + k * pack_rows, 1.0, 0.0).astype(bf16)
            part = dot(chosen, held[first + k], TN)
            back = part if back is None else back + part
        back = back.astype(bf16)
        back_out[0] = back
        grads = back[:, narrow:]
        acc_d[...] += dot(back[:, :narrow], cot[0], TN)
        acc_q[...] += dot(normed[0], grads, TN)
        qkv_sum[...] += jnp.sum(grads.astype(f32), axis=0, keepdims=True)

    @pl.when(step == last)
    def _():
        narrow = acc_d.shape[0]
        g_d[...] = acc_d[...].astype(bf16)
        for c in range(3):
            g_q[c] = acc_q[:, c * narrow : (c + 1) * narrow].astype(bf16)
        gather.far(1)
        gather.end()


def heads(lengths, four, permutation, normed, cot_all, g_1, g_2, packs, size):
    micro, total, wide = four.shape
    pack_rows = total // packs
    width = wide // 4
    deep = normed.shape[2]
    all_packs = micro * packs
    per = total // size
    lane = jnp.arange(width, dtype=jnp.int32) % 64
    power = ROPE_BASE ** (-2.0 * (lane % (ROT // 2)).astype(jnp.float32) / ROT)
    freq = jnp.where(lane < ROT, power, 0.0)[None, :]
    sign = jnp.where(lane < ROT // 2, -1.0, 1.0)[None, :]

    def by_micro(*s, after=False):
        def index(i):
            if after:
                i = jnp.where(i < all_packs, i // packs, (i - all_packs) // per)
            else:
                i = jnp.minimum(i, all_packs - 1) // packs
            return (i, 0, 0)

        return pl.BlockSpec((1,) + s, index)

    def block(w):
        def index(i):
            n = jnp.maximum(i - all_packs, 0)
            return (n // per, lax.rem(n, per), 0)

        return pl.BlockSpec((1, size, w), index)

    def fixed(*s):
        return pl.BlockSpec(s, lambda i: (0,) * len(s))

    any_ = pl.BlockSpec(memory_space=pl.ANY)
    plane = pltpu.VMEM((pack_rows, width), jnp.float32)
    return pl.pallas_call(
        partial(heads_kernel, packs, all_packs),
        grid=(all_packs + micro * per,),
        out_shape=[
            jax.ShapeDtypeStruct(four.shape, jnp.bfloat16),
            jax.ShapeDtypeStruct((width, deep), jnp.bfloat16),
            jax.ShapeDtypeStruct((3, deep, width), jnp.bfloat16),
            jax.ShapeDtypeStruct((1, 3 * width), jnp.float32),
            jax.ShapeDtypeStruct((deep // 2, g_1.shape[1] * 8), g_1.dtype),
            jax.ShapeDtypeStruct((g_2.shape[0] * 8, deep // 2), g_2.dtype),
        ],
        in_specs=[
            pl.BlockSpec(memory_space=pltpu.SMEM),
            by_micro(total, wide),
            by_micro(1, total, after=True),
            fixed(1, width),
            fixed(1, width),
            block(deep),
            block(deep),
            any_,
            any_,
        ],
        out_specs=[
            block(wide), fixed(width, deep), fixed(3, deep, width), fixed(1, 3 * width), any_, any_,
        ],
        scratch_shapes=[
            pltpu.VMEM((all_packs, pack_rows, wide), jnp.bfloat16),
            pltpu.VMEM((pack_rows, wide), jnp.bfloat16),
        ]
        + [plane] * 5
        + [pltpu.VMEM((width, deep), jnp.float32), pltpu.VMEM((deep, 3 * width), jnp.float32)]
        + join_sems(2),
        compiler_params=pltpu.CompilerParams(
            collective_id=1, has_side_effects=True, vmem_limit_bytes=56 << 20
        ),
        name="heads",
    )(
        lengths.reshape(all_packs, -1), four, permutation[:, None, :], freq, sign, normed, cot_all, g_1, g_2,
    )


def widen_kernel(source, target):
    target[...] = source[...].astype(jnp.float32)


def widen(value, size):
    rows, columns = value.shape
    block = pl.BlockSpec((size, columns), lambda i: (i, 0))
    return pl.pallas_call(
        widen_kernel,
        grid=(rows // size,),
        out_shape=jax.ShapeDtypeStruct(value.shape, jnp.float32),
        in_specs=[block],
        out_specs=block,
        compiler_params=pltpu.CompilerParams(vmem_limit_bytes=56 << 20),
        name="widen",
    )(value)


def fast_body(
    tokens, cotangent, lengths, permutation, ln_gain, ln_bias, qkv_weight, qkv_bias,
    dense_weight, dense_bias, fc1_weight, fc1_bias, fc2_weight, fc2_bias,
):
    y, h, l, x, t = place()
    f32 = jnp.float32
    micro, rows, share = tokens.shape
    width = share * 2
    total = rows * 16
    pack_rows = rows * 8
    packs = total // pack_rows
    narrow = dense_weight.shape[0] // 8
    flat = jnp.concatenate([a.reshape(-1, 128) for a in (ln_gain, ln_bias, dense_bias, fc2_bias)])
    turned = qkv_bias.reshape(24, 2, 1, qkv_bias.shape[2])
    at_y = jnp.arange(2)[None, None, :, None] == y
    turned = jnp.where(at_y, turned, jnp.zeros_like(turned)).reshape(24, 128)
    small = jnp.concatenate([flat, turned, fc1_bias])
    small = jnp.pad(small, ((0, SMALL_ROWS - small.shape[0]), (0, 0)))
    (
        tok_all, cot_all, w_q, w_d, w_1, w_2, small, normed, activ, grad_pre, four, g_w1, g_w2, cot_sum, pre_sum,
    ) = spread(
        tokens, cotangent, qkv_weight.transpose(1, 0, 2), dense_weight, fc1_weight, fc2_weight, small
    )
    small = small.reshape(2, -1).astype(f32)
    gain = small[:, 0:share].reshape(1, width)
    out_shift = (small[:, 2 * share : 3 * share] + small[:, 3 * share : 4 * share]).reshape(1, width)

    back, g_wd, g_wq, qkv_sum, j_1, j_2 = heads(
        lengths, four, permutation, normed, cot_all, g_w1, g_w2, packs, 4 * rows
    )
    g_bias = jnp.pad(jnp.concatenate([qkv_sum, pre_sum], 1), ((0, 7), (0, 0)))
    layer_out, grad_tokens, g_ln, j_q, j_d, j_b = fold(
        activ, grad_pre, back, tok_all, g_wq, g_wd, g_bias, cotangent, w_1, w_2, w_q, w_d, gain, out_shift
    )
    g_bias = j_b.reshape(8, 8, -1)[:, 0]
    g_qb = g_bias[:, : 3 * narrow].reshape(8, 3, narrow).transpose(1, 0, 2).reshape(3, -1, 64)
    g_qb = lax.dynamic_slice_in_dim(g_qb, y * qkv_bias.shape[2], qkv_bias.shape[2], 2)
    g_fb = g_bias[:, 3 * narrow :].reshape(fc1_bias.shape[0], -1)
    g_fb = lax.dynamic_slice_in_dim(g_fb, y * fc1_bias.shape[1], fc1_bias.shape[1], 1)
    cot_sum = lax.dynamic_slice_in_dim(cot_sum[0], y * share, share, 0)
    return (
        layer_out,
        grad_tokens,
        g_ln[0],
        g_ln[1],
        j_q.astype(f32).transpose(1, 0, 2),
        g_qb,
        j_d.astype(f32),
        cot_sum,
        widen(j_1, 128),
        g_fb,
        widen(j_2, 512),
        cot_sum,
    )


def fast_solution(mesh):
    small_mesh = Mesh(mesh.devices.reshape(2, 2, 2, 2, 2), AXES)
    rows = P(None, ("y", "h", "l", "x"), "t")
    weights = (
        P("y"), P("y"), P("y", None, "t"), P(None, "t", "y"), P("t", "y"), P("y"), P("y", "t"),
        P("t", "y"), P("t", "y"), P("y"),
    )
    return jax.shard_map(
        fast_body,
        mesh=small_mesh,
        in_specs=(rows, rows, P(), P()) + weights,
        out_specs=(rows, rows) + weights,
        check_vma=False,
    )


def solution(mesh):
    if fits(mesh):
        return fast_solution(mesh)
    in_specs = (
        P(None, (FS, CT), TE),
        P(None, (FS, CT), TE),
        P(),
        P(),
        P(FS),
        P(FS),
        P(FS, None, TE),
        P(None, TE, FS),
        P(TE, FS),
        P(FS),
        P(FS, TE),
        P(TE, FS),
        P(TE, FS),
        P(FS),
    )
    out_specs = (
        P(None, (FS, CT), TE),
        P(None, (FS, CT), TE),
        P(FS),
        P(FS),
        P(FS, None, TE),
        P(None, TE, FS),
        P(TE, FS),
        P(FS),
        P(FS, TE),
        P(TE, FS),
        P(TE, FS),
        P(FS),
    )
    return jax.shard_map(body, mesh=mesh, in_specs=in_specs, out_specs=out_specs, check_vma=False)
```

```python
from functools import partial

import jax
import jax.numpy as jnp
from jax import lax
from jax.experimental import pallas as pl
from jax.experimental.pallas import tpu as pltpu
from jax.sharding import Mesh
from jax.sharding import PartitionSpec as P

ROT = 32
FS, CT, TE = "fsdp", "context", "tensor"


EPSILON = 1e-05
ROPE_BASE = 10000.0
NEG_FILL = -1e30


def layer_norm(values, gain, shift):
    center = values - jnp.mean(values, axis=-1, keepdims=True)
    spread = jnp.mean(center * center, axis=-1, keepdims=True)
    return center * lax.rsqrt(spread + EPSILON) * gain + shift


def rotate(values, position):
    half = ROT // 2
    freq = ROPE_BASE ** (-2.0 * jnp.arange(half, dtype=jnp.float32) / ROT)
    angles = position[:, None] * freq[None, :]
    cosine = jnp.cos(angles)[:, None, :]
    sine = jnp.sin(angles)[:, None, :]
    first = values[..., :half]
    second = values[..., half:ROT]
    return jnp.concatenate(
        [first * cosine - second * sine, second * cosine + first * sine, values[..., ROT:]], axis=-1
    )


def segment_layout(length_row, places):
    count = length_row.shape[0]
    upto = jnp.arange(count)[:, None] >= jnp.arange(count)[None, :]
    ends = jnp.sum(jnp.where(upto, length_row[None, :], 0), axis=1)
    starts = ends - length_row
    segment = jnp.sum((places[:, None] >= ends[None, :]).astype(jnp.int32), axis=1)
    match = segment[:, None] == jnp.arange(length_row.shape[0], dtype=jnp.int32)[None, :]
    begin = jnp.sum(jnp.where(match, starts[None, :], 0), axis=1)
    return (segment, places - begin)


def rows_block(source, block_index, block_rows, head_count, head_width):
    return lax.dynamic_slice_in_dim(source, block_index * block_rows, block_rows, 0).reshape(
        block_rows, head_count, head_width
    )


def pair_mask(query_segment, query_place, key_segment, key_place):
    return (
        (query_segment[:, None] == key_segment[None, :])
        & (key_place[None, :] <= query_place[:, None])
    )[None]


def key_scores(
    query,
    keys_all,
    key_segment,
    key_place,
    query_segment,
    query_place,
    block_index,
    block_rows,
    scale,
):
    row_count, head_count, head_width = query.shape
    key_block = rows_block(keys_all, block_index, block_rows, head_count, head_width)
    scores = (
        jnp.einsum("qhe,khe->hqk", query, key_block, preferred_element_type=jnp.float32) * scale
    )
    segment_block = lax.dynamic_slice_in_dim(key_segment, block_index * block_rows, block_rows, 0)
    place_block = lax.dynamic_slice_in_dim(key_place, block_index * block_rows, block_rows, 0)
    return (scores, pair_mask(query_segment, query_place, segment_block, place_block), key_block)


def attend_forward(
    query,
    keys_all,
    values_all,
    key_segment,
    key_place,
    query_segment,
    query_place,
    first_block,
    last_block,
    block_rows,
    scale,
):
    row_count, head_count, head_width = query.shape

    def find_peak(block_index, carry):
        peak, total = carry
        scores, allowed, _ = key_scores(
            query,
            keys_all,
            key_segment,
            key_place,
            query_segment,
            query_place,
            block_index,
            block_rows,
            scale,
        )
        fresh = jnp.maximum(peak, jnp.max(jnp.where(allowed, scores, NEG_FILL), axis=-1))
        added = jnp.sum(jnp.where(allowed, jnp.exp(scores - fresh[..., None]), 0.0), axis=-1)
        return (fresh, total * jnp.exp(peak - fresh) + added)

    start_carry = (
        jnp.full((head_count, row_count), NEG_FILL, jnp.float32),
        jnp.zeros((head_count, row_count), jnp.float32),
    )
    peak, total = lax.fori_loop(first_block, last_block + 1, find_peak, start_carry)
    log_total = peak + jnp.log(total)

    def weigh(block_index, accum):
        scores, allowed, _ = key_scores(
            query,
            keys_all,
            key_segment,
            key_place,
            query_segment,
            query_place,
            block_index,
            block_rows,
            scale,
        )
        attend_weights = jnp.where(allowed, jnp.exp(scores - log_total[..., None]), 0.0).astype(
            jnp.bfloat16
        )
        values = rows_block(values_all, block_index, block_rows, head_count, head_width)
        return accum + jnp.einsum(
            "hqk,khe->qhe", attend_weights, values, preferred_element_type=jnp.float32
        )

    attended = lax.fori_loop(
        first_block, last_block + 1, weigh, jnp.zeros(query.shape, jnp.float32)
    )
    return (attended, log_total)


def attend_backward(
    query,
    keys_all,
    values_all,
    key_segment,
    key_place,
    query_segment,
    query_place,
    first_block,
    last_block,
    block_rows,
    scale,
    log_total,
    grad_out,
    delta,
):
    row_count, head_count, head_width = query.shape

    def step_back(block_index, carry):
        scores, allowed, key_block = key_scores(
            query,
            keys_all,
            key_segment,
            key_place,
            query_segment,
            query_place,
            block_index,
            block_rows,
            scale,
        )
        values = rows_block(values_all, block_index, block_rows, head_count, head_width)
        attend_weights = jnp.where(allowed, jnp.exp(scores - log_total[..., None]), 0.0)
        grad_weights = jnp.einsum(
            "qhe,khe->hqk", grad_out, values, preferred_element_type=jnp.float32
        )
        grad_scores = (attend_weights * (grad_weights - delta[..., None])).astype(jnp.bfloat16)
        grad_query = (
            carry[0]
            + jnp.einsum("hqk,khe->qhe", grad_scores, key_block, preferred_element_type=jnp.float32)
            * scale
        )
        grad_keys, grad_values = (carry[1], carry[2])
        key_part = (
            jnp.einsum("hqk,qhe->khe", grad_scores, query, preferred_element_type=jnp.float32)
            * scale
        ).reshape(block_rows, head_count * head_width)
        value_part = jnp.einsum(
            "hqk,qhe->khe",
            attend_weights.astype(jnp.bfloat16),
            grad_out,
            preferred_element_type=jnp.float32,
        ).reshape(block_rows, head_count * head_width)
        block_start = block_index * block_rows
        grad_keys = lax.dynamic_update_slice_in_dim(
            grad_keys,
            lax.dynamic_slice_in_dim(grad_keys, block_start, block_rows, 0) + key_part,
            block_start,
            0,
        )
        grad_values = lax.dynamic_update_slice_in_dim(
            grad_values,
            lax.dynamic_slice_in_dim(grad_values, block_start, block_rows, 0) + value_part,
            block_start,
            0,
        )
        return (grad_query, grad_keys, grad_values)

    start_carry = (
        jnp.zeros(query.shape, jnp.float32),
        jnp.zeros(keys_all.shape, jnp.float32),
        jnp.zeros(values_all.shape, jnp.float32),
    )
    return lax.fori_loop(first_block, last_block + 1, step_back, start_carry)


def body(
    tokens,
    cotangent,
    lengths,
    permutation,
    ln_gain,
    ln_bias,
    qkv_weight,
    qkv_bias,
    dense_weight,
    dense_bias,
    fc1_weight,
    fc1_bias,
    fc2_weight,
    fc2_bias,
):
    gain_all, shift_all, w_qkv, b_qkv, w_dense, b_dense, w_fc1, b_fc1, w_fc2, b_fc2 = (
        lax.all_gather(ln_gain, FS, axis=0, tiled=True),
        lax.all_gather(ln_bias, FS, axis=0, tiled=True),
        lax.all_gather(qkv_weight, FS, axis=0, tiled=True),
        lax.all_gather(qkv_bias, FS, axis=2, tiled=True),
        lax.all_gather(dense_weight, FS, axis=1, tiled=True),
        lax.all_gather(dense_bias, FS, axis=0, tiled=True),
        lax.all_gather(fc1_weight, FS, axis=0, tiled=True),
        lax.all_gather(fc1_bias, FS, axis=1, tiled=True),
        lax.all_gather(fc2_weight, FS, axis=1, tiled=True),
        lax.all_gather(fc2_bias, FS, axis=0, tiled=True),
    )
    gain_f = gain_all.astype(jnp.float32)
    shift_f = shift_all.astype(jnp.float32)
    local_width = w_qkv.shape[2]
    head_count = b_qkv.shape[1]
    head_width = b_qkv.shape[2]
    hidden_local = w_fc1.shape[1]
    qkv_shift = b_qkv.astype(jnp.float32).reshape(3, local_width)
    fc1_shift = b_fc1.astype(jnp.float32).reshape(hidden_local)
    micro_count = tokens.shape[0]
    row_count = tokens.shape[1]
    feature_share = tokens.shape[2]
    all_rows = micro_count * row_count
    pack_length = row_count * lax.axis_size(CT)
    block_rows = min(512, pack_length)
    group_index = lax.axis_index((FS, CT))
    pack_index = lax.axis_index(FS)
    context_index = lax.axis_index(CT)
    tensor_index = lax.axis_index(TE)
    out_shift = lax.dynamic_slice_in_dim(
        b_dense.astype(jnp.float32) + b_fc2.astype(jnp.float32),
        tensor_index * feature_share,
        feature_share,
        0,
    )
    scale = head_width ** (-0.5)
    counting = jnp.arange(row_count, dtype=jnp.int32)
    pack_places = jnp.arange(pack_length, dtype=jnp.int32)
    query_place = lax.dynamic_slice_in_dim(pack_places, context_index * row_count, row_count, 0)
    last_query_block = (context_index * row_count + row_count - 1) // block_rows
    sent_tokens = []
    sent_cot = []
    slot_sources = []
    arrive_slots = []
    return_orders = []
    key_segments = []
    query_segments = []
    query_positions = []
    first_blocks = []
    length_rows = []
    for micro_index in range(micro_count):
        perm_row = permutation[micro_index]
        own_targets = lax.dynamic_slice_in_dim(perm_row, group_index * row_count, row_count, 0)
        send_order = jnp.argsort(own_targets // row_count, stable=True)
        return_orders.append(jnp.zeros(row_count, jnp.int32).at[send_order].set(counting))
        here = perm_row // row_count == group_index
        arriving = jnp.argsort(jnp.where(here, 0, 1), stable=True)[:row_count]
        arrive_slot = perm_row[arriving] % row_count
        arrive_slots.append(arrive_slot)
        slot_sources.append(jnp.zeros(row_count, jnp.int32).at[arrive_slot].set(counting))
        sent_tokens.append(tokens[micro_index][send_order])
        sent_cot.append(cotangent[micro_index][send_order])
        length_row = lax.dynamic_index_in_dim(lengths[micro_index], pack_index, 0, keepdims=False)
        length_rows.append(length_row)
        key_segment, key_position = segment_layout(length_row, pack_places)
        key_segments.append(key_segment)
        query_segments.append(
            lax.dynamic_slice_in_dim(key_segment, context_index * row_count, row_count, 0)
        )
        query_position = lax.dynamic_slice_in_dim(
            key_position, context_index * row_count, row_count, 0
        )
        query_positions.append(query_position)
        first_blocks.append((query_place[0] - query_position[0]) // block_rows)
    received = (
        lax.all_to_all(
            jnp.stack(sent_tokens), (FS, CT), split_axis=1, concat_axis=1, tiled=True
        ),
        lax.all_to_all(
            jnp.stack(sent_cot), (FS, CT), split_axis=1, concat_axis=1, tiled=True
        ),
    )
    own_tokens = jnp.concatenate(
        [received[0][m][slot_sources[m]] for m in range(micro_count)], axis=0
    )
    own_cot = jnp.concatenate([received[1][m][slot_sources[m]] for m in range(micro_count)], axis=0)
    full_tokens, full_cot = (
        lax.all_gather(own_tokens, TE, axis=1, tiled=True),
        lax.all_gather(own_cot, TE, axis=1, tiled=True),
    )
    normed, norm_back = jax.vjp(layer_norm, full_tokens.astype(jnp.float32), gain_f, shift_f)
    normed_b = normed.astype(jnp.bfloat16)
    qkv = jnp.einsum("rd,dce->rce", normed_b, w_qkv, preferred_element_type=jnp.float32) + qkv_shift
    angle_pos = jnp.concatenate(query_positions, axis=0).astype(jnp.float32)
    query_rot, rope_back = jax.vjp(
        lambda inner: rotate(inner, angle_pos), qkv[:, 0].reshape(all_rows, head_count, head_width)
    )
    key_rot = rotate(qkv[:, 1].reshape(all_rows, head_count, head_width), angle_pos)
    query_b = query_rot.astype(jnp.bfloat16)
    key_b = key_rot.reshape(all_rows, local_width).astype(jnp.bfloat16)
    value_b = qkv[:, 2].astype(jnp.bfloat16)
    keys_all, values_all = (
        lax.all_gather(
            key_b.reshape(micro_count, row_count, local_width), CT, axis=1, tiled=True
        ),
        lax.all_gather(
            value_b.reshape(micro_count, row_count, local_width), CT, axis=1, tiled=True
        ),
    )
    attended_list = []
    log_list = []
    for micro_index in range(micro_count):
        rows = slice(micro_index * row_count, (micro_index + 1) * row_count)
        attended_one, log_one = attend_forward(
            query_b[rows],
            keys_all[micro_index],
            values_all[micro_index],
            key_segments[micro_index],
            pack_places,
            query_segments[micro_index],
            query_place,
            first_blocks[micro_index],
            last_query_block,
            block_rows,
            scale,
        )
        attended_list.append(attended_one)
        log_list.append(log_one)
    attended = jnp.concatenate(attended_list, axis=0)
    attended_b = attended.reshape(all_rows, local_width).astype(jnp.bfloat16)
    pre_act = jnp.dot(normed_b, w_fc1, preferred_element_type=jnp.float32) + fc1_shift
    activ, gelu_back = jax.vjp(partial(jax.nn.gelu, approximate=True), pre_act)
    activ_b = activ.astype(jnp.bfloat16)
    partial_out = jnp.dot(attended_b, w_dense, preferred_element_type=jnp.float32) + jnp.dot(
        activ_b, w_fc2, preferred_element_type=jnp.float32
    )
    branch = lax.psum_scatter(
        partial_out.astype(jnp.bfloat16), TE, scatter_dimension=1, tiled=True
    ).astype(jnp.float32)
    layer_rows = (own_tokens.astype(jnp.float32) + branch + out_shift).astype(jnp.bfloat16)
    grad_attended = jnp.einsum(
        "rd,ed->re", full_cot, w_dense, preferred_element_type=jnp.float32
    ).astype(jnp.bfloat16)
    grad_activ = jnp.einsum("rd,hd->rh", full_cot, w_fc2, preferred_element_type=jnp.float32)
    grad_pre = gelu_back(grad_activ)[0].astype(jnp.bfloat16)
    grad_heads = grad_attended.reshape(all_rows, head_count, head_width)
    delta_list = []
    for micro_index in range(micro_count):
        rows = slice(micro_index * row_count, (micro_index + 1) * row_count)
        delta_list.append(
            jnp.einsum(
                "qhe,qhe->hq", grad_heads[rows].astype(jnp.float32), attended_list[micro_index]
            )
        )
    query_grads = []
    key_parts = []
    value_parts = []
    for micro_index in range(micro_count):
        rows = slice(micro_index * row_count, (micro_index + 1) * row_count)
        grad_query_one, grad_keys_one, grad_values_one = attend_backward(
            query_b[rows],
            keys_all[micro_index],
            values_all[micro_index],
            key_segments[micro_index],
            pack_places,
            query_segments[micro_index],
            query_place,
            first_blocks[micro_index],
            last_query_block,
            block_rows,
            scale,
            log_list[micro_index],
            grad_heads[rows],
            delta_list[micro_index],
        )
        query_grads.append(grad_query_one)
        key_parts.append(grad_keys_one)
        value_parts.append(grad_values_one)
    grad_keys, grad_values = (
        lax.psum_scatter(
            jnp.stack(key_parts).astype(jnp.bfloat16), CT, scatter_dimension=1, tiled=True
        ).astype(jnp.float32),
        lax.psum_scatter(
            jnp.stack(value_parts).astype(jnp.bfloat16), CT, scatter_dimension=1, tiled=True
        ).astype(jnp.float32),
    )
    grad_keys = grad_keys.reshape(all_rows, local_width)
    grad_values = grad_values.reshape(all_rows, local_width)
    grad_query = jnp.concatenate(query_grads, axis=0)
    grad_query_pre = rope_back(grad_query)[0].reshape(all_rows, local_width)
    grad_key_pre = rope_back(grad_keys.reshape(all_rows, head_count, head_width))[0].reshape(
        all_rows, local_width
    )
    grad_qkv = jnp.stack([grad_query_pre, grad_key_pre, grad_values], axis=1).astype(jnp.bfloat16)
    grad_normed_part = jnp.einsum(
        "rce,dce->rd", grad_qkv, w_qkv, preferred_element_type=jnp.float32
    ) + jnp.einsum("rh,dh->rd", grad_pre, w_fc1, preferred_element_type=jnp.float32)
    grad_normed = lax.psum(grad_normed_part.astype(jnp.bfloat16), TE).astype(jnp.float32)
    grad_input, grad_gain, grad_shift = norm_back(grad_normed)
    cot_f = full_cot.astype(jnp.float32)
    grad_own = lax.dynamic_slice_in_dim(
        cot_f + grad_input, tensor_index * feature_share, feature_share, 1
    ).astype(jnp.bfloat16)
    cot_total = jnp.sum(cot_f, axis=0)
    part_qkv_w = jnp.einsum("rd,rce->dce", normed_b, grad_qkv, preferred_element_type=jnp.float32)
    part_qkv_b = jnp.sum(grad_qkv.astype(jnp.float32), axis=0).reshape(b_qkv.shape)
    part_dense_w = jnp.einsum("re,rd->ed", attended_b, full_cot, preferred_element_type=jnp.float32)
    part_fc1_w = jnp.einsum("rd,rh->dh", normed_b, grad_pre, preferred_element_type=jnp.float32)
    part_fc1_b = jnp.sum(grad_pre.astype(jnp.float32), axis=0).reshape(b_fc1.shape)
    part_fc2_w = jnp.einsum("rh,rd->hd", activ_b, full_cot, preferred_element_type=jnp.float32)
    back_rows = []
    back_grads = []
    for micro_index in range(micro_count):
        rows = slice(micro_index * row_count, (micro_index + 1) * row_count)
        back_rows.append(layer_rows[rows][arrive_slots[micro_index]])
        back_grads.append(grad_own[rows][arrive_slots[micro_index]])
    returned = (
        lax.all_to_all(
            jnp.stack(back_rows), (FS, CT), split_axis=1, concat_axis=1, tiled=True
        ),
        lax.all_to_all(
            jnp.stack(back_grads), (FS, CT), split_axis=1, concat_axis=1, tiled=True
        ),
    )
    layer_out = jnp.stack([returned[0][m][return_orders[m]] for m in range(micro_count)])
    grad_tokens = jnp.stack([returned[1][m][return_orders[m]] for m in range(micro_count)])
    shares = (
        lax.psum_scatter(
            grad_gain.astype(jnp.bfloat16), (FS, CT), scatter_dimension=0, tiled=True
        ).astype(jnp.float32),
        lax.psum_scatter(
            grad_shift.astype(jnp.bfloat16), (FS, CT), scatter_dimension=0, tiled=True
        ).astype(jnp.float32),
        lax.psum_scatter(
            part_qkv_w.astype(jnp.bfloat16), (FS, CT), scatter_dimension=0, tiled=True
        ).astype(jnp.float32),
        lax.psum_scatter(
            part_qkv_b.astype(jnp.bfloat16), (FS, CT), scatter_dimension=2, tiled=True
        ).astype(jnp.float32),
        lax.psum_scatter(
            part_dense_w.astype(jnp.bfloat16), (FS, CT), scatter_dimension=1, tiled=True
        ).astype(jnp.float32),
        lax.psum_scatter(
            cot_total.astype(jnp.bfloat16), (FS, CT), scatter_dimension=0, tiled=True
        ).astype(jnp.float32),
        lax.psum_scatter(
            part_fc1_w.astype(jnp.bfloat16), (FS, CT), scatter_dimension=0, tiled=True
        ).astype(jnp.float32),
        lax.psum_scatter(
            part_fc1_b.astype(jnp.bfloat16), (FS, CT), scatter_dimension=1, tiled=True
        ).astype(jnp.float32),
        lax.psum_scatter(
            part_fc2_w.astype(jnp.bfloat16), (FS, CT), scatter_dimension=1, tiled=True
        ).astype(jnp.float32),
        lax.psum_scatter(
            cot_total.astype(jnp.bfloat16), (FS, CT), scatter_dimension=0, tiled=True
        ).astype(jnp.float32),
    )
    reduced = (
        lax.all_gather(shares[0].astype(jnp.bfloat16), CT, axis=0, tiled=True).astype(
            jnp.float32
        ),
        lax.all_gather(shares[1].astype(jnp.bfloat16), CT, axis=0, tiled=True).astype(
            jnp.float32
        ),
        lax.all_gather(shares[2].astype(jnp.bfloat16), CT, axis=0, tiled=True).astype(
            jnp.float32
        ),
        lax.all_gather(shares[3].astype(jnp.bfloat16), CT, axis=2, tiled=True).astype(
            jnp.float32
        ),
        lax.all_gather(shares[4].astype(jnp.bfloat16), CT, axis=1, tiled=True).astype(
            jnp.float32
        ),
        lax.all_gather(shares[5].astype(jnp.bfloat16), CT, axis=0, tiled=True).astype(
            jnp.float32
        ),
        lax.all_gather(shares[6].astype(jnp.bfloat16), CT, axis=0, tiled=True).astype(
            jnp.float32
        ),
        lax.all_gather(shares[7].astype(jnp.bfloat16), CT, axis=1, tiled=True).astype(
            jnp.float32
        ),
        lax.all_gather(shares[8].astype(jnp.bfloat16), CT, axis=1, tiled=True).astype(
            jnp.float32
        ),
        lax.all_gather(shares[9].astype(jnp.bfloat16), CT, axis=0, tiled=True).astype(
            jnp.float32
        ),
    )
    return (
        layer_out,
        grad_tokens,
        reduced[0],
        reduced[1],
        reduced[2],
        reduced[3],
        reduced[4],
        reduced[5],
        reduced[6],
        reduced[7],
        reduced[8],
        reduced[9],
    )


MESH = pl.DeviceIdType.MESH
AXES = ("y", "h", "l", "x", "t")
BLOCK = 256
SPAN = 512


def fits(mesh):
    return (mesh.shape[FS], mesh.shape[CT], mesh.shape[TE]) == (2, 8, 2)


def place():
    return tuple(lax.axis_index(a) for a in AXES)


def greet(peers):
    barrier = pltpu.get_barrier_semaphore()
    total = 0
    for device, there in peers:
        if there is True:
            pl.semaphore_signal(barrier, inc=1, device_id=device, device_id_type=MESH)
            total += 1
        else:

            @pl.when(there)
            def _(device=device):
                pl.semaphore_signal(barrier, inc=1, device_id=device, device_id_type=MESH)

            total = total + there.astype(jnp.int32)
    pl.semaphore_wait(barrier, total)


NN = (((1,), (0,)), ((), ()))
NT = (((1,), (1,)), ((), ()))
TN = (((0,), (0,)), ((), ()))


def dot(a, b, dims=NN):
    return lax.dot_general(a, b, dims, preferred_element_type=jnp.float32)


ROOT = 0.7978845608028654
CUBE = 0.044715
GROUPS = tuple((dy, dx, j) for j in range(4) for dx in (0, 1) for dy in (0, 1))
SMALL_ROWS = 80
SEQUENCES = 4


def spread_kernel(
    own_rows, w_q, w_d, w_1, w_2, small,
    all_rows, q_out, d_out, o_1, o_2, small_out, normed_out, activ_out, pre_out, four_out,
    g_1, g_2, cot_sum, pre_sum,
    v_q, v_d, v_1, v_2, v_s, acc_1, acc_2, rows_v, normed_v, activ_v, pre_v, four_v,
    local_sem, send_sem, recv_sem, in_sem, out_sem,
):
    y, h, l, x, t = place()
    z = 2 * h + l
    rows, half = own_rows.shape[1], own_rows.shape[2]
    other_y, other_x, other_t = {"y": 1 - y}, {"x": 1 - x}, {"t": 1 - t}

    def along(zz):
        return {"h": zz // 2, "l": lax.rem(zz, 2)}

    greet(
        [(other_y, True), (other_x, True), (other_t, True)]
        + [(along(lax.max(z - 1, 0)), z > 0), (along(lax.min(z + 1, 3)), z < 3)]
    )
    units = [(0, 1), (1, 3)]
    numbers = {}

    def number(key):
        return numbers.setdefault(key, len(numbers))

    def group_at(dy, dx, zz):
        yy = 1 - y if dy else y
        xx = 1 - x if dx else x
        return yy * 8 + zz * 2 + xx

    def region(unit, chunk, core):
        m, n = units[unit]
        dy, dx, way, k = chunk
        zz = z - k if way == "up" else z + k
        columns = pl.ds(pl.multiple_of(core * half, half), half)
        if dy is None:
            return all_rows.at[pl.ds(m, n), :, zz, :, columns]
        yy = 1 - y if dy else y
        xx = 1 - x if dx else x
        return all_rows.at[pl.ds(m, n), yy, zz, pl.ds(pl.multiple_of(xx * rows, rows), rows), columns]

    def own(unit):
        m, n = units[unit]
        return own_rows.at[pl.ds(m, n)]

    started = []

    def link(unit, source, target, key, device):
        i = number((unit,) + key)
        return pltpu.make_async_remote_copy(
            src_ref=source, dst_ref=target, send_sem=send_sem.at[i], recv_sem=recv_sem.at[i],
            device_id=device, device_id_type=MESH,
        )

    def send(unit, chunk, key, device):
        source = own(unit) if chunk == (0, 0, "up", 0) else region(unit, chunk, t)
        link(unit, source, region(unit, chunk, t), key, device).start()

    def arrive(unit, chunk, key, core):
        ref = region(unit, chunk, core)
        link(unit, ref, ref, key, other_t).wait_recv()

    def sent(unit, chunk, key):
        ref = region(unit, chunk, t)
        link(unit, ref, ref, key, other_t).wait_send()

    def when(there, what):
        if there is True:
            what()
        else:
            pl.when(there)(what)

    def there_of(way, k):
        return True if k == 0 else (z >= k if way == "up" else z + k <= 3)

    def to_core(unit, chunk):
        key = chunk + ("core",)
        send(unit, chunk, key, other_t)
        started.append((unit, chunk, key, None))

    def onward(unit, chunk, axis):
        dy, dx, way, k = chunk
        key = ((1, dx, way, k) if axis == "y" else (dy, 1, way, k)) + ("link",)
        send(unit, chunk, key, other_y if axis == "y" else other_x)
        started.append((unit, chunk, key, None))

    def up_down(unit, chunk):
        dy, dx, way, k = chunk
        for going in ("up", "down") if k == 0 else (way,):
            can = z < 3 if going == "up" else z > 0
            key = (dy, dx, going, k + 1, "link")
            target = along(lax.min(z + 1, 3) if going == "up" else lax.max(z - 1, 0))
            when(can, lambda: send(unit, chunk, key, target))
            started.append((unit, chunk, key, going))

    def got(unit, chunk):
        arrive(unit, chunk, chunk + ("link",), t)

    steps = [[("up", 0)], [("up", 1), ("down", 1)], [("up", 2), ("down", 2)], [("up", 3), ("down", 3)]]

    def z_step(s):
        for way, k in steps[s]:
            def act(c=(0, 0, way, k)):
                got(1, c)
                if c[3] < 3:
                    up_down(1, c)
                onward(1, c, "x")
                onward(1, c, "y")
                to_core(1, c)
            when(there_of(way, k), act)

    def y_step(s):
        for way, k in steps[s]:
            def act(c=(1, 0, way, k)):
                got(1, c)
                onward(1, c, "x")
                to_core(1, c)
            when(there_of(way, k), act)

    def x_step(s, dy):
        for way, k in steps[s]:
            def act(c=(dy, 1, way, k)):
                got(1, c)
                to_core(1, c)
            when(there_of(way, k), act)

    def first_step(s):
        for way, k in steps[s]:
            def act(c=(None, None, way, k)):
                got(0, c)
                if c[3] < 3:
                    up_down(0, c)
                to_core(0, c)
            when(there_of(way, k), act)

    nearest = [
        [(("up", 0), True)],
        [(("up", 1), z > 0), (("down", 1), z == 0)],
        [(("down", 2), z == 0), (("down", 1), (z == 1) | (z == 2)), (("up", 2), z == 3)],
        [(("down", 3), z == 0), (("down", 2), z == 1), (("up", 2), z == 2), (("up", 3), z == 3)],
    ]

    def z_at(j):
        if j == 0:
            return z
        options = [(0, 1, 2, 3), (1, 0, 2, 3), (2, 1, 3, 0), (3, 2, 1, 0)]
        value = options[3][j]
        for zz in (2, 1, 0):
            value = jnp.where(z == zz, options[zz][j], value)
        return value

    def load(group, slot):
        here = pl.ds(pl.multiple_of(lax.rem(group, 2) * rows, rows), rows)
        return pltpu.make_async_copy(
            all_rows.at[:, group // 8, lax.rem(group // 2, 4), here], rows_v.at[slot], in_sem.at[slot]
        )

    def stores(group, slot):
        there = pl.ds(pl.multiple_of(group * rows, rows), rows)
        pairs = ((normed_v, normed_out), (activ_v, activ_out), (pre_v, pre_out), (four_v, four_out))
        return [
            pltpu.make_async_copy(source.at[slot], target.at[:, there], out_sem.at[slot, n])
            for n, (source, target) in enumerate(pairs)
        ]

    def fetch(i):
        dy, dx, j = GROUPS[i]
        for (way, k), there in nearest[j]:
            def wait(way=way, k=k):
                chunks = [(1, (dy, dx, way, k))]
                if not dy and not dx:
                    chunks.append((0, (None, None, way, k)))
                for u, c in chunks:
                    arrive(u, c, c + ("core",), 1 - t)
            when(there, wait)
        load(group_at(dy, dx, z_at(j)), i % 2).start()

    block = (y * 4 + l * 2 + x, (1 - y) * 4 + l * 2 + x)
    depth = w_1.shape[0]
    wide, narrow = w_1.shape[1] // 8, w_d.shape[0] // 8
    row = pl.ds(pl.multiple_of(y * depth, depth), depth)

    def pieces(b):
        w = pl.ds(pl.multiple_of(b * wide, wide), wide)
        n = pl.ds(pl.multiple_of(b * narrow, narrow), narrow)
        return [
            (small, small_out.at[y]),
            (w_1.at[:, w], o_1.at[row]),
            (w_2.at[w], o_2.at[:, row]),
            (w_q.at[:, :, n], q_out.at[:, row]),
            (w_d.at[n], d_out.at[:, row]),
        ]

    first, corner = (0, 0, "up", 0), (None, None, "up", 0)
    up_down(1, first)
    for u in range(2):
        onward(u, first, "y")
    weights, locals_ = [], []
    for i, (source, target) in enumerate(pieces(block[1])):
        copy = link("w", source, target, (i,), other_y)
        copy.start()
        weights.append(copy)
    for u in range(2):
        onward(u, first, "x")
    to_core(1, first)
    pairs = [(own(u), region(u, first, t)) for u in range(2)] + pieces(block[0])
    for source, target in pairs:
        copy = pltpu.make_async_copy(source, target, local_sem.at[len(locals_)])
        copy.start()
        locals_.append(copy)
    acc_1[...] = jnp.zeros_like(acc_1)
    acc_2[...] = jnp.zeros_like(acc_2)
    cot_sum[...] = jnp.zeros_like(cot_sum)
    pre_sum[...] = jnp.zeros_like(pre_sum)
    got(0, (1, 0, "up", 0))
    onward(0, (1, 0, "up", 0), "x")
    z_step(1)
    for dy in (0, 1):
        got(0, (dy, 1, "up", 0))
    locals_[0].wait()
    up_down(0, corner)
    to_core(0, corner)
    for event in ((y_step, 0), (z_step, 2), (y_step, 1), (x_step, 0, 0), (x_step, 0, 1)):
        event[0](*event[1:])
    for copy in locals_[1:]:
        copy.wait()
    fetch(0)
    for copy in weights:
        copy.wait_recv()
    into = []
    for n, (source, target) in enumerate(
        ((q_out, v_q), (d_out, v_d), (o_1, v_1), (o_2, v_2), (small_out, v_s))
    ):
        copy = pltpu.make_async_copy(source, target, local_sem.at[n])
        copy.start()
        into.append(copy)
    for copy in into:
        copy.wait()
    both = v_s[...].astype(jnp.float32)

    def line(at):
        n = half // 128
        return jnp.concatenate([both[yy, at + r : at + r + 1, :] for yy in range(2) for r in range(n)], axis=1)

    gain, shift = line(0), line(half // 128)
    summed = both[0] + both[1]
    base = 4 * half // 128
    index = lax.broadcasted_iota(jnp.int32, summed.shape, 0)

    def pick(values, at):
        return jnp.sum(jnp.where(index == at, values, 0.0), axis=0, keepdims=True)

    q_shift = [pick(summed, base + c * 8 + block[0]) for c in range(3)]
    f_shift = jnp.concatenate(
        [pick(both[yy], base + 24 + 2 * block[0] + r) for r in range(2) for yy in range(2)], axis=1
    )
    events = {
        0: [(first_step, 1)],
        1: [(z_step, 3)],
        2: [(y_step, 2)],
        3: [(x_step, 1, 0)],
        4: [(x_step, 1, 1)],
        5: [(first_step, 2)],
        7: [(y_step, 3)],
        8: [(x_step, 2, 0), (x_step, 2, 1)],
        10: [(first_step, 3)],
        12: [(x_step, 3, 0)],
        14: [(x_step, 3, 1)],
    }
    count = len(GROUPS)

    def chosen(step):
        value = group_at(*GROUPS[-1][:2], z_at(GROUPS[-1][2]))
        for i in range(count - 1):
            dy, dx, j = GROUPS[i]
            value = jnp.where(step == i, group_at(dy, dx, z_at(j)), value)
        return value

    f32, bf16 = jnp.float32, jnp.bfloat16

    def work(step, carry):
        slot = lax.rem(step, 2)
        for i in range(count - 1):

            @pl.when(step == i)
            def _(i=i):
                for event in events.get(i, []):
                    event[0](*event[1:])
                fetch(i + 1)

        group = chosen(step)
        load(group, slot).wait()

        @pl.when(step >= 2)
        def _():
            for copy in stores(chosen(step - 2), slot):
                copy.wait()

        values = rows_v[slot, 0:2].reshape(2 * rows, -1).astype(f32)
        center = values - jnp.mean(values, axis=1, keepdims=True)
        r = lax.rsqrt(jnp.mean(center * center, axis=1, keepdims=True) + EPSILON)
        normed = (center * r * gain + shift).astype(bf16)
        normed_v[slot] = normed.reshape(2, rows, -1)
        cots = rows_v[slot, 2:4].reshape(2 * rows, -1)
        pre = dot(normed, v_1[...]) + f_shift
        square = pre * pre
        curve = jnp.tanh(ROOT * (pre + CUBE * pre * square))
        activ = (0.5 * pre * (1.0 + curve)).astype(bf16)
        slope = 0.5 * (1.0 + curve) + 0.5 * pre * (1.0 - curve * curve) * (ROOT * (1.0 + 3.0 * CUBE * square))
        grad_pre = (dot(cots, v_2[...], NT) * slope).astype(bf16)
        activ_v[slot] = activ.reshape(2, rows, -1)
        pre_v[slot] = grad_pre.reshape(2, rows, -1)
        for c in range(3):
            at = slice(c * narrow, (c + 1) * narrow)
            four_v[slot, :, :, at] = (dot(normed, v_q[c]) + q_shift[c]).astype(bf16).reshape(2, rows, -1)
        four_v[slot, :, :, 3 * narrow :] = dot(cots, v_d[...], NT).astype(bf16).reshape(2, rows, -1)
        acc_1[...] += dot(normed, grad_pre, TN)
        acc_2[...] += dot(activ, cots, TN)
        cot_sum[...] += jnp.sum(cots.astype(f32), axis=0, keepdims=True)
        pre_sum[...] += jnp.sum(grad_pre.astype(f32), axis=0, keepdims=True)
        for copy in stores(group, slot):
            copy.start()
        return carry

    lax.fori_loop(0, count, work, 0)
    g_1[...] = acc_1[...].astype(bf16)
    g_2[...] = acc_2[...].astype(bf16)
    for i in (count - 2, count - 1):
        dy, dx, j = GROUPS[i]
        for copy in stores(group_at(dy, dx, z_at(j)), i % 2):
            copy.wait()
    for copy in weights:
        copy.wait_send()
    for unit, chunk, key, going in started:
        there = there_of(*chunk[2:])
        if going is not None:
            can = z < 3 if going == "up" else z > 0
            there = can if there is True else can & there
        when(there, lambda: sent(unit, chunk[:2] + first[2:], key))


def spread(own_rows, w_q, w_d, w_1, w_2, small):
    arrays, rows, half = own_rows.shape
    micro = arrays // 2
    total, deep = rows * 16, half * 2
    wide, narrow = w_1.shape[1] // 8, w_d.shape[0] // 8
    bf16, f32 = jnp.bfloat16, jnp.float32
    shape = jax.ShapeDtypeStruct
    weights = [(3, deep, narrow), (narrow, deep), (deep, wide), (wide, deep), (2,) + small.shape]
    outs = [(arrays, 2, 4, 2 * rows, deep)] + weights
    outs += [(micro, total, deep), (micro, total, wide), (micro, total, wide), (micro, total, 4 * narrow)]
    any_, vmem = pl.BlockSpec(memory_space=pl.ANY), pl.BlockSpec(memory_space=pltpu.VMEM)
    sem = pltpu.SemaphoreType.DMA
    return pl.pallas_call(
        spread_kernel,
        out_shape=[shape(s, bf16) for s in outs + [(deep, wide), (wide, deep)]]
        + [shape((1, deep), f32), shape((1, wide), f32)],
        in_specs=[any_] * 6,
        out_specs=[any_] * len(outs) + [vmem] * 4,
        scratch_shapes=[pltpu.VMEM(s, bf16) for s in weights]
        + [pltpu.VMEM((deep, wide), f32), pltpu.VMEM((wide, deep), f32)]
        + [pltpu.VMEM((2, arrays, rows, deep), bf16)]
        + [pltpu.VMEM((2, micro, rows, w), bf16) for w in (deep, wide, wide, 4 * narrow)]
        + [sem((8,)), sem((96,)), sem((96,)), sem((2,)), sem((2, 4))],
        compiler_params=pltpu.CompilerParams(
            collective_id=0, has_side_effects=True, vmem_limit_bytes=56 << 20
        ),
        name="spread",
    )(own_rows, w_q, w_d, w_1, w_2, small)


class Join:
    def __init__(self, parts, outs, local_sem, send_sem, recv_sem, here=()):
        self.here = dict(here)
        self.parts, self.outs = parts, outs
        self.local_sem, self.send_sem, self.recv_sem = local_sem, send_sem, recv_sem
        self.y, self.h, self.l, self.x, self.t = place()
        self.device = {"y": {"y": 1 - self.y}, "l": {"l": 1 - self.l}, "x": {"x": 1 - self.x}}
        self.numbers, self.sends, self.met = {}, [], set()
        self.every = range(len(parts))
        self.first = [p[3] for p in parts]
        self.then = ["l" if p[3] == "x" else "x" for p in parts]

    def half_of(self, i, yy):
        ref, d_axis, _, _ = self.parts[i]
        if d_axis is None:
            return ref
        n = ref.shape[d_axis] // 2
        where = [slice(None)] * len(ref.shape)
        where[d_axis] = pl.ds(pl.multiple_of(yy * n, n), n)
        return ref.at[tuple(where)]

    def spot(self, i, yy, ll, xx):
        ref, _, b_axis, _ = self.parts[i]
        n = ref.shape[b_axis]
        where = [slice(None)] * len(ref.shape)
        where[b_axis] = pl.ds(pl.multiple_of((yy * 4 + ll * 2 + xx) * n, n), n)
        return self.outs[i].at[tuple(where)]

    def own(self, i, yy):
        return self.spot(i, yy, self.l, self.x)

    def beside(self, i, axis, yy):
        l, x = self.l, self.x
        return self.spot(i, yy, 1 - l if axis == "l" else l, 1 - x if axis == "x" else x)

    def copy(self, n, source, target, axis):
        return pltpu.make_async_remote_copy(
            src_ref=source, dst_ref=target, send_sem=self.send_sem.at[n], recv_sem=self.recv_sem.at[n],
            device_id=self.device[axis], device_id_type=MESH,
        )

    def send(self, i, source, target, key, axis):
        n = self.numbers.setdefault((i,) + key, len(self.numbers))
        self.copy(n, source, target, axis).start()
        self.sends.append((n, i, axis))

    def got(self, i, target, key):
        self.copy(self.numbers[(i,) + key], target, target, "y").wait_recv()

    def bring(self):
        for i in self.every:
            if i in self.here:
                continue
            self.send(i, self.half_of(i, 1 - self.y), self.own(i, self.y), ("y",), "y")

    def offer(self, axis):
        for want in (True, False):
            for i in self.every:
                if (self.first[i] == axis) is want:
                    self.send(i, self.half_of(i, self.y), self.own(i, self.y), (0, axis), axis)

    def kept(self, i):
        return pltpu.make_async_copy(self.half_of(i, self.y), self.own(i, self.y), self.local_sem.at[i])

    def kept_here(self, i):
        where = self.local_sem.at[len(self.parts) + i]
        return pltpu.make_async_copy(self.here[i], self.own(i, 1 - self.y), where)

    def keep(self):
        for i in self.every:
            self.kept(i).start()
        for i in self.here:
            self.kept_here(i).start()

    def far(self, side, axis=None):
        yy = 1 - self.y if side else self.y
        for i in self.every:
            if axis not in (None, self.then[i]):
                continue
            a = self.first[i]
            self.got(i, self.beside(i, a, yy), (side, a))
            self.send(i, self.beside(i, a, yy), self.beside(i, a, yy), (side, "far"), self.then[i])

    def brought(self, *axes):
        for n, axis in enumerate(axes):
            for i in self.every:
                ref = self.own(i, 1 - self.y)
                if i not in self.here and i not in self.met:
                    self.met.add(i)
                    self.got(i, ref, ("y",))
                self.send(i, self.here.get(i, ref), ref, (1, axis), axis)

    def end(self):
        for i in self.every:
            for side, yy in ((0, self.y), (1, 1 - self.y)):
                self.got(i, self.beside(i, self.then[i], yy), (side, self.then[i]))
                self.got(i, self.spot(i, yy, 1 - self.l, 1 - self.x), (side, "far"))
        for i in self.every:
            self.kept(i).wait()
        for i in self.here:
            self.kept_here(i).wait()
        for n, i, axis in self.sends:
            self.copy(n, self.own(i, self.y), self.own(i, self.y), axis).wait_send()


def join_sems(count):
    sem = pltpu.SemaphoreType.DMA
    return [sem((2 * count,)), sem((7 * count,)), sem((7 * count,))]


def fold_kernel(
    activ, grad_pre, back, tok_all, g_q, g_d, g_b, b_q, b_d, cot, w_1, w_2, w_q, w_d, gain, out_shift,
    layer_out, grad_out, ln_out, j_q, j_d, j_b, act_v, pre_v, back_v, tok_v, give, core_in, give_n, sum_in, stat_v, stat_in, ln_v, ln_in,
    load_sem, core_send, core_recv, hop_send, hop_recv, small_send, small_recv, *join_sem,
):
    y, h, l, x, t = place()
    rows, share = cot.shape[1], cot.shape[2]
    both = 2 * rows
    device = {"y": {"y": 1 - y}, "l": {"l": 1 - l}, "x": {"x": 1 - x}, "t": {"t": 1 - t}, "h": {"h": 1 - h}}
    narrow = w_d.shape[0]
    loads = []

    def load(source, target):
        copy = pltpu.make_async_copy(source, target, load_sem.at[len(loads)])
        copy.start()
        loads.append(copy)

    def group_rows(dy, dl, dx):
        yy = 1 - y if dy else y
        ll = 1 - l if dl else l
        xx = 1 - x if dx else x
        return pl.ds(pl.multiple_of((yy * 8 + h * 4 + ll * 2 + xx) * rows, rows), rows)

    owners = [(1, 1, 1), (1, 1, 0), (1, 0, 1), (1, 0, 0), (0, 1, 1), (0, 1, 0), (0, 0, 1), (0, 0, 0)]
    arrived = {}
    for o, owner in enumerate(owners):
        start = len(loads)
        for m in range(2):
            there = pl.ds(m * rows, rows)
            load(activ.at[m, group_rows(*owner)], act_v.at[o, there])
            load(back.at[m, group_rows(*owner)], back_v.at[o, there])
            load(grad_pre.at[m, group_rows(*owner)], pre_v.at[o, there])
        arrived[o] = loads[start:]
    start = len(loads)
    for m in range(2):
        load(tok_all.at[m, group_rows(0, 0, 0)], tok_v.at[pl.ds(m * rows, rows)])
    tok_loads = loads[start:]
    greet([(device[a], True) for a in ("t", "x", "y", "l", "h")])
    two, three = pl.ds(0, 2), pl.ds(2, 1)
    parts = [(g_q.at[two], 1, 2, "x"), (g_q.at[three], 1, 2, "l"), (g_d, 1, 0, "l"), (g_b, None, 0, "l")]
    gather = Join(
        parts, (j_q.at[two], j_q.at[three], j_d, j_b), *join_sem, here=enumerate((b_q.at[two], b_q.at[three], b_d))
    )
    gather.bring()
    gather.offer("x")
    gather.offer("l")
    gather.keep()

    def part(a, o, tt):
        columns = pl.ds(pl.multiple_of(tt * share, share), share)
        if a == 0:
            return dot(act_v[o], w_2[:, columns]) + dot(back_v[o, :, 0:narrow], w_d[:, columns])
        total = dot(pre_v[o], w_1[columns, :], NT)
        for c in range(3):
            total += dot(back_v[o, :, (c + 1) * narrow : (c + 2) * narrow], w_q[c, columns, :], NT)
        return total

    core = {}

    def offer(a, o):
        if o in arrived:
            for copy in arrived.pop(o):
                copy.wait()
        i = a * 8 + o
        give[i] = part(a, o, 1 - t).astype(jnp.bfloat16)
        core[i] = pltpu.make_async_remote_copy(
            src_ref=give.at[i], dst_ref=core_in.at[i], send_sem=core_send.at[i], recv_sem=core_recv.at[i],
            device_id=device["t"], device_id_type=MESH,
        )
        core[i].start()

    hops = {0: ("y", "l", "x"), 1: ("y", "x", "l")}
    place_of = {"y": 0, "l": 1, "x": 2}
    slots, passed = {}, {}

    def slot(a, stage, owner):
        return slots.setdefault((a, stage, owner), len(slots))

    def total_of(a, o, stage):
        i = a * 8 + o
        total = part(a, o, t)
        core[i].wait_recv()
        total += core_in[i].astype(jnp.float32)
        for s in range(stage):
            n = slot(a, s, owners[o])
            passed[n].wait_recv()
            total += sum_in[n].astype(jnp.float32)
        return total

    def pass_on(a, o, stage):
        axis = hops[a][stage]
        seen = list(owners[o])
        seen[place_of[axis]] = 0
        n = slot(a, stage, tuple(seen))
        give_n[n] = total_of(a, o, stage).astype(jnp.bfloat16)
        passed[n] = pltpu.make_async_remote_copy(
            src_ref=give_n.at[n], dst_ref=sum_in.at[n], send_sem=hop_send.at[n], recv_sem=hop_recv.at[n],
            device_id=device[axis], device_id_type=MESH,
        )
        passed[n].start()

    queue = [(1, 0), (1, 2), (1, 1), (1, 3), (0, 0), (0, 1), (0, 2), (0, 3)]
    for a, o in queue[:2]:
        offer(a, o)
    for i, (a, o) in enumerate(queue):
        if i + 2 < len(queue):
            offer(*queue[i + 2])
        pass_on(a, o, 0)
    gather.brought("l")
    for a, o in [(1, 4), (1, 6), (1, 5), (1, 7), (0, 4), (0, 5), (0, 6), (0, 7)]:
        offer(a, o)
    pass_on(1, 4, 1)
    pass_on(1, 6, 1)
    gather.brought("x")
    pass_on(1, 5, 2)
    gather.far(0, "x")
    gather.far(0, "l")
    for copy in tok_loads:
        copy.wait()
    mine = pl.ds(pl.multiple_of(t * share, share), share)
    values = tok_v[...].astype(jnp.float32)
    mean = jnp.mean(values, axis=1, keepdims=True)
    spread_of = jnp.mean((values - mean) ** 2, axis=1, keepdims=True)
    r = lax.rsqrt(spread_of + EPSILON)
    token = tok_v[:, mine].astype(jnp.float32)
    hat = (token - mean) * r
    norm_sum = total_of(1, 7, 3)
    scaled = norm_sum * gain[:, mine]
    stat_v[:, 0:128] = jnp.broadcast_to(jnp.sum(scaled, axis=1, keepdims=True), (both, 128))
    stat_v[:, 128:256] = jnp.broadcast_to(jnp.sum(scaled * hat, axis=1, keepdims=True), (both, 128))
    stat = pltpu.make_async_remote_copy(
        src_ref=stat_v, dst_ref=stat_in, send_sem=small_send.at[0], recv_sem=small_recv.at[0],
        device_id=device["t"], device_id_type=MESH,
    )
    stat.start()
    top = lax.broadcasted_iota(jnp.int32, (8, share), 0) == 0
    ln_v[0] = jnp.where(
        top, jnp.sum(norm_sum * hat, axis=0, keepdims=True), jnp.sum(norm_sum, axis=0, keepdims=True)
    )
    smalls = [stat]

    def swap(step, axis):
        copy = pltpu.make_async_remote_copy(
            src_ref=ln_v.at[step], dst_ref=ln_in.at[step], send_sem=small_send.at[step + 1],
            recv_sem=small_recv.at[step + 1], device_id=device[axis], device_id_type=MESH,
        )
        copy.start()
        smalls.append(copy)
        return copy

    first = swap(0, "h")
    pass_on(0, 4, 1)
    gather.far(1)
    pass_on(0, 5, 1)
    first.wait_recv()
    ln_v[1] = ln_v[0] + ln_in[0]
    second = swap(1, "l")
    stat.wait_recv()
    width = 2 * share
    mean_t = (stat_v[:, 0:1] + stat_in[:, 0:1]) / width
    mean_h = (stat_v[:, 128:129] + stat_in[:, 128:129]) / width
    grad = r * (scaled - mean_t - hat * mean_h)
    for m in range(2):
        grad_out[m] = (cot[m].astype(jnp.float32) + grad[m * rows : (m + 1) * rows]).astype(jnp.bfloat16)
    second.wait_recv()
    ln_v[2] = ln_v[1] + ln_in[1]
    third = swap(2, "x")
    pass_on(0, 6, 2)
    third.wait_recv()
    ln_v[3] = ln_v[2] + ln_in[2]
    fourth = swap(3, "y")
    out = token + total_of(0, 7, 3) + out_shift[:, mine]
    for m in range(2):
        layer_out[m] = out[m * rows : (m + 1) * rows].astype(jnp.bfloat16)
    fourth.wait_recv()
    ln_v[4] = ln_v[3] + ln_in[3]
    swap(4, "t").wait_recv()
    ln_out[...] = jnp.where(t == y, ln_v[4], ln_in[4])
    for copy in core.values():
        copy.wait_send()
    for copy in passed.values():
        copy.wait_send()
    for copy in smalls:
        copy.wait_send()
    gather.end()


def fold(activ, grad_pre, back, tok_all, g_q, g_d, g_b, b_q, b_d, cot, w_1, w_2, w_q, w_d, gain, out_shift):
    micro, rows, share = cot.shape
    both = micro * rows
    narrow = w_d.shape[0]
    held = lambda n, w: pltpu.VMEM((n, both, w), jnp.bfloat16)
    sem = pltpu.SemaphoreType.DMA
    any_, vmem = pl.BlockSpec(memory_space=pl.ANY), pl.BlockSpec(memory_space=pltpu.VMEM)
    return pl.pallas_call(
        fold_kernel,
        out_shape=[
            jax.ShapeDtypeStruct(cot.shape, cot.dtype),
            jax.ShapeDtypeStruct(cot.shape, cot.dtype),
            jax.ShapeDtypeStruct((8, share), jnp.float32),
            jax.ShapeDtypeStruct((3, share, share), g_q.dtype),
            jax.ShapeDtypeStruct((share, share), g_d.dtype),
            jax.ShapeDtypeStruct((64, g_b.shape[1]), g_b.dtype),
        ],
        in_specs=[any_] * 9 + [vmem] * 7,
        out_specs=[vmem] * 3 + [any_] * 3,
        scratch_shapes=[
            held(8, w_1.shape[1]),
            held(8, w_1.shape[1]),
            held(8, 4 * narrow),
            pltpu.VMEM((both, 2 * share), jnp.bfloat16),
            held(16, share),
            held(16, share),
            held(14, share),
            held(14, share),
            pltpu.VMEM((both, 256), jnp.float32),
            pltpu.VMEM((both, 256), jnp.float32),
            pltpu.VMEM((5, 8, share), jnp.float32),
            pltpu.VMEM((5, 8, share), jnp.float32),
            sem((50,)),
            sem((16,)),
            sem((16,)),
            sem((14,)),
            sem((14,)),
            sem((6,)),
            sem((6,)),
        ]
        + join_sems(4),
        compiler_params=pltpu.CompilerParams(
            collective_id=3, has_side_effects=True, vmem_limit_bytes=60 << 20
        ),
        name="fold",
    )(activ, grad_pre, back, tok_all, g_q, g_d, g_b, b_q, b_d, cot, w_1, w_2, w_q, w_d, gain, out_shift)


def swap_rotary(values):
    lane = lax.rem(lax.broadcasted_iota(jnp.int32, values.shape, 1), 64)
    half = ROT // 2
    width = values.shape[1]
    return jnp.where(
        lane < half, pltpu.roll(values, width - half, 1), pltpu.roll(values, half, 1)
    )


def attend_pack(pack, four, perm, lengths, freq, sign, back_ref, laid, gq, gk, gv, cos_v, sin_v):
    pack_rows, width = laid.shape[0], laid.shape[1] // 4
    bf16, f32 = jnp.bfloat16, jnp.float32
    scale = 64 ** (-0.5)
    lane = lax.broadcasted_iota(jnp.int32, (1, width), 1)
    total = four.shape[1]

    def starts(shape, block):
        row = lax.broadcasted_iota(jnp.int32, shape, 0) + block * BLOCK
        begin, end = jnp.zeros(shape, jnp.int32), 0
        for i in range(SEQUENCES):
            length = lengths(i)
            end = end + length
            begin += jnp.where(row >= end, length, 0)
        return row, begin

    for block in range(pack_rows // BLOCK):
        here = slice(block * BLOCK, (block + 1) * BLOCK)
        target = pack * pack_rows + block * BLOCK + lax.broadcasted_iota(jnp.int32, (BLOCK, total), 0)
        chosen = jnp.where(perm[0] == target, 1.0, 0.0).astype(bf16)
        got = dot(chosen, four[0])
        row, begin = starts((BLOCK, width), block)
        angle = (row - begin).astype(f32) * freq[...]
        cos, sin = jnp.cos(angle), jnp.sin(angle) * sign[...]
        cos_v[here, :] = cos
        sin_v[here, :] = sin
        for c in range(2):
            at = slice(c * width, (c + 1) * width)
            part = got[:, at]
            laid[here, at] = (part * cos + swap_rotary(part) * sin).astype(bf16)
        laid[here, 2 * width :] = got[:, 2 * width :].astype(bf16)
    gk[...] = jnp.zeros_like(gk)
    gv[...] = jnp.zeros_like(gv)
    for block in range(pack_rows // BLOCK):
        low = max(0, block * BLOCK - SPAN)
        high = (block + 1) * BLOCK
        here = slice(block * BLOCK, high)
        keys = laid[low:high, width : 2 * width]
        values = laid[low:high, 2 * width : 3 * width]
        row, begin = starts((BLOCK, high - low), block)
        column = lax.broadcasted_iota(jnp.int32, (BLOCK, high - low), 1) + low
        allowed = (column >= begin) & (column <= row)
        attended = None
        for head in range(2):
            mine = (lane // 64) == head
            query = jnp.where(mine, laid[here, 0:width], 0)
            grad = jnp.where(mine, laid[here, 3 * width : 4 * width], 0)
            key = jnp.where(mine, keys, 0)
            value = jnp.where(mine, values, 0)
            scores = jnp.where(allowed, dot(query, key, NT) * scale, NEG_FILL)
            peak = jnp.max(scores, axis=1, keepdims=True)
            weights = jnp.exp(scores - peak)
            weights = weights * (1.0 / jnp.sum(weights, axis=1, keepdims=True))
            weights_b = weights.astype(bf16)
            out = dot(weights_b, value)
            attended = out if attended is None else attended + out
            delta = jnp.sum(grad.astype(f32) * out, axis=1, keepdims=True)
            inner = dot(grad, value, NT)
            grad_scores = (weights * (inner - delta)).astype(bf16)
            part = dot(grad_scores, key)
            if head == 0:
                gq[here, :] = part
            else:
                gq[here, :] += part
            gk[low:high, :] += dot(grad_scores, query, TN)
            gv[low:high, :] += dot(weights_b, grad, TN)
        back_ref[here, 0:width] = attended.astype(bf16)
    for c, ref in ((1, gq), (2, gk)):
        grads = ref[...] * scale
        turned = grads * cos_v[...] - swap_rotary(grads) * sin_v[...]
        back_ref[:, c * width : (c + 1) * width] = turned.astype(bf16)
    back_ref[:, 3 * width :] = gv[...].astype(bf16)


def heads_kernel(
    packs, all_packs, lengths, four, perm, freq, sign, normed, cot, g_1, g_2,
    back_out, g_d, g_q, qkv_sum, j_1, j_2, b_q, b_d,
    held, laid, gq, gk, gv, cos_v, sin_v, acc_d, acc_q, bring_send, bring_recv, *join_sem,
):
    step = pl.program_id(0)
    last = pl.num_programs(0) - 1
    gather = Join([(g_1, 0, 1, "x"), (g_2, 1, 0, "l")], (j_1, j_2), *join_sem)
    f32, bf16 = jnp.float32, jnp.bfloat16

    @pl.when(step == 0)
    def _():
        greet([(d, True) for d in gather.device.values()])
        gather.bring()
        gather.offer("x")
        gather.offer("l")
        gather.keep()
        acc_d[...] = jnp.zeros_like(acc_d)
        acc_q[...] = jnp.zeros_like(acc_q)
        qkv_sum[...] = jnp.zeros_like(qkv_sum)

    @pl.when(step == all_packs - 1)
    def _():
        gather.far(0)

    @pl.when(step == all_packs)
    def _():
        gather.brought("x", "l")

    @pl.when(step < all_packs)
    def _():
        attend_pack(
            lax.rem(step, packs), four, perm, lambda i: lengths[step, i], freq, sign,
            held.at[step], laid, gq, gk, gv, cos_v, sin_v,
        )

    @pl.when(step >= all_packs)
    def _():
        size, total = normed.shape[1], four.shape[1]
        narrow = acc_d.shape[0]
        per = total // size
        pack_rows = held.shape[1]
        first = (step - all_packs) // per * packs
        at = pl.ds(pl.multiple_of(lax.rem(step - all_packs, per) * size, size), size)
        line = perm[0, :, at]
        row = lax.broadcasted_iota(jnp.int32, (pack_rows, size), 0)
        back = None
        for k in range(packs):
            chosen = jnp.where(line == row + k * pack_rows, 1.0, 0.0).astype(bf16)
            part = dot(chosen, held[first + k], TN)
            back = part if back is None else back + part
        back = back.astype(bf16)
        back_out[0] = back
        grads = back[:, narrow:]
        acc_d[...] += dot(back[:, :narrow], cot[0], TN)
        acc_q[...] += dot(normed[0], grads, TN)
        qkv_sum[...] += jnp.sum(grads.astype(f32), axis=0, keepdims=True)

    @pl.when(step == last)
    def _():
        narrow = acc_d.shape[0]
        g_d[...] = acc_d[...].astype(bf16)
        for c in range(3):
            g_q[c] = acc_q[:, c * narrow : (c + 1) * narrow].astype(bf16)
        half = acc_q.shape[0] // 2
        other = pl.ds(pl.multiple_of((1 - gather.y) * half, half), half)
        copies = []
        for i, (source, target) in enumerate(((g_q.at[:, other], b_q), (g_d.at[:, other], b_d))):
            copy = pltpu.make_async_remote_copy(
                src_ref=source, dst_ref=target, send_sem=bring_send.at[i], recv_sem=bring_recv.at[i],
                device_id=gather.device["y"], device_id_type=MESH,
            )
            copy.start()
            copies.append(copy)
        gather.far(1)
        gather.end()
        for copy in copies:
            copy.wait()


def heads(lengths, four, permutation, normed, all_rows, g_1, g_2, packs, size):
    micro, total, wide = four.shape
    pack_rows = total // packs
    width = wide // 4
    deep = normed.shape[2]
    all_packs = micro * packs
    per = total // size
    lane = jnp.arange(width, dtype=jnp.int32) % 64
    power = ROPE_BASE ** (-2.0 * (lane % (ROT // 2)).astype(jnp.float32) / ROT)
    freq = jnp.where(lane < ROT, power, 0.0)[None, :]
    sign = jnp.where(lane < ROT // 2, -1.0, 1.0)[None, :]

    def by_micro(*s, after=False):
        def index(i):
            if after:
                i = jnp.where(i < all_packs, i // packs, (i - all_packs) // per)
            else:
                i = jnp.minimum(i, all_packs - 1) // packs
            return (i, 0, 0)

        return pl.BlockSpec((1,) + s, index)

    def block(w, skip=0):
        def index(i):
            n = jnp.maximum(i - all_packs, 0)
            return (n // per + skip, lax.rem(n, per), 0)

        return pl.BlockSpec((1, size, w), index)

    def fixed(*s):
        return pl.BlockSpec(s, lambda i: (0,) * len(s))

    any_ = pl.BlockSpec(memory_space=pl.ANY)
    plane = pltpu.VMEM((pack_rows, width), jnp.float32)
    return pl.pallas_call(
        partial(heads_kernel, packs, all_packs),
        grid=(all_packs + micro * per,),
        out_shape=[
            jax.ShapeDtypeStruct(four.shape, jnp.bfloat16),
            jax.ShapeDtypeStruct((width, deep), jnp.bfloat16),
            jax.ShapeDtypeStruct((3, deep, width), jnp.bfloat16),
            jax.ShapeDtypeStruct((1, 3 * width), jnp.float32),
            jax.ShapeDtypeStruct((deep // 2, g_1.shape[1] * 8), g_1.dtype),
            jax.ShapeDtypeStruct((g_2.shape[0] * 8, deep // 2), g_2.dtype),
            jax.ShapeDtypeStruct((3, deep // 2, width), jnp.bfloat16),
            jax.ShapeDtypeStruct((width, deep // 2), jnp.bfloat16),
        ],
        in_specs=[
            pl.BlockSpec(memory_space=pltpu.SMEM),
            by_micro(total, wide),
            by_micro(1, total, after=True),
            fixed(1, width),
            fixed(1, width),
            block(deep),
            block(deep, micro),
            any_,
            any_,
        ],
        out_specs=[
            block(wide), fixed(width, deep), fixed(3, deep, width), fixed(1, 3 * width),
            any_, any_, any_, any_,
        ],
        scratch_shapes=[
            pltpu.VMEM((all_packs, pack_rows, wide), jnp.bfloat16),
            pltpu.VMEM((pack_rows, wide), jnp.bfloat16),
        ]
        + [plane] * 5
        + [pltpu.VMEM((width, deep), jnp.float32), pltpu.VMEM((deep, 3 * width), jnp.float32)]
        + [pltpu.SemaphoreType.DMA((2,))] * 2
        + join_sems(2),
        compiler_params=pltpu.CompilerParams(
            collective_id=1, has_side_effects=True, vmem_limit_bytes=56 << 20
        ),
        name="heads",
    )(
        lengths.reshape(all_packs, -1), four, permutation[:, None, :], freq, sign, normed, all_rows, g_1, g_2,
    )


def widen_kernel(*refs):
    half = len(refs) // 2
    for source, target in zip(refs[:half], refs[half:]):
        target[...] = source[...].astype(jnp.float32)


def widen(values, steps):
    def block(value):
        return pl.BlockSpec((value.shape[0] // steps, value.shape[1]), lambda i: (i, 0))

    return pl.pallas_call(
        widen_kernel,
        grid=(steps,),
        out_shape=[jax.ShapeDtypeStruct(v.shape, jnp.float32) for v in values],
        in_specs=[block(v) for v in values],
        out_specs=[block(v) for v in values],
        compiler_params=pltpu.CompilerParams(vmem_limit_bytes=56 << 20),
        name="widen",
    )(*values)


def fast_body(
    tokens, cotangent, lengths, permutation, ln_gain, ln_bias, qkv_weight, qkv_bias,
    dense_weight, dense_bias, fc1_weight, fc1_bias, fc2_weight, fc2_bias,
):
    y, h, l, x, t = place()
    f32 = jnp.float32
    micro, rows, share = tokens.shape
    width = share * 2
    total = rows * 16
    pack_rows = rows * 8
    packs = total // pack_rows
    narrow = dense_weight.shape[0] // 8
    flat = jnp.concatenate([a.reshape(-1, 128) for a in (ln_gain, ln_bias, dense_bias, fc2_bias)])
    turned = qkv_bias.reshape(24, 2, 1, qkv_bias.shape[2])
    at_y = jnp.arange(2)[None, None, :, None] == y
    turned = jnp.where(at_y, turned, jnp.zeros_like(turned)).reshape(24, 128)
    small = jnp.concatenate([flat, turned, fc1_bias])
    small = jnp.pad(small, ((0, SMALL_ROWS - small.shape[0]), (0, 0)))
    own_rows = jnp.concatenate([tokens, cotangent])
    (
        all_rows, w_q, w_d, w_1, w_2, small, normed, activ, grad_pre, four, g_w1, g_w2, cot_sum, pre_sum,
    ) = spread(
        own_rows, qkv_weight.transpose(1, 0, 2), dense_weight, fc1_weight, fc2_weight, small
    )
    all_rows = all_rows.reshape(2 * micro, total, width)
    small = small.reshape(2, -1).astype(f32)
    gain = small[:, 0:share].reshape(1, width)
    out_shift = (small[:, 2 * share : 3 * share] + small[:, 3 * share : 4 * share]).reshape(1, width)

    back, g_wd, g_wq, qkv_sum, j_1, j_2, b_q, b_d = heads(
        lengths, four, permutation, normed, all_rows, g_w1, g_w2, packs, 4 * rows
    )
    g_bias = jnp.pad(jnp.concatenate([qkv_sum, pre_sum], 1), ((0, 7), (0, 0)))
    layer_out, grad_tokens, g_ln, j_q, j_d, j_b = fold(
        activ, grad_pre, back, all_rows, g_wq, g_wd, g_bias, b_q, b_d, cotangent, w_1, w_2, w_q, w_d, gain, out_shift
    )
    g_bias = j_b.reshape(8, 8, -1)[:, 0]
    g_qb = g_bias[:, : 3 * narrow].reshape(8, 3, narrow).transpose(1, 0, 2).reshape(3, -1, 64)
    g_qb = lax.dynamic_slice_in_dim(g_qb, y * qkv_bias.shape[2], qkv_bias.shape[2], 2)
    g_fb = g_bias[:, 3 * narrow :].reshape(fc1_bias.shape[0], -1)
    g_fb = lax.dynamic_slice_in_dim(g_fb, y * fc1_bias.shape[1], fc1_bias.shape[1], 1)
    cot_sum = lax.dynamic_slice_in_dim(cot_sum[0], y * share, share, 0)
    j_1, j_2, j_q, j_d = widen([j_1, j_2, j_q.reshape(3 * share, share), j_d], 16)
    j_q = j_q.reshape(3, share, share)
    return (
        layer_out,
        grad_tokens,
        g_ln[0],
        g_ln[1],
        j_q.transpose(1, 0, 2),
        g_qb,
        j_d,
        cot_sum,
        j_1,
        g_fb,
        j_2,
        cot_sum,
    )


def fast_solution(mesh):
    small_mesh = Mesh(mesh.devices.reshape(2, 2, 2, 2, 2), AXES)
    rows = P(None, ("y", "h", "l", "x"), "t")
    weights = (
        P("y"), P("y"), P("y", None, "t"), P(None, "t", "y"), P("t", "y"), P("y"), P("y", "t"),
        P("t", "y"), P("t", "y"), P("y"),
    )
    return jax.shard_map(
        fast_body,
        mesh=small_mesh,
        in_specs=(rows, rows, P(), P()) + weights,
        out_specs=(rows, rows) + weights,
        check_vma=False,
    )


def solution(mesh):
    if fits(mesh):
        return fast_solution(mesh)
    in_specs = (
        P(None, (FS, CT), TE),
        P(None, (FS, CT), TE),
        P(),
        P(),
        P(FS),
        P(FS),
        P(FS, None, TE),
        P(None, TE, FS),
        P(TE, FS),
        P(FS),
        P(FS, TE),
        P(TE, FS),
        P(TE, FS),
        P(FS),
    )
    out_specs = (
        P(None, (FS, CT), TE),
        P(None, (FS, CT), TE),
        P(FS),
        P(FS),
        P(FS, None, TE),
        P(None, TE, FS),
        P(TE, FS),
        P(FS),
        P(FS, TE),
        P(TE, FS),
        P(TE, FS),
        P(FS),
    )
    return jax.shard_map(body, mesh=mesh, in_specs=in_specs, out_specs=out_specs, check_vma=False)
```

```python
from functools import partial

import jax
import jax.numpy as jnp
from jax import lax
from jax.experimental import pallas as pl
from jax.experimental.pallas import tpu as pltpu
from jax.sharding import Mesh
from jax.sharding import PartitionSpec as P

ROT = 32
FS, CT, TE = "fsdp", "context", "tensor"


EPSILON = 1e-05
ROPE_BASE = 10000.0
NEG_FILL = -1e30


def layer_norm(values, gain, shift):
    center = values - jnp.mean(values, axis=-1, keepdims=True)
    spread = jnp.mean(center * center, axis=-1, keepdims=True)
    return center * lax.rsqrt(spread + EPSILON) * gain + shift


def rotate(values, position):
    half = ROT // 2
    freq = ROPE_BASE ** (-2.0 * jnp.arange(half, dtype=jnp.float32) / ROT)
    angles = position[:, None] * freq[None, :]
    cosine = jnp.cos(angles)[:, None, :]
    sine = jnp.sin(angles)[:, None, :]
    first = values[..., :half]
    second = values[..., half:ROT]
    return jnp.concatenate(
        [first * cosine - second * sine, second * cosine + first * sine, values[..., ROT:]], axis=-1
    )


def segment_layout(length_row, places):
    count = length_row.shape[0]
    upto = jnp.arange(count)[:, None] >= jnp.arange(count)[None, :]
    ends = jnp.sum(jnp.where(upto, length_row[None, :], 0), axis=1)
    starts = ends - length_row
    segment = jnp.sum((places[:, None] >= ends[None, :]).astype(jnp.int32), axis=1)
    match = segment[:, None] == jnp.arange(length_row.shape[0], dtype=jnp.int32)[None, :]
    begin = jnp.sum(jnp.where(match, starts[None, :], 0), axis=1)
    return (segment, places - begin)


def rows_block(source, block_index, block_rows, head_count, head_width):
    return lax.dynamic_slice_in_dim(source, block_index * block_rows, block_rows, 0).reshape(
        block_rows, head_count, head_width
    )


def pair_mask(query_segment, query_place, key_segment, key_place):
    return (
        (query_segment[:, None] == key_segment[None, :])
        & (key_place[None, :] <= query_place[:, None])
    )[None]


def key_scores(
    query,
    keys_all,
    key_segment,
    key_place,
    query_segment,
    query_place,
    block_index,
    block_rows,
    scale,
):
    row_count, head_count, head_width = query.shape
    key_block = rows_block(keys_all, block_index, block_rows, head_count, head_width)
    scores = (
        jnp.einsum("qhe,khe->hqk", query, key_block, preferred_element_type=jnp.float32) * scale
    )
    segment_block = lax.dynamic_slice_in_dim(key_segment, block_index * block_rows, block_rows, 0)
    place_block = lax.dynamic_slice_in_dim(key_place, block_index * block_rows, block_rows, 0)
    return (scores, pair_mask(query_segment, query_place, segment_block, place_block), key_block)


def attend_forward(
    query,
    keys_all,
    values_all,
    key_segment,
    key_place,
    query_segment,
    query_place,
    first_block,
    last_block,
    block_rows,
    scale,
):
    row_count, head_count, head_width = query.shape

    def find_peak(block_index, carry):
        peak, total = carry
        scores, allowed, _ = key_scores(
            query,
            keys_all,
            key_segment,
            key_place,
            query_segment,
            query_place,
            block_index,
            block_rows,
            scale,
        )
        fresh = jnp.maximum(peak, jnp.max(jnp.where(allowed, scores, NEG_FILL), axis=-1))
        added = jnp.sum(jnp.where(allowed, jnp.exp(scores - fresh[..., None]), 0.0), axis=-1)
        return (fresh, total * jnp.exp(peak - fresh) + added)

    start_carry = (
        jnp.full((head_count, row_count), NEG_FILL, jnp.float32),
        jnp.zeros((head_count, row_count), jnp.float32),
    )
    peak, total = lax.fori_loop(first_block, last_block + 1, find_peak, start_carry)
    log_total = peak + jnp.log(total)

    def weigh(block_index, accum):
        scores, allowed, _ = key_scores(
            query,
            keys_all,
            key_segment,
            key_place,
            query_segment,
            query_place,
            block_index,
            block_rows,
            scale,
        )
        attend_weights = jnp.where(allowed, jnp.exp(scores - log_total[..., None]), 0.0).astype(
            jnp.bfloat16
        )
        values = rows_block(values_all, block_index, block_rows, head_count, head_width)
        return accum + jnp.einsum(
            "hqk,khe->qhe", attend_weights, values, preferred_element_type=jnp.float32
        )

    attended = lax.fori_loop(
        first_block, last_block + 1, weigh, jnp.zeros(query.shape, jnp.float32)
    )
    return (attended, log_total)


def attend_backward(
    query,
    keys_all,
    values_all,
    key_segment,
    key_place,
    query_segment,
    query_place,
    first_block,
    last_block,
    block_rows,
    scale,
    log_total,
    grad_out,
    delta,
):
    row_count, head_count, head_width = query.shape

    def step_back(block_index, carry):
        scores, allowed, key_block = key_scores(
            query,
            keys_all,
            key_segment,
            key_place,
            query_segment,
            query_place,
            block_index,
            block_rows,
            scale,
        )
        values = rows_block(values_all, block_index, block_rows, head_count, head_width)
        attend_weights = jnp.where(allowed, jnp.exp(scores - log_total[..., None]), 0.0)
        grad_weights = jnp.einsum(
            "qhe,khe->hqk", grad_out, values, preferred_element_type=jnp.float32
        )
        grad_scores = (attend_weights * (grad_weights - delta[..., None])).astype(jnp.bfloat16)
        grad_query = (
            carry[0]
            + jnp.einsum("hqk,khe->qhe", grad_scores, key_block, preferred_element_type=jnp.float32)
            * scale
        )
        grad_keys, grad_values = (carry[1], carry[2])
        key_part = (
            jnp.einsum("hqk,qhe->khe", grad_scores, query, preferred_element_type=jnp.float32)
            * scale
        ).reshape(block_rows, head_count * head_width)
        value_part = jnp.einsum(
            "hqk,qhe->khe",
            attend_weights.astype(jnp.bfloat16),
            grad_out,
            preferred_element_type=jnp.float32,
        ).reshape(block_rows, head_count * head_width)
        block_start = block_index * block_rows
        grad_keys = lax.dynamic_update_slice_in_dim(
            grad_keys,
            lax.dynamic_slice_in_dim(grad_keys, block_start, block_rows, 0) + key_part,
            block_start,
            0,
        )
        grad_values = lax.dynamic_update_slice_in_dim(
            grad_values,
            lax.dynamic_slice_in_dim(grad_values, block_start, block_rows, 0) + value_part,
            block_start,
            0,
        )
        return (grad_query, grad_keys, grad_values)

    start_carry = (
        jnp.zeros(query.shape, jnp.float32),
        jnp.zeros(keys_all.shape, jnp.float32),
        jnp.zeros(values_all.shape, jnp.float32),
    )
    return lax.fori_loop(first_block, last_block + 1, step_back, start_carry)


def body(
    tokens,
    cotangent,
    lengths,
    permutation,
    ln_gain,
    ln_bias,
    qkv_weight,
    qkv_bias,
    dense_weight,
    dense_bias,
    fc1_weight,
    fc1_bias,
    fc2_weight,
    fc2_bias,
):
    gain_all, shift_all, w_qkv, b_qkv, w_dense, b_dense, w_fc1, b_fc1, w_fc2, b_fc2 = (
        lax.all_gather(ln_gain, FS, axis=0, tiled=True),
        lax.all_gather(ln_bias, FS, axis=0, tiled=True),
        lax.all_gather(qkv_weight, FS, axis=0, tiled=True),
        lax.all_gather(qkv_bias, FS, axis=2, tiled=True),
        lax.all_gather(dense_weight, FS, axis=1, tiled=True),
        lax.all_gather(dense_bias, FS, axis=0, tiled=True),
        lax.all_gather(fc1_weight, FS, axis=0, tiled=True),
        lax.all_gather(fc1_bias, FS, axis=1, tiled=True),
        lax.all_gather(fc2_weight, FS, axis=1, tiled=True),
        lax.all_gather(fc2_bias, FS, axis=0, tiled=True),
    )
    gain_f = gain_all.astype(jnp.float32)
    shift_f = shift_all.astype(jnp.float32)
    local_width = w_qkv.shape[2]
    head_count = b_qkv.shape[1]
    head_width = b_qkv.shape[2]
    hidden_local = w_fc1.shape[1]
    qkv_shift = b_qkv.astype(jnp.float32).reshape(3, local_width)
    fc1_shift = b_fc1.astype(jnp.float32).reshape(hidden_local)
    micro_count = tokens.shape[0]
    row_count = tokens.shape[1]
    feature_share = tokens.shape[2]
    all_rows = micro_count * row_count
    pack_length = row_count * lax.axis_size(CT)
    block_rows = min(512, pack_length)
    group_index = lax.axis_index((FS, CT))
    pack_index = lax.axis_index(FS)
    context_index = lax.axis_index(CT)
    tensor_index = lax.axis_index(TE)
    out_shift = lax.dynamic_slice_in_dim(
        b_dense.astype(jnp.float32) + b_fc2.astype(jnp.float32),
        tensor_index * feature_share,
        feature_share,
        0,
    )
    scale = head_width ** (-0.5)
    counting = jnp.arange(row_count, dtype=jnp.int32)
    pack_places = jnp.arange(pack_length, dtype=jnp.int32)
    query_place = lax.dynamic_slice_in_dim(pack_places, context_index * row_count, row_count, 0)
    last_query_block = (context_index * row_count + row_count - 1) // block_rows
    sent_tokens = []
    sent_cot = []
    slot_sources = []
    arrive_slots = []
    return_orders = []
    key_segments = []
    query_segments = []
    query_positions = []
    first_blocks = []
    length_rows = []
    for micro_index in range(micro_count):
        perm_row = permutation[micro_index]
        own_targets = lax.dynamic_slice_in_dim(perm_row, group_index * row_count, row_count, 0)
        send_order = jnp.argsort(own_targets // row_count, stable=True)
        return_orders.append(jnp.zeros(row_count, jnp.int32).at[send_order].set(counting))
        here = perm_row // row_count == group_index
        arriving = jnp.argsort(jnp.where(here, 0, 1), stable=True)[:row_count]
        arrive_slot = perm_row[arriving] % row_count
        arrive_slots.append(arrive_slot)
        slot_sources.append(jnp.zeros(row_count, jnp.int32).at[arrive_slot].set(counting))
        sent_tokens.append(tokens[micro_index][send_order])
        sent_cot.append(cotangent[micro_index][send_order])
        length_row = lax.dynamic_index_in_dim(lengths[micro_index], pack_index, 0, keepdims=False)
        length_rows.append(length_row)
        key_segment, key_position = segment_layout(length_row, pack_places)
        key_segments.append(key_segment)
        query_segments.append(
            lax.dynamic_slice_in_dim(key_segment, context_index * row_count, row_count, 0)
        )
        query_position = lax.dynamic_slice_in_dim(
            key_position, context_index * row_count, row_count, 0
        )
        query_positions.append(query_position)
        first_blocks.append((query_place[0] - query_position[0]) // block_rows)
    received = (
        lax.all_to_all(
            jnp.stack(sent_tokens), (FS, CT), split_axis=1, concat_axis=1, tiled=True
        ),
        lax.all_to_all(
            jnp.stack(sent_cot), (FS, CT), split_axis=1, concat_axis=1, tiled=True
        ),
    )
    own_tokens = jnp.concatenate(
        [received[0][m][slot_sources[m]] for m in range(micro_count)], axis=0
    )
    own_cot = jnp.concatenate([received[1][m][slot_sources[m]] for m in range(micro_count)], axis=0)
    full_tokens, full_cot = (
        lax.all_gather(own_tokens, TE, axis=1, tiled=True),
        lax.all_gather(own_cot, TE, axis=1, tiled=True),
    )
    normed, norm_back = jax.vjp(layer_norm, full_tokens.astype(jnp.float32), gain_f, shift_f)
    normed_b = normed.astype(jnp.bfloat16)
    qkv = jnp.einsum("rd,dce->rce", normed_b, w_qkv, preferred_element_type=jnp.float32) + qkv_shift
    angle_pos = jnp.concatenate(query_positions, axis=0).astype(jnp.float32)
    query_rot, rope_back = jax.vjp(
        lambda inner: rotate(inner, angle_pos), qkv[:, 0].reshape(all_rows, head_count, head_width)
    )
    key_rot = rotate(qkv[:, 1].reshape(all_rows, head_count, head_width), angle_pos)
    query_b = query_rot.astype(jnp.bfloat16)
    key_b = key_rot.reshape(all_rows, local_width).astype(jnp.bfloat16)
    value_b = qkv[:, 2].astype(jnp.bfloat16)
    keys_all, values_all = (
        lax.all_gather(
            key_b.reshape(micro_count, row_count, local_width), CT, axis=1, tiled=True
        ),
        lax.all_gather(
            value_b.reshape(micro_count, row_count, local_width), CT, axis=1, tiled=True
        ),
    )
    attended_list = []
    log_list = []
    for micro_index in range(micro_count):
        rows = slice(micro_index * row_count, (micro_index + 1) * row_count)
        attended_one, log_one = attend_forward(
            query_b[rows],
            keys_all[micro_index],
            values_all[micro_index],
            key_segments[micro_index],
            pack_places,
            query_segments[micro_index],
            query_place,
            first_blocks[micro_index],
            last_query_block,
            block_rows,
            scale,
        )
        attended_list.append(attended_one)
        log_list.append(log_one)
    attended = jnp.concatenate(attended_list, axis=0)
    attended_b = attended.reshape(all_rows, local_width).astype(jnp.bfloat16)
    pre_act = jnp.dot(normed_b, w_fc1, preferred_element_type=jnp.float32) + fc1_shift
    activ, gelu_back = jax.vjp(partial(jax.nn.gelu, approximate=True), pre_act)
    activ_b = activ.astype(jnp.bfloat16)
    partial_out = jnp.dot(attended_b, w_dense, preferred_element_type=jnp.float32) + jnp.dot(
        activ_b, w_fc2, preferred_element_type=jnp.float32
    )
    branch = lax.psum_scatter(
        partial_out.astype(jnp.bfloat16), TE, scatter_dimension=1, tiled=True
    ).astype(jnp.float32)
    layer_rows = (own_tokens.astype(jnp.float32) + branch + out_shift).astype(jnp.bfloat16)
    grad_attended = jnp.einsum(
        "rd,ed->re", full_cot, w_dense, preferred_element_type=jnp.float32
    ).astype(jnp.bfloat16)
    grad_activ = jnp.einsum("rd,hd->rh", full_cot, w_fc2, preferred_element_type=jnp.float32)
    grad_pre = gelu_back(grad_activ)[0].astype(jnp.bfloat16)
    grad_heads = grad_attended.reshape(all_rows, head_count, head_width)
    delta_list = []
    for micro_index in range(micro_count):
        rows = slice(micro_index * row_count, (micro_index + 1) * row_count)
        delta_list.append(
            jnp.einsum(
                "qhe,qhe->hq", grad_heads[rows].astype(jnp.float32), attended_list[micro_index]
            )
        )
    query_grads = []
    key_parts = []
    value_parts = []
    for micro_index in range(micro_count):
        rows = slice(micro_index * row_count, (micro_index + 1) * row_count)
        grad_query_one, grad_keys_one, grad_values_one = attend_backward(
            query_b[rows],
            keys_all[micro_index],
            values_all[micro_index],
            key_segments[micro_index],
            pack_places,
            query_segments[micro_index],
            query_place,
            first_blocks[micro_index],
            last_query_block,
            block_rows,
            scale,
            log_list[micro_index],
            grad_heads[rows],
            delta_list[micro_index],
        )
        query_grads.append(grad_query_one)
        key_parts.append(grad_keys_one)
        value_parts.append(grad_values_one)
    grad_keys, grad_values = (
        lax.psum_scatter(
            jnp.stack(key_parts).astype(jnp.bfloat16), CT, scatter_dimension=1, tiled=True
        ).astype(jnp.float32),
        lax.psum_scatter(
            jnp.stack(value_parts).astype(jnp.bfloat16), CT, scatter_dimension=1, tiled=True
        ).astype(jnp.float32),
    )
    grad_keys = grad_keys.reshape(all_rows, local_width)
    grad_values = grad_values.reshape(all_rows, local_width)
    grad_query = jnp.concatenate(query_grads, axis=0)
    grad_query_pre = rope_back(grad_query)[0].reshape(all_rows, local_width)
    grad_key_pre = rope_back(grad_keys.reshape(all_rows, head_count, head_width))[0].reshape(
        all_rows, local_width
    )
    grad_qkv = jnp.stack([grad_query_pre, grad_key_pre, grad_values], axis=1).astype(jnp.bfloat16)
    grad_normed_part = jnp.einsum(
        "rce,dce->rd", grad_qkv, w_qkv, preferred_element_type=jnp.float32
    ) + jnp.einsum("rh,dh->rd", grad_pre, w_fc1, preferred_element_type=jnp.float32)
    grad_normed = lax.psum(grad_normed_part.astype(jnp.bfloat16), TE).astype(jnp.float32)
    grad_input, grad_gain, grad_shift = norm_back(grad_normed)
    cot_f = full_cot.astype(jnp.float32)
    grad_own = lax.dynamic_slice_in_dim(
        cot_f + grad_input, tensor_index * feature_share, feature_share, 1
    ).astype(jnp.bfloat16)
    cot_total = jnp.sum(cot_f, axis=0)
    part_qkv_w = jnp.einsum("rd,rce->dce", normed_b, grad_qkv, preferred_element_type=jnp.float32)
    part_qkv_b = jnp.sum(grad_qkv.astype(jnp.float32), axis=0).reshape(b_qkv.shape)
    part_dense_w = jnp.einsum("re,rd->ed", attended_b, full_cot, preferred_element_type=jnp.float32)
    part_fc1_w = jnp.einsum("rd,rh->dh", normed_b, grad_pre, preferred_element_type=jnp.float32)
    part_fc1_b = jnp.sum(grad_pre.astype(jnp.float32), axis=0).reshape(b_fc1.shape)
    part_fc2_w = jnp.einsum("rh,rd->hd", activ_b, full_cot, preferred_element_type=jnp.float32)
    back_rows = []
    back_grads = []
    for micro_index in range(micro_count):
        rows = slice(micro_index * row_count, (micro_index + 1) * row_count)
        back_rows.append(layer_rows[rows][arrive_slots[micro_index]])
        back_grads.append(grad_own[rows][arrive_slots[micro_index]])
    returned = (
        lax.all_to_all(
            jnp.stack(back_rows), (FS, CT), split_axis=1, concat_axis=1, tiled=True
        ),
        lax.all_to_all(
            jnp.stack(back_grads), (FS, CT), split_axis=1, concat_axis=1, tiled=True
        ),
    )
    layer_out = jnp.stack([returned[0][m][return_orders[m]] for m in range(micro_count)])
    grad_tokens = jnp.stack([returned[1][m][return_orders[m]] for m in range(micro_count)])
    shares = (
        lax.psum_scatter(
            grad_gain.astype(jnp.bfloat16), (FS, CT), scatter_dimension=0, tiled=True
        ).astype(jnp.float32),
        lax.psum_scatter(
            grad_shift.astype(jnp.bfloat16), (FS, CT), scatter_dimension=0, tiled=True
        ).astype(jnp.float32),
        lax.psum_scatter(
            part_qkv_w.astype(jnp.bfloat16), (FS, CT), scatter_dimension=0, tiled=True
        ).astype(jnp.float32),
        lax.psum_scatter(
            part_qkv_b.astype(jnp.bfloat16), (FS, CT), scatter_dimension=2, tiled=True
        ).astype(jnp.float32),
        lax.psum_scatter(
            part_dense_w.astype(jnp.bfloat16), (FS, CT), scatter_dimension=1, tiled=True
        ).astype(jnp.float32),
        lax.psum_scatter(
            cot_total.astype(jnp.bfloat16), (FS, CT), scatter_dimension=0, tiled=True
        ).astype(jnp.float32),
        lax.psum_scatter(
            part_fc1_w.astype(jnp.bfloat16), (FS, CT), scatter_dimension=0, tiled=True
        ).astype(jnp.float32),
        lax.psum_scatter(
            part_fc1_b.astype(jnp.bfloat16), (FS, CT), scatter_dimension=1, tiled=True
        ).astype(jnp.float32),
        lax.psum_scatter(
            part_fc2_w.astype(jnp.bfloat16), (FS, CT), scatter_dimension=1, tiled=True
        ).astype(jnp.float32),
        lax.psum_scatter(
            cot_total.astype(jnp.bfloat16), (FS, CT), scatter_dimension=0, tiled=True
        ).astype(jnp.float32),
    )
    reduced = (
        lax.all_gather(shares[0].astype(jnp.bfloat16), CT, axis=0, tiled=True).astype(
            jnp.float32
        ),
        lax.all_gather(shares[1].astype(jnp.bfloat16), CT, axis=0, tiled=True).astype(
            jnp.float32
        ),
        lax.all_gather(shares[2].astype(jnp.bfloat16), CT, axis=0, tiled=True).astype(
            jnp.float32
        ),
        lax.all_gather(shares[3].astype(jnp.bfloat16), CT, axis=2, tiled=True).astype(
            jnp.float32
        ),
        lax.all_gather(shares[4].astype(jnp.bfloat16), CT, axis=1, tiled=True).astype(
            jnp.float32
        ),
        lax.all_gather(shares[5].astype(jnp.bfloat16), CT, axis=0, tiled=True).astype(
            jnp.float32
        ),
        lax.all_gather(shares[6].astype(jnp.bfloat16), CT, axis=0, tiled=True).astype(
            jnp.float32
        ),
        lax.all_gather(shares[7].astype(jnp.bfloat16), CT, axis=1, tiled=True).astype(
            jnp.float32
        ),
        lax.all_gather(shares[8].astype(jnp.bfloat16), CT, axis=1, tiled=True).astype(
            jnp.float32
        ),
        lax.all_gather(shares[9].astype(jnp.bfloat16), CT, axis=0, tiled=True).astype(
            jnp.float32
        ),
    )
    return (
        layer_out,
        grad_tokens,
        reduced[0],
        reduced[1],
        reduced[2],
        reduced[3],
        reduced[4],
        reduced[5],
        reduced[6],
        reduced[7],
        reduced[8],
        reduced[9],
    )


MESH = pl.DeviceIdType.MESH
AXES = ("y", "h", "l", "x", "t")
BLOCK = 256
SPAN = 512


def fits(mesh):
    return (mesh.shape[FS], mesh.shape[CT], mesh.shape[TE]) == (2, 8, 2)


def place():
    return tuple(lax.axis_index(a) for a in AXES)


def greet(peers):
    barrier = pltpu.get_barrier_semaphore()
    total = 0
    for device, there in peers:
        if there is True:
            pl.semaphore_signal(barrier, inc=1, device_id=device, device_id_type=MESH)
            total += 1
        else:

            @pl.when(there)
            def _(device=device):
                pl.semaphore_signal(barrier, inc=1, device_id=device, device_id_type=MESH)

            total = total + there.astype(jnp.int32)
    pl.semaphore_wait(barrier, total)


NN = (((1,), (0,)), ((), ()))
NT = (((1,), (1,)), ((), ()))
TN = (((0,), (0,)), ((), ()))


def dot(a, b, dims=NN):
    return lax.dot_general(a, b, dims, preferred_element_type=jnp.float32)


ROOT = 0.7978845608028654
CUBE = 0.044715
GROUPS = tuple((dy, dx, j) for j in range(4) for dx in (0, 1) for dy in (0, 1))
SMALL_ROWS = 80
SEQUENCES = 4


def spread_kernel(
    own_rows, w_q, w_d, w_1, w_2, small,
    all_rows, q_out, d_out, o_1, o_2, small_out, normed_out, activ_out, pre_out, four_out,
    g_1, g_2, cot_sum, pre_sum,
    v_q, v_d, v_1, v_2, v_s, acc_1, acc_2, rows_v, normed_v, activ_v, pre_v, four_v,
    local_sem, send_sem, recv_sem, in_sem, out_sem,
):
    y, h, l, x, t = place()
    z = 2 * h + l
    rows, half = own_rows.shape[1], own_rows.shape[2]
    other_y, other_x, other_t = {"y": 1 - y}, {"x": 1 - x}, {"t": 1 - t}

    def along(zz):
        return {"h": zz // 2, "l": lax.rem(zz, 2)}

    greet(
        [(other_y, True), (other_x, True), (other_t, True)]
        + [(along(lax.max(z - 1, 0)), z > 0), (along(lax.min(z + 1, 3)), z < 3)]
    )
    units = [(0, 1), (1, 3)]
    numbers = {}

    def number(key):
        return numbers.setdefault(key, len(numbers))

    def group_at(dy, dx, zz):
        yy = 1 - y if dy else y
        xx = 1 - x if dx else x
        return yy * 8 + zz * 2 + xx

    def region(unit, chunk, core):
        m, n = units[unit]
        dy, dx, way, k = chunk
        zz = z - k if way == "up" else z + k
        columns = pl.ds(pl.multiple_of(core * half, half), half)
        if dy is None:
            return all_rows.at[pl.ds(m, n), :, zz, :, columns]
        yy = 1 - y if dy else y
        xx = 1 - x if dx else x
        return all_rows.at[pl.ds(m, n), yy, zz, pl.ds(pl.multiple_of(xx * rows, rows), rows), columns]

    def own(unit):
        m, n = units[unit]
        return own_rows.at[pl.ds(m, n)]

    started = []

    def link(unit, source, target, key, device):
        i = number((unit,) + key)
        return pltpu.make_async_remote_copy(
            src_ref=source, dst_ref=target, send_sem=send_sem.at[i], recv_sem=recv_sem.at[i],
            device_id=device, device_id_type=MESH,
        )

    def send(unit, chunk, key, device):
        source = own(unit) if chunk == (0, 0, "up", 0) else region(unit, chunk, t)
        link(unit, source, region(unit, chunk, t), key, device).start()

    def arrive(unit, chunk, key, core):
        ref = region(unit, chunk, core)
        link(unit, ref, ref, key, other_t).wait_recv()

    def sent(unit, chunk, key):
        ref = region(unit, chunk, t)
        link(unit, ref, ref, key, other_t).wait_send()

    def when(there, what):
        if there is True:
            what()
        else:
            pl.when(there)(what)

    def there_of(way, k):
        return True if k == 0 else (z >= k if way == "up" else z + k <= 3)

    def to_core(unit, chunk):
        key = chunk + ("core",)
        send(unit, chunk, key, other_t)
        started.append((unit, chunk, key, None))

    def onward(unit, chunk, axis):
        dy, dx, way, k = chunk
        key = ((1, dx, way, k) if axis == "y" else (dy, 1, way, k)) + ("link",)
        send(unit, chunk, key, other_y if axis == "y" else other_x)
        started.append((unit, chunk, key, None))

    def up_down(unit, chunk):
        dy, dx, way, k = chunk
        for going in ("up", "down") if k == 0 else (way,):
            can = z < 3 if going == "up" else z > 0
            key = (dy, dx, going, k + 1, "link")
            target = along(lax.min(z + 1, 3) if going == "up" else lax.max(z - 1, 0))
            when(can, lambda: send(unit, chunk, key, target))
            started.append((unit, chunk, key, going))

    def got(unit, chunk):
        arrive(unit, chunk, chunk + ("link",), t)

    steps = [[("up", 0)], [("up", 1), ("down", 1)], [("up", 2), ("down", 2)], [("up", 3), ("down", 3)]]

    def z_step(s):
        for way, k in steps[s]:
            def act(c=(0, 0, way, k)):
                got(1, c)
                if c[3] < 3:
                    up_down(1, c)
                onward(1, c, "x")
                onward(1, c, "y")
                to_core(1, c)
            when(there_of(way, k), act)

    def y_step(s):
        for way, k in steps[s]:
            def act(c=(1, 0, way, k)):
                got(1, c)
                onward(1, c, "x")
                to_core(1, c)
            when(there_of(way, k), act)

    def x_step(s, dy):
        for way, k in steps[s]:
            def act(c=(dy, 1, way, k)):
                got(1, c)
                to_core(1, c)
            when(there_of(way, k), act)

    def first_step(s):
        for way, k in steps[s]:
            def act(c=(None, None, way, k)):
                got(0, c)
                if c[3] < 3:
                    up_down(0, c)
                to_core(0, c)
            when(there_of(way, k), act)

    nearest = [
        [(("up", 0), True)],
        [(("up", 1), z > 0), (("down", 1), z == 0)],
        [(("down", 2), z == 0), (("down", 1), (z == 1) | (z == 2)), (("up", 2), z == 3)],
        [(("down", 3), z == 0), (("down", 2), z == 1), (("up", 2), z == 2), (("up", 3), z == 3)],
    ]

    def z_at(j):
        if j == 0:
            return z
        options = [(0, 1, 2, 3), (1, 0, 2, 3), (2, 1, 3, 0), (3, 2, 1, 0)]
        value = options[3][j]
        for zz in (2, 1, 0):
            value = jnp.where(z == zz, options[zz][j], value)
        return value

    def load(group, slot):
        here = pl.ds(pl.multiple_of(lax.rem(group, 2) * rows, rows), rows)
        return pltpu.make_async_copy(
            all_rows.at[:, group // 8, lax.rem(group // 2, 4), here], rows_v.at[slot], in_sem.at[slot]
        )

    def stores(group, slot):
        there = pl.ds(pl.multiple_of(group * rows, rows), rows)
        pairs = ((normed_v, normed_out), (activ_v, activ_out), (pre_v, pre_out), (four_v, four_out))
        return [
            pltpu.make_async_copy(source.at[slot], target.at[:, there], out_sem.at[slot, n])
            for n, (source, target) in enumerate(pairs)
        ]

    def fetch(i):
        dy, dx, j = GROUPS[i]
        for (way, k), there in nearest[j]:
            def wait(way=way, k=k):
                chunks = [(1, (dy, dx, way, k))]
                if not dy and not dx:
                    chunks.append((0, (None, None, way, k)))
                for u, c in chunks:
                    arrive(u, c, c + ("core",), 1 - t)
            when(there, wait)
        load(group_at(dy, dx, z_at(j)), i % 2).start()

    block = (y * 4 + l * 2 + x, (1 - y) * 4 + l * 2 + x)
    depth = w_1.shape[0]
    wide, narrow = w_1.shape[1] // 8, w_d.shape[0] // 8
    row = pl.ds(pl.multiple_of(y * depth, depth), depth)

    def pieces(b):
        w = pl.ds(pl.multiple_of(b * wide, wide), wide)
        n = pl.ds(pl.multiple_of(b * narrow, narrow), narrow)
        return [
            (small, small_out.at[y]),
            (w_1.at[:, w], o_1.at[row]),
            (w_2.at[w], o_2.at[:, row]),
            (w_q.at[:, :, n], q_out.at[:, row]),
            (w_d.at[n], d_out.at[:, row]),
        ]

    first, corner = (0, 0, "up", 0), (None, None, "up", 0)
    up_down(1, first)
    for u in range(2):
        onward(u, first, "y")
    weights, locals_ = [], []
    for i, (source, target) in enumerate(pieces(block[1])):
        copy = link("w", source, target, (i,), other_y)
        copy.start()
        weights.append(copy)
    for u in range(2):
        onward(u, first, "x")
    to_core(1, first)
    pairs = [(own(u), region(u, first, t)) for u in range(2)] + pieces(block[0])
    for source, target in pairs:
        copy = pltpu.make_async_copy(source, target, local_sem.at[len(locals_)])
        copy.start()
        locals_.append(copy)
    acc_1[...] = jnp.zeros_like(acc_1)
    acc_2[...] = jnp.zeros_like(acc_2)
    cot_sum[...] = jnp.zeros_like(cot_sum)
    pre_sum[...] = jnp.zeros_like(pre_sum)
    got(0, (1, 0, "up", 0))
    onward(0, (1, 0, "up", 0), "x")
    z_step(1)
    for dy in (0, 1):
        got(0, (dy, 1, "up", 0))
    locals_[0].wait()
    up_down(0, corner)
    to_core(0, corner)
    for event in ((y_step, 0), (z_step, 2), (y_step, 1), (x_step, 0, 0), (x_step, 0, 1)):
        event[0](*event[1:])
    for copy in locals_[1:]:
        copy.wait()
    fetch(0)
    for copy in weights:
        copy.wait_recv()
    into = []
    for n, (source, target) in enumerate(
        ((q_out, v_q), (d_out, v_d), (o_1, v_1), (o_2, v_2), (small_out, v_s))
    ):
        copy = pltpu.make_async_copy(source, target, local_sem.at[n])
        copy.start()
        into.append(copy)
    for copy in into:
        copy.wait()
    both = v_s[...].astype(jnp.float32)

    def line(at):
        n = half // 128
        return jnp.concatenate([both[yy, at + r : at + r + 1, :] for yy in range(2) for r in range(n)], axis=1)

    gain, shift = line(0), line(half // 128)
    summed = both[0] + both[1]
    base = 4 * half // 128
    index = lax.broadcasted_iota(jnp.int32, summed.shape, 0)

    def pick(values, at):
        return jnp.sum(jnp.where(index == at, values, 0.0), axis=0, keepdims=True)

    q_shift = [pick(summed, base + c * 8 + block[0]) for c in range(3)]
    f_shift = jnp.concatenate(
        [pick(both[yy], base + 24 + 2 * block[0] + r) for r in range(2) for yy in range(2)], axis=1
    )
    events = {
        0: [(first_step, 1)],
        1: [(z_step, 3)],
        2: [(y_step, 2)],
        3: [(x_step, 1, 0)],
        4: [(x_step, 1, 1)],
        5: [(first_step, 2)],
        7: [(y_step, 3)],
        8: [(x_step, 2, 0), (x_step, 2, 1)],
        10: [(first_step, 3)],
        12: [(x_step, 3, 0)],
        14: [(x_step, 3, 1)],
    }
    count = len(GROUPS)

    def chosen(step):
        value = group_at(*GROUPS[-1][:2], z_at(GROUPS[-1][2]))
        for i in range(count - 1):
            dy, dx, j = GROUPS[i]
            value = jnp.where(step == i, group_at(dy, dx, z_at(j)), value)
        return value

    f32, bf16 = jnp.float32, jnp.bfloat16

    def work(step, carry):
        slot = lax.rem(step, 2)
        for i in range(count - 1):

            @pl.when(step == i)
            def _(i=i):
                for event in events.get(i, []):
                    event[0](*event[1:])
                fetch(i + 1)

        group = chosen(step)
        load(group, slot).wait()

        @pl.when(step >= 2)
        def _():
            for copy in stores(chosen(step - 2), slot):
                copy.wait()

        values = rows_v[slot, 0:2].reshape(2 * rows, -1).astype(f32)
        center = values - jnp.mean(values, axis=1, keepdims=True)
        r = lax.rsqrt(jnp.mean(center * center, axis=1, keepdims=True) + EPSILON)
        normed = (center * r * gain + shift).astype(bf16)
        normed_v[slot] = normed.reshape(2, rows, -1)
        cots = rows_v[slot, 2:4].reshape(2 * rows, -1)
        pre = dot(normed, v_1[...]) + f_shift
        square = pre * pre
        curve = jnp.tanh(ROOT * (pre + CUBE * pre * square))
        activ = (0.5 * pre * (1.0 + curve)).astype(bf16)
        slope = 0.5 * (1.0 + curve) + 0.5 * pre * (1.0 - curve * curve) * (ROOT * (1.0 + 3.0 * CUBE * square))
        grad_pre = (dot(cots, v_2[...], NT) * slope).astype(bf16)
        activ_v[slot] = activ.reshape(2, rows, -1)
        pre_v[slot] = grad_pre.reshape(2, rows, -1)
        for c in range(3):
            at = slice(c * narrow, (c + 1) * narrow)
            four_v[slot, :, :, at] = (dot(normed, v_q[c]) + q_shift[c]).astype(bf16).reshape(2, rows, -1)
        four_v[slot, :, :, 3 * narrow :] = dot(cots, v_d[...], NT).astype(bf16).reshape(2, rows, -1)
        acc_1[...] += dot(normed, grad_pre, TN)
        acc_2[...] += dot(activ, cots, TN)
        cot_sum[...] += jnp.sum(cots.astype(f32), axis=0, keepdims=True)
        pre_sum[...] += jnp.sum(grad_pre.astype(f32), axis=0, keepdims=True)
        for copy in stores(group, slot):
            copy.start()
        return carry

    lax.fori_loop(0, count, work, 0)
    g_1[...] = acc_1[...].astype(bf16)
    g_2[...] = acc_2[...].astype(bf16)
    for i in (count - 2, count - 1):
        dy, dx, j = GROUPS[i]
        for copy in stores(group_at(dy, dx, z_at(j)), i % 2):
            copy.wait()
    for copy in weights:
        copy.wait_send()
    for unit, chunk, key, going in started:
        there = there_of(*chunk[2:])
        if going is not None:
            can = z < 3 if going == "up" else z > 0
            there = can if there is True else can & there
        when(there, lambda: sent(unit, chunk[:2] + first[2:], key))


def spread(own_rows, w_q, w_d, w_1, w_2, small):
    arrays, rows, half = own_rows.shape
    micro = arrays // 2
    total, deep = rows * 16, half * 2
    wide, narrow = w_1.shape[1] // 8, w_d.shape[0] // 8
    bf16, f32 = jnp.bfloat16, jnp.float32
    shape = jax.ShapeDtypeStruct
    weights = [(3, deep, narrow), (narrow, deep), (deep, wide), (wide, deep), (2,) + small.shape]
    outs = [(arrays, 2, 4, 2 * rows, deep)] + weights
    outs += [(micro, total, deep), (micro, total, wide), (micro, total, wide), (micro, total, 4 * narrow)]
    any_, vmem = pl.BlockSpec(memory_space=pl.ANY), pl.BlockSpec(memory_space=pltpu.VMEM)
    sem = pltpu.SemaphoreType.DMA
    return pl.pallas_call(
        spread_kernel,
        out_shape=[shape(s, bf16) for s in outs + [(deep, wide), (wide, deep)]]
        + [shape((1, deep), f32), shape((1, wide), f32)],
        in_specs=[any_] * 6,
        out_specs=[any_] * len(outs) + [vmem] * 4,
        scratch_shapes=[pltpu.VMEM(s, bf16) for s in weights]
        + [pltpu.VMEM((deep, wide), f32), pltpu.VMEM((wide, deep), f32)]
        + [pltpu.VMEM((2, arrays, rows, deep), bf16)]
        + [pltpu.VMEM((2, micro, rows, w), bf16) for w in (deep, wide, wide, 4 * narrow)]
        + [sem((8,)), sem((96,)), sem((96,)), sem((2,)), sem((2, 4))],
        compiler_params=pltpu.CompilerParams(
            collective_id=0, has_side_effects=True, vmem_limit_bytes=56 << 20
        ),
        name="spread",
    )(own_rows, w_q, w_d, w_1, w_2, small)


class Join:
    def __init__(self, parts, outs, local_sem, send_sem, recv_sem, here=()):
        self.here = dict(here)
        self.parts, self.outs = parts, outs
        self.local_sem, self.send_sem, self.recv_sem = local_sem, send_sem, recv_sem
        self.y, self.h, self.l, self.x, self.t = place()
        self.device = {"y": {"y": 1 - self.y}, "l": {"l": 1 - self.l}, "x": {"x": 1 - self.x}}
        self.numbers, self.sends, self.met = {}, [], set()
        self.every = range(len(parts))
        self.first = [p[3] for p in parts]
        self.then = ["l" if p[3] == "x" else "x" for p in parts]

    def half_of(self, i, yy):
        ref, d_axis, _, _ = self.parts[i]
        if d_axis is None:
            return ref
        n = ref.shape[d_axis] // 2
        where = [slice(None)] * len(ref.shape)
        where[d_axis] = pl.ds(pl.multiple_of(yy * n, n), n)
        return ref.at[tuple(where)]

    def spot(self, i, yy, ll, xx):
        ref, _, b_axis, _ = self.parts[i]
        n = ref.shape[b_axis]
        where = [slice(None)] * len(ref.shape)
        where[b_axis] = pl.ds(pl.multiple_of((yy * 4 + ll * 2 + xx) * n, n), n)
        return self.outs[i].at[tuple(where)]

    def own(self, i, yy):
        return self.spot(i, yy, self.l, self.x)

    def beside(self, i, axis, yy):
        l, x = self.l, self.x
        return self.spot(i, yy, 1 - l if axis == "l" else l, 1 - x if axis == "x" else x)

    def copy(self, n, source, target, axis):
        return pltpu.make_async_remote_copy(
            src_ref=source, dst_ref=target, send_sem=self.send_sem.at[n], recv_sem=self.recv_sem.at[n],
            device_id=self.device[axis], device_id_type=MESH,
        )

    def send(self, i, source, target, key, axis):
        n = self.numbers.setdefault((i,) + key, len(self.numbers))
        self.copy(n, source, target, axis).start()
        self.sends.append((n, i, axis))

    def got(self, i, target, key):
        self.copy(self.numbers[(i,) + key], target, target, "y").wait_recv()

    def bring(self):
        for i in self.every:
            if i in self.here:
                continue
            self.send(i, self.half_of(i, 1 - self.y), self.own(i, self.y), ("y",), "y")

    def offer(self, axis):
        for want in (True, False):
            for i in self.every:
                if (self.first[i] == axis) is want:
                    self.send(i, self.half_of(i, self.y), self.own(i, self.y), (0, axis), axis)

    def kept(self, i):
        return pltpu.make_async_copy(self.half_of(i, self.y), self.own(i, self.y), self.local_sem.at[i])

    def kept_here(self, i):
        where = self.local_sem.at[len(self.parts) + i]
        return pltpu.make_async_copy(self.here[i], self.own(i, 1 - self.y), where)

    def keep(self):
        for i in self.every:
            self.kept(i).start()
        for i in self.here:
            self.kept_here(i).start()

    def far(self, side, axis=None):
        yy = 1 - self.y if side else self.y
        for i in self.every:
            if axis not in (None, self.then[i]):
                continue
            a = self.first[i]
            self.got(i, self.beside(i, a, yy), (side, a))
            self.send(i, self.beside(i, a, yy), self.beside(i, a, yy), (side, "far"), self.then[i])

    def brought(self, *axes):
        for n, axis in enumerate(axes):
            for i in self.every:
                ref = self.own(i, 1 - self.y)
                if i not in self.here and i not in self.met:
                    self.met.add(i)
                    self.got(i, ref, ("y",))
                self.send(i, self.here.get(i, ref), ref, (1, axis), axis)

    def end(self):
        for i in self.every:
            for side, yy in ((0, self.y), (1, 1 - self.y)):
                self.got(i, self.beside(i, self.then[i], yy), (side, self.then[i]))
                self.got(i, self.spot(i, yy, 1 - self.l, 1 - self.x), (side, "far"))
        for i in self.every:
            self.kept(i).wait()
        for i in self.here:
            self.kept_here(i).wait()
        for n, i, axis in self.sends:
            self.copy(n, self.own(i, self.y), self.own(i, self.y), axis).wait_send()


def join_sems(count):
    sem = pltpu.SemaphoreType.DMA
    return [sem((2 * count,)), sem((7 * count,)), sem((7 * count,))]


def fold_kernel(
    activ, grad_pre, back, tok_all, g_q, g_d, g_b, b_q, b_d, cot, w_1, w_2, w_q, w_d, gain, out_shift,
    layer_out, grad_out, ln_out, j_q, j_d, j_b, act_v, pre_v, back_v, tok_v, give, core_in, give_n, sum_in, stat_v, stat_in, ln_v, ln_in,
    load_sem, core_send, core_recv, hop_send, hop_recv, small_send, small_recv, *join_sem,
):
    y, h, l, x, t = place()
    rows, share = cot.shape[1], cot.shape[2]
    both = 2 * rows
    device = {"y": {"y": 1 - y}, "l": {"l": 1 - l}, "x": {"x": 1 - x}, "t": {"t": 1 - t}, "h": {"h": 1 - h}}
    narrow = w_d.shape[0]
    loads = []

    def load(source, target):
        copy = pltpu.make_async_copy(source, target, load_sem.at[len(loads)])
        copy.start()
        loads.append(copy)

    def group_rows(dy, dl, dx):
        yy = 1 - y if dy else y
        ll = 1 - l if dl else l
        xx = 1 - x if dx else x
        return pl.ds(pl.multiple_of((yy * 8 + h * 4 + ll * 2 + xx) * rows, rows), rows)

    owners = [(1, 1, 1), (1, 1, 0), (1, 0, 1), (1, 0, 0), (0, 1, 1), (0, 1, 0), (0, 0, 1), (0, 0, 0)]
    arrived = {}
    for o, owner in enumerate(owners):
        start = len(loads)
        for m in range(2):
            there = pl.ds(m * rows, rows)
            load(activ.at[m, group_rows(*owner)], act_v.at[o, there])
            load(back.at[m, group_rows(*owner)], back_v.at[o, there])
            load(grad_pre.at[m, group_rows(*owner)], pre_v.at[o, there])
        arrived[o] = loads[start:]
    start = len(loads)
    for m in range(2):
        load(tok_all.at[m, group_rows(0, 0, 0)], tok_v.at[pl.ds(m * rows, rows)])
    tok_loads = loads[start:]
    greet([(device[a], True) for a in ("t", "x", "y", "l", "h")])
    two, three = pl.ds(0, 2), pl.ds(2, 1)
    parts = [(g_q.at[two], 1, 2, "x"), (g_q.at[three], 1, 2, "l"), (g_d, 1, 0, "l"), (g_b, None, 0, "l")]
    gather = Join(
        parts, (j_q.at[two], j_q.at[three], j_d, j_b), *join_sem, here=enumerate((b_q.at[two], b_q.at[three], b_d))
    )
    gather.bring()
    gather.offer("x")
    gather.offer("l")
    gather.keep()

    def part(a, o, tt):
        columns = pl.ds(pl.multiple_of(tt * share, share), share)
        if a == 0:
            return dot(act_v[o], w_2[:, columns]) + dot(back_v[o, :, 0:narrow], w_d[:, columns])
        total = dot(pre_v[o], w_1[columns, :], NT)
        for c in range(3):
            total += dot(back_v[o, :, (c + 1) * narrow : (c + 2) * narrow], w_q[c, columns, :], NT)
        return total

    core = {}

    def offer(a, o):
        if o in arrived:
            for copy in arrived.pop(o):
                copy.wait()
        i = a * 8 + o
        give[i] = part(a, o, 1 - t).astype(jnp.bfloat16)
        core[i] = pltpu.make_async_remote_copy(
            src_ref=give.at[i], dst_ref=core_in.at[i], send_sem=core_send.at[i], recv_sem=core_recv.at[i],
            device_id=device["t"], device_id_type=MESH,
        )
        core[i].start()

    hops = {0: ("y", "l", "x"), 1: ("y", "x", "l")}
    place_of = {"y": 0, "l": 1, "x": 2}
    slots, passed = {}, {}

    def slot(a, stage, owner):
        return slots.setdefault((a, stage, owner), len(slots))

    def total_of(a, o, stage):
        i = a * 8 + o
        total = part(a, o, t)
        core[i].wait_recv()
        total += core_in[i].astype(jnp.float32)
        for s in range(stage):
            n = slot(a, s, owners[o])
            passed[n].wait_recv()
            total += sum_in[n].astype(jnp.float32)
        return total

    def pass_on(a, o, stage):
        axis = hops[a][stage]
        seen = list(owners[o])
        seen[place_of[axis]] = 0
        n = slot(a, stage, tuple(seen))
        give_n[n] = total_of(a, o, stage).astype(jnp.bfloat16)
        passed[n] = pltpu.make_async_remote_copy(
            src_ref=give_n.at[n], dst_ref=sum_in.at[n], send_sem=hop_send.at[n], recv_sem=hop_recv.at[n],
            device_id=device[axis], device_id_type=MESH,
        )
        passed[n].start()

    queue = [(1, 0), (1, 2), (1, 1), (1, 3), (0, 0), (0, 1), (0, 2), (0, 3)]
    for a, o in queue[:2]:
        offer(a, o)
    for i, (a, o) in enumerate(queue):
        if i + 2 < len(queue):
            offer(*queue[i + 2])
        pass_on(a, o, 0)
    gather.brought("l")
    for a, o in [(1, 4), (1, 6), (1, 5), (1, 7), (0, 4), (0, 5), (0, 6), (0, 7)]:
        offer(a, o)
    pass_on(1, 4, 1)
    pass_on(1, 6, 1)
    gather.brought("x")
    pass_on(1, 5, 2)
    gather.far(0, "x")
    gather.far(0, "l")
    for copy in tok_loads:
        copy.wait()
    mine = pl.ds(pl.multiple_of(t * share, share), share)
    values = tok_v[...].astype(jnp.float32)
    mean = jnp.mean(values, axis=1, keepdims=True)
    spread_of = jnp.mean((values - mean) ** 2, axis=1, keepdims=True)
    r = lax.rsqrt(spread_of + EPSILON)
    token = tok_v[:, mine].astype(jnp.float32)
    hat = (token - mean) * r
    norm_sum = total_of(1, 7, 3)
    scaled = norm_sum * gain[:, mine]
    stat_v[:, 0:128] = jnp.broadcast_to(jnp.sum(scaled, axis=1, keepdims=True), (both, 128))
    stat_v[:, 128:256] = jnp.broadcast_to(jnp.sum(scaled * hat, axis=1, keepdims=True), (both, 128))
    stat = pltpu.make_async_remote_copy(
        src_ref=stat_v, dst_ref=stat_in, send_sem=small_send.at[0], recv_sem=small_recv.at[0],
        device_id=device["t"], device_id_type=MESH,
    )
    stat.start()
    top = lax.broadcasted_iota(jnp.int32, (8, share), 0) == 0
    ln_v[0] = jnp.where(
        top, jnp.sum(norm_sum * hat, axis=0, keepdims=True), jnp.sum(norm_sum, axis=0, keepdims=True)
    )
    smalls = [stat]

    def swap(step, axis):
        copy = pltpu.make_async_remote_copy(
            src_ref=ln_v.at[step], dst_ref=ln_in.at[step], send_sem=small_send.at[step + 1],
            recv_sem=small_recv.at[step + 1], device_id=device[axis], device_id_type=MESH,
        )
        copy.start()
        smalls.append(copy)
        return copy

    first = swap(0, "h")
    pass_on(0, 4, 1)
    gather.far(1)
    pass_on(0, 5, 1)
    first.wait_recv()
    ln_v[1] = ln_v[0] + ln_in[0]
    second = swap(1, "l")
    stat.wait_recv()
    width = 2 * share
    mean_t = (stat_v[:, 0:1] + stat_in[:, 0:1]) / width
    mean_h = (stat_v[:, 128:129] + stat_in[:, 128:129]) / width
    grad = r * (scaled - mean_t - hat * mean_h)
    for m in range(2):
        grad_out[m] = (cot[m].astype(jnp.float32) + grad[m * rows : (m + 1) * rows]).astype(jnp.bfloat16)
    second.wait_recv()
    ln_v[2] = ln_v[1] + ln_in[1]
    third = swap(2, "x")
    pass_on(0, 6, 2)
    third.wait_recv()
    ln_v[3] = ln_v[2] + ln_in[2]
    fourth = swap(3, "y")
    out = token + total_of(0, 7, 3) + out_shift[:, mine]
    for m in range(2):
        layer_out[m] = out[m * rows : (m + 1) * rows].astype(jnp.bfloat16)
    fourth.wait_recv()
    ln_v[4] = ln_v[3] + ln_in[3]
    swap(4, "t").wait_recv()
    ln_out[...] = jnp.where(t == y, ln_v[4], ln_in[4])
    for copy in core.values():
        copy.wait_send()
    for copy in passed.values():
        copy.wait_send()
    for copy in smalls:
        copy.wait_send()
    gather.end()


def fold(activ, grad_pre, back, tok_all, g_q, g_d, g_b, b_q, b_d, cot, w_1, w_2, w_q, w_d, gain, out_shift):
    micro, rows, share = cot.shape
    both = micro * rows
    narrow = w_d.shape[0]
    held = lambda n, w: pltpu.VMEM((n, both, w), jnp.bfloat16)
    sem = pltpu.SemaphoreType.DMA
    any_, vmem = pl.BlockSpec(memory_space=pl.ANY), pl.BlockSpec(memory_space=pltpu.VMEM)
    return pl.pallas_call(
        fold_kernel,
        out_shape=[
            jax.ShapeDtypeStruct(cot.shape, cot.dtype),
            jax.ShapeDtypeStruct(cot.shape, cot.dtype),
            jax.ShapeDtypeStruct((8, share), jnp.float32),
            jax.ShapeDtypeStruct((3, share, share), g_q.dtype),
            jax.ShapeDtypeStruct((share, share), g_d.dtype),
            jax.ShapeDtypeStruct((64, g_b.shape[1]), g_b.dtype),
        ],
        in_specs=[any_] * 9 + [vmem] * 7,
        out_specs=[vmem] * 3 + [any_] * 3,
        scratch_shapes=[
            held(8, w_1.shape[1]),
            held(8, w_1.shape[1]),
            held(8, 4 * narrow),
            pltpu.VMEM((both, 2 * share), jnp.bfloat16),
            held(16, share),
            held(16, share),
            held(14, share),
            held(14, share),
            pltpu.VMEM((both, 256), jnp.float32),
            pltpu.VMEM((both, 256), jnp.float32),
            pltpu.VMEM((5, 8, share), jnp.float32),
            pltpu.VMEM((5, 8, share), jnp.float32),
            sem((50,)),
            sem((16,)),
            sem((16,)),
            sem((14,)),
            sem((14,)),
            sem((6,)),
            sem((6,)),
        ]
        + join_sems(4),
        compiler_params=pltpu.CompilerParams(
            collective_id=3, has_side_effects=True, vmem_limit_bytes=60 << 20
        ),
        name="fold",
    )(activ, grad_pre, back, tok_all, g_q, g_d, g_b, b_q, b_d, cot, w_1, w_2, w_q, w_d, gain, out_shift)


def swap_rotary(values):
    lane = lax.rem(lax.broadcasted_iota(jnp.int32, values.shape, 1), 64)
    half = ROT // 2
    width = values.shape[1]
    return jnp.where(
        lane < half, pltpu.roll(values, width - half, 1), pltpu.roll(values, half, 1)
    )


def attend_pack(pack, four, perm, lengths, freq, sign, back_ref, laid, gq, gk, gv, cos_v, sin_v):
    pack_rows, width = laid.shape[0], laid.shape[1] // 4
    bf16, f32 = jnp.bfloat16, jnp.float32
    scale = 64 ** (-0.5)
    lane = lax.broadcasted_iota(jnp.int32, (1, width), 1)
    total = four.shape[1]

    def starts(shape, block):
        row = lax.broadcasted_iota(jnp.int32, shape, 0) + block * BLOCK
        begin, end = jnp.zeros(shape, jnp.int32), 0
        for i in range(SEQUENCES):
            length = lengths(i)
            end = end + length
            begin += jnp.where(row >= end, length, 0)
        return row, begin

    for block in range(pack_rows // BLOCK):
        here = slice(block * BLOCK, (block + 1) * BLOCK)
        target = pack * pack_rows + block * BLOCK + lax.broadcasted_iota(jnp.int32, (BLOCK, total), 0)
        chosen = jnp.where(perm[0] == target, 1.0, 0.0).astype(bf16)
        got = dot(chosen, four[0])
        row, begin = starts((BLOCK, width), block)
        angle = (row - begin).astype(f32) * freq[...]
        cos, sin = jnp.cos(angle), jnp.sin(angle) * sign[...]
        cos_v[here, :] = cos
        sin_v[here, :] = sin
        for c in range(2):
            at = slice(c * width, (c + 1) * width)
            part = got[:, at]
            laid[here, at] = (part * cos + swap_rotary(part) * sin).astype(bf16)
        laid[here, 2 * width :] = got[:, 2 * width :].astype(bf16)
    gk[...] = jnp.zeros_like(gk)
    gv[...] = jnp.zeros_like(gv)
    for block in range(pack_rows // BLOCK):
        low = max(0, block * BLOCK - SPAN)
        high = (block + 1) * BLOCK
        here = slice(block * BLOCK, high)
        keys = laid[low:high, width : 2 * width]
        values = laid[low:high, 2 * width : 3 * width]
        row, begin = starts((BLOCK, high - low), block)
        column = lax.broadcasted_iota(jnp.int32, (BLOCK, high - low), 1) + low
        allowed = (column >= begin) & (column <= row)
        attended = None
        for head in range(2):
            mine = (lane // 64) == head
            query = jnp.where(mine, laid[here, 0:width], 0)
            grad = jnp.where(mine, laid[here, 3 * width : 4 * width], 0)
            key = jnp.where(mine, keys, 0)
            value = jnp.where(mine, values, 0)
            scores = jnp.where(allowed, dot(query, key, NT) * scale, NEG_FILL)
            peak = jnp.max(scores, axis=1, keepdims=True)
            weights = jnp.exp(scores - peak)
            weights = weights * (1.0 / jnp.sum(weights, axis=1, keepdims=True))
            weights_b = weights.astype(bf16)
            out = dot(weights_b, value)
            attended = out if attended is None else attended + out
            delta = jnp.sum(grad.astype(f32) * out, axis=1, keepdims=True)
            inner = dot(grad, value, NT)
            grad_scores = (weights * (inner - delta)).astype(bf16)
            part = dot(grad_scores, key)
            if head == 0:
                gq[here, :] = part
            else:
                gq[here, :] += part
            gk[low:high, :] += dot(grad_scores, query, TN)
            gv[low:high, :] += dot(weights_b, grad, TN)
        back_ref[here, 0:width] = attended.astype(bf16)
    for c, ref in ((1, gq), (2, gk)):
        grads = ref[...] * scale
        turned = grads * cos_v[...] - swap_rotary(grads) * sin_v[...]
        back_ref[:, c * width : (c + 1) * width] = turned.astype(bf16)
    back_ref[:, 3 * width :] = gv[...].astype(bf16)


def heads_kernel(
    packs, all_packs, lengths, four, perm, freq, sign, normed, cot, g_1, g_2,
    back_out, g_d, g_q, qkv_sum, j_1, j_2, b_q, b_d,
    held, laid, gq, gk, gv, cos_v, sin_v, acc_d, acc_q, bring_send, bring_recv, *join_sem,
):
    step = pl.program_id(0)
    last = pl.num_programs(0) - 1
    gather = Join([(g_1, 0, 1, "x"), (g_2, 1, 0, "l")], (j_1, j_2), *join_sem)
    f32, bf16 = jnp.float32, jnp.bfloat16

    @pl.when(step == 0)
    def _():
        greet([(d, True) for d in gather.device.values()])
        gather.bring()
        gather.offer("x")
        gather.offer("l")
        gather.keep()
        acc_d[...] = jnp.zeros_like(acc_d)
        acc_q[...] = jnp.zeros_like(acc_q)
        qkv_sum[...] = jnp.zeros_like(qkv_sum)

    @pl.when(step == all_packs - 1)
    def _():
        gather.far(0)

    @pl.when(step == all_packs)
    def _():
        gather.brought("x", "l")

    @pl.when(step < all_packs)
    def _():
        attend_pack(
            lax.rem(step, packs), four, perm, lambda i: lengths[step, i], freq, sign,
            held.at[step], laid, gq, gk, gv, cos_v, sin_v,
        )

    @pl.when(step >= all_packs)
    def _():
        size, total = normed.shape[1], four.shape[1]
        narrow = acc_d.shape[0]
        per = total // size
        pack_rows = held.shape[1]
        first = (step - all_packs) // per * packs
        at = pl.ds(pl.multiple_of(lax.rem(step - all_packs, per) * size, size), size)
        line = perm[0, :, at]
        row = lax.broadcasted_iota(jnp.int32, (pack_rows, size), 0)
        back = None
        for k in range(packs):
            chosen = jnp.where(line == row + k * pack_rows, 1.0, 0.0).astype(bf16)
            part = dot(chosen, held[first + k], TN)
            back = part if back is None else back + part
        back = back.astype(bf16)
        back_out[0] = back
        grads = back[:, narrow:]
        acc_d[...] += dot(back[:, :narrow], cot[0], TN)
        acc_q[...] += dot(normed[0], grads, TN)
        qkv_sum[...] += jnp.sum(grads.astype(f32), axis=0, keepdims=True)

    @pl.when(step == last)
    def _():
        narrow = acc_d.shape[0]
        g_d[...] = acc_d[...].astype(bf16)
        for c in range(3):
            g_q[c] = acc_q[:, c * narrow : (c + 1) * narrow].astype(bf16)
        half = acc_q.shape[0] // 2
        other = pl.ds(pl.multiple_of((1 - gather.y) * half, half), half)
        copies = []
        for i, (source, target) in enumerate(((g_q.at[:, other], b_q), (g_d.at[:, other], b_d))):
            copy = pltpu.make_async_remote_copy(
                src_ref=source, dst_ref=target, send_sem=bring_send.at[i], recv_sem=bring_recv.at[i],
                device_id=gather.device["y"], device_id_type=MESH,
            )
            copy.start()
            copies.append(copy)
        gather.far(1)
        gather.end()
        for copy in copies:
            copy.wait()


def heads(lengths, four, permutation, normed, all_rows, g_1, g_2, packs, size):
    micro, total, wide = four.shape
    pack_rows = total // packs
    width = wide // 4
    deep = normed.shape[2]
    all_packs = micro * packs
    per = total // size
    lane = jnp.arange(width, dtype=jnp.int32) % 64
    power = ROPE_BASE ** (-2.0 * (lane % (ROT // 2)).astype(jnp.float32) / ROT)
    freq = jnp.where(lane < ROT, power, 0.0)[None, :]
    sign = jnp.where(lane < ROT // 2, -1.0, 1.0)[None, :]

    def by_micro(*s, after=False):
        def index(i):
            if after:
                i = jnp.where(i < all_packs, i // packs, (i - all_packs) // per)
            else:
                i = jnp.minimum(i, all_packs - 1) // packs
            return (i, 0, 0)

        return pl.BlockSpec((1,) + s, index)

    def block(w, skip=0):
        def index(i):
            n = jnp.maximum(i - all_packs, 0)
            return (n // per + skip, lax.rem(n, per), 0)

        return pl.BlockSpec((1, size, w), index)

    def fixed(*s):
        return pl.BlockSpec(s, lambda i: (0,) * len(s))

    any_ = pl.BlockSpec(memory_space=pl.ANY)
    plane = pltpu.VMEM((pack_rows, width), jnp.float32)
    return pl.pallas_call(
        partial(heads_kernel, packs, all_packs),
        grid=(all_packs + micro * per,),
        out_shape=[
            jax.ShapeDtypeStruct(four.shape, jnp.bfloat16),
            jax.ShapeDtypeStruct((width, deep), jnp.bfloat16),
            jax.ShapeDtypeStruct((3, deep, width), jnp.bfloat16),
            jax.ShapeDtypeStruct((1, 3 * width), jnp.float32),
            jax.ShapeDtypeStruct((deep // 2, g_1.shape[1] * 8), g_1.dtype),
            jax.ShapeDtypeStruct((g_2.shape[0] * 8, deep // 2), g_2.dtype),
            jax.ShapeDtypeStruct((3, deep // 2, width), jnp.bfloat16),
            jax.ShapeDtypeStruct((width, deep // 2), jnp.bfloat16),
        ],
        in_specs=[
            pl.BlockSpec(memory_space=pltpu.SMEM),
            by_micro(total, wide),
            by_micro(1, total, after=True),
            fixed(1, width),
            fixed(1, width),
            block(deep),
            block(deep, micro),
            any_,
            any_,
        ],
        out_specs=[
            block(wide), fixed(width, deep), fixed(3, deep, width), fixed(1, 3 * width),
            any_, any_, any_, any_,
        ],
        scratch_shapes=[
            pltpu.VMEM((all_packs, pack_rows, wide), jnp.bfloat16),
            pltpu.VMEM((pack_rows, wide), jnp.bfloat16),
        ]
        + [plane] * 5
        + [pltpu.VMEM((width, deep), jnp.float32), pltpu.VMEM((deep, 3 * width), jnp.float32)]
        + [pltpu.SemaphoreType.DMA((2,))] * 2
        + join_sems(2),
        compiler_params=pltpu.CompilerParams(
            collective_id=1, has_side_effects=True, vmem_limit_bytes=56 << 20
        ),
        name="heads",
    )(
        lengths.reshape(all_packs, -1), four, permutation[:, None, :], freq, sign, normed, all_rows, g_1, g_2,
    )


def widen_kernel(*refs):
    half = len(refs) // 2
    for source, target in zip(refs[:half], refs[half:]):
        target[...] = source[...].astype(jnp.float32)


def widen(values, steps):
    def block(value):
        return pl.BlockSpec((value.shape[0] // steps, value.shape[1]), lambda i: (i, 0))

    return pl.pallas_call(
        widen_kernel,
        grid=(steps,),
        out_shape=[jax.ShapeDtypeStruct(v.shape, jnp.float32) for v in values],
        in_specs=[block(v) for v in values],
        out_specs=[block(v) for v in values],
        compiler_params=pltpu.CompilerParams(vmem_limit_bytes=56 << 20),
        name="widen",
    )(*values)


def fast_body(
    tokens, cotangent, lengths, permutation, ln_gain, ln_bias, qkv_weight, qkv_bias,
    dense_weight, dense_bias, fc1_weight, fc1_bias, fc2_weight, fc2_bias,
):
    y, h, l, x, t = place()
    f32 = jnp.float32
    micro, rows, share = tokens.shape
    width = share * 2
    total = rows * 16
    pack_rows = rows * 8
    packs = total // pack_rows
    narrow = dense_weight.shape[0] // 8
    flat = jnp.concatenate([a.reshape(-1, 128) for a in (ln_gain, ln_bias, dense_bias, fc2_bias)])
    turned = qkv_bias.reshape(24, 2, 1, qkv_bias.shape[2])
    at_y = jnp.arange(2)[None, None, :, None] == y
    turned = jnp.where(at_y, turned, jnp.zeros_like(turned)).reshape(24, 128)
    small = jnp.concatenate([flat, turned, fc1_bias])
    small = jnp.pad(small, ((0, SMALL_ROWS - small.shape[0]), (0, 0)))
    own_rows = jnp.concatenate([tokens, cotangent])
    (
        all_rows, w_q, w_d, w_1, w_2, small, normed, activ, grad_pre, four, g_w1, g_w2, cot_sum, pre_sum,
    ) = spread(
        own_rows, qkv_weight.transpose(1, 0, 2), dense_weight, fc1_weight, fc2_weight, small
    )
    all_rows = all_rows.reshape(2 * micro, total, width)
    small = small.reshape(2, -1).astype(f32)
    gain = small[:, 0:share].reshape(1, width)
    out_shift = (small[:, 2 * share : 3 * share] + small[:, 3 * share : 4 * share]).reshape(1, width)

    back, g_wd, g_wq, qkv_sum, j_1, j_2, b_q, b_d = heads(
        lengths, four, permutation, normed, all_rows, g_w1, g_w2, packs, 4 * rows
    )
    g_bias = jnp.pad(jnp.concatenate([qkv_sum, pre_sum], 1), ((0, 7), (0, 0)))
    layer_out, grad_tokens, g_ln, j_q, j_d, j_b = fold(
        activ, grad_pre, back, all_rows, g_wq, g_wd, g_bias, b_q, b_d, cotangent, w_1, w_2, w_q, w_d, gain, out_shift
    )
    g_bias = j_b.reshape(8, 8, -1)[:, 0]
    g_qb = g_bias[:, : 3 * narrow].reshape(8, 3, narrow).transpose(1, 0, 2).reshape(3, -1, 64)
    g_qb = lax.dynamic_slice_in_dim(g_qb, y * qkv_bias.shape[2], qkv_bias.shape[2], 2)
    g_fb = g_bias[:, 3 * narrow :].reshape(fc1_bias.shape[0], -1)
    g_fb = lax.dynamic_slice_in_dim(g_fb, y * fc1_bias.shape[1], fc1_bias.shape[1], 1)
    cot_sum = lax.dynamic_slice_in_dim(cot_sum[0], y * share, share, 0)
    j_1, j_2, j_q, j_d = widen([j_1, j_2, j_q.reshape(3 * share, share), j_d], 8)
    j_q = j_q.reshape(3, share, share)
    return (
        layer_out,
        grad_tokens,
        g_ln[0],
        g_ln[1],
        j_q.transpose(1, 0, 2),
        g_qb,
        j_d,
        cot_sum,
        j_1,
        g_fb,
        j_2,
        cot_sum,
    )


def fast_solution(mesh):
    small_mesh = Mesh(mesh.devices.reshape(2, 2, 2, 2, 2), AXES)
    rows = P(None, ("y", "h", "l", "x"), "t")
    weights = (
        P("y"), P("y"), P("y", None, "t"), P(None, "t", "y"), P("t", "y"), P("y"), P("y", "t"),
        P("t", "y"), P("t", "y"), P("y"),
    )
    return jax.shard_map(
        fast_body,
        mesh=small_mesh,
        in_specs=(rows, rows, P(), P()) + weights,
        out_specs=(rows, rows) + weights,
        check_vma=False,
    )


def solution(mesh):
    if fits(mesh):
        return fast_solution(mesh)
    in_specs = (
        P(None, (FS, CT), TE),
        P(None, (FS, CT), TE),
        P(),
        P(),
        P(FS),
        P(FS),
        P(FS, None, TE),
        P(None, TE, FS),
        P(TE, FS),
        P(FS),
        P(FS, TE),
        P(TE, FS),
        P(TE, FS),
        P(FS),
    )
    out_specs = (
        P(None, (FS, CT), TE),
        P(None, (FS, CT), TE),
        P(FS),
        P(FS),
        P(FS, None, TE),
        P(None, TE, FS),
        P(TE, FS),
        P(FS),
        P(FS, TE),
        P(TE, FS),
        P(TE, FS),
        P(FS),
    )
    return jax.shard_map(body, mesh=mesh, in_specs=in_specs, out_specs=out_specs, check_vma=False)
```
